32 devices in a mesh: ctx: 8 (over y, x, core), fsdp: 4 (over z).
Axes of the slice: x: 2, y: 2, z: 4, core: 2. Of those that a mesh axis runs over, the one named last changes fastest.
Arguments:
- tokens: bfloat16 [4, 1024, 1600], P('fsdp', 'ctx'), may hold values from -6 to 6
- cotangent: bfloat16 [4, 1024, 1600], P('fsdp', 'ctx'), may hold values from -6 to 6
- deal_table: int32 [8], replicated, may hold values from 0 to 7, each once
- norm_gain: bfloat16 [1600], P('fsdp'), may hold values from 0.5 to 1.5
- query_weight: bfloat16 [1600, 1600], P('fsdp'), may hold values from -0.15625 to 0.15625
- key_weight: bfloat16 [1600, 320], P('fsdp'), may hold values from -0.15625 to 0.15625
- value_weight: bfloat16 [1600, 320], P('fsdp'), may hold values from -0.15625 to 0.15625
- attention_out: bfloat16 [1600, 1600], P('fsdp'), may hold values from -0.15625 to 0.15625
- attention_gain: bfloat16 [1600], P('fsdp'), may hold values from 0.5 to 1.5
- mixer_in: bfloat16 [1600, 6400], P('fsdp'), may hold values from -0.15625 to 0.15625
- filter_kernel: bfloat16 [4, 3200], P(None, 'fsdp'), may hold values from -3 to 3
- filter_bias: bfloat16 [3200], P('fsdp'), may hold values from -3 to 3
- select_weight: bfloat16 [3200, 132], P('fsdp'), may hold values from -0.109375 to 0.109375
- step_weight: bfloat16 [100, 3200], P(None, 'fsdp'), may hold values from -0.625 to 0.625
- step_bias: bfloat16 [3200], P('fsdp'), may hold values from -8 to -5
- decay_log: bfloat16 [3200, 16], P('fsdp'), may hold values from -4 to 3
- skip_gain: bfloat16 [3200], P('fsdp'), may hold values from 0.049804688 to 0.5
- mixer_gain: bfloat16 [3200], P('fsdp'), may hold values from 0.5 to 1.5
- mixer_out: bfloat16 [3200, 1600], P('fsdp'), may hold values from -0.109375 to 0.109375
- post_gain: bfloat16 [1600], P('fsdp'), may hold values from 0.5 to 1.5
- gate_weight: bfloat16 [1600, 5504], P('fsdp'), may hold values from -0.15625 to 0.15625
- up_weight: bfloat16 [1600, 5504], P('fsdp'), may hold values from -0.15625 to 0.15625
- down_weight: bfloat16 [5504, 1600], P('fsdp'), may hold values from -0.078125 to 0.078125
Outputs:
- layer_out: bfloat16 [4, 1024, 1600], P('fsdp', 'ctx')
- tokens_grad: bfloat16 [4, 1024, 1600], P('fsdp', 'ctx')
- norm_gain_grad: float32 [1600], P('fsdp')
- query_grad: float32 [1600, 1600], P('fsdp')
- key_grad: float32 [1600, 320], P('fsdp')
- value_grad: float32 [1600, 320], P('fsdp')
- attention_out_grad: float32 [1600, 1600], P('fsdp')
- attention_gain_grad: float32 [1600], P('fsdp')
- mixer_in_grad: float32 [1600, 6400], P('fsdp')
- filter_kernel_grad: float32 [4, 3200], P(None, 'fsdp')
- filter_bias_grad: float32 [3200], P('fsdp')
- select_grad: float32 [3200, 132], P('fsdp')
- step_weight_grad: float32 [100, 3200], P(None, 'fsdp')
- step_bias_grad: float32 [3200], P('fsdp')
- decay_log_grad: float32 [3200, 16], P('fsdp')
- skip_gain_grad: float32 [3200], P('fsdp')
- mixer_gain_grad: float32 [3200], P('fsdp')
- mixer_out_grad: float32 [3200, 1600], P('fsdp')
- post_gain_grad: float32 [1600], P('fsdp')
- gate_grad: float32 [1600, 5504], P('fsdp')
- up_grad: float32 [1600, 5504], P('fsdp')
- down_grad: float32 [5504, 1600], P('fsdp')
The draws below stay inside these ranges and needn't reach their ends.
Inputs may be any that keep to these rules, and one draw needn't show every extreme that they name: Each value appears once; ctx index i holds block deal_table[i] and block 15 - deal_table[i] of every sequence of its fsdp index.
All inputs are finite; a program needn't handle non-finite values.
Results may differ from the reference program's by a relative error of at most 0.023.
Values may be sent and summed in bfloat16 or wider, within the bound.
No kernel may reach another device: no remote copies, remote signals or barrier semaphores. Data moves between devices by JAX's collectives and lax.ppermute only.
A program may use at most 512 MiB of HBM per device.

```python
import math
import jax
import jax.numpy as jnp
from jax import lax

D = 1600
HEADS = 25
KV_HEADS = 5
HEAD_DIM = 64
DI = 3200
NS = 16
CONV = 4
RANK = 100
FF = 5504
BLK = 64
PAIRS = 8
LEN = 1024
SEQS = 4


def levels(rng, dims, shards, smallest, high):
    loudness = 1.0
    for axis_at, parts in shards:
        heights = jax.random.uniform(jax.random.fold_in(jax.random.fold_in(rng, 6), axis_at), (parts,), jnp.float32, smallest / len(shards), high / len(shards))
        loudness = loudness * jnp.repeat(jnp.exp(heights), dims[axis_at] // parts).reshape((-1,) + (1,) * (len(dims) - 1 - axis_at))
    return loudness


def gaussian(stream_key, shape, deviation, most, split=(), held_as=jnp.bfloat16):
    values = jax.random.normal(stream_key, shape, jnp.float32) * deviation
    if len(split) > 0:
        values = levels(stream_key, shape, split, -0.22, 0.18) * values
    return jnp.clip(values, min=-most, max=most).astype(held_as)


def setup_inputs(seed: int = 0) -> dict:
    keys = jax.random.split(jax.random.key(seed), 24)
    return {
        "tokens": gaussian(keys[0], (SEQS, LEN, D), 1.0, 6.0, ((0, 4), (1, 8))),
        "cotangent": gaussian(keys[1], (SEQS, LEN, D), 1.0, 6.0, ((0, 4), (1, 8))),
        "deal_table": jax.random.permutation(keys[2], PAIRS).astype(jnp.int32),
        "norm_gain": jnp.clip(1.0 + 0.1 * jax.random.normal(keys[3], (D,), jnp.float32), 0.5, 1.5).astype(jnp.bfloat16),
        "query_weight": gaussian(keys[4], (D, HEADS * HEAD_DIM), D ** -0.5, 0.15625, ((0, 4),)),
        "key_weight": gaussian(keys[5], (D, KV_HEADS * HEAD_DIM), D ** -0.5, 0.15625, ((0, 4),)),
        "value_weight": gaussian(keys[6], (D, KV_HEADS * HEAD_DIM), D ** -0.5, 0.15625, ((0, 4),)),
        "attention_out": gaussian(keys[7], (HEADS * HEAD_DIM, D), (HEADS * HEAD_DIM) ** -0.5, 0.15625, ((0, 4),)),
        "attention_gain": jnp.clip(1.0 + 0.1 * jax.random.normal(keys[8], (HEADS * HEAD_DIM,), jnp.float32), 0.5, 1.5).astype(jnp.bfloat16),
        "mixer_in": gaussian(keys[9], (D, 2 * DI), D ** -0.5, 0.15625, ((0, 4),)),
        "filter_kernel": gaussian(keys[10], (CONV, DI), CONV ** -0.5, 3.0, ((1, 4),)),
        "filter_bias": gaussian(keys[11], (DI,), 0.5, 3.0, ((0, 4),)),
        "select_weight": gaussian(keys[12], (DI, RANK + 2 * NS), DI ** -0.5, 0.109375, ((0, 4),)),
        "step_weight": gaussian(keys[13], (RANK, DI), RANK ** -0.5, 0.625, ((1, 4),)),
        "step_bias": jnp.clip(-8.0 + 3.0 * jax.random.uniform(keys[14], (DI,), jnp.float32) ** levels(keys[14], (DI,), ((0, 4),), -0.2, 0.2), -8.0, -5.0).astype(jnp.bfloat16),
        "decay_log": jnp.clip(-4.0 + 7.0 * jax.random.uniform(keys[15], (DI, NS), jnp.float32) ** levels(keys[15], (DI, NS), ((0, 4),), -0.2, 0.2), -4.0, 3.0).astype(jnp.bfloat16),
        "skip_gain": jnp.clip(jnp.exp(math.log(0.5) - 2.306499 * jax.random.uniform(keys[16], (DI,), jnp.float32) ** levels(keys[16], (DI,), ((0, 4),), -0.2, 0.2)), 0.049804688, 0.5).astype(jnp.bfloat16),
        "mixer_gain": jnp.clip(1.0 + 0.1 * jax.random.normal(keys[17], (DI,), jnp.float32), 0.5, 1.5).astype(jnp.bfloat16),
        "mixer_out": gaussian(keys[18], (DI, D), DI ** -0.5, 0.109375, ((0, 4),)),
        "post_gain": jnp.clip(1.0 + 0.1 * jax.random.normal(keys[19], (D,), jnp.float32), 0.5, 1.5).astype(jnp.bfloat16),
        "gate_weight": gaussian(keys[20], (D, FF), D ** -0.5, 0.15625, ((0, 4),)),
        "up_weight": gaussian(keys[21], (D, FF), D ** -0.5, 0.15625, ((0, 4),)),
        "down_weight": gaussian(keys[22], (FF, D), FF ** -0.5, 0.078125, ((0, 4),)),
    }


EPS = 1e-05
HIGH = lax.Precision.HIGHEST
NEG = -1e+30

@jax.custom_vjp
def low(v):
    return lax.optimization_barrier(v.astype(jnp.bfloat16)).astype(jnp.float32)

@jax.custom_vjp
def low_back(v):
    return v

def low_keep(v):
    return (low(v), None)

def low_pass(kept, grad):
    return (grad,)

def back_keep(v):
    return (v, None)

def back_low(kept, grad):
    return (low(grad),)
low.defvjp(low_keep, low_pass)
low_back.defvjp(back_keep, back_low)

def round_both(values):
    return low(low_back(values))

def product(left, right):
    return jnp.dot(left, right, precision=HIGH, preferred_element_type=jnp.float32)

def rms_norm(values, gain):
    return values * lax.rsqrt(lax.optimization_barrier(jnp.mean(values * values, axis=-1, keepdims=True)) + EPS) * gain

def silu(values):
    return values * jax.nn.sigmoid(values)

def softplus(values):
    return jnp.maximum(values, 0.0) + jnp.log1p(jnp.exp(-jnp.abs(values)))

def attention(query_rows, key_rows, value_rows):
    length = query_rows.shape[0]
    group_size = HEADS // KV_HEADS
    width = min(512, length)
    query_heads = query_rows.reshape(length // width, width, KV_HEADS, group_size, HEAD_DIM)
    key_heads = key_rows.reshape(length, KV_HEADS, HEAD_DIM)
    value_heads = value_rows.reshape(length, KV_HEADS, HEAD_DIM)
    key_pos = jnp.arange(length, dtype=jnp.int32)
    score_scale = 1.0 / math.sqrt(HEAD_DIM)

    @jax.checkpoint
    def one_block(inputs):
        block_query, first = inputs
        scores = jnp.einsum('qkgd,tkd->kgqt', block_query, key_heads, precision=HIGH) * score_scale
        query_pos = first + jnp.arange(width, dtype=jnp.int32)
        allowed = key_pos[None, :] <= query_pos[:, None]
        scores = low_back(jnp.where(allowed, scores, NEG))
        peak = lax.optimization_barrier(jnp.max(scores, axis=-1, keepdims=True))
        weights = jnp.exp(scores - peak)
        probability = low(weights / lax.optimization_barrier(jnp.sum(weights, axis=-1, keepdims=True)))
        result = jnp.einsum('kgqt,tkd->qkgd', probability, value_heads, precision=HIGH)
        return result.reshape(width, HEADS * HEAD_DIM)
    starts = jnp.arange(length // width, dtype=jnp.int32) * width
    return lax.map(one_block, (query_heads, starts)).reshape(length, HEADS * HEAD_DIM)

def selective_scan(rate, inputs, write_vec, read_vec, decay_mat):
    length = rate.shape[0]
    count = length // BLK

    def blocked(values):
        return values.reshape(count, BLK, values.shape[-1])

    def advance(state, token):
        step_rate, step_input, step_write, step_read = token
        state = jnp.exp(step_rate[:, None] * decay_mat) * state + (step_rate * step_input)[:, None] * step_write[None, :]
        return (state, lax.optimization_barrier(jnp.sum(state * step_read[None, :], axis=-1)))

    @jax.checkpoint
    def one_block(state, pieces):
        return lax.scan(advance, state, pieces)
    start = jnp.zeros((DI, NS), jnp.float32)
    final, outputs = lax.scan(one_block, start, (blocked(rate), blocked(inputs), blocked(write_vec), blocked(read_vec)))
    return outputs.reshape(length, DI)

def layer(inputs_now, weights):
    norm_gain, query_weight, key_weight, value_weight, attention_out, attention_gain, mixer_in, filter_kernel, filter_bias, select_weight, step_weight, step_bias, decay_log, skip_gain, mixer_gain, mixer_out, post_gain, gate_weight, up_weight, down_weight = weights
    length = inputs_now.shape[0]
    hidden = low(rms_norm(inputs_now, norm_gain))
    query_rows = round_both(product(hidden, query_weight))
    key_rows = round_both(product(hidden, key_weight))
    value_rows = round_both(product(hidden, value_weight))
    attended = low_back(attention(query_rows, key_rows, value_rows))
    attend_normed = low(rms_norm(attended, attention_gain))
    attend_branch = low_back(product(attend_normed, attention_out))
    projected = low_back(product(hidden, mixer_in))
    inner = low(projected[:, :DI])
    gate_z = projected[:, DI:]
    padded = jnp.concatenate([jnp.zeros((CONV - 1, DI), jnp.float32), inner], axis=0)
    total = filter_bias
    for offset in range(CONV):
        total = total + filter_kernel[offset] * padded[offset:offset + length]
    mixed_input = low(silu(total))
    selected = low_back(product(mixed_input, select_weight))
    rank_low = low(selected[:, :RANK])
    write_vec = selected[:, RANK:RANK + NS]
    read_vec = selected[:, RANK + NS:]
    rate = softplus(low_back(product(rank_low, step_weight)) + step_bias)
    scanned = selective_scan(rate, mixed_input, write_vec, read_vec, -jnp.exp(decay_log))
    gated = (scanned + skip_gain * mixed_input) * silu(gate_z)
    mixer_normed = low(rms_norm(gated, mixer_gain))
    mixer_branch = low_back(product(mixer_normed, mixer_out))
    mixed = inputs_now + 0.5 * (attend_branch + mixer_branch)
    post = low(rms_norm(mixed, post_gain))
    gate_now = low_back(product(post, gate_weight))
    up_now = low_back(product(post, up_weight))
    ffn_hidden = low(silu(gate_now) * up_now)
    return mixed + low_back(product(ffn_hidden, down_weight))

def reference(tokens, cotangent, deal_table, norm_gain, query_weight, key_weight, value_weight, attention_out, attention_gain, mixer_in, filter_kernel, filter_bias, select_weight, step_weight, step_bias, decay_log, skip_gain, mixer_gain, mixer_out, post_gain, gate_weight, up_weight, down_weight):
    weights = tuple((item.astype(jnp.float32) for item in (norm_gain, query_weight, key_weight, value_weight, attention_out, attention_gain, mixer_in, filter_kernel, filter_bias, select_weight, step_weight, step_bias, decay_log, skip_gain, mixer_gain, mixer_out, post_gain, gate_weight, up_weight, down_weight)))
    blocks = 2 * PAIRS
    slot_blocks = jnp.stack([deal_table, blocks - 1 - deal_table], axis=1).reshape(blocks).astype(jnp.int32)
    slot_order = jnp.argsort(slot_blocks).astype(jnp.int32)

    def natural(values):
        return values.reshape(blocks, BLK, D)[slot_order].reshape(LEN, D)

    def dealt(values):
        return values.reshape(blocks, BLK, D)[slot_blocks].reshape(LEN, D)

    def one_sequence(totals, pieces):
        seq_tokens, seq_cotangent = pieces
        inputs_now = natural(seq_tokens.astype(jnp.float32))
        upstream = natural(seq_cotangent.astype(jnp.float32))
        result, pull = jax.vjp(layer, inputs_now, weights)
        inputs_grad, weight_grads = pull(upstream)
        totals = jax.tree.map(lambda left, right: left + right, totals, weight_grads)
        return (totals, (dealt(result).astype(jnp.bfloat16), dealt(inputs_grad).astype(jnp.bfloat16)))
    zeros = tuple((jnp.zeros(item.shape, jnp.float32) for item in weights))
    totals, (outputs, grads) = lax.scan(one_sequence, zeros, (tokens, cotangent))
    return (outputs, grads, totals[0], totals[1], totals[2], totals[3], totals[4], totals[5], totals[6], totals[7], totals[8], totals[9], totals[10], totals[11], totals[12], totals[13], totals[14], totals[15], totals[16], totals[17], totals[18], totals[19])
```

```python
import math

import jax
import jax.numpy as jnp
from jax import lax
from jax.experimental import pallas as pl
from jax.experimental.pallas import tpu as pltpu
from jax.sharding import PartitionSpec as P

HEADS = 25
KV_HEADS = 5
HEAD_DIM = 64
GROUP = HEADS // KV_HEADS
CONV = 4
RANK = 100
NS = 16
EPS = 1e-05
NEG = -1e30
SCALE = 1.0 / math.sqrt(HEAD_DIM)
STEP = 16
VMEM = 56 * 1024 * 1024
SIDE = 64
bf16 = jnp.bfloat16
f32 = jnp.float32


def up_to(value, unit):
    return -(-value // unit) * unit


def dot(left, right, contract=((1,), (0,)), precision=None):
    return lax.dot_general(
        left, right, (contract, ((), ())), preferred_element_type=f32, precision=precision
    )


def dot_tn(left, right):
    return dot(left, right, ((0,), (0,)))


def dot_nt(left, right):
    return dot(left, right, ((1,), (1,)))


def pad_to(values, axis, size):
    widths = [(0, 0)] * values.ndim
    widths[axis] = (0, size - values.shape[axis])
    return jnp.pad(values, widths)


def masks(size):
    return list(range(0, size, 2)) + list(range(1, size, 2))


def swap(values, mask, size):
    return lax.ppermute(values, "ctx", [(i, i ^ mask) for i in range(size)])


def gather_ctx(values, size):
    near = jnp.concatenate([values] + [swap(values, m, size) for m in range(2, size, 2)])
    return jnp.concatenate([near, swap(near, 1, size)])


def scatter_ctx(values, size):
    parts = values.reshape((size, values.shape[0] // size) + values.shape[1:])
    half = size // 2
    got = swap(parts[half:], 1, size)
    near = parts[:half].astype(f32) + got.astype(f32)
    sent = near.astype(bf16)
    total = near[0]
    for k in range(1, half):
        total = total + swap(sent[k], 2 * k, size).astype(f32)
    return total


def swap_aligned(values, mask, size):
    order = masks(size)
    got = swap(values, mask, size).reshape((size, values.shape[0] // size) + values.shape[1:])
    picked = [got[order.index(m ^ mask)] for m in order]
    return jnp.concatenate(picked).astype(f32)


def sum_ctx(values, size):
    near = (values.astype(f32) + swap_aligned(values, 1, size)).astype(bf16)
    total = near.astype(f32)
    for m in range(2, size, 2):
        total = total + swap_aligned(near, m, size)
    return total


def after(values, *earlier):
    return lax.optimization_barrier((values,) + earlier)[0]


def block_call(body, order, count, ins, outs, scratch, name):
    return pl.pallas_call(
        body,
        grid_spec=pltpu.PrefetchScalarGridSpec(
            num_scalar_prefetch=1,
            grid=(count,),
            in_specs=[spec for _, spec in ins],
            out_specs=[spec for _, spec in outs],
            scratch_shapes=scratch,
        ),
        out_shape=[shape for shape, _ in outs],
        compiler_params=pltpu.CompilerParams(
            dimension_semantics=("arbitrary",), vmem_limit_bytes=VMEM
        ),
        name=name,
    )(order, *[value for value, _ in ins])


def whole(shape):
    zeros = (0,) * len(shape)
    return pl.BlockSpec(shape, lambda i, order: zeros)


def rows(block, width, pick):
    return pl.BlockSpec((block, width), lambda i, order: (order[pick(i)], 0))


def columns_at(block, width, pick, index):
    return pl.BlockSpec((block, width), lambda i, order: (order[pick(i)], index))


def leaf(shape, dtype):
    return jax.ShapeDtypeStruct(shape, dtype)


def filter_taps(ext, vecs, block):
    total = vecs[3:4, :]
    for j in range(CONV):
        total = total + vecs[4 + j : 5 + j, :] * ext[5 + j : 5 + j + block, :]
    return total


def filter_forward_body(block):
    def body(order, inner, vecs, select, mixed_o, selected_o, ext):
        step = pl.program_id(0)

        @pl.when(step == 0)
        def _():
            ext[0:8, :] = jnp.zeros((8, ext.shape[1]), f32)

        @pl.when(step > 0)
        def _():
            ext[0:8, :] = ext[block : block + 8, :]

        ext[8 : block + 8, :] = inner[...].astype(bf16).astype(f32)
        total = filter_taps(ext, vecs, block)
        mixed = (total * jax.nn.sigmoid(total)).astype(bf16)
        mixed_o[...] = mixed
        selected_o[...] = dot(mixed, select[...]).astype(bf16)

    return body


def rate_of(selected, step_weight, vecs):
    rank = selected[...].astype(bf16)
    raw = dot(rank, step_weight[...]) + vecs[0:1, :]
    rate = jnp.maximum(raw, 0.0) + jnp.log1p(jnp.exp(-jnp.abs(raw)))
    return rank, raw, rate


def scan_forward_body(block):
    def body(
        order, selected, sides, mixed, gate_z, step_weight, vecs, decay,
        scanned_o, starts_o, scaled_o, squares_o, state_s, rate_s, drive_s,
    ):
        @pl.when(pl.program_id(0) == 0)
        def _():
            state_s[...] = jnp.zeros_like(state_s)

        _, _, rate = rate_of(selected, step_weight, vecs)
        wide = mixed[...].astype(f32)
        rate_s[...] = rate
        drive_s[...] = rate * wide
        starts_o[0] = state_s[...]
        decay_mat = decay[...]

        def group(g, state):
            base = pl.multiple_of(g * STEP, STEP)
            rates = rate_s[pl.ds(base, STEP), :]
            drives = drive_s[pl.ds(base, STEP), :]
            side = sides[0, g]
            for j in range(STEP):
                state = (
                    jnp.exp(rates[j : j + 1, :] * decay_mat) * state
                    + drives[j : j + 1, :] * side[:NS, j : j + 1]
                )
                scanned_o[pl.ds(base + j, 1), :] = jnp.sum(
                    state * side[NS:, j : j + 1], axis=0, keepdims=True
                )
            return state

        state_s[...] = lax.fori_loop(0, block // STEP, group, state_s[...])
        gate = gate_z[...]
        gated = (scanned_o[...] + vecs[1:2, :] * wide) * (gate * jax.nn.sigmoid(gate))
        scaled_o[...] = (gated * vecs[2:3, :]).astype(bf16)
        squares_o[...] = jnp.broadcast_to(
            jnp.sum(gated * gated, axis=1, keepdims=True), squares_o.shape
        )

    return body


def scan_backward_body(block):
    def body(
        order, selected, sides, mixed, gate_z, scanned, grad_in, scalars, starts, step_weight, vecs, decay,
        normed_o, dgate_o, dmixed_o, draw_o, drank_o, dsides_o, vec_o, step_o, decay_o,
        lam_s, rate_s, drive_s, dscan_s, drate_s, pull_s, hist_s, factor_s, read_s, write_s,
    ):
        width = decay.shape[1]

        @pl.when(pl.program_id(0) == 0)
        def _():
            lam_s[...] = jnp.zeros_like(lam_s)
            vec_o[...] = jnp.zeros_like(vec_o)
            step_o[...] = jnp.zeros_like(step_o)
            decay_o[...] = jnp.zeros_like(decay_o)

        rank, raw, rate = rate_of(selected, step_weight, vecs)
        wide = mixed[...].astype(f32)
        rate_s[...] = rate
        drive_s[...] = rate * wide
        gate = gate_z[...]
        sig = jax.nn.sigmoid(gate)
        act = gate * sig
        before = scanned[...] + vecs[1:2, :] * wide
        gated = before * act
        norm = scalars[:, 2:3]
        centre = scalars[:, 3:4]
        grad = grad_in[...]
        gated_norm = gated * norm
        normed_o[...] = (gated_norm * vecs[2:3, :]).astype(bf16)
        dgated = norm * (vecs[2:3, :] * grad) - gated * centre
        dscan = dgated * act
        dscan_s[...] = dscan
        dgate_o[...] = (dgated * before * (sig * (1.0 + gate * (1.0 - sig)))).astype(bf16)
        vec_o[1:2, :] += jnp.sum(dscan * wide, axis=0, keepdims=True)
        vec_o[2:3, :] += jnp.sum(grad * gated_norm, axis=0, keepdims=True)
        decay_mat = decay[...]

        def forward(g, state):
            base = pl.multiple_of(g * STEP, STEP)
            rates = rate_s[pl.ds(base, STEP), :]
            drives = drive_s[pl.ds(base, STEP), :]
            side = sides[0, g]
            for j in range(STEP):
                factor = jnp.exp(rates[j : j + 1, :] * decay_mat)
                factor_s[base + j] = factor
                state = factor * state + drives[j : j + 1, :] * side[:NS, j : j + 1]
                hist_s[base + j + 1] = state
            return state

        hist_s[0] = starts[0]
        lax.fori_loop(0, block // STEP, forward, starts[0])

        def fold(values):
            total = values[:, 0:128]
            for at in range(128, width, 128):
                total = total + values[:, at : at + 128]
            return total

        def backward(i, carry):
            lam_in, decay_sum = carry
            g = block // STEP - 1 - i
            base = pl.multiple_of(g * STEP, STEP)
            rates = rate_s[pl.ds(base, STEP), :]
            drives = drive_s[pl.ds(base, STEP), :]
            dscans = dscan_s[pl.ds(base, STEP), :]
            side = sides[0, g]
            for j in range(STEP - 1, -1, -1):
                at = base + j
                row = dscans[j : j + 1, :]
                lam = lam_in + row * side[NS:, j : j + 1]
                read_s[pl.ds(at * NS, NS), :] = fold(hist_s[at + 1] * row)
                write_s[pl.ds(at * NS, NS), :] = fold(lam * drives[j : j + 1, :])
                pull = jnp.sum(lam * side[:NS, j : j + 1], axis=0, keepdims=True)
                lam_in = factor_s[at] * lam
                kept = lam_in * hist_s[at]
                decay_sum = decay_sum + rates[j : j + 1, :] * kept
                drate_s[pl.ds(at, 1), :] = jnp.sum(decay_mat * kept, axis=0, keepdims=True)
                pull_s[pl.ds(at, 1), :] = pull
            return (lam_in, decay_sum)

        lam, decay_sum = lax.fori_loop(
            0, block // STEP, backward, (lam_s[...], jnp.zeros_like(lam_s))
        )
        lam_s[...] = lam
        decay_o[...] += decay_sum * decay_mat
        pulled = pull_s[...]
        draw = (drate_s[...] + wide * pulled) * jax.nn.sigmoid(raw)
        vec_o[0:1, :] += jnp.sum(draw, axis=0, keepdims=True)
        low = draw.astype(bf16)
        draw_o[...] = low
        dmixed_o[...] = vecs[1:2, :] * dscan + rate * pulled
        drank_o[...] = dot_nt(low, step_weight[...])
        step_o[...] += dot_tn(rank, low)
        ones = jnp.ones((8, 128), f32)
        high = lax.Precision.HIGHEST
        dsides_o[0, 0] = dot(ones, write_s[...], ((1,), (1,)), high)
        dsides_o[0, 1] = dot(ones, read_s[...], ((1,), (1,)), high)

    return body


def filter_backward_body(block, count):
    def body(
        order, inner, inner_before, mixed, dmixed, dselected, select, vecs,
        dinner_o, select_o, vec_o, ext, ext_grad,
    ):
        step = pl.program_id(0)

        @pl.when(step == 0)
        def _():
            ext_grad[block : block + 8, :] = jnp.zeros((8, ext.shape[1]), f32)
            select_o[...] = jnp.zeros_like(select_o)
            vec_o[...] = jnp.zeros_like(vec_o)

        @pl.when(step > 0)
        def _():
            ext_grad[block : block + 8, :] = ext_grad[0:8, :]

        first = jnp.where(step == count - 1, 0.0, 1.0)
        ext[0:8, :] = inner_before[block - 8 :, :].astype(bf16).astype(f32) * first
        ext[8 : block + 8, :] = inner[...].astype(bf16).astype(f32)
        total = filter_taps(ext, vecs, block)
        sig = jax.nn.sigmoid(total)
        low = dselected[...]
        dmix = dmixed[...] + dot_nt(low, select[...])
        dfilt = dmix * (sig * (1.0 + total * (1.0 - sig)))
        ext_grad[0:block, :] = dfilt
        dinner = jnp.zeros_like(dfilt)
        vec_o[3:4, :] += jnp.sum(dfilt, axis=0, keepdims=True)
        for j in range(CONV):
            at = CONV - 1 - j
            dinner = dinner + vecs[4 + j : 5 + j, :] * ext_grad[at : at + block, :]
            vec_o[4 + j : 5 + j, :] += jnp.sum(
                dfilt * ext[5 + j : 5 + j + block, :], axis=0, keepdims=True
            )
        dinner_o[...] = dinner.astype(bf16)
        select_o[...] += dot_tn(low, mixed[...])

    return body


def half_mask(half):
    lane = lax.broadcasted_iota(jnp.int32, (1, 128), 1)
    return jnp.where((lane >= 64 * half) & (lane < 64 * half + 64), 1.0, 0.0)


def softmax_rows(query, key, allowed):
    scores = jnp.where(allowed, dot_nt(query, key) * SCALE, NEG)
    weights = jnp.exp(scores - jnp.max(scores, axis=-1, keepdims=True))
    return weights * (1.0 / jnp.sum(weights, axis=-1, keepdims=True))


def attention_forward_body(valid, query, key, value, query_pos, key_pos, gain, out_o, scaled_o, squares_o):
    allowed = key_pos[...] <= query_pos[...]
    squares = jnp.zeros((query.shape[0], 1), f32)
    for at in range(0, query.shape[1], 128):
        key_tile = key[:, at : at + 128]
        value_tile = value[:, at : at + 128]
        tile = jnp.zeros((query.shape[0], 128), f32)
        for half in range(2):
            mask = half_mask(half)
            part = query[:, at : at + 128] * mask.astype(bf16)
            probs = softmax_rows(part, key_tile, allowed).astype(bf16)
            live = valid[at // 64 + half].astype(f32)
            tile = tile + dot(probs, value_tile) * (mask * live)
        out_o[:, at : at + 128] = tile
        scaled_o[:, at : at + 128] = (tile * gain[:, at : at + 128]).astype(bf16)
        squares = squares + jnp.sum(tile * tile, axis=1, keepdims=True)
    squares_o[...] = jnp.broadcast_to(squares, squares_o.shape)


def attention_backward_body(
    valid, query, key, value, query_pos, key_pos, gain, out, grad_in, scalars,
    dquery_o, dkey_o, dvalue_o, normed_o, gain_o, dkey_s, dvalue_s,
):
    @pl.when(pl.program_id(0) == 0)
    def _():
        dkey_s[...] = jnp.zeros_like(dkey_s)
        dvalue_s[...] = jnp.zeros_like(dvalue_s)
        gain_o[...] = jnp.zeros_like(gain_o)

    allowed = key_pos[...] <= query_pos[...]
    norm = scalars[:, 0:1]
    centre = scalars[:, 1:2]
    for at in range(0, query.shape[1], 128):
        lanes = slice(at, at + 128)
        key_tile = key[:, lanes]
        value_tile = value[:, lanes]
        attended = out[:, lanes]
        grad = grad_in[:, lanes]
        normed = attended * norm
        normed_o[:, lanes] = (normed * gain[:, lanes]).astype(bf16)
        gain_o[0:1, lanes] += jnp.sum(grad * normed, axis=0, keepdims=True)
        dout = (norm * (gain[:, lanes] * grad) - attended * centre).astype(bf16)
        dquery = jnp.zeros(attended.shape, f32)
        dkey = jnp.zeros((key.shape[0], 128), f32)
        dvalue = jnp.zeros((key.shape[0], 128), f32)
        for half in range(2):
            mask = half_mask(half)
            part = query[:, lanes] * mask.astype(bf16)
            dpart = dout * mask.astype(bf16)
            probs = softmax_rows(part, key_tile, allowed)
            dprobs = dot_nt(dpart, value_tile)
            mean = jnp.sum(dprobs * probs, axis=-1, keepdims=True)
            dscores = (probs * (dprobs - mean)).astype(bf16)
            dvalue = dvalue + dot_tn(probs.astype(bf16), dpart)
            dquery = dquery + dot(dscores, key_tile) * (mask * SCALE)
            dkey = dkey + dot_tn(dscores, part) * SCALE
        dquery_o[:, lanes] = dquery.astype(bf16)
        dkey_s[:, lanes] += dkey
        dvalue_s[:, lanes] += dvalue

    @pl.when(pl.program_id(0) == pl.num_programs(0) - 1)
    def _():
        dkey_o[...] = dkey_s[...].astype(bf16)
        dvalue_o[...] = dvalue_s[...].astype(bf16)


def pack_body(groups, out_wide, width, piece):
    window = up_to(piece + 127, 128)

    def body(index, weight, out_o, acc):
        acc[...] = jnp.zeros_like(acc)
        for start, at in groups:
            source = start + index[0] * piece
            tile = jnp.minimum(source // 128, (width - window) // 128)
            base = pl.multiple_of(tile * 128, 128)
            low = at % 128
            span = up_to(low + piece, 128)
            row = lax.broadcasted_iota(jnp.int32, (window, span), 0)
            lane = lax.broadcasted_iota(jnp.int32, (window, span), 1) - low
            pick = (row - (source - base) == lane) & (lane >= 0) & (lane < piece)
            pick = jnp.where(pick, 1.0, 0.0).astype(bf16)
            acc[:, at - low : at - low + span] += dot(weight[:, pl.ds(base, window)], pick)
        out_o[...] = acc[...].astype(bf16)

    return body


def row_block(count):
    return 80 if count % 80 == 0 else count


def pack_columns(weight, index, groups, out_wide, piece, name):
    count, width = weight.shape
    block = row_block(count)
    return block_call(
        pack_body(groups, out_wide, width, piece),
        index,
        count // block,
        [(weight, pl.BlockSpec((block, width), lambda i, index: (i, 0)))],
        [
            (
                leaf((count, out_wide), bf16),
                pl.BlockSpec((block, out_wide), lambda i, index: (i, 0)),
            )
        ],
        [pltpu.VMEM((block, out_wide), f32)],
        name,
    )[0]


def unpack_columns(gathered, where, moves, widths, size, name):
    total, width = gathered.shape
    count = total // size
    block = row_block(count)

    def body(where, source, *outs):
        for index in range(size):
            values = source[where[index]].astype(f32)
            for out, first, stride, at, piece in moves:
                start = first + index * stride
                piece = min(piece, widths[out] - start)
                if piece > 0:
                    outs[out][:, start : start + piece] = values[:, at : at + piece]

    return block_call(
        body,
        where,
        count // block,
        [
            (
                gathered.reshape(size, count, width),
                pl.BlockSpec((size, block, width), lambda i, where: (0, i, 0)),
            )
        ],
        [
            (leaf((count, full), f32), pl.BlockSpec((block, full), lambda i, where: (i, 0)))
            for full in widths
        ],
        [],
        name,
    )


def unpack_rows(gathered, where, piece, size, name):
    total, width = gathered.shape
    lanes = 256

    def body(where, source, out):
        for index in range(size):
            out[index * piece : (index + 1) * piece, :] = source[where[index]].astype(f32)[:piece]

    return block_call(
        body,
        where,
        -(-width // lanes),
        [
            (
                gathered.reshape(size, total // size, width),
                pl.BlockSpec((size, total // size, lanes), lambda i, where: (0, 0, i)),
            )
        ],
        [
            (
                leaf((size * piece, width), f32),
                pl.BlockSpec((size * piece, lanes), lambda i, where: (0, i)),
            )
        ],
        [],
        name,
    )[0]


def inverse_rms(values):
    return lax.rsqrt(jnp.mean(values * values, axis=-1, keepdims=True) + EPS)


def norm_backward(values, norm, gain, grad):
    scaled = grad * gain
    centre = norm**3 * jnp.mean(values * scaled, axis=-1, keepdims=True)
    return norm * scaled - values * centre, jnp.sum(grad * values * norm, axis=0)


def split_low(values):
    high = lax.reduce_precision(values, 8, 7)
    return [high.astype(bf16), (values - high).astype(bf16)]


def on_device(
    tokens, cotangent, deal_table, norm_gain, query_weight, key_weight, value_weight, attention_out,
    attention_gain, mixer_in, filter_kernel, filter_bias, select_weight, step_weight, step_bias, decay_log,
    skip_gain, mixer_gain, mixer_out, post_gain, gate_weight, up_weight, down_weight,
):
    n = lax.axis_size("ctx")
    m = lax.axis_size("fsdp")
    c = lax.axis_index("ctx")
    z = lax.axis_index("fsdp")
    own = tokens.shape[1]
    block = own // 2
    total_rows = own * n
    count = 2 * n
    width = tokens.shape[2]
    shard = width // m
    heads = -(-HEADS // n)
    heads += heads % 2
    head_width = heads * HEAD_DIM
    shard_channels = filter_bias.shape[0]
    piece = shard_channels // n
    channels = m * piece
    wide = up_to(channels, 128)
    inner_all = shard_channels * m
    shard_hidden = down_weight.shape[0]
    hidden_piece = shard_hidden // n
    hidden_units = m * hidden_piece
    hidden_wide = up_to(hidden_units, 256)
    out_piece = width // n
    out_wide = up_to(out_piece, 128)

    def gather_z(values, tiled=True):
        return lax.all_gather(values, "fsdp", axis=0, tiled=tiled)

    def columns(values, start, size):
        return lax.dynamic_slice_in_dim(values, start, size, axis=1)

    small_rows = jnp.concatenate(
        [
            select_weight,
            step_weight.T,
            decay_log,
            filter_kernel.T,
            filter_bias[:, None],
            step_bias[:, None],
            skip_gain[:, None],
            mixer_gain[:, None],
        ],
        axis=1,
    )
    small_width = small_rows.shape[1]
    small_rows = lax.dynamic_slice_in_dim(small_rows, c * piece, piece, axis=0)
    gains = jnp.stack([norm_gain, attention_gain, post_gain]).reshape(-1)
    gain_rows = -(-3 * shard // small_width)
    gains = pad_to(gains, 0, gain_rows * small_width).reshape(gain_rows, small_width)
    small_local = jnp.concatenate([small_rows, gains])
    turned = [
        lax.ppermute(small_local, "fsdp", [(i, (i + k) % m) for i in range(m)])
        for k in range(m - 1, 0, -1)
    ] + [small_local]
    small_all = lax.dynamic_slice_in_dim(jnp.stack(turned + turned), m - 1 - z, m, axis=0)
    small = small_all[:, :piece].reshape(channels, small_width)
    gains_all = small_all[:, piece:].reshape(m, gain_rows * small_width)[:, : 3 * shard]
    gains_all = jnp.moveaxis(gains_all.reshape(m, 3, shard), 0, 1).reshape(3, width).astype(f32)
    first_gain, attend_gain, after_gain = gains_all[0:1], gains_all[1:2], gains_all[2:3]

    own_index = c.reshape(1)
    in_groups = [
        (p * inner_all + f * shard_channels, p * wide + f * piece) for p in range(2) for f in range(m)
    ]
    in_local = pack_columns(mixer_in, own_index, in_groups, 2 * wide, piece, "pack_mixer")
    in_weight = gather_z(in_local)

    def first_group(index):
        return jnp.minimum(index * heads // GROUP, KV_HEADS - 1)

    group_at = first_group(c)
    kv_pad = (KV_HEADS + 1) * HEAD_DIM
    pair = 2 * HEAD_DIM
    attend_local = jnp.concatenate(
        [
            columns(
                pad_to(after(query_weight, in_local), 1, n * head_width), c * head_width, head_width
            ),
            columns(pad_to(key_weight, 1, kv_pad), group_at * HEAD_DIM, pair),
            columns(pad_to(value_weight, 1, kv_pad), group_at * HEAD_DIM, pair),
            pad_to(columns(attention_out, c * out_piece, out_piece), 1, out_wide),
        ],
        axis=1,
    )
    attend_all = gather_z(attend_local)
    head_ids = c * heads + jnp.arange(heads, dtype=jnp.int32)
    valid = (head_ids < HEADS).astype(jnp.int32)
    upper = jnp.minimum(head_ids // GROUP, KV_HEADS - 1) > group_at

    def per_head(pair_weight):
        both = pair_weight.reshape(width, 2, 1, HEAD_DIM)
        picked = jnp.where(upper[None, :, None], both[:, 1], both[:, 0])
        return picked.reshape(width, head_width)

    query_own = attend_all[:, :head_width]
    key_own = per_head(attend_all[:, head_width : head_width + pair])
    value_own = per_head(attend_all[:, head_width + pair : head_width + 2 * pair])
    attend_in = jnp.concatenate([query_own, key_own, value_own], axis=1)
    group_in = attend_all[:, : head_width + 2 * pair]
    out_columns = attend_all[:, head_width + 2 * pair : head_width + 2 * pair + out_piece]
    out_own = lax.all_to_all(
        pad_to(out_columns, 0, n * head_width).reshape(n, head_width, out_piece), "ctx", 0, 0
    )
    out_own = jnp.moveaxis(out_own, 0, 1).reshape(head_width, width)

    def row_slices(weight, size, full):
        cut = pad_to(lax.dynamic_slice_in_dim(weight, c * size, size, axis=0), 0, up_to(size, 16))
        cut = gather_z(cut, tiled=False)[:, :size].reshape(m * size, width)
        return pad_to(cut, 0, full)

    attend_local = after(attend_local, in_local)
    mixer_out_own = row_slices(after(mixer_out, attend_local), piece, wide)
    pair_groups = [(f * shard_hidden, f * hidden_piece) for f in range(m)]
    pair_local = jnp.concatenate(
        [
            pack_columns(
                after(weight, attend_local), own_index, pair_groups, hidden_wide, hidden_piece, name
            )
            for weight, name in ((gate_weight, "pack_gate"), (up_weight, "pack_up"))
        ],
        axis=1,
    )
    pair_weight = gather_z(pair_local)
    down_own = row_slices(after(down_weight, pair_local), hidden_piece, hidden_wide)

    others = c ^ jnp.array(masks(n), dtype=jnp.int32)
    firsts = deal_table[others]
    places = jnp.stack([firsts, count - 1 - firsts], axis=1).reshape(count)
    ids = jnp.arange(count, dtype=jnp.int32)
    order = jnp.sum(jnp.where(places[None, :] == ids[:, None], ids[None, :], 0), axis=1)
    position = (places[:, None] * block + jnp.arange(block, dtype=jnp.int32)[None, :]).reshape(-1)

    small_t = pad_to(small.astype(f32).T, 1, wide)
    select_own = pad_to(pad_to(small[:, : RANK + 2 * NS], 0, wide), 1, 256)
    step_own = pad_to(small_t[RANK + 2 * NS : 2 * RANK + 2 * NS], 0, 128).astype(bf16)
    at = 2 * RANK + 2 * NS
    decay_own = -jnp.exp(small_t[at : at + NS])
    at += NS
    vecs = jnp.concatenate([small_t[at + CONV + 1 : at + CONV + 4], small_t[at + CONV : at + CONV + 1], small_t[at : at + CONV]])

    upstream = cotangent[0]
    upstream_all = gather_ctx(upstream, n)
    inputs = tokens[0].astype(f32)
    first_norm = inverse_rms(inputs)
    hidden = gather_ctx((inputs * first_norm * first_gain).astype(bf16), n)
    projected = dot(hidden, in_weight)
    heads_in = dot(hidden, attend_in).astype(bf16)

    forward = lambda i: i
    reverse = lambda i: count - 1 - i
    mixed_in, selected_part = block_call(
        filter_forward_body(block),
        order,
        count,
        [
            (projected, columns_at(block, wide, forward, 0)),
            (vecs, whole(vecs.shape)),
            (select_own, whole(select_own.shape)),
        ],
        [
            (leaf((total_rows, wide), bf16), rows(block, wide, forward)),
            (leaf((total_rows, 256), bf16), rows(block, 256, forward)),
        ],
        [pltpu.VMEM((block + 8, wide), f32)],
        "filter_forward",
    )
    selected = sum_ctx(selected_part, n)

    query_block = min(256, total_rows)
    query_count = total_rows // query_block
    query_pos = position[:, None]
    key_pos = position[None, :]
    own_gain = lax.dynamic_slice_in_dim(
        pad_to(attend_gain, 1, n * head_width), c * head_width, head_width, axis=1
    )

    def part(index):
        return pl.BlockSpec((total_rows, head_width), lambda i, order: (0, index))

    def tall(size):
        return pl.BlockSpec((query_block, size), lambda i, order: (i, 0))

    attend_ins = [
        (heads_in, tall(head_width)),
        (heads_in, part(1)),
        (heads_in, part(2)),
        (query_pos, tall(1)),
        (key_pos, whole(key_pos.shape)),
        (own_gain, whole(own_gain.shape)),
    ]
    attended, attended_scaled, attended_squares = block_call(
        attention_forward_body,
        valid,
        query_count,
        attend_ins,
        [
            (leaf((total_rows, head_width), f32), tall(head_width)),
            (leaf((total_rows, head_width), bf16), tall(head_width)),
            (leaf((total_rows, 128), f32), tall(128)),
        ],
        [],
        "attention_forward",
    )

    def branch_out(scaled, squares, weight):
        product = dot(scaled, weight)
        side = jnp.broadcast_to(squares[:, :1], (total_rows, SIDE))
        sent = jnp.concatenate([product.astype(bf16), side.astype(bf16)], axis=1)
        got = scatter_ctx(sent, n)
        return got[:, :width], got[:, width : width + 1]

    attend_sum, attend_squares = branch_out(attended_scaled, attended_squares, out_own)
    attend_norm = lax.rsqrt(attend_squares / (HEADS * HEAD_DIM) + EPS)

    sides = selected[:, RANK : RANK + 2 * NS].reshape(count, block // STEP, STEP, 2 * NS)
    sides = jnp.swapaxes(sides, 2, 3)
    side_spec = lambda pick: pl.BlockSpec((1,) + sides.shape[1:], lambda i, order: (order[pick(i)], 0, 0, 0))
    start_spec = lambda pick: pl.BlockSpec((1, NS, wide), lambda i, order: (order[pick(i)], 0, 0))
    scanned, starts, mixer_scaled, mixer_squares = block_call(
        scan_forward_body(block),
        order,
        count,
        [
            (selected, rows(block, 128, forward)),
            (sides, side_spec(forward)),
            (mixed_in, rows(block, wide, forward)),
            (projected, columns_at(block, wide, forward, 1)),
            (step_own, whole(step_own.shape)),
            (vecs, whole(vecs.shape)),
            (decay_own, whole(decay_own.shape)),
        ],
        [
            (leaf((total_rows, wide), f32), rows(block, wide, forward)),
            (leaf((count, NS, wide), f32), start_spec(forward)),
            (leaf((total_rows, wide), bf16), rows(block, wide, forward)),
            (leaf((total_rows, 128), f32), rows(block, 128, forward)),
        ],
        [
            pltpu.VMEM((NS, wide), f32),
            pltpu.VMEM((block, wide), f32),
            pltpu.VMEM((block, wide), f32),
        ],
        "scan_forward",
    )
    mixer_sum, mixer_squares = branch_out(mixer_scaled, mixer_squares, mixer_out_own)
    mixer_norm = lax.rsqrt(mixer_squares / inner_all + EPS)

    mixed = inputs + 0.5 * (attend_norm * attend_sum + mixer_norm * mixer_sum)
    post_norm = inverse_rms(mixed)
    post = gather_ctx((mixed * post_norm * after_gain).astype(bf16), n)
    both = dot(post, pair_weight)
    gate_now, up_now = both[:, :hidden_wide], both[:, hidden_wide:]
    gate_sig = jax.nn.sigmoid(gate_now)
    gate_act = gate_now * gate_sig
    unit = (gate_act * up_now).astype(bf16)
    ffn_out = scatter_ctx(dot(unit, down_own).astype(bf16), n)
    layer_out = (mixed + ffn_out).astype(bf16)[None]

    dunit = dot_nt(upstream_all, down_own)
    dboth = jnp.concatenate(
        [
            dunit * up_now * (gate_sig * (1.0 + gate_now * (1.0 - gate_sig))),
            dunit * gate_act,
        ],
        axis=1,
    ).astype(bf16)
    dpost = scatter_ctx(dot_nt(dboth, pair_weight).astype(bf16), n)
    dnorm, post_gain_part = norm_backward(mixed, post_norm, after_gain, dpost)
    dmixed = upstream.astype(f32) + dnorm

    def scatter_z(values):
        return lax.psum_scatter(values, "fsdp", scatter_dimension=0, tiled=True)

    def row_grads(part, size):
        part = pad_to(part[: m * size].reshape(m, size, width), 1, up_to(size, 16)).astype(bf16)
        return scatter_z(part.reshape(-1, width))

    pair_part = dot_tn(post, dboth).astype(bf16)
    down_part = dot_tn(unit, upstream_all)
    dmixed, pair_part = lax.optimization_barrier((dmixed, pair_part))
    pair_grad = scatter_z(pair_part)

    dbranch = (0.5 * dmixed).astype(bf16)
    dbranch_wide = dbranch.astype(f32)
    attend_centre = (
        attend_norm**3
        * jnp.sum(dbranch_wide * attend_sum, axis=1, keepdims=True)
        / (HEADS * HEAD_DIM)
    )
    mixer_centre = (
        mixer_norm**3 * jnp.sum(dbranch_wide * mixer_sum, axis=1, keepdims=True) / inner_all
    )
    extra = []
    for item in (attend_norm, attend_centre, mixer_norm, mixer_centre):
        extra += split_low(item)
    payload = jnp.concatenate([dbranch, pad_to(jnp.concatenate(extra, axis=1), 1, SIDE)], axis=1)
    payload = gather_ctx(payload, n)
    payload, down_part = lax.optimization_barrier((payload, down_part))
    down_grad = row_grads(down_part, hidden_piece)
    dbranch_all = payload[:, :width]
    scalars = payload[:, width : width + 8].astype(f32).reshape(total_rows, 4, 2).sum(axis=2)
    scalars = pad_to(scalars, 1, 128)

    dattend_in = dot_nt(dbranch_all, out_own)
    dmixer_in = dot_nt(dbranch_all, mixer_out_own)

    normed_s, dgate_z, dmixed_in, draw, drank, dsides, scan_vecs, step_part, decay_part = block_call(
        scan_backward_body(block),
        order,
        count,
        [
            (selected, rows(block, 128, reverse)),
            (sides, side_spec(reverse)),
            (mixed_in, rows(block, wide, reverse)),
            (projected, columns_at(block, wide, reverse, 1)),
            (scanned, rows(block, wide, reverse)),
            (dmixer_in, rows(block, wide, reverse)),
            (scalars, rows(block, 128, reverse)),
            (starts, start_spec(reverse)),
            (step_own, whole(step_own.shape)),
            (vecs, whole(vecs.shape)),
            (decay_own, whole(decay_own.shape)),
        ],
        [
            (leaf((total_rows, wide), bf16), rows(block, wide, reverse)),
            (leaf((total_rows, wide), bf16), rows(block, wide, reverse)),
            (leaf((total_rows, wide), f32), rows(block, wide, reverse)),
            (leaf((total_rows, wide), bf16), rows(block, wide, reverse)),
            (leaf((total_rows, 128), f32), rows(block, 128, reverse)),
            (
                leaf((count, 2, 8, block * NS), f32),
                pl.BlockSpec(
                    (1, 2, 8, block * NS), lambda i, order: (order[reverse(i)], 0, 0, 0)
                ),
            ),
            (leaf((8, wide), f32), whole((8, wide))),
            (leaf((128, wide), f32), whole((128, wide))),
            (leaf((NS, wide), f32), whole((NS, wide))),
        ],
        [
            pltpu.VMEM((NS, wide), f32),
            pltpu.VMEM((block, wide), f32),
            pltpu.VMEM((block, wide), f32),
            pltpu.VMEM((block, wide), f32),
            pltpu.VMEM((block, wide), f32),
            pltpu.VMEM((block, wide), f32),
            pltpu.VMEM((block + 1, NS, wide), f32),
            pltpu.VMEM((block, NS, wide), f32),
            pltpu.VMEM((block * NS, 128), f32),
            pltpu.VMEM((block * NS, 128), f32),
        ],
        "scan_backward",
    )
    dsides = jnp.swapaxes(dsides[:, :, 0, :].reshape(count, 2, block, NS), 1, 2)
    dselected_part = jnp.concatenate(
        [drank[:, :RANK], dsides.reshape(total_rows, 2 * NS)], axis=1
    ).astype(bf16)
    dselected = sum_ctx(pad_to(dselected_part, 1, 256), n).astype(bf16)

    dquery, dkey, dvalue, normed_a, attend_gain_part = block_call(
        attention_backward_body,
        valid,
        query_count,
        attend_ins
        + [
            (attended, tall(head_width)),
            (dattend_in, tall(head_width)),
            (scalars, tall(128)),
        ],
        [
            (leaf((total_rows, head_width), bf16), tall(head_width)),
            (leaf((total_rows, head_width), bf16), whole((total_rows, head_width))),
            (leaf((total_rows, head_width), bf16), whole((total_rows, head_width))),
            (leaf((total_rows, head_width), bf16), tall(head_width)),
            (leaf((8, head_width), f32), whole((8, head_width))),
        ],
        [
            pltpu.VMEM((total_rows, head_width), f32),
            pltpu.VMEM((total_rows, head_width), f32),
        ],
        "attention_backward",
    )
    lane_head = jnp.arange(head_width, dtype=jnp.int32) // HEAD_DIM
    lane_dim = jnp.arange(head_width, dtype=jnp.int32) % HEAD_DIM
    target = jnp.where(jnp.repeat(upper, HEAD_DIM), HEAD_DIM, 0) + lane_dim
    fold = (target[:, None] == jnp.arange(pair, dtype=jnp.int32)[None, :]).astype(bf16)
    dkey = dot(dkey, fold).astype(bf16)
    dvalue = dot(dvalue, fold).astype(bf16)
    dheads = jnp.concatenate([dquery, dkey, dvalue], axis=1)

    out_part = dot_tn(normed_a, dbranch_all).astype(bf16)
    out_part = lax.all_to_all(
        jnp.moveaxis(out_part.reshape(head_width, n, out_piece), 1, 0), "ctx", 0, 0
    )
    out_part = out_part.reshape(n * head_width, out_piece)[:width]
    attend_part = jnp.concatenate(
        [
            dot_tn(hidden, dheads).astype(bf16),
            pad_to(out_part, 1, out_wide),
            dot_tn(hidden, dgate_z).astype(bf16),
        ],
        axis=1,
    )
    attend_grad = scatter_z(attend_part)
    mixer_out_grad = row_grads(dot_tn(normed_s, dbranch_all), piece)

    dinner, select_part, filter_vecs = block_call(
        filter_backward_body(block, count),
        order,
        count,
        [
            (projected, columns_at(block, wide, reverse, 0)),
            (projected, columns_at(block, wide, lambda i: jnp.maximum(count - 2 - i, 0), 0)),
            (mixed_in, rows(block, wide, reverse)),
            (dmixed_in, rows(block, wide, reverse)),
            (dselected, rows(block, 256, reverse)),
            (select_own, whole(select_own.shape)),
            (vecs, whole(vecs.shape)),
        ],
        [
            (leaf((total_rows, wide), bf16), rows(block, wide, reverse)),
            (leaf((256, wide), f32), whole((256, wide))),
            (leaf((8, wide), f32), whole((8, wide))),
        ],
        [pltpu.VMEM((block + 8, wide), f32), pltpu.VMEM((block + 8, wide), f32)],
        "filter_backward",
    )
    dhidden = (
        dot_nt(dinner, in_weight[:, :wide])
        + dot_nt(dgate_z, in_weight[:, wide:])
        + dot_nt(dheads, group_in)
    )
    dhidden = scatter_ctx(dhidden.astype(bf16), n)
    dfirst, first_gain_part = norm_backward(inputs, first_norm, first_gain, dhidden)
    tokens_grad = (dmixed + dfirst).astype(bf16)[None]

    small_grad = jnp.concatenate(
        [
            select_part[: RANK + 2 * NS],
            step_part[:RANK],
            decay_part,
            filter_vecs[4 : 4 + CONV],
            filter_vecs[3:4],
            scan_vecs[0:3],
        ]
    )[:, :channels]
    attend_gain_full = lax.dynamic_update_slice_in_dim(
        jnp.zeros((1, n * head_width), f32), attend_gain_part[0:1], c * head_width, axis=1
    )[0, :width]
    gain_part = jnp.stack([first_gain_part, attend_gain_full, post_gain_part]).reshape(3, m, shard)
    gain_part = pad_to(
        jnp.moveaxis(gain_part, 1, 0).reshape(m, 3 * shard), 1, gain_rows * small_width
    )
    small_part = jnp.concatenate(
        [
            small_grad.T.reshape(m, piece, small_width),
            gain_part.reshape(m, gain_rows, small_width),
        ],
        axis=1,
    )
    small_rows_count = up_to(piece + gain_rows, 2 * 16 * wide // small_width) * small_width // wide
    small_part = pad_to(
        small_part.reshape(m, -1), 1, small_rows_count * wide
    ).reshape(m, small_rows_count, wide)
    in_part = dot_tn(hidden, dinner).reshape(m, shard, wide)
    in_grad = scatter_z(
        jnp.concatenate([in_part, small_part], axis=1).astype(bf16).reshape(-1, wide)
    )

    spots = jnp.array([masks(n).index(mask) for mask in range(n)], dtype=jnp.int32)
    where = spots[c ^ jnp.arange(n, dtype=jnp.int32)]
    pair_grad = gather_ctx(pair_grad, n)
    gate_grad, up_grad = unpack_columns(
        pair_grad,
        where,
        [
            (k, f * shard_hidden, hidden_piece, k * hidden_wide + f * hidden_piece, hidden_piece)
            for k in range(2)
            for f in range(m)
        ],
        [weight.shape[1] for weight in (gate_weight, up_weight)],
        n,
        "unpack_pair",
    )
    down_grad = unpack_rows(gather_ctx(down_grad, n), where, hidden_piece, n, "unpack_down")
    mixer_out_grad = unpack_rows(gather_ctx(mixer_out_grad, n), where, piece, n, "unpack_mixer")
    attend_grad = gather_ctx(attend_grad, n)
    kv_wide = n * pair
    out_at = head_width + 2 * pair
    gate_at = out_at + out_wide
    query_grad, key_parts, value_parts, out_grad, gate_half = unpack_columns(
        attend_grad,
        where,
        [
            (0, 0, head_width, 0, head_width),
            (1, 0, pair, head_width, pair),
            (2, 0, pair, head_width + pair, pair),
            (3, 0, out_piece, out_at, out_piece),
        ]
        + [(4, f * shard_channels, piece, gate_at + f * piece, piece) for f in range(m)],
        [width, kv_wide, kv_wide, width, inner_all],
        n,
        "unpack_attention",
    )

    def group_sum(parts):
        total = jnp.zeros((shard, kv_pad), f32)
        for index in range(n):
            low_at = min(index * heads // GROUP, KV_HEADS - 1) * HEAD_DIM
            item = parts[:, index * pair : (index + 1) * pair]
            total = total + jnp.pad(item, ((0, 0), (low_at, kv_pad - pair - low_at)))
        return total[:, : KV_HEADS * HEAD_DIM]

    in_grad = gather_ctx(in_grad, n).reshape(n, shard + small_rows_count, wide)
    (inner_half,) = unpack_columns(
        in_grad[:, :shard].reshape(n * shard, wide),
        where,
        [(0, f * shard_channels, piece, f * piece, piece) for f in range(m)],
        [inner_all],
        n,
        "unpack_inner",
    )
    mixer_in_grad = jnp.concatenate([inner_half, gate_half], axis=1)
    small_sum = in_grad[:, shard:].astype(f32).reshape(n, -1)[:, : (piece + gain_rows) * small_width]
    small_sum = small_sum[where].reshape(n, piece + gain_rows, small_width)
    channel_grad = small_sum[:, :piece].reshape(shard_channels, small_width)
    gain_grad = jnp.sum(small_sum[:, piece:], axis=0).reshape(-1)[: 3 * shard].reshape(3, shard)

    at = RANK + 2 * NS
    select_grad = channel_grad[:, :at]
    step_grad = channel_grad[:, at : at + RANK].T
    at += RANK
    decay_grad = channel_grad[:, at : at + NS]
    at += NS
    kernel_grad = channel_grad[:, at : at + CONV].T
    at += CONV
    return (
        layer_out,
        tokens_grad,
        gain_grad[0],
        query_grad,
        group_sum(key_parts),
        group_sum(value_parts),
        out_grad,
        gain_grad[1],
        mixer_in_grad,
        kernel_grad,
        channel_grad[:, at],
        select_grad,
        step_grad,
        channel_grad[:, at + 1],
        decay_grad,
        channel_grad[:, at + 2],
        channel_grad[:, at + 3],
        mixer_out_grad,
        gain_grad[2],
        gate_grad,
        up_grad,
        down_grad,
    )


def solution(mesh):
    rows_spec = P("fsdp", None)
    lanes_spec = P(None, "fsdp")
    flat = P("fsdp")
    activations = P("fsdp", "ctx", None)
    weight_specs = (
        flat, rows_spec, rows_spec, rows_spec, rows_spec, flat, rows_spec, lanes_spec, flat, rows_spec,
        lanes_spec, flat, rows_spec, flat, flat, rows_spec, flat, rows_spec, rows_spec, rows_spec,
    )
    return jax.shard_map(
        on_device,
        mesh=mesh,
        in_specs=(activations, activations, P()) + weight_specs,
        out_specs=(activations, activations) + weight_specs,
        check_vma=False,
    )
```

```python
import math

import jax
import jax.numpy as jnp
from jax import lax
from jax.experimental import pallas as pl
from jax.experimental.pallas import tpu as pltpu
from jax.sharding import PartitionSpec as P

HEADS = 25
KV_HEADS = 5
HEAD_DIM = 64
GROUP = HEADS // KV_HEADS
CONV = 4
RANK = 100
NS = 16
EPS = 1e-05
NEG = -1e30
SCALE = 1.0 / math.sqrt(HEAD_DIM)
STEP = 16
VMEM = 56 * 1024 * 1024
SIDE = 64
bf16 = jnp.bfloat16
f32 = jnp.float32


def up_to(value, unit):
    return -(-value // unit) * unit


def dot(left, right, contract=((1,), (0,)), precision=None):
    return lax.dot_general(
        left, right, (contract, ((), ())), preferred_element_type=f32, precision=precision
    )


def dot_tn(left, right):
    return dot(left, right, ((0,), (0,)))


def dot_nt(left, right):
    return dot(left, right, ((1,), (1,)))


def pad_to(values, axis, size):
    widths = [(0, 0)] * values.ndim
    widths[axis] = (0, size - values.shape[axis])
    return jnp.pad(values, widths)


def masks(size):
    return list(range(0, size, 2)) + list(range(1, size, 2))


def swap(values, mask, size):
    return lax.ppermute(values, "ctx", [(i, i ^ mask) for i in range(size)])


def gather_ctx(values, size):
    near = jnp.concatenate([values] + [swap(values, m, size) for m in range(2, size, 2)])
    return jnp.concatenate([near, swap(near, 1, size)])


def scatter_ctx(values, size):
    parts = values.reshape((size, values.shape[0] // size) + values.shape[1:])
    half = size // 2
    got = swap(parts[half:], 1, size)
    near = parts[:half].astype(f32) + got.astype(f32)
    sent = near.astype(bf16)
    total = near[0]
    for k in range(1, half):
        total = total + swap(sent[k], 2 * k, size).astype(f32)
    return total


def swap_aligned(values, mask, size):
    order = masks(size)
    got = swap(values, mask, size).reshape((size, values.shape[0] // size) + values.shape[1:])
    picked = [got[order.index(m ^ mask)] for m in order]
    return jnp.concatenate(picked).astype(f32)


def sum_ctx(values, size):
    near = (values.astype(f32) + swap_aligned(values, 1, size)).astype(bf16)
    total = near.astype(f32)
    for m in range(2, size, 2):
        total = total + swap_aligned(near, m, size)
    return total


def block_call(body, order, count, ins, outs, scratch, name, earlier=()):
    given = len(ins)
    ins = list(ins) + [(value, pl.BlockSpec(memory_space=pl.ANY)) for value in earlier]

    def trimmed(*refs):
        return body(*refs[: 1 + given], *refs[1 + len(ins) :])

    return pl.pallas_call(
        trimmed,
        grid_spec=pltpu.PrefetchScalarGridSpec(
            num_scalar_prefetch=1,
            grid=(count,),
            in_specs=[spec for _, spec in ins],
            out_specs=[spec for _, spec in outs],
            scratch_shapes=scratch,
        ),
        out_shape=[shape for shape, _ in outs],
        compiler_params=pltpu.CompilerParams(
            dimension_semantics=("arbitrary",), vmem_limit_bytes=VMEM
        ),
        name=name,
    )(order, *[value for value, _ in ins])


def after(values, *earlier):
    def body(*refs):
        del refs

    spec = pl.BlockSpec(memory_space=pl.ANY)
    return pl.pallas_call(
        body,
        in_specs=[spec] * (1 + len(earlier)),
        out_specs=spec,
        out_shape=leaf(values.shape, values.dtype),
        input_output_aliases={0: 0},
        name="after",
    )(values, *earlier)


def whole(shape):
    zeros = (0,) * len(shape)
    return pl.BlockSpec(shape, lambda i, order: zeros)


def rows(block, width, pick):
    return pl.BlockSpec((block, width), lambda i, order: (order[pick(i)], 0))


def columns_at(block, width, pick, index):
    return pl.BlockSpec((block, width), lambda i, order: (order[pick(i)], index))


def leaf(shape, dtype):
    return jax.ShapeDtypeStruct(shape, dtype)


def filter_taps(ext, vecs, block):
    total = vecs[3:4, :]
    for j in range(CONV):
        total = total + vecs[4 + j : 5 + j, :] * ext[5 + j : 5 + j + block, :]
    return total


def filter_forward_body(block):
    def body(order, inner, vecs, select, mixed_o, selected_o, ext):
        step = pl.program_id(0)

        @pl.when(step == 0)
        def _():
            ext[0:8, :] = jnp.zeros((8, ext.shape[1]), f32)

        @pl.when(step > 0)
        def _():
            ext[0:8, :] = ext[block : block + 8, :]

        ext[8 : block + 8, :] = inner[...].astype(bf16).astype(f32)
        total = filter_taps(ext, vecs, block)
        mixed = (total * jax.nn.sigmoid(total)).astype(bf16)
        mixed_o[...] = mixed
        selected_o[...] = dot(mixed, select[...]).astype(bf16)

    return body


def rate_of(selected, step_weight, vecs):
    rank = selected[...].astype(bf16)
    raw = dot(rank, step_weight[...]) + vecs[0:1, :]
    rate = jnp.maximum(raw, 0.0) + jnp.log1p(jnp.exp(-jnp.abs(raw)))
    return rank, raw, rate


def scan_forward_body(block):
    def body(
        order, selected, sides, mixed, gate_z, step_weight, vecs, decay,
        scanned_o, starts_o, scaled_o, squares_o, state_s, rate_s, drive_s,
    ):
        @pl.when(pl.program_id(0) == 0)
        def _():
            state_s[...] = jnp.zeros_like(state_s)

        _, _, rate = rate_of(selected, step_weight, vecs)
        wide = mixed[...].astype(f32)
        rate_s[...] = rate
        drive_s[...] = rate * wide
        starts_o[0] = state_s[...]
        decay_mat = decay[...]

        def group(g, state):
            base = pl.multiple_of(g * STEP, STEP)
            rates = rate_s[pl.ds(base, STEP), :]
            drives = drive_s[pl.ds(base, STEP), :]
            side = sides[0, g]
            for j in range(STEP):
                state = (
                    jnp.exp(rates[j : j + 1, :] * decay_mat) * state
                    + drives[j : j + 1, :] * side[:NS, j : j + 1]
                )
                scanned_o[pl.ds(base + j, 1), :] = jnp.sum(
                    state * side[NS:, j : j + 1], axis=0, keepdims=True
                )
            return state

        state_s[...] = lax.fori_loop(0, block // STEP, group, state_s[...])
        gate = gate_z[...]
        gated = (scanned_o[...] + vecs[1:2, :] * wide) * (gate * jax.nn.sigmoid(gate))
        scaled_o[...] = (gated * vecs[2:3, :]).astype(bf16)
        squares_o[...] = jnp.broadcast_to(
            jnp.sum(gated * gated, axis=1, keepdims=True), squares_o.shape
        )

    return body


def scan_backward_body(block):
    def body(
        order, selected, sides, mixed, gate_z, scanned, grad_in, scalars, starts, step_weight, vecs, decay,
        normed_o, dgate_o, dmixed_o, draw_o, drank_o, dsides_o, vec_o, step_o, decay_o,
        lam_s, rate_s, drive_s, dscan_s, drate_s, pull_s, hist_s, factor_s, read_s, write_s,
    ):
        width = decay.shape[1]

        @pl.when(pl.program_id(0) == 0)
        def _():
            lam_s[...] = jnp.zeros_like(lam_s)
            vec_o[...] = jnp.zeros_like(vec_o)
            step_o[...] = jnp.zeros_like(step_o)
            decay_o[...] = jnp.zeros_like(decay_o)

        rank, raw, rate = rate_of(selected, step_weight, vecs)
        wide = mixed[...].astype(f32)
        rate_s[...] = rate
        drive_s[...] = rate * wide
        gate = gate_z[...]
        sig = jax.nn.sigmoid(gate)
        act = gate * sig
        before = scanned[...] + vecs[1:2, :] * wide
        gated = before * act
        norm = scalars[:, 2:3]
        centre = scalars[:, 3:4]
        grad = grad_in[...]
        gated_norm = gated * norm
        normed_o[...] = (gated_norm * vecs[2:3, :]).astype(bf16)
        dgated = norm * (vecs[2:3, :] * grad) - gated * centre
        dscan = dgated * act
        dscan_s[...] = dscan
        dgate_o[...] = (dgated * before * (sig * (1.0 + gate * (1.0 - sig)))).astype(bf16)
        vec_o[1:2, :] += jnp.sum(dscan * wide, axis=0, keepdims=True)
        vec_o[2:3, :] += jnp.sum(grad * gated_norm, axis=0, keepdims=True)
        decay_mat = decay[...]

        def forward(g, state):
            base = pl.multiple_of(g * STEP, STEP)
            rates = rate_s[pl.ds(base, STEP), :]
            drives = drive_s[pl.ds(base, STEP), :]
            side = sides[0, g]
            for j in range(STEP):
                factor = jnp.exp(rates[j : j + 1, :] * decay_mat)
                factor_s[base + j] = factor
                state = factor * state + drives[j : j + 1, :] * side[:NS, j : j + 1]
                hist_s[base + j + 1] = state
            return state

        hist_s[0] = starts[0]
        lax.fori_loop(0, block // STEP, forward, starts[0])

        def fold(values):
            total = values[:, 0:128]
            for at in range(128, width, 128):
                total = total + values[:, at : at + 128]
            return total

        def backward(i, carry):
            lam_in, decay_sum = carry
            g = block // STEP - 1 - i
            base = pl.multiple_of(g * STEP, STEP)
            rates = rate_s[pl.ds(base, STEP), :]
            drives = drive_s[pl.ds(base, STEP), :]
            dscans = dscan_s[pl.ds(base, STEP), :]
            side = sides[0, g]
            for j in range(STEP - 1, -1, -1):
                at = base + j
                row = dscans[j : j + 1, :]
                lam = lam_in + row * side[NS:, j : j + 1]
                read_s[pl.ds(at * NS, NS), :] = fold(hist_s[at + 1] * row)
                write_s[pl.ds(at * NS, NS), :] = fold(lam * drives[j : j + 1, :])
                pull = jnp.sum(lam * side[:NS, j : j + 1], axis=0, keepdims=True)
                lam_in = factor_s[at] * lam
                kept = lam_in * hist_s[at]
                decay_sum = decay_sum + rates[j : j + 1, :] * kept
                drate_s[pl.ds(at, 1), :] = jnp.sum(decay_mat * kept, axis=0, keepdims=True)
                pull_s[pl.ds(at, 1), :] = pull
            return (lam_in, decay_sum)

        lam, decay_sum = lax.fori_loop(
            0, block // STEP, backward, (lam_s[...], jnp.zeros_like(lam_s))
        )
        lam_s[...] = lam
        decay_o[...] += decay_sum * decay_mat
        pulled = pull_s[...]
        draw = (drate_s[...] + wide * pulled) * jax.nn.sigmoid(raw)
        vec_o[0:1, :] += jnp.sum(draw, axis=0, keepdims=True)
        low = draw.astype(bf16)
        draw_o[...] = low
        dmixed_o[...] = vecs[1:2, :] * dscan + rate * pulled
        drank_o[...] = dot_nt(low, step_weight[...])
        step_o[...] += dot_tn(rank, low)
        ones = jnp.ones((8, 128), f32)
        high = lax.Precision.HIGHEST
        dsides_o[0, 0] = dot(ones, write_s[...], ((1,), (1,)), high)
        dsides_o[0, 1] = dot(ones, read_s[...], ((1,), (1,)), high)

    return body


def filter_backward_body(block, count):
    def body(
        order, inner, inner_before, mixed, dmixed, dselected, select, vecs,
        dinner_o, select_o, vec_o, ext, ext_grad,
    ):
        step = pl.program_id(0)

        @pl.when(step == 0)
        def _():
            ext_grad[block : block + 8, :] = jnp.zeros((8, ext.shape[1]), f32)
            select_o[...] = jnp.zeros_like(select_o)
            vec_o[...] = jnp.zeros_like(vec_o)

        @pl.when(step > 0)
        def _():
            ext_grad[block : block + 8, :] = ext_grad[0:8, :]

        first = jnp.where(step == count - 1, 0.0, 1.0)
        ext[0:8, :] = inner_before[block - 8 :, :].astype(bf16).astype(f32) * first
        ext[8 : block + 8, :] = inner[...].astype(bf16).astype(f32)
        total = filter_taps(ext, vecs, block)
        sig = jax.nn.sigmoid(total)
        low = dselected[...]
        dmix = dmixed[...] + dot_nt(low, select[...])
        dfilt = dmix * (sig * (1.0 + total * (1.0 - sig)))
        ext_grad[0:block, :] = dfilt
        dinner = jnp.zeros_like(dfilt)
        vec_o[3:4, :] += jnp.sum(dfilt, axis=0, keepdims=True)
        for j in range(CONV):
            at = CONV - 1 - j
            dinner = dinner + vecs[4 + j : 5 + j, :] * ext_grad[at : at + block, :]
            vec_o[4 + j : 5 + j, :] += jnp.sum(
                dfilt * ext[5 + j : 5 + j + block, :], axis=0, keepdims=True
            )
        dinner_o[...] = dinner.astype(bf16)
        select_o[...] += dot_tn(low, mixed[...])

    return body


def half_mask(half):
    lane = lax.broadcasted_iota(jnp.int32, (1, 128), 1)
    return jnp.where((lane >= 64 * half) & (lane < 64 * half + 64), 1.0, 0.0)


def softmax_rows(query, key, allowed):
    scores = jnp.where(allowed, dot_nt(query, key) * SCALE, NEG)
    weights = jnp.exp(scores - jnp.max(scores, axis=-1, keepdims=True))
    return weights * (1.0 / jnp.sum(weights, axis=-1, keepdims=True))


def attention_forward_body(valid, query, key, value, query_pos, key_pos, gain, out_o, scaled_o, squares_o):
    allowed = key_pos[...] <= query_pos[...]
    squares = jnp.zeros((query.shape[0], 1), f32)
    for at in range(0, query.shape[1], 128):
        key_tile = key[:, at : at + 128]
        value_tile = value[:, at : at + 128]
        tile = jnp.zeros((query.shape[0], 128), f32)
        for half in range(2):
            mask = half_mask(half)
            part = query[:, at : at + 128] * mask.astype(bf16)
            probs = softmax_rows(part, key_tile, allowed).astype(bf16)
            live = valid[at // 64 + half].astype(f32)
            tile = tile + dot(probs, value_tile) * (mask * live)
        out_o[:, at : at + 128] = tile
        scaled_o[:, at : at + 128] = (tile * gain[:, at : at + 128]).astype(bf16)
        squares = squares + jnp.sum(tile * tile, axis=1, keepdims=True)
    squares_o[...] = jnp.broadcast_to(squares, squares_o.shape)


def attention_backward_body(
    valid, query, key, value, query_pos, key_pos, gain, out, grad_in, scalars,
    dquery_o, dkey_o, dvalue_o, normed_o, gain_o, dkey_s, dvalue_s,
):
    @pl.when(pl.program_id(0) == 0)
    def _():
        dkey_s[...] = jnp.zeros_like(dkey_s)
        dvalue_s[...] = jnp.zeros_like(dvalue_s)
        gain_o[...] = jnp.zeros_like(gain_o)

    allowed = key_pos[...] <= query_pos[...]
    norm = scalars[:, 0:1]
    centre = scalars[:, 1:2]
    for at in range(0, query.shape[1], 128):
        lanes = slice(at, at + 128)
        key_tile = key[:, lanes]
        value_tile = value[:, lanes]
        attended = out[:, lanes]
        grad = grad_in[:, lanes]
        normed = attended * norm
        normed_o[:, lanes] = (normed * gain[:, lanes]).astype(bf16)
        gain_o[0:1, lanes] += jnp.sum(grad * normed, axis=0, keepdims=True)
        dout = (norm * (gain[:, lanes] * grad) - attended * centre).astype(bf16)
        dquery = jnp.zeros(attended.shape, f32)
        dkey = jnp.zeros((key.shape[0], 128), f32)
        dvalue = jnp.zeros((key.shape[0], 128), f32)
        for half in range(2):
            mask = half_mask(half)
            part = query[:, lanes] * mask.astype(bf16)
            dpart = dout * mask.astype(bf16)
            probs = softmax_rows(part, key_tile, allowed)
            dprobs = dot_nt(dpart, value_tile)
            mean = jnp.sum(dprobs * probs, axis=-1, keepdims=True)
            dscores = (probs * (dprobs - mean)).astype(bf16)
            dvalue = dvalue + dot_tn(probs.astype(bf16), dpart)
            dquery = dquery + dot(dscores, key_tile) * (mask * SCALE)
            dkey = dkey + dot_tn(dscores, part) * SCALE
        dquery_o[:, lanes] = dquery.astype(bf16)
        dkey_s[:, lanes] += dkey
        dvalue_s[:, lanes] += dvalue

    @pl.when(pl.program_id(0) == pl.num_programs(0) - 1)
    def _():
        dkey_o[...] = dkey_s[...].astype(bf16)
        dvalue_o[...] = dvalue_s[...].astype(bf16)


def pack_body(groups, out_wide, width, piece):
    window = up_to(piece + 127, 128)

    def body(index, weight, out_o, acc):
        acc[...] = jnp.zeros_like(acc)
        for start, at in groups:
            source = start + index[0] * piece
            tile = jnp.minimum(source // 128, (width - window) // 128)
            base = pl.multiple_of(tile * 128, 128)
            low = at % 128
            span = up_to(low + piece, 128)
            row = lax.broadcasted_iota(jnp.int32, (window, span), 0)
            lane = lax.broadcasted_iota(jnp.int32, (window, span), 1) - low
            pick = (row - (source - base) == lane) & (lane >= 0) & (lane < piece)
            pick = jnp.where(pick, 1.0, 0.0).astype(bf16)
            acc[:, at - low : at - low + span] += dot(weight[:, pl.ds(base, window)], pick)
        out_o[...] = acc[...].astype(bf16)

    return body


def row_block(count):
    return 80 if count % 80 == 0 else count


def join_body(axis):
    def body(index, *refs):
        at = 0
        for ref in refs[:-1]:
            size = ref.shape[axis]
            if axis == 0:
                refs[-1][at : at + size, :] = ref[...]
            else:
                refs[-1][:, at : at + size] = ref[...]
            at += size

    return body


def join(parts, index, axis, name, earlier):
    shape = list(parts[0].shape)
    shape[axis] = sum(part.shape[axis] for part in parts)
    return block_call(
        join_body(axis),
        index,
        1,
        [(part, whole(part.shape)) for part in parts],
        [(leaf(tuple(shape), bf16), whole(tuple(shape)))],
        [],
        name,
        earlier,
    )[0]


def pack_columns(weight, index, groups, out_wide, piece, name, earlier=()):
    count, width = weight.shape
    block = row_block(count)
    return block_call(
        pack_body(groups, out_wide, width, piece),
        index,
        count // block,
        [(weight, pl.BlockSpec((block, width), lambda i, index: (i, 0)))],
        [
            (
                leaf((count, out_wide), bf16),
                pl.BlockSpec((block, out_wide), lambda i, index: (i, 0)),
            )
        ],
        [pltpu.VMEM((block, out_wide), f32)],
        name,
        earlier,
    )[0]


def unpack_columns(gathered, where, moves, widths, size, name):
    total, width = gathered.shape
    count = total // size
    block = row_block(count)

    def body(where, source, *outs):
        for index in range(size):
            values = source[where[index]].astype(f32)
            for out, first, stride, at, piece in moves:
                start = first + index * stride
                piece = min(piece, widths[out] - start)
                if piece > 0:
                    outs[out][:, start : start + piece] = values[:, at : at + piece]

    return block_call(
        body,
        where,
        count // block,
        [
            (
                gathered.reshape(size, count, width),
                pl.BlockSpec((size, block, width), lambda i, where: (0, i, 0)),
            )
        ],
        [
            (leaf((count, full), f32), pl.BlockSpec((block, full), lambda i, where: (i, 0)))
            for full in widths
        ],
        [],
        name,
    )


def unpack_rows(gathered, where, piece, size, name):
    total, width = gathered.shape
    lanes = 256

    def body(where, source, out):
        for index in range(size):
            out[index * piece : (index + 1) * piece, :] = source[where[index]].astype(f32)[:piece]

    return block_call(
        body,
        where,
        -(-width // lanes),
        [
            (
                gathered.reshape(size, total // size, width),
                pl.BlockSpec((size, total // size, lanes), lambda i, where: (0, 0, i)),
            )
        ],
        [
            (
                leaf((size * piece, width), f32),
                pl.BlockSpec((size * piece, lanes), lambda i, where: (0, i)),
            )
        ],
        [],
        name,
    )[0]


def inverse_rms(values):
    return lax.rsqrt(jnp.mean(values * values, axis=-1, keepdims=True) + EPS)


def norm_backward(values, norm, gain, grad):
    scaled = grad * gain
    centre = norm**3 * jnp.mean(values * scaled, axis=-1, keepdims=True)
    return norm * scaled - values * centre, jnp.sum(grad * values * norm, axis=0)


def split_low(values):
    high = lax.reduce_precision(values, 8, 7)
    return [high.astype(bf16), (values - high).astype(bf16)]


def on_device(
    tokens, cotangent, deal_table, norm_gain, query_weight, key_weight, value_weight, attention_out,
    attention_gain, mixer_in, filter_kernel, filter_bias, select_weight, step_weight, step_bias, decay_log,
    skip_gain, mixer_gain, mixer_out, post_gain, gate_weight, up_weight, down_weight,
):
    n = lax.axis_size("ctx")
    m = lax.axis_size("fsdp")
    c = lax.axis_index("ctx")
    z = lax.axis_index("fsdp")
    own = tokens.shape[1]
    block = own // 2
    total_rows = own * n
    count = 2 * n
    width = tokens.shape[2]
    shard = width // m
    heads = -(-HEADS // n)
    heads += heads % 2
    head_width = heads * HEAD_DIM
    shard_channels = filter_bias.shape[0]
    piece = shard_channels // n
    channels = m * piece
    wide = up_to(channels, 128)
    inner_all = shard_channels * m
    shard_hidden = down_weight.shape[0]
    hidden_piece = shard_hidden // n
    hidden_units = m * hidden_piece
    hidden_wide = up_to(hidden_units, 256)
    out_piece = width // n
    out_wide = up_to(out_piece, 128)

    def gather_z(values, tiled=True):
        return lax.all_gather(values, "fsdp", axis=0, tiled=tiled)

    def columns(values, start, size):
        return lax.dynamic_slice_in_dim(values, start, size, axis=1)

    own_index = c.reshape(1)
    in_groups = [
        (p * inner_all + f * shard_channels, p * wide + f * piece) for p in range(2) for f in range(m)
    ]
    in_local = pack_columns(mixer_in, own_index, in_groups, 2 * wide, piece, "pack_mixer")
    small_rows = jnp.concatenate(
        [
            select_weight,
            step_weight.T,
            decay_log,
            filter_kernel.T,
            filter_bias[:, None],
            step_bias[:, None],
            skip_gain[:, None],
            mixer_gain[:, None],
        ],
        axis=1,
    )
    small_width = small_rows.shape[1]
    small_rows = lax.dynamic_slice_in_dim(small_rows, c * piece, piece, axis=0)
    gains = jnp.stack([norm_gain, attention_gain, post_gain]).reshape(-1)
    gain_rows = -(-3 * shard // small_width)
    gains = pad_to(gains, 0, gain_rows * small_width).reshape(gain_rows, small_width)
    small_local = after(jnp.concatenate([small_rows, gains]), in_local)
    turned = [
        lax.ppermute(small_local, "fsdp", [(i, (i + k) % m) for i in range(m)])
        for k in range(m - 1, 0, -1)
    ] + [small_local]
    small_all = lax.dynamic_slice_in_dim(jnp.stack(turned + turned), m - 1 - z, m, axis=0)
    small = small_all[:, :piece].reshape(channels, small_width)
    gains_all = small_all[:, piece:].reshape(m, gain_rows * small_width)[:, : 3 * shard]
    gains_all = jnp.moveaxis(gains_all.reshape(m, 3, shard), 0, 1).reshape(3, width).astype(f32)
    first_gain, attend_gain, after_gain = gains_all[0:1], gains_all[1:2], gains_all[2:3]

    in_weight = gather_z(in_local)

    def first_group(index):
        return jnp.minimum(index * heads // GROUP, KV_HEADS - 1)

    group_at = first_group(c)
    kv_pad = (KV_HEADS + 1) * HEAD_DIM
    pair = 2 * HEAD_DIM
    attend_local = join(
        [
            columns(pad_to(query_weight, 1, n * head_width), c * head_width, head_width),
            columns(pad_to(key_weight, 1, kv_pad), group_at * HEAD_DIM, pair),
            columns(pad_to(value_weight, 1, kv_pad), group_at * HEAD_DIM, pair),
            pad_to(columns(attention_out, c * out_piece, out_piece), 1, out_wide),
        ],
        own_index,
        1,
        "pack_attention",
        [in_weight],
    )
    attend_all = gather_z(attend_local)
    head_ids = c * heads + jnp.arange(heads, dtype=jnp.int32)
    valid = (head_ids < HEADS).astype(jnp.int32)
    upper = jnp.minimum(head_ids // GROUP, KV_HEADS - 1) > group_at

    def per_head(pair_weight):
        both = pair_weight.reshape(width, 2, 1, HEAD_DIM)
        picked = jnp.where(upper[None, :, None], both[:, 1], both[:, 0])
        return picked.reshape(width, head_width)

    query_own = attend_all[:, :head_width]
    key_own = per_head(attend_all[:, head_width : head_width + pair])
    value_own = per_head(attend_all[:, head_width + pair : head_width + 2 * pair])
    attend_in = jnp.concatenate([query_own, key_own, value_own], axis=1)
    group_in = attend_all[:, : head_width + 2 * pair]
    out_columns = attend_all[:, head_width + 2 * pair : head_width + 2 * pair + out_piece]
    out_own = lax.all_to_all(
        pad_to(out_columns, 0, n * head_width).reshape(n, head_width, out_piece), "ctx", 0, 0
    )
    out_own = jnp.moveaxis(out_own, 0, 1).reshape(head_width, width)

    inputs = tokens[0].astype(f32)
    first_norm = inverse_rms(inputs)
    hidden = gather_ctx((inputs * first_norm * first_gain).astype(bf16), n)

    def row_slice(weight, size):
        cut = lax.dynamic_slice_in_dim(weight, c * size, size, axis=0)
        return pad_to(cut, 0, up_to(size, 16))

    piece_rows, hidden_rows = up_to(piece, 16), up_to(hidden_piece, 16)
    rows_local = join(
        [row_slice(mixer_out, piece), row_slice(down_weight, hidden_piece)],
        own_index,
        0,
        "pack_rows",
        [in_local],
    )
    rows_local = after(rows_local, attend_all)
    rows_all = gather_z(rows_local, tiled=False)
    mixer_out_own = pad_to(rows_all[:, :piece].reshape(channels, width), 0, wide)
    down_own = rows_all[:, piece_rows : piece_rows + hidden_piece].reshape(hidden_units, width)
    down_own = pad_to(down_own, 0, hidden_wide)
    pair_groups = [(f * shard_hidden, f * hidden_piece) for f in range(m)]
    pair_local = jnp.concatenate(
        [
            pack_columns(weight, own_index, pair_groups, hidden_wide, hidden_piece, name, [in_local])
            for weight, name in ((gate_weight, "pack_gate"), (up_weight, "pack_up"))
        ],
        axis=1,
    )
    pair_local = after(pair_local, rows_all)
    pair_weight = gather_z(pair_local)

    others = c ^ jnp.array(masks(n), dtype=jnp.int32)
    firsts = deal_table[others]
    places = jnp.stack([firsts, count - 1 - firsts], axis=1).reshape(count)
    ids = jnp.arange(count, dtype=jnp.int32)
    order = jnp.sum(jnp.where(places[None, :] == ids[:, None], ids[None, :], 0), axis=1)
    position = (places[:, None] * block + jnp.arange(block, dtype=jnp.int32)[None, :]).reshape(-1)

    small_t = pad_to(small.astype(f32).T, 1, wide)
    select_own = pad_to(pad_to(small[:, : RANK + 2 * NS], 0, wide), 1, 256)
    step_own = pad_to(small_t[RANK + 2 * NS : 2 * RANK + 2 * NS], 0, 128).astype(bf16)
    at = 2 * RANK + 2 * NS
    decay_own = -jnp.exp(small_t[at : at + NS])
    at += NS
    vecs = jnp.concatenate([small_t[at + CONV + 1 : at + CONV + 4], small_t[at + CONV : at + CONV + 1], small_t[at : at + CONV]])

    upstream = cotangent[0]
    upstream_all = gather_ctx(upstream, n)
    projected = dot(hidden, in_weight)
    heads_in = dot(hidden, attend_in).astype(bf16)

    forward = lambda i: i
    reverse = lambda i: count - 1 - i
    mixed_in, selected_part = block_call(
        filter_forward_body(block),
        order,
        count,
        [
            (projected, columns_at(block, wide, forward, 0)),
            (vecs, whole(vecs.shape)),
            (select_own, whole(select_own.shape)),
        ],
        [
            (leaf((total_rows, wide), bf16), rows(block, wide, forward)),
            (leaf((total_rows, 256), bf16), rows(block, 256, forward)),
        ],
        [pltpu.VMEM((block + 8, wide), f32)],
        "filter_forward",
    )
    selected = sum_ctx(selected_part, n)

    query_block = min(256, total_rows)
    query_count = total_rows // query_block
    query_pos = position[:, None]
    key_pos = position[None, :]
    own_gain = lax.dynamic_slice_in_dim(
        pad_to(attend_gain, 1, n * head_width), c * head_width, head_width, axis=1
    )

    def part(index):
        return pl.BlockSpec((total_rows, head_width), lambda i, order: (0, index))

    def tall(size):
        return pl.BlockSpec((query_block, size), lambda i, order: (i, 0))

    attend_ins = [
        (heads_in, tall(head_width)),
        (heads_in, part(1)),
        (heads_in, part(2)),
        (query_pos, tall(1)),
        (key_pos, whole(key_pos.shape)),
        (own_gain, whole(own_gain.shape)),
    ]
    attended, attended_scaled, attended_squares = block_call(
        attention_forward_body,
        valid,
        query_count,
        attend_ins,
        [
            (leaf((total_rows, head_width), f32), tall(head_width)),
            (leaf((total_rows, head_width), bf16), tall(head_width)),
            (leaf((total_rows, 128), f32), tall(128)),
        ],
        [],
        "attention_forward",
    )

    def branch_out(scaled, squares, weight):
        product = dot(scaled, weight)
        side = jnp.broadcast_to(squares[:, :1], (total_rows, SIDE))
        sent = jnp.concatenate([product.astype(bf16), side.astype(bf16)], axis=1)
        got = scatter_ctx(sent, n)
        return got[:, :width], got[:, width : width + 1]

    attend_sum, attend_squares = branch_out(attended_scaled, attended_squares, out_own)
    attend_norm = lax.rsqrt(attend_squares / (HEADS * HEAD_DIM) + EPS)

    sides = selected[:, RANK : RANK + 2 * NS].reshape(count, block // STEP, STEP, 2 * NS)
    sides = jnp.swapaxes(sides, 2, 3)
    side_spec = lambda pick: pl.BlockSpec((1,) + sides.shape[1:], lambda i, order: (order[pick(i)], 0, 0, 0))
    start_spec = lambda pick: pl.BlockSpec((1, NS, wide), lambda i, order: (order[pick(i)], 0, 0))
    scanned, starts, mixer_scaled, mixer_squares = block_call(
        scan_forward_body(block),
        order,
        count,
        [
            (selected, rows(block, 128, forward)),
            (sides, side_spec(forward)),
            (mixed_in, rows(block, wide, forward)),
            (projected, columns_at(block, wide, forward, 1)),
            (step_own, whole(step_own.shape)),
            (vecs, whole(vecs.shape)),
            (decay_own, whole(decay_own.shape)),
        ],
        [
            (leaf((total_rows, wide), f32), rows(block, wide, forward)),
            (leaf((count, NS, wide), f32), start_spec(forward)),
            (leaf((total_rows, wide), bf16), rows(block, wide, forward)),
            (leaf((total_rows, 128), f32), rows(block, 128, forward)),
        ],
        [
            pltpu.VMEM((NS, wide), f32),
            pltpu.VMEM((block, wide), f32),
            pltpu.VMEM((block, wide), f32),
        ],
        "scan_forward",
    )
    mixer_sum, mixer_squares = branch_out(mixer_scaled, mixer_squares, mixer_out_own)
    mixer_norm = lax.rsqrt(mixer_squares / inner_all + EPS)

    mixed = inputs + 0.5 * (attend_norm * attend_sum + mixer_norm * mixer_sum)
    post_norm = inverse_rms(mixed)
    post = gather_ctx((mixed * post_norm * after_gain).astype(bf16), n)
    both = dot(post, pair_weight)
    gate_now, up_now = both[:, :hidden_wide], both[:, hidden_wide:]
    gate_sig = jax.nn.sigmoid(gate_now)
    gate_act = gate_now * gate_sig
    unit = (gate_act * up_now).astype(bf16)
    ffn_out = scatter_ctx(dot(unit, down_own).astype(bf16), n)
    layer_out = (mixed + ffn_out).astype(bf16)[None]

    dunit = dot_nt(upstream_all, down_own)
    dboth = jnp.concatenate(
        [
            dunit * up_now * (gate_sig * (1.0 + gate_now * (1.0 - gate_sig))),
            dunit * gate_act,
        ],
        axis=1,
    ).astype(bf16)
    dpost = scatter_ctx(dot_nt(dboth, pair_weight).astype(bf16), n)
    dnorm, post_gain_part = norm_backward(mixed, post_norm, after_gain, dpost)
    dmixed = upstream.astype(f32) + dnorm

    def scatter_z(values):
        return lax.psum_scatter(values, "fsdp", scatter_dimension=0, tiled=True)

    def row_grads(part, size):
        part = pad_to(part[: m * size].reshape(m, size, width), 1, up_to(size, 16)).astype(bf16)
        return scatter_z(part.reshape(-1, width))

    pair_part = dot_tn(post, dboth).astype(bf16)
    down_part = dot_tn(unit, upstream_all).astype(bf16)
    pair_grad = scatter_z(pair_part)
    pair_all = gather_ctx(pair_grad, n)

    dbranch = (0.5 * dmixed).astype(bf16)
    dbranch_wide = dbranch.astype(f32)
    attend_centre = (
        attend_norm**3
        * jnp.sum(dbranch_wide * attend_sum, axis=1, keepdims=True)
        / (HEADS * HEAD_DIM)
    )
    mixer_centre = (
        mixer_norm**3 * jnp.sum(dbranch_wide * mixer_sum, axis=1, keepdims=True) / inner_all
    )
    extra = []
    for item in (attend_norm, attend_centre, mixer_norm, mixer_centre):
        extra += split_low(item)
    payload = jnp.concatenate([dbranch, pad_to(jnp.concatenate(extra, axis=1), 1, SIDE)], axis=1)
    payload = gather_ctx(after(payload, pair_part), n)
    payload = after(payload, down_part)
    down_grad = row_grads(down_part, hidden_piece)
    dbranch_all = payload[:, :width]
    scalars = payload[:, width : width + 8].astype(f32).reshape(total_rows, 4, 2).sum(axis=2)
    scalars = pad_to(scalars, 1, 128)

    dattend_in = dot_nt(dbranch_all, out_own)
    dmixer_in = dot_nt(dbranch_all, mixer_out_own)

    normed_s, dgate_z, dmixed_in, draw, drank, dsides, scan_vecs, step_part, decay_part = block_call(
        scan_backward_body(block),
        order,
        count,
        [
            (selected, rows(block, 128, reverse)),
            (sides, side_spec(reverse)),
            (mixed_in, rows(block, wide, reverse)),
            (projected, columns_at(block, wide, reverse, 1)),
            (scanned, rows(block, wide, reverse)),
            (dmixer_in, rows(block, wide, reverse)),
            (scalars, rows(block, 128, reverse)),
            (starts, start_spec(reverse)),
            (step_own, whole(step_own.shape)),
            (vecs, whole(vecs.shape)),
            (decay_own, whole(decay_own.shape)),
        ],
        [
            (leaf((total_rows, wide), bf16), rows(block, wide, reverse)),
            (leaf((total_rows, wide), bf16), rows(block, wide, reverse)),
            (leaf((total_rows, wide), f32), rows(block, wide, reverse)),
            (leaf((total_rows, wide), bf16), rows(block, wide, reverse)),
            (leaf((total_rows, 128), f32), rows(block, 128, reverse)),
            (
                leaf((count, 2, 8, block * NS), f32),
                pl.BlockSpec(
                    (1, 2, 8, block * NS), lambda i, order: (order[reverse(i)], 0, 0, 0)
                ),
            ),
            (leaf((8, wide), f32), whole((8, wide))),
            (leaf((128, wide), f32), whole((128, wide))),
            (leaf((NS, wide), f32), whole((NS, wide))),
        ],
        [
            pltpu.VMEM((NS, wide), f32),
            pltpu.VMEM((block, wide), f32),
            pltpu.VMEM((block, wide), f32),
            pltpu.VMEM((block, wide), f32),
            pltpu.VMEM((block, wide), f32),
            pltpu.VMEM((block, wide), f32),
            pltpu.VMEM((block + 1, NS, wide), f32),
            pltpu.VMEM((block, NS, wide), f32),
            pltpu.VMEM((block * NS, 128), f32),
            pltpu.VMEM((block * NS, 128), f32),
        ],
        "scan_backward",
    )
    dsides = jnp.swapaxes(dsides[:, :, 0, :].reshape(count, 2, block, NS), 1, 2)
    dselected_part = jnp.concatenate(
        [drank[:, :RANK], dsides.reshape(total_rows, 2 * NS)], axis=1
    ).astype(bf16)
    dselected = sum_ctx(pad_to(dselected_part, 1, 256), n).astype(bf16)

    dquery, dkey, dvalue, normed_a, attend_gain_part = block_call(
        attention_backward_body,
        valid,
        query_count,
        attend_ins
        + [
            (attended, tall(head_width)),
            (dattend_in, tall(head_width)),
            (scalars, tall(128)),
        ],
        [
            (leaf((total_rows, head_width), bf16), tall(head_width)),
            (leaf((total_rows, head_width), bf16), whole((total_rows, head_width))),
            (leaf((total_rows, head_width), bf16), whole((total_rows, head_width))),
            (leaf((total_rows, head_width), bf16), tall(head_width)),
            (leaf((8, head_width), f32), whole((8, head_width))),
        ],
        [
            pltpu.VMEM((total_rows, head_width), f32),
            pltpu.VMEM((total_rows, head_width), f32),
        ],
        "attention_backward",
        [pair_grad],
    )
    lane_head = jnp.arange(head_width, dtype=jnp.int32) // HEAD_DIM
    lane_dim = jnp.arange(head_width, dtype=jnp.int32) % HEAD_DIM
    target = jnp.where(jnp.repeat(upper, HEAD_DIM), HEAD_DIM, 0) + lane_dim
    fold = (target[:, None] == jnp.arange(pair, dtype=jnp.int32)[None, :]).astype(bf16)
    dkey = dot(dkey, fold).astype(bf16)
    dvalue = dot(dvalue, fold).astype(bf16)
    dheads = jnp.concatenate([dquery, dkey, dvalue], axis=1)

    out_part = dot_tn(normed_a, dbranch_all).astype(bf16)
    out_part = lax.all_to_all(
        jnp.moveaxis(out_part.reshape(head_width, n, out_piece), 1, 0), "ctx", 0, 0
    )
    out_part = out_part.reshape(n * head_width, out_piece)[:width]
    attend_part = jnp.concatenate(
        [
            dot_tn(hidden, dheads).astype(bf16),
            pad_to(out_part, 1, out_wide),
            dot_tn(hidden, dgate_z).astype(bf16),
        ],
        axis=1,
    )
    attend_grad = scatter_z(attend_part)
    mixer_out_grad = row_grads(dot_tn(normed_s, dbranch_all), piece)

    dinner, select_part, filter_vecs = block_call(
        filter_backward_body(block, count),
        order,
        count,
        [
            (projected, columns_at(block, wide, reverse, 0)),
            (projected, columns_at(block, wide, lambda i: jnp.maximum(count - 2 - i, 0), 0)),
            (mixed_in, rows(block, wide, reverse)),
            (dmixed_in, rows(block, wide, reverse)),
            (dselected, rows(block, 256, reverse)),
            (select_own, whole(select_own.shape)),
            (vecs, whole(vecs.shape)),
        ],
        [
            (leaf((total_rows, wide), bf16), rows(block, wide, reverse)),
            (leaf((256, wide), f32), whole((256, wide))),
            (leaf((8, wide), f32), whole((8, wide))),
        ],
        [pltpu.VMEM((block + 8, wide), f32), pltpu.VMEM((block + 8, wide), f32)],
        "filter_backward",
        [pair_all, down_grad],
    )
    dhidden = (
        dot_nt(dinner, in_weight[:, :wide])
        + dot_nt(dgate_z, in_weight[:, wide:])
        + dot_nt(dheads, group_in)
    )
    dhidden = scatter_ctx(dhidden.astype(bf16), n)
    dfirst, first_gain_part = norm_backward(inputs, first_norm, first_gain, dhidden)
    tokens_grad = (dmixed + dfirst).astype(bf16)[None]

    small_grad = jnp.concatenate(
        [
            select_part[: RANK + 2 * NS],
            step_part[:RANK],
            decay_part,
            filter_vecs[4 : 4 + CONV],
            filter_vecs[3:4],
            scan_vecs[0:3],
        ]
    )[:, :channels]
    attend_gain_full = lax.dynamic_update_slice_in_dim(
        jnp.zeros((1, n * head_width), f32), attend_gain_part[0:1], c * head_width, axis=1
    )[0, :width]
    gain_part = jnp.stack([first_gain_part, attend_gain_full, post_gain_part]).reshape(3, m, shard)
    gain_part = pad_to(
        jnp.moveaxis(gain_part, 1, 0).reshape(m, 3 * shard), 1, gain_rows * small_width
    )
    small_part = jnp.concatenate(
        [
            small_grad.T.reshape(m, piece, small_width),
            gain_part.reshape(m, gain_rows, small_width),
        ],
        axis=1,
    )
    small_rows_count = up_to(piece + gain_rows, 2 * 16 * wide // small_width) * small_width // wide
    small_part = pad_to(
        small_part.reshape(m, -1), 1, small_rows_count * wide
    ).reshape(m, small_rows_count, wide)
    in_part = dot_tn(hidden, dinner).reshape(m, shard, wide)
    in_grad = scatter_z(
        jnp.concatenate([in_part, small_part], axis=1).astype(bf16).reshape(-1, wide)
    )

    spots = jnp.array([masks(n).index(mask) for mask in range(n)], dtype=jnp.int32)
    where = spots[c ^ jnp.arange(n, dtype=jnp.int32)]
    gate_grad, up_grad = unpack_columns(
        pair_all,
        where,
        [
            (k, f * shard_hidden, hidden_piece, k * hidden_wide + f * hidden_piece, hidden_piece)
            for k in range(2)
            for f in range(m)
        ],
        [weight.shape[1] for weight in (gate_weight, up_weight)],
        n,
        "unpack_pair",
    )
    down_grad = unpack_rows(gather_ctx(down_grad, n), where, hidden_piece, n, "unpack_down")
    mixer_out_grad = unpack_rows(gather_ctx(mixer_out_grad, n), where, piece, n, "unpack_mixer")
    attend_grad = gather_ctx(attend_grad, n)
    kv_wide = n * pair
    out_at = head_width + 2 * pair
    gate_at = out_at + out_wide
    query_grad, key_parts, value_parts, out_grad, gate_half = unpack_columns(
        attend_grad,
        where,
        [
            (0, 0, head_width, 0, head_width),
            (1, 0, pair, head_width, pair),
            (2, 0, pair, head_width + pair, pair),
            (3, 0, out_piece, out_at, out_piece),
        ]
        + [(4, f * shard_channels, piece, gate_at + f * piece, piece) for f in range(m)],
        [width, kv_wide, kv_wide, width, inner_all],
        n,
        "unpack_attention",
    )

    def group_sum(parts):
        total = jnp.zeros((shard, kv_pad), f32)
        for index in range(n):
            low_at = min(index * heads // GROUP, KV_HEADS - 1) * HEAD_DIM
            item = parts[:, index * pair : (index + 1) * pair]
            total = total + jnp.pad(item, ((0, 0), (low_at, kv_pad - pair - low_at)))
        return total[:, : KV_HEADS * HEAD_DIM]

    in_grad = gather_ctx(in_grad, n).reshape(n, shard + small_rows_count, wide)
    (inner_half,) = unpack_columns(
        in_grad[:, :shard].reshape(n * shard, wide),
        where,
        [(0, f * shard_channels, piece, f * piece, piece) for f in range(m)],
        [inner_all],
        n,
        "unpack_inner",
    )
    mixer_in_grad = jnp.concatenate([inner_half, gate_half], axis=1)
    small_sum = in_grad[:, shard:].astype(f32).reshape(n, -1)[:, : (piece + gain_rows) * small_width]
    small_sum = small_sum[where].reshape(n, piece + gain_rows, small_width)
    channel_grad = small_sum[:, :piece].reshape(shard_channels, small_width)
    gain_grad = jnp.sum(small_sum[:, piece:], axis=0).reshape(-1)[: 3 * shard].reshape(3, shard)

    at = RANK + 2 * NS
    select_grad = channel_grad[:, :at]
    step_grad = channel_grad[:, at : at + RANK].T
    at += RANK
    decay_grad = channel_grad[:, at : at + NS]
    at += NS
    kernel_grad = channel_grad[:, at : at + CONV].T
    at += CONV
    return (
        layer_out,
        tokens_grad,
        gain_grad[0],
        query_grad,
        group_sum(key_parts),
        group_sum(value_parts),
        out_grad,
        gain_grad[1],
        mixer_in_grad,
        kernel_grad,
        channel_grad[:, at],
        select_grad,
        step_grad,
        channel_grad[:, at + 1],
        decay_grad,
        channel_grad[:, at + 2],
        channel_grad[:, at + 3],
        mixer_out_grad,
        gain_grad[2],
        gate_grad,
        up_grad,
        down_grad,
    )


def solution(mesh):
    rows_spec = P("fsdp", None)
    lanes_spec = P(None, "fsdp")
    flat = P("fsdp")
    activations = P("fsdp", "ctx", None)
    weight_specs = (
        flat, rows_spec, rows_spec, rows_spec, rows_spec, flat, rows_spec, lanes_spec, flat, rows_spec,
        lanes_spec, flat, rows_spec, flat, flat, rows_spec, flat, rows_spec, rows_spec, rows_spec,
    )
    return jax.shard_map(
        on_device,
        mesh=mesh,
        in_specs=(activations, activations, P()) + weight_specs,
        out_specs=(activations, activations) + weight_specs,
        check_vma=False,
    )
```

```python
import math

import jax
import jax.numpy as jnp
from jax import lax
from jax.experimental import pallas as pl
from jax.experimental.pallas import tpu as pltpu
from jax.sharding import PartitionSpec as P

HEADS = 25
KV_HEADS = 5
HEAD_DIM = 64
GROUP = HEADS // KV_HEADS
CONV = 4
RANK = 100
NS = 16
EPS = 1e-05
NEG = -1e30
SCALE = 1.0 / math.sqrt(HEAD_DIM)
STEP = 16
VMEM = 56 * 1024 * 1024
SIDE = 64
bf16 = jnp.bfloat16
f32 = jnp.float32


def up_to(value, unit):
    return -(-value // unit) * unit


def dot(left, right, contract=((1,), (0,)), precision=None):
    return lax.dot_general(
        left, right, (contract, ((), ())), preferred_element_type=f32, precision=precision
    )


def dot_tn(left, right):
    return dot(left, right, ((0,), (0,)))


def dot_nt(left, right):
    return dot(left, right, ((1,), (1,)))


def pad_to(values, axis, size):
    widths = [(0, 0)] * values.ndim
    widths[axis] = (0, size - values.shape[axis])
    return jnp.pad(values, widths)


def masks(size):
    return list(range(0, size, 2)) + list(range(1, size, 2))


def swap(values, mask, size):
    return lax.ppermute(values, "ctx", [(i, i ^ mask) for i in range(size)])


def swaps(values, size):
    near = [values] + [swap(values, m, size) for m in range(2, size, 2)]
    return near + [swap(item, 1, size) for item in near]


def assemble(parts, *earlier):
    count = len(parts)
    step = parts[0].shape[0]
    shape = (count * step,) + parts[0].shape[1:]

    def body(*refs):
        out, sems = refs[-2:]
        copies = [
            pltpu.make_async_copy(refs[j], out.at[pl.ds(j * step, step)], sems.at[j])
            for j in range(count)
        ]
        for copy in copies:
            copy.start()
        for copy in copies:
            copy.wait()

    spec = pl.BlockSpec(memory_space=pl.ANY)
    return pl.pallas_call(
        body,
        in_specs=[spec] * (count + len(earlier)),
        out_specs=spec,
        out_shape=leaf(shape, parts[0].dtype),
        scratch_shapes=[pltpu.SemaphoreType.DMA((count,))],
        name="assemble",
    )(*parts, *earlier)


def gather_ctx(values, size):
    return assemble(swaps(values, size))


def split_dot(size, *products):
    def half(at):
        total = None
        for left, right, contract in products:
            rows_now = left.shape[0] // 2
            item = dot(left[at * rows_now : (at + 1) * rows_now], right, contract)
            total = item if total is None else total + item
        return total.astype(bf16)

    return half(0), half(1)


def fold_body(count, step):
    def body(index, near, got, own_o, *sent_o):
        for j in range(count):
            rows_now = slice(j * step, (j + 1) * step)
            total = near[rows_now, :].astype(f32) + got[rows_now, :].astype(f32)
            if j == 0:
                own_o[...] = total
            else:
                sent_o[j - 1][...] = total.astype(bf16)

    return body


def scatter_ctx(near, far, size, index):
    half = size // 2
    step, width = near.shape[0] // half, near.shape[1]
    got = swap(far, 1, size)
    total, *sent = block_call(
        fold_body(half, step),
        index,
        1,
        [(near, whole(near.shape)), (got, whole(near.shape))],
        [(leaf((step, width), f32), whole((step, width)))]
        + [(leaf((step, width), bf16), whole((step, width)))] * (half - 1),
        [],
        "fold_halves",
    )
    for k in range(1, half):
        total = total + swap(sent[k - 1], 2 * k, size).astype(f32)
    return total


def block_call(body, order, count, ins, outs, scratch, name, earlier=()):
    given = len(ins)
    ins = list(ins) + [(value, pl.BlockSpec(memory_space=pl.ANY)) for value in earlier]

    def trimmed(*refs):
        return body(*refs[: 1 + given], *refs[1 + len(ins) :])

    return pl.pallas_call(
        trimmed,
        grid_spec=pltpu.PrefetchScalarGridSpec(
            num_scalar_prefetch=1,
            grid=(count,),
            in_specs=[spec for _, spec in ins],
            out_specs=[spec for _, spec in outs],
            scratch_shapes=scratch,
        ),
        out_shape=[shape for shape, _ in outs],
        compiler_params=pltpu.CompilerParams(
            dimension_semantics=("arbitrary",), vmem_limit_bytes=VMEM
        ),
        name=name,
    )(order, *[value for value, _ in ins])


def after(values, *earlier):
    def body(*refs):
        del refs

    spec = pl.BlockSpec(memory_space=pl.ANY)
    return pl.pallas_call(
        body,
        in_specs=[spec] * (1 + len(earlier)),
        out_specs=spec,
        out_shape=leaf(values.shape, values.dtype),
        input_output_aliases={0: 0},
        name="after",
    )(values, *earlier)


def whole(shape):
    zeros = (0,) * len(shape)
    return pl.BlockSpec(shape, lambda i, order: zeros)


def rows(block, width, pick):
    return pl.BlockSpec((block, width), lambda i, order: (order[pick(i)], 0))


def columns_at(block, width, pick, index):
    return pl.BlockSpec((block, width), lambda i, order: (order[pick(i)], index))


def leaf(shape, dtype):
    return jax.ShapeDtypeStruct(shape, dtype)


def filter_taps(ext, vecs, block):
    total = vecs[3:4, :]
    for j in range(CONV):
        total = total + vecs[4 + j : 5 + j, :] * ext[5 + j : 5 + j + block, :]
    return total


def filter_forward_body(block):
    def body(order, projected, vecs, select, mixed_o, selected_o, ext):
        step = pl.program_id(0)
        held = projected.shape[1] // 2

        @pl.when(step == 0)
        def _():
            ext[...] = jnp.zeros_like(ext)

        @pl.when(step > 0)
        def _():
            ext[0:8, :] = ext[block : block + 8, :]

        ext[8 : block + 8, 0:held] = projected[:, 0:held].astype(bf16).astype(f32)
        total = filter_taps(ext, vecs, block)
        mixed = (total * jax.nn.sigmoid(total)).astype(bf16)
        mixed_o[...] = mixed
        selected_o[...] = dot(mixed, select[...]).astype(bf16)

    return body


def rate_of(selected, step_weight, vecs):
    rank = selected[...].astype(bf16)
    raw = dot(rank, step_weight[...]) + vecs[0:1, :]
    rate = jnp.maximum(raw, 0.0) + jnp.log1p(jnp.exp(-jnp.abs(raw)))
    return rank, raw, rate


def scan_forward_body(block):
    def body(
        order, selected, sides, mixed, projected, step_weight, vecs, decay,
        scanned_o, starts_o, scaled_o, state_s, rate_s, drive_s, gate_s,
    ):
        held = projected.shape[1] // 2

        @pl.when(pl.program_id(0) == 0)
        def _():
            state_s[...] = jnp.zeros_like(state_s)
            gate_s[...] = jnp.zeros_like(gate_s)

        gate_s[:, 0:held] = projected[...][:, held:]

        _, _, rate = rate_of(selected, step_weight, vecs)
        wide = mixed[...].astype(f32)
        rate_s[...] = rate
        drive_s[...] = rate * wide
        starts_o[0] = state_s[...]
        decay_mat = decay[...]

        def group(g, state):
            base = pl.multiple_of(g * STEP, STEP)
            rates = rate_s[pl.ds(base, STEP), :]
            drives = drive_s[pl.ds(base, STEP), :]
            side = sides[0, g]
            for j in range(STEP):
                state = (
                    jnp.exp(rates[j : j + 1, :] * decay_mat) * state
                    + drives[j : j + 1, :] * side[:NS, j : j + 1]
                )
                scanned_o[pl.ds(base + j, 1), :] = jnp.sum(
                    state * side[NS:, j : j + 1], axis=0, keepdims=True
                )
            return state

        state_s[...] = lax.fori_loop(0, block // STEP, group, state_s[...])
        gate = gate_s[...]
        gated = (scanned_o[...] + vecs[1:2, :] * wide) * (gate * jax.nn.sigmoid(gate))
        lane = lax.broadcasted_iota(jnp.int32, gated.shape, 1)
        squares = jnp.sum(gated * gated, axis=1, keepdims=True)
        scaled_o[...] = jnp.where(lane == held, squares, gated * vecs[2:3, :]).astype(bf16)

    return body


def scan_backward_body(block):
    def body(
        order, selected, sides, mixed, projected, scanned, grad_in, scalars, starts, step_weight, vecs, decay,
        normed_o, dgate_o, dmixed_o, drank_o, dsides_o, vec_o, step_o, decay_o,
        gate_s, lam_s, rate_s, drive_s, dscan_s, drate_s, pull_s, hist_s, factor_s, read_s, write_s,
    ):
        width = decay.shape[1]
        held = projected.shape[1] // 2

        @pl.when(pl.program_id(0) == 0)
        def _():
            gate_s[...] = jnp.zeros_like(gate_s)
            lam_s[...] = jnp.zeros_like(lam_s)
            vec_o[...] = jnp.zeros_like(vec_o)
            step_o[...] = jnp.zeros_like(step_o)
            decay_o[...] = jnp.zeros_like(decay_o)

        rank, raw, rate = rate_of(selected, step_weight, vecs)
        wide = mixed[...].astype(f32)
        rate_s[...] = rate
        drive_s[...] = rate * wide
        gate_s[:, 0:held] = projected[...][:, held:]
        gate = gate_s[...]
        sig = jax.nn.sigmoid(gate)
        act = gate * sig
        before = scanned[...] + vecs[1:2, :] * wide
        gated = before * act
        norm = scalars[:, 2:3]
        centre = scalars[:, 3:4]
        grad = grad_in[...]
        gated_norm = gated * norm
        normed_o[...] = (gated_norm * vecs[2:3, :])[:, 0:held].astype(bf16)
        dgated = norm * (vecs[2:3, :] * grad) - gated * centre
        dscan = dgated * act
        dscan_s[...] = dscan
        dgate = dgated * before * (sig * (1.0 + gate * (1.0 - sig)))
        dgate_o[...] = dgate[:, 0:held].astype(bf16)
        vec_o[1:2, :] += jnp.sum(dscan * wide, axis=0, keepdims=True)
        vec_o[2:3, :] += jnp.sum(grad * gated_norm, axis=0, keepdims=True)
        decay_mat = decay[...]

        def forward(g, state):
            base = pl.multiple_of(g * STEP, STEP)
            rates = rate_s[pl.ds(base, STEP), :]
            drives = drive_s[pl.ds(base, STEP), :]
            side = sides[0, g]
            for j in range(STEP):
                factor = jnp.exp(rates[j : j + 1, :] * decay_mat)
                factor_s[base + j] = factor
                state = factor * state + drives[j : j + 1, :] * side[:NS, j : j + 1]
                hist_s[base + j + 1] = state
            return state

        hist_s[0] = starts[0]
        lax.fori_loop(0, block // STEP, forward, starts[0])

        def fold(values):
            total = values[:, 0:128]
            for at in range(128, width, 128):
                total = total + values[:, at : at + 128]
            return total

        def backward(i, carry):
            lam_in, decay_sum = carry
            g = block // STEP - 1 - i
            base = pl.multiple_of(g * STEP, STEP)
            rates = rate_s[pl.ds(base, STEP), :]
            drives = drive_s[pl.ds(base, STEP), :]
            dscans = dscan_s[pl.ds(base, STEP), :]
            side = sides[0, g]
            for j in range(STEP - 1, -1, -1):
                at = base + j
                row = dscans[j : j + 1, :]
                lam = lam_in + row * side[NS:, j : j + 1]
                read_s[pl.ds(at * NS, NS), :] = fold(hist_s[at + 1] * row)
                write_s[pl.ds(at * NS, NS), :] = fold(lam * drives[j : j + 1, :])
                pull = jnp.sum(lam * side[:NS, j : j + 1], axis=0, keepdims=True)
                lam_in = factor_s[at] * lam
                kept = lam_in * hist_s[at]
                decay_sum = decay_sum + rates[j : j + 1, :] * kept
                drate_s[pl.ds(at, 1), :] = jnp.sum(decay_mat * kept, axis=0, keepdims=True)
                pull_s[pl.ds(at, 1), :] = pull
            return (lam_in, decay_sum)

        lam, decay_sum = lax.fori_loop(
            0, block // STEP, backward, (lam_s[...], jnp.zeros_like(lam_s))
        )
        lam_s[...] = lam
        decay_o[...] += decay_sum * decay_mat
        pulled = pull_s[...]
        draw = (drate_s[...] + wide * pulled) * jax.nn.sigmoid(raw)
        vec_o[0:1, :] += jnp.sum(draw, axis=0, keepdims=True)
        low = draw.astype(bf16)
        dmixed_o[...] = vecs[1:2, :] * dscan + rate * pulled
        drank_o[...] = dot_nt(low, step_weight[...])
        step_o[...] += dot_tn(rank, low)
        ones = jnp.ones((8, 128), f32)
        high = lax.Precision.HIGHEST
        dsides_o[0, 0] = dot(ones, write_s[...], ((1,), (1,)), high)
        dsides_o[0, 1] = dot(ones, read_s[...], ((1,), (1,)), high)

    return body


def filter_backward_body(block, count):
    def body(
        order, projected, before, dgate, mixed, dmixed, dselected, select, vecs,
        dprojected_o, select_o, vec_o, ext, ext_grad, both_s,
    ):
        step = pl.program_id(0)
        held = projected.shape[1] // 2

        @pl.when(step == 0)
        def _():
            ext[...] = jnp.zeros_like(ext)
            ext_grad[block : block + 8, :] = jnp.zeros((8, ext.shape[1]), f32)
            select_o[...] = jnp.zeros_like(select_o)
            vec_o[...] = jnp.zeros_like(vec_o)

        @pl.when(step > 0)
        def _():
            ext_grad[block : block + 8, :] = ext_grad[0:8, :]

        first = jnp.where(step == count - 1, 0.0, 1.0)
        ext[0:8, 0:held] = before[block - 8 :, 0:held].astype(bf16).astype(f32) * first
        ext[8 : block + 8, 0:held] = projected[:, 0:held].astype(bf16).astype(f32)
        total = filter_taps(ext, vecs, block)
        sig = jax.nn.sigmoid(total)
        low = dselected[...]
        dmix = dmixed[...] + dot_nt(low, select[...])
        dfilt = dmix * (sig * (1.0 + total * (1.0 - sig)))
        ext_grad[0:block, :] = dfilt
        dinner = jnp.zeros_like(dfilt)
        vec_o[3:4, :] += jnp.sum(dfilt, axis=0, keepdims=True)
        for j in range(CONV):
            at = CONV - 1 - j
            dinner = dinner + vecs[4 + j : 5 + j, :] * ext_grad[at : at + block, :]
            vec_o[4 + j : 5 + j, :] += jnp.sum(
                dfilt * ext[5 + j : 5 + j + block, :], axis=0, keepdims=True
            )
        both_s[:, 0:held] = dinner[:, 0:held]
        both_s[:, held:] = dgate[...].astype(f32)
        dprojected_o[...] = both_s[...].astype(bf16)
        select_o[...] += dot_tn(low, mixed[...])

    return body


def half_mask(half):
    lane = lax.broadcasted_iota(jnp.int32, (1, 128), 1)
    return jnp.where((lane >= 64 * half) & (lane < 64 * half + 64), 1.0, 0.0)


def softmax_rows(query, key, allowed):
    scores = jnp.where(allowed, dot_nt(query, key) * SCALE, NEG)
    weights = jnp.exp(scores - jnp.max(scores, axis=-1, keepdims=True))
    return weights * (1.0 / jnp.sum(weights, axis=-1, keepdims=True))


def attention_forward_body(valid, query, key, value, query_pos, key_pos, gain, out_o, scaled_o):
    allowed = key_pos[...] <= query_pos[...]
    squares = jnp.zeros((query.shape[0], 1), f32)
    for at in range(0, query.shape[1], 128):
        key_tile = key[:, at : at + 128]
        value_tile = value[:, at : at + 128]
        tile = jnp.zeros((query.shape[0], 128), f32)
        for half in range(2):
            mask = half_mask(half)
            part = query[:, at : at + 128] * mask.astype(bf16)
            probs = softmax_rows(part, key_tile, allowed).astype(bf16)
            live = valid[at // 64 + half].astype(f32)
            tile = tile + dot(probs, value_tile) * (mask * live)
        out_o[:, at : at + 128] = tile
        scaled_o[:, at : at + 128] = (tile * gain[:, at : at + 128]).astype(bf16)
        squares = squares + jnp.sum(tile * tile, axis=1, keepdims=True)
    at = query.shape[1]
    lane = lax.broadcasted_iota(jnp.int32, (query.shape[0], 128), 1)
    scaled_o[:, at : at + 128] = jnp.where(lane == 0, squares, 0.0).astype(bf16)


def unit_body(both, dunit, unit_o, dboth_o):
    held = dunit.shape[1]
    values = both[...]
    gate, up = values[:, :held], values[:, held:]
    grad = dunit[...]
    sig = jax.nn.sigmoid(gate)
    act = gate * sig
    unit_o[...] = (act * up).astype(bf16)
    dgate = grad * up * (sig * (1.0 + gate * (1.0 - sig)))
    dboth_o[...] = jnp.concatenate([dgate, grad * act], axis=1).astype(bf16)


def norm_body(index, gain, *refs):
    out = refs[-1]
    step = refs[0].shape[0]
    for j, ref in enumerate(refs[:-1]):
        values = ref[...].astype(f32)
        norm = lax.rsqrt(jnp.mean(values * values, axis=1, keepdims=True) + EPS)
        out[j * step : (j + 1) * step, :] = (values * norm * gain[...]).astype(bf16)


def attention_backward_body(
    valid, query, key, value, query_pos, key_pos, gain, out, grad_in, scalars,
    dquery_o, dpair_o, normed_o, gain_o, dkey_s, dvalue_s,
):
    @pl.when(pl.program_id(0) == 0)
    def _():
        dkey_s[...] = jnp.zeros_like(dkey_s)
        dvalue_s[...] = jnp.zeros_like(dvalue_s)
        gain_o[...] = jnp.zeros_like(gain_o)

    allowed = key_pos[...] <= query_pos[...]
    norm = scalars[:, 0:1]
    centre = scalars[:, 1:2]
    for at in range(0, query.shape[1], 128):
        lanes = slice(at, at + 128)
        key_tile = key[:, lanes]
        value_tile = value[:, lanes]
        attended = out[:, lanes]
        grad = grad_in[:, lanes]
        normed = attended * norm
        normed_o[:, lanes] = (normed * gain[:, lanes]).astype(bf16)
        gain_o[0:1, lanes] += jnp.sum(grad * normed, axis=0, keepdims=True)
        dout = (norm * (gain[:, lanes] * grad) - attended * centre).astype(bf16)
        dquery = jnp.zeros(attended.shape, f32)
        dkey = jnp.zeros((key.shape[0], 128), f32)
        dvalue = jnp.zeros((key.shape[0], 128), f32)
        for half in range(2):
            mask = half_mask(half)
            part = query[:, lanes] * mask.astype(bf16)
            dpart = dout * mask.astype(bf16)
            probs = softmax_rows(part, key_tile, allowed)
            dprobs = dot_nt(dpart, value_tile)
            mean = jnp.sum(dprobs * probs, axis=-1, keepdims=True)
            dscores = (probs * (dprobs - mean)).astype(bf16)
            dvalue = dvalue + dot_tn(probs.astype(bf16), dpart)
            dquery = dquery + dot(dscores, key_tile) * (mask * SCALE)
            dkey = dkey + dot_tn(dscores, part) * SCALE
        dquery_o[:, lanes] = dquery.astype(bf16)
        dkey_s[:, lanes] += dkey
        dvalue_s[:, lanes] += dvalue

    @pl.when(pl.program_id(0) == pl.num_programs(0) - 1)
    def _():
        held = dkey_s.shape[1]
        dpair_o[:, :held] = dkey_s[...].astype(bf16)
        dpair_o[:, held:] = dvalue_s[...].astype(bf16)


def pack_body(groups, width, piece):
    window = up_to(piece + 127, 128)

    def body(index, *refs):
        out_o, acc = refs[-2:]
        acc[...] = jnp.zeros_like(acc)
        for which, start, at in groups:
            weight = refs[which]
            source = start + index[0] * piece
            tile = jnp.minimum(source // 128, (width - window) // 128)
            base = pl.multiple_of(tile * 128, 128)
            low = at % 128
            span = up_to(low + piece, 128)
            row = lax.broadcasted_iota(jnp.int32, (window, span), 0)
            lane = lax.broadcasted_iota(jnp.int32, (window, span), 1) - low
            pick = (row - (source - base) == lane) & (lane >= 0) & (lane < piece)
            pick = jnp.where(pick, 1.0, 0.0).astype(bf16)
            acc[:, at - low : at - low + span] += dot(weight[:, pl.ds(base, window)], pick)
        out_o[...] = acc[:, : out_o.shape[1]].astype(bf16)

    return body


def row_block(count):
    return 80 if count % 80 == 0 else count


def join_body(axis):
    def body(index, *refs):
        at = 0
        for ref in refs[:-1]:
            size = ref.shape[axis]
            if axis == 0:
                refs[-1][at : at + size, :] = ref[...]
            else:
                refs[-1][:, at : at + size] = ref[...]
            at += size

    return body


def join(parts, index, axis, name, earlier):
    shape = list(parts[0].shape)
    shape[axis] = sum(part.shape[axis] for part in parts)
    return block_call(
        join_body(axis),
        index,
        1,
        [(part, whole(part.shape)) for part in parts],
        [(leaf(tuple(shape), bf16), whole(tuple(shape)))],
        [],
        name,
        earlier,
    )[0]


def pack_columns(weights, index, groups, out_wide, piece, name, earlier=()):
    count, width = weights[0].shape
    block = row_block(count)
    return block_call(
        pack_body(groups, width, piece),
        index,
        count // block,
        [(weight, pl.BlockSpec((block, width), lambda i, index: (i, 0))) for weight in weights],
        [
            (
                leaf((count, out_wide), bf16),
                pl.BlockSpec((block, out_wide), lambda i, index: (i, 0)),
            )
        ],
        [pltpu.VMEM((block, up_to(out_wide, 128)), f32)],
        name,
        earlier,
    )[0]


def unpack_columns(gathered, where, moves, widths, size, name, count=None):
    width = gathered.shape[-1]
    gathered = gathered.reshape(size, -1, width)
    count = count or gathered.shape[1]
    block = row_block(count)

    def body(where, source, *outs):
        for index in range(size):
            values = source[where[index]].astype(f32)
            for out, first, stride, at, piece in moves:
                start = first + index * stride
                piece = min(piece, widths[out] - start)
                if piece > 0:
                    outs[out][:, start : start + piece] = values[:, at : at + piece]

    return block_call(
        body,
        where,
        count // block,
        [
            (
                gathered,
                pl.BlockSpec((size, block, width), lambda i, where: (0, i, 0)),
            )
        ],
        [
            (leaf((count, full), f32), pl.BlockSpec((block, full), lambda i, where: (i, 0)))
            for full in widths
        ],
        [],
        name,
    )


def unpack_rows(gathered, where, piece, size, width, turned, name):
    total, full = gathered.shape
    lanes = 256

    def body(where, source, out):
        for index in range(size):
            values = source[where[index]].astype(f32)
            put = slice(index * piece, (index + 1) * piece)
            if turned:
                out[:, put] = values.T[:, :piece]
            else:
                out[put, :] = values[:piece]

    shape = (width, size * piece) if turned else (size * piece, width)
    out_block = (lanes, size * piece) if turned else (size * piece, lanes)
    spot = (lambda i, where: (i, 0)) if turned else (lambda i, where: (0, i))

    return block_call(
        body,
        where,
        -(-width // lanes),
        [
            (
                gathered.reshape(size, total // size, full),
                pl.BlockSpec((size, total // size, lanes), lambda i, where: (0, 0, i)),
            )
        ],
        [(leaf(shape, f32), pl.BlockSpec(out_block, spot))],
        [],
        name,
    )[0]


def inverse_rms(values):
    return lax.rsqrt(jnp.mean(values * values, axis=-1, keepdims=True) + EPS)


def norm_backward(values, norm, gain, grad):
    scaled = grad * gain
    centre = norm**3 * jnp.mean(values * scaled, axis=-1, keepdims=True)
    return norm * scaled - values * centre, jnp.sum(grad * values * norm, axis=0)


def split_low(values):
    high = lax.reduce_precision(values, 8, 7)
    return [high.astype(bf16), (values - high).astype(bf16)]


def on_device(
    tokens, cotangent, deal_table, norm_gain, query_weight, key_weight, value_weight, attention_out,
    attention_gain, mixer_in, filter_kernel, filter_bias, select_weight, step_weight, step_bias, decay_log,
    skip_gain, mixer_gain, mixer_out, post_gain, gate_weight, up_weight, down_weight,
):
    n = lax.axis_size("ctx")
    m = lax.axis_size("fsdp")
    c = lax.axis_index("ctx")
    z = lax.axis_index("fsdp")
    own = tokens.shape[1]
    block = own // 2
    total_rows = own * n
    count = 2 * n
    width = tokens.shape[2]
    shard = width // m
    heads = -(-HEADS // n)
    heads += heads % 2
    head_width = heads * HEAD_DIM
    shard_channels = filter_bias.shape[0]
    piece = shard_channels // n
    channels = m * piece
    inner_all = shard_channels * m
    shard_hidden = down_weight.shape[0]
    hidden_piece = shard_hidden // n
    piece_rows, hidden_rows = up_to(piece, 16), up_to(hidden_piece, 16)
    held, hidden_held = m * piece_rows, m * hidden_rows
    wide = up_to(held + 1, 128)
    sent_width = width + SIDE
    out_piece = width // n
    out_wide = up_to(out_piece, 128)

    def gather_z(values, tiled=True):
        return lax.all_gather(values, "fsdp", axis=0, tiled=tiled)

    def columns(values, start, size):
        return lax.dynamic_slice_in_dim(values, start, size, axis=1)

    in_groups = [
        (0, p * inner_all + f * shard_channels, p * held + f * piece_rows)
        for p in range(2)
        for f in range(m)
    ]
    in_local = pack_columns([mixer_in], c.reshape(1), in_groups, 2 * held, piece, "pack_mixer")
    in_weight = gather_z(in_local)
    own_index = after(c.reshape(1), in_local)
    c = own_index[0]
    token_parts = swaps(after(tokens[0], in_local), n)
    small_rows = jnp.concatenate(
        [
            select_weight,
            step_weight.T,
            decay_log,
            filter_kernel.T,
            filter_bias[:, None],
            step_bias[:, None],
            skip_gain[:, None],
            mixer_gain[:, None],
        ],
        axis=1,
    )
    small_width = small_rows.shape[1]
    small_rows = lax.dynamic_slice_in_dim(small_rows, c * piece, piece, axis=0)
    gains = jnp.stack([norm_gain, attention_gain, post_gain]).reshape(-1)
    gain_rows = -(-3 * shard // small_width)
    gains = pad_to(gains, 0, gain_rows * small_width).reshape(gain_rows, small_width)
    small_local = jnp.concatenate([small_rows, gains])
    turned = [
        lax.ppermute(small_local, "fsdp", [(i, (i + k) % m) for i in range(m)])
        for k in range(m - 1, 0, -1)
    ] + [small_local]
    small_all = lax.dynamic_slice_in_dim(jnp.stack(turned + turned), m - 1 - z, m, axis=0)
    small = pad_to(small_all[:, :piece], 1, piece_rows).reshape(held, small_width)
    gains_all = small_all[:, piece:].reshape(m, gain_rows * small_width)[:, : 3 * shard]
    gains_all = jnp.moveaxis(gains_all.reshape(m, 3, shard), 0, 1).reshape(3, width).astype(f32)
    first_gain, attend_gain, after_gain = gains_all[0:1], gains_all[1:2], gains_all[2:3]

    def first_group(index):
        return jnp.minimum(index * heads // GROUP, KV_HEADS - 1)

    group_at = first_group(c)
    kv_pad = (KV_HEADS + 1) * HEAD_DIM
    pair = 2 * HEAD_DIM
    attend_local = join(
        [
            columns(pad_to(query_weight, 1, n * head_width), c * head_width, head_width),
            columns(pad_to(key_weight, 1, kv_pad), group_at * HEAD_DIM, pair),
            columns(pad_to(value_weight, 1, kv_pad), group_at * HEAD_DIM, pair),
        ],
        own_index,
        1,
        "pack_attention",
        [in_local],
    )
    head_ids = c * heads + jnp.arange(heads, dtype=jnp.int32)
    valid = (head_ids < HEADS).astype(jnp.int32)
    upper = jnp.minimum(head_ids // GROUP, KV_HEADS - 1) > group_at

    def row_slice(weight, size):
        cut = lax.dynamic_slice_in_dim(weight, c * size, size, axis=0)
        return pad_to(cut, 0, up_to(size, 16))

    out_cut = columns(attention_out, c * out_piece, out_piece).reshape(-1)
    out_rows = up_to(-(-out_cut.shape[0] // width), 16)
    rows_local = join(
        [
            row_slice(mixer_out, piece),
            pad_to(out_cut, 0, out_rows * width).reshape(out_rows, width),
        ],
        own_index,
        0,
        "pack_rows",
        [in_local],
    )
    pair_groups = [
        (k, f * shard_hidden, k * hidden_held + f * hidden_rows) for k in range(2) for f in range(m)
    ]
    pair_local = pack_columns(
        [gate_weight, up_weight],
        own_index,
        pair_groups,
        2 * hidden_held,
        hidden_piece,
        "pack_pair",
        [in_local],
    )
    down_local = row_slice(down_weight, hidden_piece)

    inputs = tokens[0].astype(f32)
    first_norm = inverse_rms(inputs)
    hidden = block_call(
        norm_body,
        own_index,
        1,
        [(first_gain, whole(first_gain.shape))]
        + [(item, whole(item.shape)) for item in token_parts],
        [(leaf((total_rows, width), bf16), whole((total_rows, width)))],
        [],
        "norm_tokens",
        [attend_local, rows_local, pair_local],
    )[0]

    projected = dot(hidden, in_weight)
    attend_all = gather_z(after(attend_local, in_weight))

    def extended(weight, rows_now, at):
        weight = jnp.pad(weight, ((0, rows_now - weight.shape[0]), (0, SIDE)))
        spot = (jnp.arange(rows_now) == at)[:, None] & (jnp.arange(sent_width) == width)[None, :]
        return jnp.where(spot, jnp.ones((), bf16), weight)

    lane_dim = jnp.arange(head_width, dtype=jnp.int32) % HEAD_DIM
    target = jnp.where(jnp.repeat(upper, HEAD_DIM), HEAD_DIM, 0) + lane_dim
    target = jnp.concatenate([target, target + pair])
    side_now = jnp.arange(2 * head_width, dtype=jnp.int32) // head_width
    spread = (target[None, :] == jnp.arange(2 * pair, dtype=jnp.int32)[:, None]) & (
        side_now[None, :] == (jnp.arange(2 * pair, dtype=jnp.int32) // pair)[:, None]
    )
    spread = spread.astype(bf16)

    others = c ^ jnp.array(masks(n), dtype=jnp.int32)
    firsts = deal_table[others]
    places = jnp.stack([firsts, count - 1 - firsts], axis=1).reshape(count)
    ids = jnp.arange(count, dtype=jnp.int32)
    order = jnp.sum(jnp.where(places[None, :] == ids[:, None], ids[None, :], 0), axis=1)
    position = (places[:, None] * block + jnp.arange(block, dtype=jnp.int32)[None, :]).reshape(-1)

    small_t = pad_to(small.astype(f32).T, 1, wide)
    select_own = pad_to(pad_to(small[:, : RANK + 2 * NS], 0, wide), 1, 256)
    step_own = pad_to(small_t[RANK + 2 * NS : 2 * RANK + 2 * NS], 0, 128).astype(bf16)
    at = 2 * RANK + 2 * NS
    decay_own = -jnp.exp(small_t[at : at + NS])
    at += NS
    vecs = jnp.concatenate([small_t[at + CONV + 1 : at + CONV + 4], small_t[at + CONV : at + CONV + 1], small_t[at : at + CONV]])

    def halves(values):
        return values[: total_rows // 2], values[total_rows // 2 :]

    upstream = cotangent[0]
    upstream_all = gather_ctx(upstream, n)
    heads_in = dot(hidden, attend_all).astype(bf16)
    pair_in = dot(heads_in[:, head_width:], spread).astype(bf16)

    forward = lambda i: i
    reverse = lambda i: count - 1 - i
    mixed_in, selected_part = block_call(
        filter_forward_body(block),
        order,
        count,
        [
            (projected, rows(block, 2 * held, forward)),
            (vecs, whole(vecs.shape)),
            (select_own, whole(select_own.shape)),
        ],
        [
            (leaf((total_rows, wide), bf16), rows(block, wide, forward)),
            (leaf((total_rows, 256), bf16), rows(block, 256, forward)),
        ],
        [pltpu.VMEM((block + 8, wide), f32)],
        "filter_forward",
    )
    selected_own = scatter_ctx(*halves(selected_part), n, own_index)
    rows_all = gather_z(after(rows_local, attend_all, selected_own), tiled=False)
    mixer_out_own = extended(rows_all[:, :piece_rows].reshape(held, width), wide, held)
    out_columns = rows_all[:, piece_rows:].reshape(m, -1)[:, : shard * out_piece]
    out_columns = out_columns.reshape(width, out_piece)
    out_own = lax.all_to_all(
        pad_to(out_columns, 0, n * head_width).reshape(n, head_width, out_piece), "ctx", 0, 0
    )
    out_own = jnp.moveaxis(out_own, 0, 1).reshape(head_width, width)
    out_own = extended(out_own, head_width + 128, head_width)

    query_block = min(256, total_rows)
    query_count = total_rows // query_block
    query_pos = position[:, None]
    key_pos = position[None, :]
    own_gain = lax.dynamic_slice_in_dim(
        pad_to(attend_gain, 1, n * head_width), c * head_width, head_width, axis=1
    )

    def part(index):
        return pl.BlockSpec((total_rows, head_width), lambda i, order: (0, index))

    def tall(size):
        return pl.BlockSpec((query_block, size), lambda i, order: (i, 0))

    attend_ins = [
        (heads_in, tall(head_width)),
        (pair_in, part(0)),
        (pair_in, part(1)),
        (query_pos, tall(1)),
        (key_pos, whole(key_pos.shape)),
        (own_gain, whole(own_gain.shape)),
    ]
    attended, attended_scaled = block_call(
        attention_forward_body,
        valid,
        query_count,
        attend_ins,
        [
            (leaf((total_rows, head_width), f32), tall(head_width)),
            (leaf((total_rows, head_width + 128), bf16), tall(head_width + 128)),
        ],
        [],
        "attention_forward",
    )

    plain = ((1,), (0,))
    across = ((1,), (1,))

    def branch_out(scaled, weight):
        got = scatter_ctx(*split_dot(n, (scaled, weight, plain)), n, own_index)
        return got[:, :width], got[:, width : width + 1]

    attend_sum, attend_squares = branch_out(attended_scaled, out_own)
    attend_norm = lax.rsqrt(attend_squares / (HEADS * HEAD_DIM) + EPS)

    selected = assemble(swaps(after(selected_own, pair_in), n), attended)
    sides = selected[:, RANK : RANK + 2 * NS].reshape(count, block // STEP, STEP, 2 * NS)
    sides = jnp.swapaxes(sides, 2, 3)
    side_spec = lambda pick: pl.BlockSpec((1,) + sides.shape[1:], lambda i, order: (order[pick(i)], 0, 0, 0))
    start_spec = lambda pick: pl.BlockSpec((1, NS, wide), lambda i, order: (order[pick(i)], 0, 0))
    scanned, starts, mixer_scaled = block_call(
        scan_forward_body(block),
        order,
        count,
        [
            (selected, rows(block, 128, forward)),
            (sides, side_spec(forward)),
            (mixed_in, rows(block, wide, forward)),
            (projected, rows(block, 2 * held, forward)),
            (step_own, whole(step_own.shape)),
            (vecs, whole(vecs.shape)),
            (decay_own, whole(decay_own.shape)),
        ],
        [
            (leaf((total_rows, wide), f32), rows(block, wide, forward)),
            (leaf((count, NS, wide), f32), start_spec(forward)),
            (leaf((total_rows, wide), bf16), rows(block, wide, forward)),
        ],
        [
            pltpu.VMEM((NS, wide), f32),
            pltpu.VMEM((block, wide), f32),
            pltpu.VMEM((block, wide), f32),
            pltpu.VMEM((block, wide), f32),
        ],
        "scan_forward",
    )
    pair_weight = gather_z(after(pair_local, rows_all, scanned))
    mixer_sum, mixer_squares = branch_out(mixer_scaled, mixer_out_own)
    mixer_norm = lax.rsqrt(mixer_squares / inner_all + EPS)

    mixed = inputs + 0.5 * (attend_norm * attend_sum + mixer_norm * mixer_sum)
    post_norm = inverse_rms(mixed)
    post = gather_ctx((mixed * post_norm * after_gain).astype(bf16), n)
    down_own = gather_z(after(down_local, pair_weight, post))
    both = dot(post, pair_weight)
    dunit = dot_nt(upstream_all, down_own)

    def strip(size):
        return pl.BlockSpec((own, size), lambda i: (i, 0))

    unit, dboth = pl.pallas_call(
        unit_body,
        grid=(n,),
        in_specs=[strip(2 * hidden_held), strip(hidden_held)],
        out_specs=[strip(hidden_held), strip(2 * hidden_held)],
        out_shape=[
            leaf((total_rows, hidden_held), bf16),
            leaf((total_rows, 2 * hidden_held), bf16),
        ],
        compiler_params=pltpu.CompilerParams(vmem_limit_bytes=VMEM),
        name="hidden_units",
    )(both, dunit)

    dpost = scatter_ctx(*split_dot(n, (dboth, pair_weight, across)), n, own_index)
    dnorm, post_gain_part = norm_backward(mixed, post_norm, after_gain, dpost)
    dmixed = upstream.astype(f32) + dnorm

    def scatter_z(values):
        return lax.psum_scatter(values, "fsdp", scatter_dimension=0, tiled=True)

    pair_part = dot_tn(post, dboth).astype(bf16)
    down_part = dot_tn(unit, upstream_all).astype(bf16)
    pair_grad = scatter_z(pair_part)
    pair_parts = swaps(pair_grad, n)
    down_grad = scatter_z(down_part)
    ffn_out = scatter_ctx(*split_dot(n, (unit, down_own, plain)), n, own_index)
    layer_out = (mixed + ffn_out).astype(bf16)[None]

    dbranch = (0.5 * dmixed).astype(bf16)
    dbranch_wide = dbranch.astype(f32)
    attend_centre = (
        attend_norm**3
        * jnp.sum(dbranch_wide * attend_sum, axis=1, keepdims=True)
        / (HEADS * HEAD_DIM)
    )
    mixer_centre = (
        mixer_norm**3 * jnp.sum(dbranch_wide * mixer_sum, axis=1, keepdims=True) / inner_all
    )
    extra = []
    for item in (attend_norm, attend_centre, mixer_norm, mixer_centre):
        extra += split_low(item)
    payload = jnp.concatenate([dbranch, pad_to(jnp.concatenate(extra, axis=1), 1, SIDE)], axis=1)
    payload = gather_ctx(after(payload, pair_part), n)
    scalars = payload[:, width : width + 8].astype(f32).reshape(total_rows, 4, 2).sum(axis=2)
    scalars = pad_to(scalars, 1, 128)

    dattend_in = dot_nt(payload, out_own)
    dmixer_in = dot_nt(payload, mixer_out_own)

    dquery, dpair, normed_a, attend_gain_part = block_call(
        attention_backward_body,
        valid,
        query_count,
        attend_ins
        + [
            (attended, tall(head_width)),
            (dattend_in, tall(head_width + 128)),
            (scalars, tall(128)),
        ],
        [
            (leaf((total_rows, head_width), bf16), tall(head_width)),
            (leaf((total_rows, 2 * head_width), bf16), whole((total_rows, 2 * head_width))),
            (leaf((total_rows, head_width), bf16), tall(head_width)),
            (leaf((8, head_width), f32), whole((8, head_width))),
        ],
        [
            pltpu.VMEM((total_rows, head_width), f32),
            pltpu.VMEM((total_rows, head_width), f32),
        ],
        "attention_backward",
        [down_part],
    )
    dheads = jnp.concatenate([dquery, dot_nt(dpair, spread).astype(bf16)], axis=1)

    out_part = dot_tn(normed_a, payload)[:, :width].astype(bf16)
    out_part = lax.all_to_all(
        jnp.moveaxis(out_part.reshape(head_width, n, out_piece), 1, 0), "ctx", 0, 0
    )
    out_part = out_part.reshape(n * head_width, out_piece)[:width]
    attend_part = jnp.concatenate(
        [dot_tn(hidden, dheads).astype(bf16), pad_to(out_part, 1, out_wide)], axis=1
    )
    attend_grad = scatter_z(attend_part)

    normed_s, dgate_z, dmixed_in, drank, dsides, scan_vecs, step_part, decay_part = block_call(
        scan_backward_body(block),
        order,
        count,
        [
            (selected, rows(block, 128, reverse)),
            (sides, side_spec(reverse)),
            (mixed_in, rows(block, wide, reverse)),
            (projected, rows(block, 2 * held, reverse)),
            (scanned, rows(block, wide, reverse)),
            (dmixer_in, rows(block, wide, reverse)),
            (scalars, rows(block, 128, reverse)),
            (starts, start_spec(reverse)),
            (step_own, whole(step_own.shape)),
            (vecs, whole(vecs.shape)),
            (decay_own, whole(decay_own.shape)),
        ],
        [
            (leaf((total_rows, held), bf16), rows(block, held, reverse)),
            (leaf((total_rows, held), bf16), rows(block, held, reverse)),
            (leaf((total_rows, wide), f32), rows(block, wide, reverse)),
            (leaf((total_rows, 128), f32), rows(block, 128, reverse)),
            (
                leaf((count, 2, 8, block * NS), f32),
                pl.BlockSpec(
                    (1, 2, 8, block * NS), lambda i, order: (order[reverse(i)], 0, 0, 0)
                ),
            ),
            (leaf((8, wide), f32), whole((8, wide))),
            (leaf((128, wide), f32), whole((128, wide))),
            (leaf((NS, wide), f32), whole((NS, wide))),
        ],
        [
            pltpu.VMEM((block, wide), f32),
            pltpu.VMEM((NS, wide), f32),
            pltpu.VMEM((block, wide), f32),
            pltpu.VMEM((block, wide), f32),
            pltpu.VMEM((block, wide), f32),
            pltpu.VMEM((block, wide), f32),
            pltpu.VMEM((block, wide), f32),
            pltpu.VMEM((block + 1, NS, wide), f32),
            pltpu.VMEM((block, NS, wide), f32),
            pltpu.VMEM((block * NS, 128), f32),
            pltpu.VMEM((block * NS, 128), f32),
        ],
        "scan_backward",
        [attend_part, pair_grad],
    )
    dsides = jnp.swapaxes(dsides[:, :, 0, :].reshape(count, 2, block, NS), 1, 2)
    dselected_part = jnp.concatenate(
        [drank[:, :RANK], dsides.reshape(total_rows, 2 * NS)], axis=1
    ).astype(bf16)
    dselected_part = after(pad_to(dselected_part, 1, 256), *pair_parts[1 : n // 2])
    dselected = gather_ctx(scatter_ctx(*halves(dselected_part), n, own_index), n).astype(bf16)
    mixer_part = dot_tn(normed_s, payload).astype(bf16)
    mixer_out_grad = scatter_z(mixer_part)


    dprojected, select_part, filter_vecs = block_call(
        filter_backward_body(block, count),
        order,
        count,
        [
            (projected, rows(block, 2 * held, reverse)),
            (projected, rows(block, 2 * held, lambda i: jnp.maximum(count - 2 - i, 0))),
            (dgate_z, rows(block, held, reverse)),
            (mixed_in, rows(block, wide, reverse)),
            (dmixed_in, rows(block, wide, reverse)),
            (dselected, rows(block, 256, reverse)),
            (select_own, whole(select_own.shape)),
            (vecs, whole(vecs.shape)),
        ],
        [
            (leaf((total_rows, 2 * held), bf16), rows(block, 2 * held, reverse)),
            (leaf((256, wide), f32), whole((256, wide))),
            (leaf((8, wide), f32), whole((8, wide))),
        ],
        [
            pltpu.VMEM((block + 8, wide), f32),
            pltpu.VMEM((block + 8, wide), f32),
            pltpu.VMEM((block, 2 * held), f32),
        ],
        "filter_backward",
        [mixer_part],
    )
    dhidden = scatter_ctx(
        *split_dot(n, (dprojected, in_weight, across), (dheads, attend_all, across)), n, own_index
    )
    dfirst, first_gain_part = norm_backward(inputs, first_norm, first_gain, dhidden)
    tokens_grad = (dmixed + dfirst).astype(bf16)[None]

    small_grad = jnp.concatenate(
        [
            select_part[: RANK + 2 * NS],
            step_part[:RANK],
            decay_part,
            filter_vecs[4 : 4 + CONV],
            filter_vecs[3:4],
            scan_vecs[0:3],
        ]
    )[:, :held]
    attend_gain_full = lax.dynamic_update_slice_in_dim(
        jnp.zeros((1, n * head_width), f32), attend_gain_part[0:1], c * head_width, axis=1
    )[0, :width]
    gain_part = jnp.stack([first_gain_part, attend_gain_full, post_gain_part]).reshape(3, m, shard)
    gain_part = pad_to(
        jnp.moveaxis(gain_part, 1, 0).reshape(m, 3 * shard), 1, gain_rows * small_width
    )
    small_part = jnp.concatenate(
        [
            small_grad.T.reshape(m, piece_rows, small_width)[:, :piece],
            gain_part.reshape(m, gain_rows, small_width),
        ],
        axis=1,
    )
    small_count = up_to(-(-small_part.shape[1] * small_width // (2 * held)), 16)
    small_part = pad_to(small_part.reshape(m, -1), 1, small_count * 2 * held)
    small_part = small_part.reshape(m, small_count, 2 * held).astype(bf16)
    in_part = dot_tn(hidden, dprojected).astype(bf16).reshape(m, shard, 2 * held)
    in_grad = scatter_z(jnp.concatenate([in_part, small_part], axis=1).reshape(-1, 2 * held))

    spots = jnp.array([masks(n).index(mask) for mask in range(n)], dtype=jnp.int32)
    where = spots[c ^ jnp.arange(n, dtype=jnp.int32)]
    gate_grad, up_grad = unpack_columns(
        assemble(pair_parts),
        where,
        [
            (k, f * shard_hidden, hidden_piece, k * hidden_held + f * hidden_rows, hidden_piece)
            for k in range(2)
            for f in range(m)
        ],
        [weight.shape[1] for weight in (gate_weight, up_weight)],
        n,
        "unpack_pair",
    )
    down_turned = unpack_rows(
        gather_ctx(down_grad, n), where, hidden_piece, n, width, True, "unpack_down"
    )
    mixer_out_grad = unpack_rows(
        gather_ctx(mixer_out_grad, n), where, piece, n, width, False, "unpack_mixer"
    )
    attend_grad = gather_ctx(attend_grad, n)
    kv_wide = n * pair
    out_at = head_width + 2 * pair
    query_grad, key_parts, value_parts, out_grad = unpack_columns(
        attend_grad,
        where,
        [
            (0, 0, head_width, 0, head_width),
            (1, 0, pair, head_width, pair),
            (2, 0, pair, head_width + pair, pair),
            (3, 0, out_piece, out_at, out_piece),
        ],
        [width, kv_wide, kv_wide, width],
        n,
        "unpack_attention",
    )

    def group_sum(parts):
        total = jnp.zeros((shard, kv_pad), f32)
        for index in range(n):
            low_at = min(index * heads // GROUP, KV_HEADS - 1) * HEAD_DIM
            item = parts[:, index * pair : (index + 1) * pair]
            total = total + jnp.pad(item, ((0, 0), (low_at, kv_pad - pair - low_at)))
        return total[:, : KV_HEADS * HEAD_DIM]

    in_grad = after(in_grad, gate_grad, down_turned)
    in_grad = gather_ctx(in_grad, n).reshape(n, shard + small_count, 2 * held)
    (mixer_in_grad,) = unpack_columns(
        in_grad,
        where,
        [
            (0, p * inner_all + f * shard_channels, piece, p * held + f * piece_rows, piece)
            for p in range(2)
            for f in range(m)
        ],
        [2 * inner_all],
        n,
        "unpack_inner",
        shard,
    )
    small_sum = in_grad[:, shard:].astype(f32).reshape(n, -1)[:, : (piece + gain_rows) * small_width]
    small_sum = small_sum[where].reshape(n, piece + gain_rows, small_width)
    channel_grad = small_sum[:, :piece].reshape(shard_channels, small_width)
    gain_grad = jnp.sum(small_sum[:, piece:], axis=0).reshape(-1)[: 3 * shard].reshape(3, shard)

    at = RANK + 2 * NS
    select_grad = channel_grad[:, :at]
    step_grad = channel_grad[:, at : at + RANK].T
    at += RANK
    decay_grad = channel_grad[:, at : at + NS]
    at += NS
    kernel_grad = channel_grad[:, at : at + CONV].T
    at += CONV
    return (
        layer_out,
        tokens_grad,
        gain_grad[0],
        query_grad,
        group_sum(key_parts),
        group_sum(value_parts),
        out_grad,
        gain_grad[1],
        mixer_in_grad,
        kernel_grad,
        channel_grad[:, at],
        select_grad,
        step_grad,
        channel_grad[:, at + 1],
        decay_grad,
        channel_grad[:, at + 2],
        channel_grad[:, at + 3],
        mixer_out_grad,
        gain_grad[2],
        gate_grad,
        up_grad,
        down_turned.T,
    )


def solution(mesh):
    rows_spec = P("fsdp", None)
    lanes_spec = P(None, "fsdp")
    flat = P("fsdp")
    activations = P("fsdp", "ctx", None)
    weight_specs = (
        flat, rows_spec, rows_spec, rows_spec, rows_spec, flat, rows_spec, lanes_spec, flat, rows_spec,
        lanes_spec, flat, rows_spec, flat, flat, rows_spec, flat, rows_spec, rows_spec, rows_spec,
    )
    return jax.shard_map(
        on_device,
        mesh=mesh,
        in_specs=(activations, activations, P()) + weight_specs,
        out_specs=(activations, activations) + weight_specs,
        check_vma=False,
    )
```

```python
import math

import jax
import jax.numpy as jnp
from jax import lax
from jax.experimental import pallas as pl
from jax.experimental.pallas import tpu as pltpu
from jax.sharding import PartitionSpec as P

HEADS = 25
KV_HEADS = 5
HEAD_DIM = 64
GROUP = HEADS // KV_HEADS
CONV = 4
RANK = 100
NS = 16
EPS = 1e-05
NEG = -1e30
SCALE = 1.0 / math.sqrt(HEAD_DIM)
STEP = 16
VMEM = 56 * 1024 * 1024
SIDE = 64
bf16 = jnp.bfloat16
f32 = jnp.float32


def up_to(value, unit):
    return -(-value // unit) * unit


def dot(left, right, contract=((1,), (0,)), precision=None):
    return lax.dot_general(
        left, right, (contract, ((), ())), preferred_element_type=f32, precision=precision
    )


def dot_tn(left, right):
    return dot(left, right, ((0,), (0,)))


def dot_nt(left, right):
    return dot(left, right, ((1,), (1,)))


def pad_to(values, axis, size):
    widths = [(0, 0)] * values.ndim
    widths[axis] = (0, size - values.shape[axis])
    return jnp.pad(values, widths)


def masks(size):
    return list(range(0, size, 2)) + list(range(1, size, 2))


def swap(values, mask, size):
    return lax.ppermute(values, "ctx", [(i, i ^ mask) for i in range(size)])


def swaps(values, size):
    near = [values] + [swap(values, m, size) for m in range(2, size, 2)]
    return near + [swap(item, 1, size) for item in near]


def assemble(parts, *earlier):
    count = len(parts)
    step = parts[0].shape[0]
    shape = (count * step,) + parts[0].shape[1:]

    def body(*refs):
        for j in range(count):
            refs[-1][j * step : (j + 1) * step] = refs[j][...]

    spec = pl.BlockSpec(parts[0].shape, lambda: (0,) * len(shape))
    return pl.pallas_call(
        body,
        in_specs=[spec] * count + [pl.BlockSpec(memory_space=pl.ANY)] * len(earlier),
        out_specs=pl.BlockSpec(shape, lambda: (0,) * len(shape)),
        out_shape=leaf(shape, parts[0].dtype),
        compiler_params=pltpu.CompilerParams(vmem_limit_bytes=VMEM),
        name="assemble",
    )(*parts, *earlier)


def gather_ctx(values, size):
    return assemble(swaps(values, size))


def split_dot(size, *products):
    def half(at):
        total = None
        for left, right, contract in products:
            rows_now = left.shape[0] // 2
            item = dot(left[at * rows_now : (at + 1) * rows_now], right, contract)
            total = item if total is None else total + item
        return total.astype(bf16)

    return half(0), half(1)


def fold_body(count, step):
    def body(index, near, got, own_o, *sent_o):
        for j in range(count):
            rows_now = slice(j * step, (j + 1) * step)
            total = near[rows_now, :].astype(f32) + got[rows_now, :].astype(f32)
            if j == 0:
                own_o[...] = total
            else:
                sent_o[j - 1][...] = total.astype(bf16)

    return body


def scatter_ctx(near, far, size, index):
    half = size // 2
    step, width = near.shape[0] // half, near.shape[1]
    got = swap(far, 1, size)
    total, *sent = block_call(
        fold_body(half, step),
        index,
        1,
        [(near, whole(near.shape)), (got, whole(near.shape))],
        [(leaf((step, width), f32), whole((step, width)))]
        + [(leaf((step, width), bf16), whole((step, width)))] * (half - 1),
        [],
        "fold_halves",
    )
    for k in range(1, half):
        total = total + swap(sent[k - 1], 2 * k, size).astype(f32)
    return total


def block_call(body, order, count, ins, outs, scratch, name, earlier=()):
    given = len(ins)
    ins = list(ins) + [(value, pl.BlockSpec(memory_space=pl.ANY)) for value in earlier]

    def trimmed(*refs):
        return body(*refs[: 1 + given], *refs[1 + len(ins) :])

    return pl.pallas_call(
        trimmed,
        grid_spec=pltpu.PrefetchScalarGridSpec(
            num_scalar_prefetch=1,
            grid=(count,),
            in_specs=[spec for _, spec in ins],
            out_specs=[spec for _, spec in outs],
            scratch_shapes=scratch,
        ),
        out_shape=[shape for shape, _ in outs],
        compiler_params=pltpu.CompilerParams(
            dimension_semantics=("arbitrary",), vmem_limit_bytes=VMEM
        ),
        name=name,
    )(order, *[value for value, _ in ins])


def after(values, *earlier):
    def body(*refs):
        del refs

    spec = pl.BlockSpec(memory_space=pl.ANY)
    return pl.pallas_call(
        body,
        in_specs=[spec] * (1 + len(earlier)),
        out_specs=spec,
        out_shape=leaf(values.shape, values.dtype),
        input_output_aliases={0: 0},
        name="after",
    )(values, *earlier)


def whole(shape):
    zeros = (0,) * len(shape)
    return pl.BlockSpec(shape, lambda i, order: zeros)


def rows(block, width, pick):
    return pl.BlockSpec((block, width), lambda i, order: (order[pick(i)], 0))


def columns_at(block, width, pick, index):
    return pl.BlockSpec((block, width), lambda i, order: (order[pick(i)], index))


def leaf(shape, dtype):
    return jax.ShapeDtypeStruct(shape, dtype)


def filter_taps(ext, vecs, block):
    total = vecs[3:4, :]
    for j in range(CONV):
        total = total + vecs[4 + j : 5 + j, :] * ext[5 + j : 5 + j + block, :]
    return total


def filter_forward_body(block):
    def body(order, projected, vecs, select, mixed_o, selected_o, ext):
        step = pl.program_id(0)
        held = projected.shape[1] // 2

        @pl.when(step == 0)
        def _():
            ext[...] = jnp.zeros_like(ext)

        @pl.when(step > 0)
        def _():
            ext[0:8, :] = ext[block : block + 8, :]

        ext[8 : block + 8, 0:held] = projected[:, 0:held].astype(bf16).astype(f32)
        total = filter_taps(ext, vecs, block)
        mixed = (total * jax.nn.sigmoid(total)).astype(bf16)
        mixed_o[...] = mixed
        selected_o[...] = dot(mixed, select[...]).astype(bf16)

    return body


def rate_of(selected, step_weight, vecs):
    rank = selected[...].astype(bf16)
    raw = dot(rank, step_weight[...]) + vecs[0:1, :]
    rate = jnp.maximum(raw, 0.0) + jnp.log1p(jnp.exp(-jnp.abs(raw)))
    return rank, raw, rate


def scan_forward_body(block):
    def body(
        order, selected, sides, mixed, projected, step_weight, vecs, decay,
        scanned_o, starts_o, scaled_o, state_s, rate_s, drive_s, gate_s,
    ):
        held = projected.shape[1] // 2

        @pl.when(pl.program_id(0) == 0)
        def _():
            state_s[...] = jnp.zeros_like(state_s)
            gate_s[...] = jnp.zeros_like(gate_s)

        gate_s[:, 0:held] = projected[...][:, held:]

        _, _, rate = rate_of(selected, step_weight, vecs)
        wide = mixed[...].astype(f32)
        rate_s[...] = rate
        drive_s[...] = rate * wide
        starts_o[0] = state_s[...]
        decay_mat = decay[...]

        def group(g, state):
            base = pl.multiple_of(g * STEP, STEP)
            rates = rate_s[pl.ds(base, STEP), :]
            drives = drive_s[pl.ds(base, STEP), :]
            side = sides[0, g]
            for j in range(STEP):
                state = (
                    jnp.exp(rates[j : j + 1, :] * decay_mat) * state
                    + drives[j : j + 1, :] * side[:NS, j : j + 1]
                )
                scanned_o[pl.ds(base + j, 1), :] = jnp.sum(
                    state * side[NS:, j : j + 1], axis=0, keepdims=True
                )
            return state

        state_s[...] = lax.fori_loop(0, block // STEP, group, state_s[...])
        gate = gate_s[...]
        gated = (scanned_o[...] + vecs[1:2, :] * wide) * (gate * jax.nn.sigmoid(gate))
        lane = lax.broadcasted_iota(jnp.int32, gated.shape, 1)
        squares = jnp.sum(gated * gated, axis=1, keepdims=True)
        scaled_o[...] = jnp.where(lane == held, squares, gated * vecs[2:3, :]).astype(bf16)

    return body


def scan_backward_body(block):
    def body(
        order, selected, sides, mixed, projected, scanned, grad_in, scalars, starts, step_weight, vecs, decay,
        normed_o, dgate_o, dmixed_o, drank_o, dsides_o, vec_o, step_o, decay_o,
        gate_s, lam_s, rate_s, drive_s, dscan_s, drate_s, pull_s, hist_s, factor_s, read_s, write_s,
    ):
        width = decay.shape[1]
        held = projected.shape[1] // 2

        @pl.when(pl.program_id(0) == 0)
        def _():
            gate_s[...] = jnp.zeros_like(gate_s)
            lam_s[...] = jnp.zeros_like(lam_s)
            vec_o[...] = jnp.zeros_like(vec_o)
            step_o[...] = jnp.zeros_like(step_o)
            decay_o[...] = jnp.zeros_like(decay_o)

        rank, raw, rate = rate_of(selected, step_weight, vecs)
        wide = mixed[...].astype(f32)
        rate_s[...] = rate
        drive_s[...] = rate * wide
        gate_s[:, 0:held] = projected[...][:, held:]
        gate = gate_s[...]
        sig = jax.nn.sigmoid(gate)
        act = gate * sig
        before = scanned[...] + vecs[1:2, :] * wide
        gated = before * act
        norm = scalars[:, 2:3]
        centre = scalars[:, 3:4]
        grad = grad_in[...]
        gated_norm = gated * norm
        normed_o[...] = (gated_norm * vecs[2:3, :])[:, 0:held].astype(bf16)
        dgated = norm * (vecs[2:3, :] * grad) - gated * centre
        dscan = dgated * act
        dscan_s[...] = dscan
        dgate = dgated * before * (sig * (1.0 + gate * (1.0 - sig)))
        dgate_o[...] = dgate[:, 0:held].astype(bf16)
        vec_o[1:2, :] += jnp.sum(dscan * wide, axis=0, keepdims=True)
        vec_o[2:3, :] += jnp.sum(grad * gated_norm, axis=0, keepdims=True)
        decay_mat = decay[...]

        def forward(g, state):
            base = pl.multiple_of(g * STEP, STEP)
            rates = rate_s[pl.ds(base, STEP), :]
            drives = drive_s[pl.ds(base, STEP), :]
            side = sides[0, g]
            for j in range(STEP):
                factor = jnp.exp(rates[j : j + 1, :] * decay_mat)
                factor_s[base + j] = factor
                state = factor * state + drives[j : j + 1, :] * side[:NS, j : j + 1]
                hist_s[base + j + 1] = state
            return state

        hist_s[0] = starts[0]
        lax.fori_loop(0, block // STEP, forward, starts[0])

        def fold(values):
            total = values[:, 0:128]
            for at in range(128, width, 128):
                total = total + values[:, at : at + 128]
            return total

        def backward(i, carry):
            lam_in, decay_sum = carry
            g = block // STEP - 1 - i
            base = pl.multiple_of(g * STEP, STEP)
            rates = rate_s[pl.ds(base, STEP), :]
            drives = drive_s[pl.ds(base, STEP), :]
            dscans = dscan_s[pl.ds(base, STEP), :]
            side = sides[0, g]
            for j in range(STEP - 1, -1, -1):
                at = base + j
                row = dscans[j : j + 1, :]
                lam = lam_in + row * side[NS:, j : j + 1]
                read_s[pl.ds(at * NS, NS), :] = fold(hist_s[at + 1] * row)
                write_s[pl.ds(at * NS, NS), :] = fold(lam * drives[j : j + 1, :])
                pull = jnp.sum(lam * side[:NS, j : j + 1], axis=0, keepdims=True)
                lam_in = factor_s[at] * lam
                kept = lam_in * hist_s[at]
                decay_sum = decay_sum + rates[j : j + 1, :] * kept
                drate_s[pl.ds(at, 1), :] = jnp.sum(decay_mat * kept, axis=0, keepdims=True)
                pull_s[pl.ds(at, 1), :] = pull
            return (lam_in, decay_sum)

        lam, decay_sum = lax.fori_loop(
            0, block // STEP, backward, (lam_s[...], jnp.zeros_like(lam_s))
        )
        lam_s[...] = lam
        decay_o[...] += decay_sum * decay_mat
        pulled = pull_s[...]
        draw = (drate_s[...] + wide * pulled) * jax.nn.sigmoid(raw)
        vec_o[0:1, :] += jnp.sum(draw, axis=0, keepdims=True)
        low = draw.astype(bf16)
        dmixed_o[...] = vecs[1:2, :] * dscan + rate * pulled
        drank_o[...] = dot_nt(low, step_weight[...])
        step_o[...] += dot_tn(rank, low)
        ones = jnp.ones((8, 128), f32)
        high = lax.Precision.HIGHEST
        dsides_o[0, 0] = dot(ones, write_s[...], ((1,), (1,)), high)
        dsides_o[0, 1] = dot(ones, read_s[...], ((1,), (1,)), high)

    return body


def filter_backward_body(block, count):
    def body(
        order, projected, before, dgate, mixed, dmixed, dselected, select, vecs,
        dprojected_o, select_o, vec_o, ext, ext_grad, both_s,
    ):
        step = pl.program_id(0)
        held = projected.shape[1] // 2

        @pl.when(step == 0)
        def _():
            ext[...] = jnp.zeros_like(ext)
            ext_grad[block : block + 8, :] = jnp.zeros((8, ext.shape[1]), f32)
            select_o[...] = jnp.zeros_like(select_o)
            vec_o[...] = jnp.zeros_like(vec_o)

        @pl.when(step > 0)
        def _():
            ext_grad[block : block + 8, :] = ext_grad[0:8, :]

        first = jnp.where(step == count - 1, 0.0, 1.0)
        ext[0:8, 0:held] = before[block - 8 :, 0:held].astype(bf16).astype(f32) * first
        ext[8 : block + 8, 0:held] = projected[:, 0:held].astype(bf16).astype(f32)
        total = filter_taps(ext, vecs, block)
        sig = jax.nn.sigmoid(total)
        low = dselected[...]
        dmix = dmixed[...] + dot_nt(low, select[...])
        dfilt = dmix * (sig * (1.0 + total * (1.0 - sig)))
        ext_grad[0:block, :] = dfilt
        dinner = jnp.zeros_like(dfilt)
        vec_o[3:4, :] += jnp.sum(dfilt, axis=0, keepdims=True)
        for j in range(CONV):
            at = CONV - 1 - j
            dinner = dinner + vecs[4 + j : 5 + j, :] * ext_grad[at : at + block, :]
            vec_o[4 + j : 5 + j, :] += jnp.sum(
                dfilt * ext[5 + j : 5 + j + block, :], axis=0, keepdims=True
            )
        both_s[:, 0:held] = dinner[:, 0:held]
        both_s[:, held:] = dgate[...].astype(f32)
        dprojected_o[...] = both_s[...].astype(bf16)
        select_o[...] += dot_tn(low, mixed[...])

    return body


def half_mask(half):
    lane = lax.broadcasted_iota(jnp.int32, (1, 128), 1)
    return jnp.where((lane >= 64 * half) & (lane < 64 * half + 64), 1.0, 0.0)


def softmax_rows(query, key, allowed):
    scores = jnp.where(allowed, dot_nt(query, key) * SCALE, NEG)
    weights = jnp.exp(scores - jnp.max(scores, axis=-1, keepdims=True))
    return weights * (1.0 / jnp.sum(weights, axis=-1, keepdims=True))


def attention_forward_body(valid, query, key, value, query_pos, key_pos, gain, out_o, scaled_o):
    allowed = key_pos[...] <= query_pos[...]
    squares = jnp.zeros((query.shape[0], 1), f32)
    for at in range(0, query.shape[1], 128):
        key_tile = key[:, at : at + 128]
        value_tile = value[:, at : at + 128]
        tile = jnp.zeros((query.shape[0], 128), f32)
        for half in range(2):
            mask = half_mask(half)
            part = query[:, at : at + 128] * mask.astype(bf16)
            probs = softmax_rows(part, key_tile, allowed).astype(bf16)
            live = valid[at // 64 + half].astype(f32)
            tile = tile + dot(probs, value_tile) * (mask * live)
        out_o[:, at : at + 128] = tile
        scaled_o[:, at : at + 128] = (tile * gain[:, at : at + 128]).astype(bf16)
        squares = squares + jnp.sum(tile * tile, axis=1, keepdims=True)
    at = query.shape[1]
    lane = lax.broadcasted_iota(jnp.int32, (query.shape[0], 128), 1)
    scaled_o[:, at : at + 128] = jnp.where(lane == 0, squares, 0.0).astype(bf16)


def unit_body(both, dunit, unit_o, dboth_o):
    held = dunit.shape[1]
    values = both[...]
    gate, up = values[:, :held], values[:, held:]
    grad = dunit[...]
    sig = jax.nn.sigmoid(gate)
    act = gate * sig
    unit_o[...] = (act * up).astype(bf16)
    dgate = grad * up * (sig * (1.0 + gate * (1.0 - sig)))
    dboth_o[...] = jnp.concatenate([dgate, grad * act], axis=1).astype(bf16)


def norm_body(index, gain, *refs):
    out = refs[-1]
    step = refs[0].shape[0]
    for j, ref in enumerate(refs[:-1]):
        values = ref[...].astype(f32)
        norm = lax.rsqrt(jnp.mean(values * values, axis=1, keepdims=True) + EPS)
        out[j * step : (j + 1) * step, :] = (values * norm * gain[...]).astype(bf16)


def attention_backward_body(
    valid, query, key, value, query_pos, key_pos, gain, out, grad_in, scalars,
    dquery_o, dpair_o, normed_o, gain_o, dkey_s, dvalue_s,
):
    @pl.when(pl.program_id(0) == 0)
    def _():
        dkey_s[...] = jnp.zeros_like(dkey_s)
        dvalue_s[...] = jnp.zeros_like(dvalue_s)
        gain_o[...] = jnp.zeros_like(gain_o)

    allowed = key_pos[...] <= query_pos[...]
    norm = scalars[:, 0:1]
    centre = scalars[:, 1:2]
    for at in range(0, query.shape[1], 128):
        lanes = slice(at, at + 128)
        key_tile = key[:, lanes]
        value_tile = value[:, lanes]
        attended = out[:, lanes]
        grad = grad_in[:, lanes]
        normed = attended * norm
        normed_o[:, lanes] = (normed * gain[:, lanes]).astype(bf16)
        gain_o[0:1, lanes] += jnp.sum(grad * normed, axis=0, keepdims=True)
        dout = (norm * (gain[:, lanes] * grad) - attended * centre).astype(bf16)
        dquery = jnp.zeros(attended.shape, f32)
        dkey = jnp.zeros((key.shape[0], 128), f32)
        dvalue = jnp.zeros((key.shape[0], 128), f32)
        for half in range(2):
            mask = half_mask(half)
            part = query[:, lanes] * mask.astype(bf16)
            dpart = dout * mask.astype(bf16)
            probs = softmax_rows(part, key_tile, allowed)
            dprobs = dot_nt(dpart, value_tile)
            mean = jnp.sum(dprobs * probs, axis=-1, keepdims=True)
            dscores = (probs * (dprobs - mean)).astype(bf16)
            dvalue = dvalue + dot_tn(probs.astype(bf16), dpart)
            dquery = dquery + dot(dscores, key_tile) * (mask * SCALE)
            dkey = dkey + dot_tn(dscores, part) * SCALE
        dquery_o[:, lanes] = dquery.astype(bf16)
        dkey_s[:, lanes] += dkey
        dvalue_s[:, lanes] += dvalue

    @pl.when(pl.program_id(0) == pl.num_programs(0) - 1)
    def _():
        held = dkey_s.shape[1]
        dpair_o[:, :held] = dkey_s[...].astype(bf16)
        dpair_o[:, held:] = dvalue_s[...].astype(bf16)


def pack_body(groups, width, piece):
    window = up_to(piece + 127, 128)

    def body(index, *refs):
        out_o, acc = refs[-2:]
        acc[...] = jnp.zeros_like(acc)
        for which, start, at in groups:
            weight = refs[which]
            source = start + index[0] * piece
            tile = jnp.minimum(source // 128, (width - window) // 128)
            base = pl.multiple_of(tile * 128, 128)
            low = at % 128
            span = up_to(low + piece, 128)
            row = lax.broadcasted_iota(jnp.int32, (window, span), 0)
            lane = lax.broadcasted_iota(jnp.int32, (window, span), 1) - low
            pick = (row - (source - base) == lane) & (lane >= 0) & (lane < piece)
            pick = jnp.where(pick, 1.0, 0.0).astype(bf16)
            acc[:, at - low : at - low + span] += dot(weight[:, pl.ds(base, window)], pick)
        out_o[...] = acc[:, : out_o.shape[1]].astype(bf16)

    return body


def row_block(count):
    return 80 if count % 80 == 0 else count


def join_body(axis):
    def body(index, *refs):
        at = 0
        for ref in refs[:-1]:
            size = ref.shape[axis]
            if axis == 0:
                refs[-1][at : at + size, :] = ref[...]
            else:
                refs[-1][:, at : at + size] = ref[...]
            at += size

    return body


def join(parts, index, axis, name, earlier):
    shape = list(parts[0].shape)
    shape[axis] = sum(part.shape[axis] for part in parts)
    return block_call(
        join_body(axis),
        index,
        1,
        [(part, whole(part.shape)) for part in parts],
        [(leaf(tuple(shape), bf16), whole(tuple(shape)))],
        [],
        name,
        earlier,
    )[0]


def pack_columns(weights, index, groups, out_wide, piece, name, earlier=()):
    count, width = weights[0].shape
    block = row_block(count)
    return block_call(
        pack_body(groups, width, piece),
        index,
        count // block,
        [(weight, pl.BlockSpec((block, width), lambda i, index: (i, 0))) for weight in weights],
        [
            (
                leaf((count, out_wide), bf16),
                pl.BlockSpec((block, out_wide), lambda i, index: (i, 0)),
            )
        ],
        [pltpu.VMEM((block, up_to(out_wide, 128)), f32)],
        name,
        earlier,
    )[0]


def unpack_columns(parts, where, moves, widths, name, count=None):
    size = len(parts)
    width = parts[0].shape[1]
    count = count or parts[0].shape[0]
    block = row_block(count)

    def body(where, *refs):
        sources, outs, held = refs[:size], refs[size:-1], refs[-1]
        for j in range(size):
            held[j] = sources[j][...]
        for index in range(size):
            values = held[where[index]].astype(f32)
            for out, first, stride, at, piece in moves:
                start = first + index * stride
                piece = min(piece, widths[out] - start)
                if piece > 0:
                    outs[out][:, start : start + piece] = values[:, at : at + piece]

    return block_call(
        body,
        where,
        count // block,
        [(part, pl.BlockSpec((block, width), lambda i, where: (i, 0))) for part in parts],
        [
            (leaf((count, full), f32), pl.BlockSpec((block, full), lambda i, where: (i, 0)))
            for full in widths
        ],
        [pltpu.VMEM((size, block, width), bf16)],
        name,
    )


def unpack_rows(parts, where, piece, width, turned, name):
    size = len(parts)
    count, full = parts[0].shape
    lanes = 256

    def body(where, *refs):
        sources, out, held = refs[:size], refs[-2], refs[-1]
        for j in range(size):
            held[j] = sources[j][...]
        for index in range(size):
            values = held[where[index]].astype(f32)
            put = slice(index * piece, (index + 1) * piece)
            if turned:
                out[:, put] = values.T[:, :piece]
            else:
                out[put, :] = values[:piece]

    shape = (width, size * piece) if turned else (size * piece, width)
    out_block = (lanes, size * piece) if turned else (size * piece, lanes)
    spot = (lambda i, where: (i, 0)) if turned else (lambda i, where: (0, i))
    return block_call(
        body,
        where,
        -(-width // lanes),
        [(part, pl.BlockSpec((count, lanes), lambda i, where: (0, i))) for part in parts],
        [(leaf(shape, f32), pl.BlockSpec(out_block, spot))],
        [pltpu.VMEM((size, count, lanes), bf16)],
        name,
    )[0]


def inverse_rms(values):
    return lax.rsqrt(jnp.mean(values * values, axis=-1, keepdims=True) + EPS)


def norm_backward(values, norm, gain, grad):
    scaled = grad * gain
    centre = norm**3 * jnp.mean(values * scaled, axis=-1, keepdims=True)
    return norm * scaled - values * centre, jnp.sum(grad * values * norm, axis=0)


def split_low(values):
    high = lax.reduce_precision(values, 8, 7)
    return [high.astype(bf16), (values - high).astype(bf16)]


def on_device(
    tokens, cotangent, deal_table, norm_gain, query_weight, key_weight, value_weight, attention_out,
    attention_gain, mixer_in, filter_kernel, filter_bias, select_weight, step_weight, step_bias, decay_log,
    skip_gain, mixer_gain, mixer_out, post_gain, gate_weight, up_weight, down_weight,
):
    n = lax.axis_size("ctx")
    m = lax.axis_size("fsdp")
    c = lax.axis_index("ctx")
    z = lax.axis_index("fsdp")
    own = tokens.shape[1]
    block = own // 2
    total_rows = own * n
    count = 2 * n
    width = tokens.shape[2]
    shard = width // m
    heads = -(-HEADS // n)
    heads += heads % 2
    head_width = heads * HEAD_DIM
    shard_channels = filter_bias.shape[0]
    piece = shard_channels // n
    channels = m * piece
    inner_all = shard_channels * m
    shard_hidden = down_weight.shape[0]
    hidden_piece = shard_hidden // n
    piece_rows, hidden_rows = up_to(piece, 16), up_to(hidden_piece, 16)
    held, hidden_held = m * piece_rows, m * hidden_rows
    wide = up_to(held + 1, 128)
    sent_width = width + SIDE
    out_piece = width // n
    out_wide = up_to(out_piece, 128)

    def gather_z(values, tiled=True):
        return lax.all_gather(values, "fsdp", axis=0, tiled=tiled)

    def columns(values, start, size):
        return lax.dynamic_slice_in_dim(values, start, size, axis=1)

    in_groups = [
        (0, p * inner_all + f * shard_channels, p * held + f * piece_rows)
        for p in range(2)
        for f in range(m)
    ]
    in_local = pack_columns([mixer_in], c.reshape(1), in_groups, 2 * held, piece, "pack_mixer")
    in_weight = gather_z(in_local)
    own_index = after(c.reshape(1), in_local)
    c = own_index[0]
    token_parts = swaps(after(tokens[0], in_local), n)
    small_rows = jnp.concatenate(
        [
            select_weight,
            step_weight.T,
            decay_log,
            filter_kernel.T,
            filter_bias[:, None],
            step_bias[:, None],
            skip_gain[:, None],
            mixer_gain[:, None],
        ],
        axis=1,
    )
    small_width = small_rows.shape[1]
    small_rows = lax.dynamic_slice_in_dim(small_rows, c * piece, piece, axis=0)
    gains = jnp.stack([norm_gain, attention_gain, post_gain]).reshape(-1)
    gain_rows = -(-3 * shard // small_width)
    gains = pad_to(gains, 0, gain_rows * small_width).reshape(gain_rows, small_width)
    small_local = jnp.concatenate([small_rows, gains])
    turned = [
        lax.ppermute(small_local, "fsdp", [(i, (i + k) % m) for i in range(m)])
        for k in range(m - 1, 0, -1)
    ] + [small_local]
    small_all = lax.dynamic_slice_in_dim(jnp.stack(turned + turned), m - 1 - z, m, axis=0)
    small = pad_to(small_all[:, :piece], 1, piece_rows).reshape(held, small_width)
    gains_all = small_all[:, piece:].reshape(m, gain_rows * small_width)[:, : 3 * shard]
    gains_all = jnp.moveaxis(gains_all.reshape(m, 3, shard), 0, 1).reshape(3, width).astype(f32)
    first_gain, attend_gain, after_gain = gains_all[0:1], gains_all[1:2], gains_all[2:3]

    def first_group(index):
        return jnp.minimum(index * heads // GROUP, KV_HEADS - 1)

    group_at = first_group(c)
    kv_pad = (KV_HEADS + 1) * HEAD_DIM
    pair = 2 * HEAD_DIM
    attend_local = join(
        [
            columns(pad_to(query_weight, 1, n * head_width), c * head_width, head_width),
            columns(pad_to(key_weight, 1, kv_pad), group_at * HEAD_DIM, pair),
            columns(pad_to(value_weight, 1, kv_pad), group_at * HEAD_DIM, pair),
        ],
        own_index,
        1,
        "pack_attention",
        [in_local],
    )
    head_ids = c * heads + jnp.arange(heads, dtype=jnp.int32)
    valid = (head_ids < HEADS).astype(jnp.int32)
    upper = jnp.minimum(head_ids // GROUP, KV_HEADS - 1) > group_at

    def row_slice(weight, size):
        cut = lax.dynamic_slice_in_dim(weight, c * size, size, axis=0)
        return pad_to(cut, 0, up_to(size, 16))

    out_cut = columns(attention_out, c * out_piece, out_piece).reshape(-1)
    out_rows = up_to(-(-out_cut.shape[0] // width), 16)
    rows_local = join(
        [
            row_slice(mixer_out, piece),
            pad_to(out_cut, 0, out_rows * width).reshape(out_rows, width),
        ],
        own_index,
        0,
        "pack_rows",
        [in_local],
    )
    pair_groups = [
        (k, f * shard_hidden, k * hidden_held + f * hidden_rows) for k in range(2) for f in range(m)
    ]
    pair_local = pack_columns(
        [gate_weight, up_weight],
        own_index,
        pair_groups,
        2 * hidden_held,
        hidden_piece,
        "pack_pair",
        [in_local],
    )
    down_local = row_slice(down_weight, hidden_piece)

    inputs = tokens[0].astype(f32)
    first_norm = inverse_rms(inputs)
    hidden = block_call(
        norm_body,
        own_index,
        1,
        [(first_gain, whole(first_gain.shape))]
        + [(item, whole(item.shape)) for item in token_parts],
        [(leaf((total_rows, width), bf16), whole((total_rows, width)))],
        [],
        "norm_tokens",
        [attend_local, rows_local, pair_local],
    )[0]

    projected = dot(hidden, in_weight)
    attend_all = gather_z(after(attend_local, in_weight))

    def extended(weight, rows_now, at):
        weight = jnp.pad(weight, ((0, rows_now - weight.shape[0]), (0, SIDE)))
        spot = (jnp.arange(rows_now) == at)[:, None] & (jnp.arange(sent_width) == width)[None, :]
        return jnp.where(spot, jnp.ones((), bf16), weight)

    lane_dim = jnp.arange(head_width, dtype=jnp.int32) % HEAD_DIM
    target = jnp.where(jnp.repeat(upper, HEAD_DIM), HEAD_DIM, 0) + lane_dim
    target = jnp.concatenate([target, target + pair])
    side_now = jnp.arange(2 * head_width, dtype=jnp.int32) // head_width
    spread = (target[None, :] == jnp.arange(2 * pair, dtype=jnp.int32)[:, None]) & (
        side_now[None, :] == (jnp.arange(2 * pair, dtype=jnp.int32) // pair)[:, None]
    )
    spread = spread.astype(bf16)

    others = c ^ jnp.array(masks(n), dtype=jnp.int32)
    firsts = deal_table[others]
    places = jnp.stack([firsts, count - 1 - firsts], axis=1).reshape(count)
    ids = jnp.arange(count, dtype=jnp.int32)
    order = jnp.sum(jnp.where(places[None, :] == ids[:, None], ids[None, :], 0), axis=1)
    position = (places[:, None] * block + jnp.arange(block, dtype=jnp.int32)[None, :]).reshape(-1)

    small_t = pad_to(small.astype(f32).T, 1, wide)
    select_own = pad_to(pad_to(small[:, : RANK + 2 * NS], 0, wide), 1, 256)
    step_own = pad_to(small_t[RANK + 2 * NS : 2 * RANK + 2 * NS], 0, 128).astype(bf16)
    at = 2 * RANK + 2 * NS
    decay_own = -jnp.exp(small_t[at : at + NS])
    at += NS
    vecs = jnp.concatenate([small_t[at + CONV + 1 : at + CONV + 4], small_t[at + CONV : at + CONV + 1], small_t[at : at + CONV]])

    def halves(values):
        return values[: total_rows // 2], values[total_rows // 2 :]

    upstream = cotangent[0]
    upstream_all = gather_ctx(upstream, n)
    heads_in = dot(hidden, attend_all).astype(bf16)
    pair_in = dot(heads_in[:, head_width:], spread).astype(bf16)

    forward = lambda i: i
    reverse = lambda i: count - 1 - i
    mixed_in, selected_part = block_call(
        filter_forward_body(block),
        order,
        count,
        [
            (projected, rows(block, 2 * held, forward)),
            (vecs, whole(vecs.shape)),
            (select_own, whole(select_own.shape)),
        ],
        [
            (leaf((total_rows, wide), bf16), rows(block, wide, forward)),
            (leaf((total_rows, 256), bf16), rows(block, 256, forward)),
        ],
        [pltpu.VMEM((block + 8, wide), f32)],
        "filter_forward",
    )
    selected_own = scatter_ctx(*halves(selected_part), n, own_index)
    rows_all = gather_z(after(rows_local, attend_all, selected_own), tiled=False)
    mixer_out_own = extended(rows_all[:, :piece_rows].reshape(held, width), wide, held)
    out_columns = rows_all[:, piece_rows:].reshape(m, -1)[:, : shard * out_piece]
    out_columns = out_columns.reshape(width, out_piece)
    out_own = lax.all_to_all(
        pad_to(out_columns, 0, n * head_width).reshape(n, head_width, out_piece), "ctx", 0, 0
    )
    out_own = jnp.moveaxis(out_own, 0, 1).reshape(head_width, width)
    out_own = extended(out_own, head_width + 128, head_width)

    query_block = min(256, total_rows)
    query_count = total_rows // query_block
    query_pos = position[:, None]
    key_pos = position[None, :]
    own_gain = lax.dynamic_slice_in_dim(
        pad_to(attend_gain, 1, n * head_width), c * head_width, head_width, axis=1
    )

    def part(index):
        return pl.BlockSpec((total_rows, head_width), lambda i, order: (0, index))

    def tall(size):
        return pl.BlockSpec((query_block, size), lambda i, order: (i, 0))

    attend_ins = [
        (heads_in, tall(head_width)),
        (pair_in, part(0)),
        (pair_in, part(1)),
        (query_pos, tall(1)),
        (key_pos, whole(key_pos.shape)),
        (own_gain, whole(own_gain.shape)),
    ]
    attended, attended_scaled = block_call(
        attention_forward_body,
        valid,
        query_count,
        attend_ins,
        [
            (leaf((total_rows, head_width), f32), tall(head_width)),
            (leaf((total_rows, head_width + 128), bf16), tall(head_width + 128)),
        ],
        [],
        "attention_forward",
    )

    plain = ((1,), (0,))
    across = ((1,), (1,))

    def branch_out(scaled, weight):
        got = scatter_ctx(*split_dot(n, (scaled, weight, plain)), n, own_index)
        return got[:, :width], got[:, width : width + 1]

    attend_sum, attend_squares = branch_out(attended_scaled, out_own)
    attend_norm = lax.rsqrt(attend_squares / (HEADS * HEAD_DIM) + EPS)

    selected = assemble(swaps(after(selected_own, pair_in), n), attended)
    sides = selected[:, RANK : RANK + 2 * NS].reshape(count, block // STEP, STEP, 2 * NS)
    sides = jnp.swapaxes(sides, 2, 3)
    side_spec = lambda pick: pl.BlockSpec((1,) + sides.shape[1:], lambda i, order: (order[pick(i)], 0, 0, 0))
    start_spec = lambda pick: pl.BlockSpec((1, NS, wide), lambda i, order: (order[pick(i)], 0, 0))
    scanned, starts, mixer_scaled = block_call(
        scan_forward_body(block),
        order,
        count,
        [
            (selected, rows(block, 128, forward)),
            (sides, side_spec(forward)),
            (mixed_in, rows(block, wide, forward)),
            (projected, rows(block, 2 * held, forward)),
            (step_own, whole(step_own.shape)),
            (vecs, whole(vecs.shape)),
            (decay_own, whole(decay_own.shape)),
        ],
        [
            (leaf((total_rows, wide), f32), rows(block, wide, forward)),
            (leaf((count, NS, wide), f32), start_spec(forward)),
            (leaf((total_rows, wide), bf16), rows(block, wide, forward)),
        ],
        [
            pltpu.VMEM((NS, wide), f32),
            pltpu.VMEM((block, wide), f32),
            pltpu.VMEM((block, wide), f32),
            pltpu.VMEM((block, wide), f32),
        ],
        "scan_forward",
    )
    pair_weight = gather_z(after(pair_local, rows_all, scanned))
    mixer_sum, mixer_squares = branch_out(mixer_scaled, mixer_out_own)
    mixer_norm = lax.rsqrt(mixer_squares / inner_all + EPS)

    mixed = inputs + 0.5 * (attend_norm * attend_sum + mixer_norm * mixer_sum)
    post_norm = inverse_rms(mixed)
    post = gather_ctx((mixed * post_norm * after_gain).astype(bf16), n)
    down_own = gather_z(after(down_local, pair_weight, post))
    both = dot(post, pair_weight)
    dunit = dot_nt(upstream_all, down_own)

    def strip(size):
        return pl.BlockSpec((own, size), lambda i: (i, 0))

    unit, dboth = pl.pallas_call(
        unit_body,
        grid=(n,),
        in_specs=[strip(2 * hidden_held), strip(hidden_held)],
        out_specs=[strip(hidden_held), strip(2 * hidden_held)],
        out_shape=[
            leaf((total_rows, hidden_held), bf16),
            leaf((total_rows, 2 * hidden_held), bf16),
        ],
        compiler_params=pltpu.CompilerParams(vmem_limit_bytes=VMEM),
        name="hidden_units",
    )(both, dunit)

    dpost = scatter_ctx(*split_dot(n, (dboth, pair_weight, across)), n, own_index)
    dnorm, post_gain_part = norm_backward(mixed, post_norm, after_gain, dpost)
    dmixed = upstream.astype(f32) + dnorm

    def scatter_z(values):
        return lax.psum_scatter(values, "fsdp", scatter_dimension=0, tiled=True)

    pair_part = dot_tn(post, dboth).astype(bf16)
    down_part = dot_tn(unit, upstream_all).astype(bf16)
    pair_grad = scatter_z(pair_part)
    pair_parts = swaps(pair_grad, n)
    down_grad = scatter_z(down_part)
    ffn_out = scatter_ctx(*split_dot(n, (unit, down_own, plain)), n, own_index)
    layer_out = (mixed + ffn_out).astype(bf16)[None]

    dbranch = (0.5 * dmixed).astype(bf16)
    dbranch_wide = dbranch.astype(f32)
    attend_centre = (
        attend_norm**3
        * jnp.sum(dbranch_wide * attend_sum, axis=1, keepdims=True)
        / (HEADS * HEAD_DIM)
    )
    mixer_centre = (
        mixer_norm**3 * jnp.sum(dbranch_wide * mixer_sum, axis=1, keepdims=True) / inner_all
    )
    extra = []
    for item in (attend_norm, attend_centre, mixer_norm, mixer_centre):
        extra += split_low(item)
    payload = jnp.concatenate([dbranch, pad_to(jnp.concatenate(extra, axis=1), 1, SIDE)], axis=1)
    payload = gather_ctx(after(payload, pair_part), n)
    scalars = payload[:, width : width + 8].astype(f32).reshape(total_rows, 4, 2).sum(axis=2)
    scalars = pad_to(scalars, 1, 128)

    dattend_in = dot_nt(payload, out_own)
    dmixer_in = dot_nt(payload, mixer_out_own)

    dquery, dpair, normed_a, attend_gain_part = block_call(
        attention_backward_body,
        valid,
        query_count,
        attend_ins
        + [
            (attended, tall(head_width)),
            (dattend_in, tall(head_width + 128)),
            (scalars, tall(128)),
        ],
        [
            (leaf((total_rows, head_width), bf16), tall(head_width)),
            (leaf((total_rows, 2 * head_width), bf16), whole((total_rows, 2 * head_width))),
            (leaf((total_rows, head_width), bf16), tall(head_width)),
            (leaf((8, head_width), f32), whole((8, head_width))),
        ],
        [
            pltpu.VMEM((total_rows, head_width), f32),
            pltpu.VMEM((total_rows, head_width), f32),
        ],
        "attention_backward",
        [down_part],
    )
    dheads = jnp.concatenate([dquery, dot_nt(dpair, spread).astype(bf16)], axis=1)

    out_part = dot_tn(normed_a, payload)[:, :width].astype(bf16)
    out_part = lax.all_to_all(
        jnp.moveaxis(out_part.reshape(head_width, n, out_piece), 1, 0), "ctx", 0, 0
    )
    out_part = out_part.reshape(n * head_width, out_piece)[:width]
    attend_part = jnp.concatenate(
        [dot_tn(hidden, dheads).astype(bf16), pad_to(out_part, 1, out_wide)], axis=1
    )
    attend_grad = scatter_z(attend_part)

    normed_s, dgate_z, dmixed_in, drank, dsides, scan_vecs, step_part, decay_part = block_call(
        scan_backward_body(block),
        order,
        count,
        [
            (selected, rows(block, 128, reverse)),
            (sides, side_spec(reverse)),
            (mixed_in, rows(block, wide, reverse)),
            (projected, rows(block, 2 * held, reverse)),
            (scanned, rows(block, wide, reverse)),
            (dmixer_in, rows(block, wide, reverse)),
            (scalars, rows(block, 128, reverse)),
            (starts, start_spec(reverse)),
            (step_own, whole(step_own.shape)),
            (vecs, whole(vecs.shape)),
            (decay_own, whole(decay_own.shape)),
        ],
        [
            (leaf((total_rows, held), bf16), rows(block, held, reverse)),
            (leaf((total_rows, held), bf16), rows(block, held, reverse)),
            (leaf((total_rows, wide), f32), rows(block, wide, reverse)),
            (leaf((total_rows, 128), f32), rows(block, 128, reverse)),
            (
                leaf((count, 2, 8, block * NS), f32),
                pl.BlockSpec(
                    (1, 2, 8, block * NS), lambda i, order: (order[reverse(i)], 0, 0, 0)
                ),
            ),
            (leaf((8, wide), f32), whole((8, wide))),
            (leaf((128, wide), f32), whole((128, wide))),
            (leaf((NS, wide), f32), whole((NS, wide))),
        ],
        [
            pltpu.VMEM((block, wide), f32),
            pltpu.VMEM((NS, wide), f32),
            pltpu.VMEM((block, wide), f32),
            pltpu.VMEM((block, wide), f32),
            pltpu.VMEM((block, wide), f32),
            pltpu.VMEM((block, wide), f32),
            pltpu.VMEM((block, wide), f32),
            pltpu.VMEM((block + 1, NS, wide), f32),
            pltpu.VMEM((block, NS, wide), f32),
            pltpu.VMEM((block * NS, 128), f32),
            pltpu.VMEM((block * NS, 128), f32),
        ],
        "scan_backward",
        [attend_part, pair_grad],
    )
    dsides = jnp.swapaxes(dsides[:, :, 0, :].reshape(count, 2, block, NS), 1, 2)
    dselected_part = jnp.concatenate(
        [drank[:, :RANK], dsides.reshape(total_rows, 2 * NS)], axis=1
    ).astype(bf16)
    dselected_part = after(pad_to(dselected_part, 1, 256), *pair_parts[1 : n // 2])
    dselected = gather_ctx(scatter_ctx(*halves(dselected_part), n, own_index), n).astype(bf16)
    mixer_part = dot_tn(normed_s, payload).astype(bf16)
    mixer_out_grad = scatter_z(mixer_part)


    dprojected, select_part, filter_vecs = block_call(
        filter_backward_body(block, count),
        order,
        count,
        [
            (projected, rows(block, 2 * held, reverse)),
            (projected, rows(block, 2 * held, lambda i: jnp.maximum(count - 2 - i, 0))),
            (dgate_z, rows(block, held, reverse)),
            (mixed_in, rows(block, wide, reverse)),
            (dmixed_in, rows(block, wide, reverse)),
            (dselected, rows(block, 256, reverse)),
            (select_own, whole(select_own.shape)),
            (vecs, whole(vecs.shape)),
        ],
        [
            (leaf((total_rows, 2 * held), bf16), rows(block, 2 * held, reverse)),
            (leaf((256, wide), f32), whole((256, wide))),
            (leaf((8, wide), f32), whole((8, wide))),
        ],
        [
            pltpu.VMEM((block + 8, wide), f32),
            pltpu.VMEM((block + 8, wide), f32),
            pltpu.VMEM((block, 2 * held), f32),
        ],
        "filter_backward",
        [mixer_part],
    )
    dhidden = scatter_ctx(
        *split_dot(n, (dprojected, in_weight, across), (dheads, attend_all, across)), n, own_index
    )
    dfirst, first_gain_part = norm_backward(inputs, first_norm, first_gain, dhidden)
    tokens_grad = (dmixed + dfirst).astype(bf16)[None]

    small_grad = jnp.concatenate(
        [
            select_part[: RANK + 2 * NS],
            step_part[:RANK],
            decay_part,
            filter_vecs[4 : 4 + CONV],
            filter_vecs[3:4],
            scan_vecs[0:3],
        ]
    )[:, :held]
    attend_gain_full = lax.dynamic_update_slice_in_dim(
        jnp.zeros((1, n * head_width), f32), attend_gain_part[0:1], c * head_width, axis=1
    )[0, :width]
    gain_part = jnp.stack([first_gain_part, attend_gain_full, post_gain_part]).reshape(3, m, shard)
    gain_part = pad_to(
        jnp.moveaxis(gain_part, 1, 0).reshape(m, 3 * shard), 1, gain_rows * small_width
    )
    small_part = jnp.concatenate(
        [
            small_grad.T.reshape(m, piece_rows, small_width)[:, :piece],
            gain_part.reshape(m, gain_rows, small_width),
        ],
        axis=1,
    )
    small_count = up_to(-(-small_part.shape[1] * small_width // (2 * held)), 16)
    small_part = pad_to(small_part.reshape(m, -1), 1, small_count * 2 * held)
    small_part = small_part.reshape(m, small_count, 2 * held).astype(bf16)
    in_part = dot_tn(hidden, dprojected).astype(bf16).reshape(m, shard, 2 * held)
    in_grad = scatter_z(jnp.concatenate([in_part, small_part], axis=1).reshape(-1, 2 * held))

    spots = jnp.array([masks(n).index(mask) for mask in range(n)], dtype=jnp.int32)
    where = spots[c ^ jnp.arange(n, dtype=jnp.int32)]
    gate_grad, up_grad = unpack_columns(
        pair_parts,
        where,
        [
            (k, f * shard_hidden, hidden_piece, k * hidden_held + f * hidden_rows, hidden_piece)
            for k in range(2)
            for f in range(m)
        ],
        [weight.shape[1] for weight in (gate_weight, up_weight)],
        "unpack_pair",
    )
    down_turned = unpack_rows(
        swaps(down_grad, n), where, hidden_piece, width, True, "unpack_down"
    )
    mixer_out_grad = unpack_rows(
        swaps(mixer_out_grad, n), where, piece, width, False, "unpack_mixer"
    )
    attend_grad = swaps(attend_grad, n)
    kv_wide = n * pair
    out_at = head_width + 2 * pair
    query_grad, key_parts, value_parts, out_grad = unpack_columns(
        attend_grad,
        where,
        [
            (0, 0, head_width, 0, head_width),
            (1, 0, pair, head_width, pair),
            (2, 0, pair, head_width + pair, pair),
            (3, 0, out_piece, out_at, out_piece),
        ],
        [width, kv_wide, kv_wide, width],
        "unpack_attention",
    )

    def group_sum(parts):
        total = jnp.zeros((shard, kv_pad), f32)
        for index in range(n):
            low_at = min(index * heads // GROUP, KV_HEADS - 1) * HEAD_DIM
            item = parts[:, index * pair : (index + 1) * pair]
            total = total + jnp.pad(item, ((0, 0), (low_at, kv_pad - pair - low_at)))
        return total[:, : KV_HEADS * HEAD_DIM]

    in_grad = after(in_grad, gate_grad, down_turned)
    in_grad = swaps(in_grad, n)
    (mixer_in_grad,) = unpack_columns(
        in_grad,
        where,
        [
            (0, p * inner_all + f * shard_channels, piece, p * held + f * piece_rows, piece)
            for p in range(2)
            for f in range(m)
        ],
        [2 * inner_all],
        "unpack_inner",
        shard,
    )
    small_sum = jnp.stack([item[shard:] for item in in_grad]).astype(f32)
    small_sum = small_sum.reshape(n, -1)[:, : (piece + gain_rows) * small_width]
    small_sum = small_sum[where].reshape(n, piece + gain_rows, small_width)
    channel_grad = small_sum[:, :piece].reshape(shard_channels, small_width)
    gain_grad = jnp.sum(small_sum[:, piece:], axis=0).reshape(-1)[: 3 * shard].reshape(3, shard)

    at = RANK + 2 * NS
    select_grad = channel_grad[:, :at]
    step_grad = channel_grad[:, at : at + RANK].T
    at += RANK
    decay_grad = channel_grad[:, at : at + NS]
    at += NS
    kernel_grad = channel_grad[:, at : at + CONV].T
    at += CONV
    return (
        layer_out,
        tokens_grad,
        gain_grad[0],
        query_grad,
        group_sum(key_parts),
        group_sum(value_parts),
        out_grad,
        gain_grad[1],
        mixer_in_grad,
        kernel_grad,
        channel_grad[:, at],
        select_grad,
        step_grad,
        channel_grad[:, at + 1],
        decay_grad,
        channel_grad[:, at + 2],
        channel_grad[:, at + 3],
        mixer_out_grad,
        gain_grad[2],
        gate_grad,
        up_grad,
        down_turned.T,
    )


def solution(mesh):
    rows_spec = P("fsdp", None)
    lanes_spec = P(None, "fsdp")
    flat = P("fsdp")
    activations = P("fsdp", "ctx", None)
    weight_specs = (
        flat, rows_spec, rows_spec, rows_spec, rows_spec, flat, rows_spec, lanes_spec, flat, rows_spec,
        lanes_spec, flat, rows_spec, flat, flat, rows_spec, flat, rows_spec, rows_spec, rows_spec,
    )
    return jax.shard_map(
        on_device,
        mesh=mesh,
        in_specs=(activations, activations, P()) + weight_specs,
        out_specs=(activations, activations) + weight_specs,
        check_vma=False,
    )
```

```python
import math

import jax
import jax.numpy as jnp
from jax import lax
from jax.experimental import pallas as pl
from jax.experimental.pallas import tpu as pltpu
from jax.sharding import PartitionSpec as P

HEADS = 25
KV_HEADS = 5
HEAD_DIM = 64
GROUP = HEADS // KV_HEADS
CONV = 4
RANK = 100
NS = 16
EPS = 1e-05
NEG = -1e30
SCALE = 1.0 / math.sqrt(HEAD_DIM)
STEP = 16
VMEM = 56 * 1024 * 1024
SIDE = 64
SIDE_AT = HEADS * HEAD_DIM % 128
bf16 = jnp.bfloat16
f32 = jnp.float32


def up_to(value, unit):
    return -(-value // unit) * unit


def dot(left, right, contract=((1,), (0,)), precision=None):
    return lax.dot_general(
        left, right, (contract, ((), ())), preferred_element_type=f32, precision=precision
    )


def dot_tn(left, right):
    return dot(left, right, ((0,), (0,)))


def dot_nt(left, right):
    return dot(left, right, ((1,), (1,)))


def pad_to(values, axis, size):
    widths = [(0, 0)] * values.ndim
    widths[axis] = (0, size - values.shape[axis])
    return jnp.pad(values, widths)


def masks(size):
    return list(range(0, size, 2)) + list(range(1, size, 2))


def swap(values, mask, size):
    return lax.ppermute(values, "ctx", [(i, i ^ mask) for i in range(size)])


def swaps(values, size):
    near = [values] + [swap(values, m, size) for m in range(2, size, 2)]
    return near + [swap(item, 1, size) for item in near]


def assemble(parts, *earlier):
    count = len(parts)
    step = parts[0].shape[0]
    shape = (count * step,) + parts[0].shape[1:]

    def body(*refs):
        for j in range(count):
            refs[-1][j * step : (j + 1) * step] = refs[j][...]

    spec = pl.BlockSpec(parts[0].shape, lambda: (0,) * len(shape))
    return pl.pallas_call(
        body,
        in_specs=[spec] * count + [pl.BlockSpec(memory_space=pl.ANY)] * len(earlier),
        out_specs=pl.BlockSpec(shape, lambda: (0,) * len(shape)),
        out_shape=leaf(shape, parts[0].dtype),
        compiler_params=pltpu.CompilerParams(vmem_limit_bytes=VMEM),
        name="assemble",
    )(*parts, *earlier)


def gather_ctx(values, size):
    return assemble(swaps(values, size))


def product_rows(pairs, at, rows_now, dtype, name, earlier=()):
    count = pairs[0][1].shape[0]
    step = min(256, count)

    def body(*refs):
        total = dot_nt(refs[0][...], refs[1][...])
        for k in range(2, 2 * len(pairs), 2):
            total = total + dot_nt(refs[k][...], refs[k + 1][...])
        refs[-1][...] = total.astype(dtype)

    specs, values = [], []
    for left, right in pairs:
        depth = left.shape[1]
        specs.append(pl.BlockSpec((rows_now, depth), lambda i: (at, 0)))
        specs.append(pl.BlockSpec((step, depth), lambda i: (i, 0)))
        values += [left, right]
    return pl.pallas_call(
        body,
        grid=(-(-count // step),),
        in_specs=specs + [pl.BlockSpec(memory_space=pl.ANY)] * len(earlier),
        out_specs=pl.BlockSpec((rows_now, step), lambda i: (0, i)),
        out_shape=leaf((rows_now, count), dtype),
        compiler_params=pltpu.CompilerParams(vmem_limit_bytes=VMEM),
        name=name,
    )(*values, *earlier)


def product_columns(left, right, at, rows_now, name, earlier=()):
    depth, count = right.shape
    step = min(256, count)

    def body(*refs):
        refs[-1][...] = dot(refs[0][...], refs[1][...]).astype(bf16)

    return pl.pallas_call(
        body,
        grid=(-(-count // step),),
        in_specs=[
            pl.BlockSpec((rows_now, depth), lambda i: (at, 0)),
            pl.BlockSpec((depth, step), lambda i: (0, i)),
        ]
        + [pl.BlockSpec(memory_space=pl.ANY)] * len(earlier),
        out_specs=pl.BlockSpec((rows_now, step), lambda i: (0, i)),
        out_shape=leaf((rows_now, count), bf16),
        compiler_params=pltpu.CompilerParams(vmem_limit_bytes=VMEM),
        name=name,
    )(left, right, *earlier)


def split_columns(left, right, name, earlier=()):
    half = left.shape[0] // 2
    far = product_columns(left, right, 1, half, name, earlier)
    return product_columns(left, right, 0, half, name), far


def split_rows(pairs, name, earlier=()):
    half = pairs[0][0].shape[0] // 2
    far = product_rows(pairs, 1, half, bf16, name, earlier)
    return product_rows(pairs, 0, half, bf16, name), far


def fold_body(count, step):
    def body(index, near, got, own_o, *sent_o):
        for j in range(count):
            rows_now = slice(j * step, (j + 1) * step)
            total = near[rows_now, :].astype(f32) + got[rows_now, :].astype(f32)
            if j == 0:
                own_o[...] = total
            else:
                sent_o[j - 1][...] = total.astype(bf16)

    return body


def scatter_parts(near, far, size, index):
    half = size // 2
    step, width = near.shape[0] // half, near.shape[1]
    got = swap(far, 1, size)
    total, *sent = block_call(
        fold_body(half, step),
        index,
        1,
        [(near, whole(near.shape)), (got, whole(near.shape))],
        [(leaf((step, width), f32), whole((step, width)))]
        + [(leaf((step, width), bf16), whole((step, width)))] * (half - 1),
        [],
        "fold_halves",
    )
    return [total] + [swap(sent[k - 1], 2 * k, size) for k in range(1, half)]


def scatter_ctx(near, far, size, index):
    total, *others = scatter_parts(near, far, size, index)
    for item in others:
        total = total + item.astype(f32)
    return total


def block_call(body, order, count, ins, outs, scratch, name, earlier=()):
    given = len(ins)
    ins = list(ins) + [(value, pl.BlockSpec(memory_space=pl.ANY)) for value in earlier]

    def trimmed(*refs):
        return body(*refs[: 1 + given], *refs[1 + len(ins) :])

    return pl.pallas_call(
        trimmed,
        grid_spec=pltpu.PrefetchScalarGridSpec(
            num_scalar_prefetch=1,
            grid=(count,),
            in_specs=[spec for _, spec in ins],
            out_specs=[spec for _, spec in outs],
            scratch_shapes=scratch,
        ),
        out_shape=[shape for shape, _ in outs],
        compiler_params=pltpu.CompilerParams(
            dimension_semantics=("arbitrary",), vmem_limit_bytes=VMEM
        ),
        name=name,
    )(order, *[value for value, _ in ins])


def after(values, *earlier):
    def body(*refs):
        del refs

    spec = pl.BlockSpec(memory_space=pl.ANY)
    return pl.pallas_call(
        body,
        in_specs=[spec] * (1 + len(earlier)),
        out_specs=spec,
        out_shape=leaf(values.shape, values.dtype),
        input_output_aliases={0: 0},
        name="after",
    )(values, *earlier)


def whole(shape):
    zeros = (0,) * len(shape)
    return pl.BlockSpec(shape, lambda i, order: zeros)


def rows(block, width, pick):
    return pl.BlockSpec((block, width), lambda i, order: (order[pick(i)], 0))


def columns_at(block, width, pick, index):
    return pl.BlockSpec((block, width), lambda i, order: (order[pick(i)], index))


def leaf(shape, dtype):
    return jax.ShapeDtypeStruct(shape, dtype)


def filter_taps(ext, vecs, block):
    total = vecs[3:4, :]
    for j in range(CONV):
        total = total + vecs[4 + j : 5 + j, :] * ext[5 + j : 5 + j + block, :]
    return total


def filter_forward_body(block):
    def body(order, projected, vecs, select, mixed_o, selected_o, ext):
        step = pl.program_id(0)
        held = projected.shape[1] // 2

        @pl.when(step == 0)
        def _():
            ext[...] = jnp.zeros_like(ext)

        @pl.when(step > 0)
        def _():
            ext[0:8, :] = ext[block : block + 8, :]

        ext[8 : block + 8, 0:held] = projected[:, 0:held].astype(bf16).astype(f32)
        total = filter_taps(ext, vecs, block)
        mixed = (total * jax.nn.sigmoid(total)).astype(bf16)
        mixed_o[...] = mixed
        selected_o[...] = dot(mixed, select[...]).astype(bf16)

    return body


def side_scalar(scalars, index):
    at = SIDE_AT + 2 * index
    values = scalars[...].astype(f32)
    return values[:, at : at + 1] + values[:, at + 1 : at + 2]


def turn_sides(selected, sides_s):
    turned = selected[:, 128:256].T
    for g in range(sides_s.shape[0]):
        sides_s[g] = turned[: 2 * NS, g * STEP : (g + 1) * STEP]


def rate_of(selected, step_weight, vecs):
    rank = selected[:, 0:128].astype(bf16)
    raw = dot(rank, step_weight[...]) + vecs[0:1, :]
    rate = jnp.maximum(raw, 0.0) + jnp.log1p(jnp.exp(-jnp.abs(raw)))
    return rank, raw, rate


def scan_forward_body(block):
    def body(
        order, selected, mixed, projected, step_weight, vecs, decay,
        scanned_o, starts_o, scaled_o, state_s, rate_s, drive_s, gate_s, sides_s,
    ):
        held = projected.shape[1] // 2

        @pl.when(pl.program_id(0) == 0)
        def _():
            state_s[...] = jnp.zeros_like(state_s)
            gate_s[...] = jnp.zeros_like(gate_s)

        gate_s[:, 0:held] = projected[...][:, held:]
        turn_sides(selected, sides_s)

        _, _, rate = rate_of(selected, step_weight, vecs)
        wide = mixed[...].astype(f32)
        rate_s[...] = rate
        drive_s[...] = rate * wide
        starts_o[0] = state_s[...]
        decay_mat = decay[...]

        def group(g, state):
            base = pl.multiple_of(g * STEP, STEP)
            rates = rate_s[pl.ds(base, STEP), :]
            drives = drive_s[pl.ds(base, STEP), :]
            side = sides_s[g]
            for j in range(STEP):
                state = (
                    jnp.exp(rates[j : j + 1, :] * decay_mat) * state
                    + drives[j : j + 1, :] * side[:NS, j : j + 1]
                )
                scanned_o[pl.ds(base + j, 1), :] = jnp.sum(
                    state * side[NS:, j : j + 1], axis=0, keepdims=True
                )
            return state

        state_s[...] = lax.fori_loop(0, block // STEP, group, state_s[...])
        gate = gate_s[...]
        gated = (scanned_o[...] + vecs[1:2, :] * wide) * (gate * jax.nn.sigmoid(gate))
        lane = lax.broadcasted_iota(jnp.int32, gated.shape, 1)
        squares = jnp.sum(gated * gated, axis=1, keepdims=True)
        scaled_o[...] = jnp.where(lane == held, squares, gated * vecs[2:3, :]).astype(bf16)

    return body


def scan_backward_body(block):
    def body(
        order, selected, mixed, projected, scanned, grad_in, scalars, starts, step_weight, vecs, decay,
        normed_o, dgate_o, dmixed_o, dselected_o, vec_o, step_o, decay_o,
        sides_s, gate_s, lam_s, rate_s, drive_s, dscan_s, drate_s, pull_s, hist_s, factor_s, read_s, write_s,
    ):
        width = decay.shape[1]
        held = projected.shape[1] // 2

        @pl.when(pl.program_id(0) == 0)
        def _():
            gate_s[...] = jnp.zeros_like(gate_s)
            lam_s[...] = jnp.zeros_like(lam_s)
            vec_o[...] = jnp.zeros_like(vec_o)
            step_o[...] = jnp.zeros_like(step_o)
            decay_o[...] = jnp.zeros_like(decay_o)

        rank, raw, rate = rate_of(selected, step_weight, vecs)
        wide = mixed[...].astype(f32)
        rate_s[...] = rate
        drive_s[...] = rate * wide
        turn_sides(selected, sides_s)
        gate_s[:, 0:held] = projected[...][:, held:]
        gate = gate_s[...]
        sig = jax.nn.sigmoid(gate)
        act = gate * sig
        before = scanned[...] + vecs[1:2, :] * wide
        gated = before * act
        norm = side_scalar(scalars, 2)
        centre = side_scalar(scalars, 3)
        grad = grad_in[...]
        gated_norm = gated * norm
        normed_o[...] = (gated_norm * vecs[2:3, :])[:, 0:held].astype(bf16)
        dgated = norm * (vecs[2:3, :] * grad) - gated * centre
        dscan = dgated * act
        dscan_s[...] = dscan
        dgate = dgated * before * (sig * (1.0 + gate * (1.0 - sig)))
        dgate_o[...] = dgate[:, 0:held].astype(bf16)
        vec_o[1:2, :] += jnp.sum(dscan * wide, axis=0, keepdims=True)
        vec_o[2:3, :] += jnp.sum(grad * gated_norm, axis=0, keepdims=True)
        decay_mat = decay[...]

        def forward(g, state):
            base = pl.multiple_of(g * STEP, STEP)
            rates = rate_s[pl.ds(base, STEP), :]
            drives = drive_s[pl.ds(base, STEP), :]
            side = sides_s[g]
            for j in range(STEP):
                factor = jnp.exp(rates[j : j + 1, :] * decay_mat)
                factor_s[base + j] = factor
                state = factor * state + drives[j : j + 1, :] * side[:NS, j : j + 1]
                hist_s[base + j + 1] = state
            return state

        hist_s[0] = starts[0]
        lax.fori_loop(0, block // STEP, forward, starts[0])

        def fold(values):
            total = values[:, 0:128]
            for at in range(128, width, 128):
                total = total + values[:, at : at + 128]
            return total

        def backward(i, carry):
            lam_in, decay_sum = carry
            g = block // STEP - 1 - i
            base = pl.multiple_of(g * STEP, STEP)
            rates = rate_s[pl.ds(base, STEP), :]
            drives = drive_s[pl.ds(base, STEP), :]
            dscans = dscan_s[pl.ds(base, STEP), :]
            side = sides_s[g]
            for j in range(STEP - 1, -1, -1):
                at = base + j
                row = dscans[j : j + 1, :]
                lam = lam_in + row * side[NS:, j : j + 1]
                read_s[pl.ds(at * NS, NS), :] = fold(hist_s[at + 1] * row)
                write_s[pl.ds(at * NS, NS), :] = fold(lam * drives[j : j + 1, :])
                pull = jnp.sum(lam * side[:NS, j : j + 1], axis=0, keepdims=True)
                lam_in = factor_s[at] * lam
                kept = lam_in * hist_s[at]
                decay_sum = decay_sum + rates[j : j + 1, :] * kept
                drate_s[pl.ds(at, 1), :] = jnp.sum(decay_mat * kept, axis=0, keepdims=True)
                pull_s[pl.ds(at, 1), :] = pull
            return (lam_in, decay_sum)

        lam, decay_sum = lax.fori_loop(
            0, block // STEP, backward, (lam_s[...], jnp.zeros_like(lam_s))
        )
        lam_s[...] = lam
        decay_o[...] += decay_sum * decay_mat
        pulled = pull_s[...]
        draw = (drate_s[...] + wide * pulled) * jax.nn.sigmoid(raw)
        vec_o[0:1, :] += jnp.sum(draw, axis=0, keepdims=True)
        low = draw.astype(bf16)
        dmixed_o[...] = vecs[1:2, :] * dscan + rate * pulled
        step_o[...] += dot_tn(rank, low)
        ones = jnp.ones((128, 128), f32)
        high = lax.Precision.HIGHEST
        row = lax.broadcasted_iota(jnp.int32, (block * NS, 128), 0) % NS
        lane = lax.broadcasted_iota(jnp.int32, (block * NS, 128), 1)
        summed = jnp.where(
            lane == row, dot(write_s[...], ones, precision=high), 0.0
        ) + jnp.where(lane == row + NS, dot(read_s[...], ones, precision=high), 0.0)
        token = lax.broadcasted_iota(jnp.int32, (block, block * NS), 0)
        spot = lax.broadcasted_iota(jnp.int32, (block, block * NS), 1) // NS
        collect = jnp.where(token == spot, 1.0, 0.0)
        dselected_o[:, 0:128] = dot_nt(low, step_weight[...]).astype(bf16)
        dselected_o[:, 128:256] = dot(collect, summed, precision=high).astype(bf16)

    return body


def filter_backward_body(block, count):
    def body(
        order, projected, before, dgate, mixed, dmixed, dselected, select, vecs,
        dprojected_o, select_o, vec_o, ext, ext_grad, both_s,
    ):
        step = pl.program_id(0)
        held = projected.shape[1] // 2

        @pl.when(step == 0)
        def _():
            ext[...] = jnp.zeros_like(ext)
            ext_grad[block : block + 8, :] = jnp.zeros((8, ext.shape[1]), f32)
            select_o[...] = jnp.zeros_like(select_o)
            vec_o[...] = jnp.zeros_like(vec_o)

        @pl.when(step > 0)
        def _():
            ext_grad[block : block + 8, :] = ext_grad[0:8, :]

        first = jnp.where(step == count - 1, 0.0, 1.0)
        ext[0:8, 0:held] = before[block - 8 :, 0:held].astype(bf16).astype(f32) * first
        ext[8 : block + 8, 0:held] = projected[:, 0:held].astype(bf16).astype(f32)
        total = filter_taps(ext, vecs, block)
        sig = jax.nn.sigmoid(total)
        low = dselected[...]
        dmix = dmixed[...] + dot_nt(low, select[...])
        dfilt = dmix * (sig * (1.0 + total * (1.0 - sig)))
        ext_grad[0:block, :] = dfilt
        dinner = jnp.zeros_like(dfilt)
        vec_o[3:4, :] += jnp.sum(dfilt, axis=0, keepdims=True)
        for j in range(CONV):
            at = CONV - 1 - j
            dinner = dinner + vecs[4 + j : 5 + j, :] * ext_grad[at : at + block, :]
            vec_o[4 + j : 5 + j, :] += jnp.sum(
                dfilt * ext[5 + j : 5 + j + block, :], axis=0, keepdims=True
            )
        both_s[:, 0:held] = dinner[:, 0:held]
        both_s[:, held:] = dgate[...].astype(f32)
        dprojected_o[...] = both_s[...].astype(bf16)
        select_o[...] += dot_tn(low, mixed[...])

    return body


def half_mask(half):
    lane = lax.broadcasted_iota(jnp.int32, (1, 128), 1)
    return jnp.where((lane >= 64 * half) & (lane < 64 * half + 64), 1.0, 0.0)


def softmax_rows(query, key, allowed):
    scores = jnp.where(allowed, dot_nt(query, key) * SCALE, NEG)
    weights = jnp.exp(scores - jnp.max(scores, axis=-1, keepdims=True))
    return weights * (1.0 / jnp.sum(weights, axis=-1, keepdims=True))


def attention_forward_body(valid, query, key, value, query_pos, key_pos, gain, out_o, scaled_o):
    allowed = key_pos[...] <= query_pos[...]
    squares = jnp.zeros((query.shape[0], 1), f32)
    for at in range(0, query.shape[1], 128):
        key_tile = key[:, at : at + 128]
        value_tile = value[:, at : at + 128]
        tile = jnp.zeros((query.shape[0], 128), f32)
        for half in range(2):
            mask = half_mask(half)
            part = query[:, at : at + 128] * mask.astype(bf16)
            probs = softmax_rows(part, key_tile, allowed).astype(bf16)
            live = valid[at // 64 + half].astype(f32)
            tile = tile + dot(probs, value_tile) * (mask * live)
        out_o[:, at : at + 128] = tile
        scaled_o[:, at : at + 128] = (tile * gain[:, at : at + 128]).astype(bf16)
        squares = squares + jnp.sum(tile * tile, axis=1, keepdims=True)
    at = query.shape[1]
    lane = lax.broadcasted_iota(jnp.int32, (query.shape[0], 128), 1)
    scaled_o[:, at : at + 128] = jnp.where(lane == 0, squares, 0.0).astype(bf16)


def unit_body(both, dunit, unit_o, dboth_o):
    held = dunit.shape[1]
    values = both[...]
    gate, up = values[:, :held], values[:, held:]
    grad = dunit[...]
    sig = jax.nn.sigmoid(gate)
    act = gate * sig
    unit_o[...] = (act * up).astype(bf16)
    dgate = grad * up * (sig * (1.0 + gate * (1.0 - sig)))
    dboth_o[...] = jnp.concatenate([dgate, grad * act], axis=1).astype(bf16)


def branch_grad_body(half, inner_all):
    def body(index, *refs):
        parts = refs[:half]
        mixed, gain, upstream, attend_sum, mixer_sum = refs[half : half + 5]
        payload_o, dmixed_o, gain_o = refs[half + 5 :]
        grad = parts[0][...]
        for item in parts[1:]:
            grad = grad + item[...].astype(f32)
        values = mixed[...]
        width = values.shape[1]
        norm = lax.rsqrt(jnp.mean(values * values, axis=1, keepdims=True) + EPS)
        scaled = grad * gain[...]
        centre = norm * norm * norm * jnp.mean(values * scaled, axis=1, keepdims=True)
        dmixed = upstream[...].astype(f32) + norm * scaled - values * centre
        dmixed_o[...] = dmixed
        total = jnp.sum(grad * values * norm, axis=0, keepdims=True)
        gain_o[...] = jnp.broadcast_to(total, gain_o.shape)
        low = (0.5 * dmixed).astype(bf16)
        payload_o[:, 0:width] = low
        wide_low = low.astype(f32)
        lane = lax.broadcasted_iota(jnp.int32, (values.shape[0], SIDE), 1)
        side = jnp.zeros((values.shape[0], SIDE), f32)
        at = 0
        for source, size in ((attend_sum, HEADS * HEAD_DIM), (mixer_sum, inner_all)):
            sums = source[...]
            factor = lax.rsqrt(sums[:, width : width + 1] / size + EPS)
            mean = jnp.sum(wide_low * sums[:, 0:width], axis=1, keepdims=True) / size
            for item in (factor, factor * factor * factor * mean):
                high = item.astype(bf16).astype(f32)
                side = jnp.where(lane == at, high, side)
                side = jnp.where(lane == at + 1, item - high, side)
                at += 2
        payload_o[:, width:] = side.astype(bf16)

    return body


def norm_body(index, gain, *refs):
    out = refs[-1]
    step = refs[0].shape[0]
    for j, ref in enumerate(refs[:-1]):
        values = ref[...].astype(f32)
        norm = lax.rsqrt(jnp.mean(values * values, axis=1, keepdims=True) + EPS)
        out[j * step : (j + 1) * step, :] = (values * norm * gain[...]).astype(bf16)


def attention_backward_body(
    valid, query, key, value, query_pos, key_pos, gain, out, grad_in, scalars,
    dquery_o, dpair_o, normed_o, gain_o, dkey_s, dvalue_s,
):
    @pl.when(pl.program_id(0) == 0)
    def _():
        dkey_s[...] = jnp.zeros_like(dkey_s)
        dvalue_s[...] = jnp.zeros_like(dvalue_s)
        gain_o[...] = jnp.zeros_like(gain_o)

    allowed = key_pos[...] <= query_pos[...]
    norm = side_scalar(scalars, 0)
    centre = side_scalar(scalars, 1)
    for at in range(0, query.shape[1], 128):
        lanes = slice(at, at + 128)
        key_tile = key[:, lanes]
        value_tile = value[:, lanes]
        attended = out[:, lanes]
        grad = grad_in[:, lanes]
        normed = attended * norm
        normed_o[:, lanes] = (normed * gain[:, lanes]).astype(bf16)
        gain_o[0:1, lanes] += jnp.sum(grad * normed, axis=0, keepdims=True)
        dout = (norm * (gain[:, lanes] * grad) - attended * centre).astype(bf16)
        dquery = jnp.zeros(attended.shape, f32)
        dkey = jnp.zeros((key.shape[0], 128), f32)
        dvalue = jnp.zeros((key.shape[0], 128), f32)
        for half in range(2):
            mask = half_mask(half)
            part = query[:, lanes] * mask.astype(bf16)
            dpart = dout * mask.astype(bf16)
            probs = softmax_rows(part, key_tile, allowed)
            dprobs = dot_nt(dpart, value_tile)
            mean = jnp.sum(dprobs * probs, axis=-1, keepdims=True)
            dscores = (probs * (dprobs - mean)).astype(bf16)
            dvalue = dvalue + dot_tn(probs.astype(bf16), dpart)
            dquery = dquery + dot(dscores, key_tile) * (mask * SCALE)
            dkey = dkey + dot_tn(dscores, part) * SCALE
        dquery_o[:, lanes] = dquery.astype(bf16)
        dkey_s[:, lanes] += dkey
        dvalue_s[:, lanes] += dvalue

    @pl.when(pl.program_id(0) == pl.num_programs(0) - 1)
    def _():
        held = dkey_s.shape[1]
        dpair_o[:, :held] = dkey_s[...].astype(bf16)
        dpair_o[:, held:] = dvalue_s[...].astype(bf16)


def pack_body(groups, width, piece):
    window = up_to(piece + 127, 128)

    def body(index, *refs):
        out_o, acc = refs[-2:]
        acc[...] = jnp.zeros_like(acc)
        for which, start, at in groups:
            weight = refs[which]
            source = start + index[0] * piece
            tile = jnp.minimum(source // 128, (width - window) // 128)
            base = pl.multiple_of(tile * 128, 128)
            low = at % 128
            span = up_to(low + piece, 128)
            row = lax.broadcasted_iota(jnp.int32, (window, span), 0)
            lane = lax.broadcasted_iota(jnp.int32, (window, span), 1) - low
            pick = (row - (source - base) == lane) & (lane >= 0) & (lane < piece)
            pick = jnp.where(pick, 1.0, 0.0).astype(bf16)
            acc[:, at - low : at - low + span] += dot(weight[:, pl.ds(base, window)], pick)
        out_o[...] = acc[:, : out_o.shape[1]].astype(bf16)

    return body


def row_block(count):
    return 80 if count % 80 == 0 else count


def join_body(axis):
    def body(index, *refs):
        at = 0
        for ref in refs[:-1]:
            size = ref.shape[axis]
            if axis == 0:
                refs[-1][at : at + size, :] = ref[...]
            else:
                refs[-1][:, at : at + size] = ref[...]
            at += size

    return body


def join(parts, index, axis, name, earlier):
    shape = list(parts[0].shape)
    shape[axis] = sum(part.shape[axis] for part in parts)
    return block_call(
        join_body(axis),
        index,
        1,
        [(part, whole(part.shape)) for part in parts],
        [(leaf(tuple(shape), bf16), whole(tuple(shape)))],
        [],
        name,
        earlier,
    )[0]


def weave(first, second, count, index):
    tall, low = first.shape[0] // count, second.shape[0] // count

    def body(index, first, second, out):
        for k in range(count):
            at = k * (tall + low)
            out[at : at + tall, :] = first[k * tall : (k + 1) * tall, :]
            out[at + tall : at + tall + low, :] = second[k * low : (k + 1) * low, :]

    shape = (count * (tall + low), first.shape[1])
    return block_call(
        body,
        index,
        1,
        [(first, whole(first.shape)), (second, whole(second.shape))],
        [(leaf(shape, bf16), whole(shape))],
        [],
        "weave",
    )[0]


def pack_columns(weights, index, groups, out_wide, piece, name, earlier=()):
    count, width = weights[0].shape
    block = row_block(count)
    return block_call(
        pack_body(groups, width, piece),
        index,
        count // block,
        [(weight, pl.BlockSpec((block, width), lambda i, index: (i, 0))) for weight in weights],
        [
            (
                leaf((count, out_wide), bf16),
                pl.BlockSpec((block, out_wide), lambda i, index: (i, 0)),
            )
        ],
        [pltpu.VMEM((block, up_to(out_wide, 128)), f32)],
        name,
        earlier,
    )[0]


def unpack_columns(groups, where, moves, widths, name, count=None):
    size = len(groups[0])
    full = [parts[0].shape[1] for parts in groups]
    count = count or groups[0][0].shape[0]
    block = row_block(count)
    given = size * len(groups)

    def body(where, *refs):
        sources, outs, kept = refs[:given], refs[given : given + len(widths)], refs[given + len(widths) :]
        for k in range(len(groups)):
            for j in range(size):
                kept[k][j] = sources[k * size + j][...]
        for index in range(size):
            values = [item[where[index]].astype(f32) for item in kept]
            for out, first, stride, at, piece in moves:
                group = 0
                while at >= full[group]:
                    at -= full[group]
                    group += 1
                start = first + index * stride
                piece = min(piece, widths[out] - start)
                if piece > 0:
                    outs[out][:, start : start + piece] = values[group][:, at : at + piece]

    return block_call(
        body,
        where,
        count // block,
        [
            (part, pl.BlockSpec((block, part.shape[1]), lambda i, where: (i, 0)))
            for parts in groups
            for part in parts
        ],
        [
            (leaf((count, wide), f32), pl.BlockSpec((block, wide), lambda i, where: (i, 0)))
            for wide in widths
        ],
        [pltpu.VMEM((size, block, wide), bf16) for wide in full],
        name,
    )


def unpack_rows(parts, where, piece, width, turned, name):
    size = len(parts)
    count, full = parts[0].shape
    lanes = 256

    def body(where, *refs):
        sources, out, held = refs[:size], refs[-2], refs[-1]
        for j in range(size):
            held[j] = sources[j][...]
        for index in range(size):
            values = held[where[index]].astype(f32)
            put = slice(index * piece, (index + 1) * piece)
            if turned:
                out[:, put] = values.T[:, :piece]
            else:
                out[put, :] = values[:piece]

    shape = (width, size * piece) if turned else (size * piece, width)
    out_block = (lanes, size * piece) if turned else (size * piece, lanes)
    spot = (lambda i, where: (i, 0)) if turned else (lambda i, where: (0, i))
    return block_call(
        body,
        where,
        -(-width // lanes),
        [(part, pl.BlockSpec((count, lanes), lambda i, where: (0, i))) for part in parts],
        [(leaf(shape, f32), pl.BlockSpec(out_block, spot))],
        [pltpu.VMEM((size, count, lanes), bf16)],
        name,
    )[0]


def inverse_rms(values):
    return lax.rsqrt(jnp.mean(values * values, axis=-1, keepdims=True) + EPS)


def norm_backward(values, norm, gain, grad):
    scaled = grad * gain
    centre = norm**3 * jnp.mean(values * scaled, axis=-1, keepdims=True)
    return norm * scaled - values * centre


def split_low(values):
    high = lax.reduce_precision(values, 8, 7)
    return [high.astype(bf16), (values - high).astype(bf16)]


def on_device(
    tokens, cotangent, deal_table, norm_gain, query_weight, key_weight, value_weight, attention_out,
    attention_gain, mixer_in, filter_kernel, filter_bias, select_weight, step_weight, step_bias, decay_log,
    skip_gain, mixer_gain, mixer_out, post_gain, gate_weight, up_weight, down_weight,
):
    n = lax.axis_size("ctx")
    m = lax.axis_size("fsdp")
    c = lax.axis_index("ctx")
    z = lax.axis_index("fsdp")
    own = tokens.shape[1]
    block = own // 2
    total_rows = own * n
    count = 2 * n
    width = tokens.shape[2]
    shard = width // m
    heads = -(-HEADS // n)
    heads += heads % 2
    head_width = heads * HEAD_DIM
    shard_channels = filter_bias.shape[0]
    piece = shard_channels // n
    channels = m * piece
    inner_all = shard_channels * m
    shard_hidden = down_weight.shape[0]
    hidden_piece = shard_hidden // n
    piece_rows, hidden_rows = up_to(piece, 16), up_to(hidden_piece, 16)
    held, hidden_held = m * piece_rows, m * hidden_rows
    wide = up_to(held + 1, 128)
    sent_width = width + SIDE
    out_piece = width // n
    out_wide = up_to(out_piece, 128)

    def gather_z(values, tiled=True):
        return lax.all_gather(values, "fsdp", axis=0, tiled=tiled)

    def columns(values, start, size):
        return lax.dynamic_slice_in_dim(values, start, size, axis=1)

    in_groups = [
        (0, p * inner_all + f * shard_channels, p * held + f * piece_rows)
        for p in range(2)
        for f in range(m)
    ]
    in_local = pack_columns([mixer_in], c.reshape(1), in_groups, 2 * held, piece, "pack_mixer")
    in_weight = gather_z(in_local)
    own_index = after(c.reshape(1), in_local)
    c = own_index[0]
    upstream = cotangent[0]
    upstream_parts = swaps(after(upstream, in_local), n)
    token_parts = swaps(after(tokens[0], *upstream_parts[1 : n // 2]), n)
    small_rows = jnp.concatenate(
        [
            select_weight,
            step_weight.T,
            decay_log,
            filter_kernel.T,
            filter_bias[:, None],
            step_bias[:, None],
            skip_gain[:, None],
            mixer_gain[:, None],
        ],
        axis=1,
    )
    small_width = small_rows.shape[1]
    small_rows = lax.dynamic_slice_in_dim(small_rows, c * piece, piece, axis=0)
    gains = jnp.stack([norm_gain, attention_gain, post_gain]).reshape(-1)
    gain_rows = -(-3 * shard // small_width)
    gains = pad_to(gains, 0, gain_rows * small_width).reshape(gain_rows, small_width)
    small_local = jnp.concatenate([small_rows, gains])
    turned = [
        lax.ppermute(small_local, "fsdp", [(i, (i + k) % m) for i in range(m)])
        for k in range(m - 1, 0, -1)
    ] + [small_local]
    small_all = lax.dynamic_slice_in_dim(jnp.stack(turned + turned), m - 1 - z, m, axis=0)
    small = pad_to(small_all[:, :piece], 1, piece_rows).reshape(held, small_width)
    gains_all = small_all[:, piece:].reshape(m, gain_rows * small_width)[:, : 3 * shard]
    gains_all = jnp.moveaxis(gains_all.reshape(m, 3, shard), 0, 1).reshape(3, width).astype(f32)
    first_gain, attend_gain, after_gain = gains_all[0:1], gains_all[1:2], gains_all[2:3]

    def first_group(index):
        return jnp.minimum(index * heads // GROUP, KV_HEADS - 1)

    group_at = first_group(c)
    kv_pad = (KV_HEADS + 1) * HEAD_DIM
    pair = 2 * HEAD_DIM
    attend_local = join(
        [
            columns(pad_to(query_weight, 1, n * head_width), c * head_width, head_width),
            columns(pad_to(key_weight, 1, kv_pad), group_at * HEAD_DIM, pair),
            columns(pad_to(value_weight, 1, kv_pad), group_at * HEAD_DIM, pair),
        ],
        own_index,
        1,
        "pack_attention",
        [in_local],
    )
    head_ids = c * heads + jnp.arange(heads, dtype=jnp.int32)
    valid = (head_ids < HEADS).astype(jnp.int32)
    upper = jnp.minimum(head_ids // GROUP, KV_HEADS - 1) > group_at

    def row_slice(weight, size):
        cut = lax.dynamic_slice_in_dim(weight, c * size, size, axis=0)
        return pad_to(cut, 0, up_to(size, 16))

    out_cut = columns(attention_out, c * out_piece, out_piece).reshape(-1)
    out_rows = up_to(-(-out_cut.shape[0] // width), 16)
    rows_local = join(
        [
            row_slice(mixer_out, piece),
            pad_to(out_cut, 0, out_rows * width).reshape(out_rows, width),
        ],
        own_index,
        0,
        "pack_rows",
        [in_local],
    )
    pair_groups = [
        (k, f * shard_hidden, k * hidden_held + f * hidden_rows) for k in range(2) for f in range(m)
    ]
    pair_local = pack_columns(
        [gate_weight, up_weight],
        own_index,
        pair_groups,
        2 * hidden_held,
        hidden_piece,
        "pack_pair",
        [in_local],
    )
    down_local = row_slice(down_weight, hidden_piece)

    inputs = tokens[0].astype(f32)
    first_norm = inverse_rms(inputs)
    hidden = block_call(
        norm_body,
        own_index,
        1,
        [(first_gain, whole(first_gain.shape))]
        + [(item, whole(item.shape)) for item in token_parts],
        [(leaf((total_rows, width), bf16), whole((total_rows, width)))],
        [],
        "norm_tokens",
        [attend_local, rows_local, pair_local, upstream_parts[-1]],
    )[0]

    projected = dot(hidden, in_weight)
    attend_all = gather_z(after(attend_local, first_gain))
    rows_all = gather_z(after(rows_local, projected), tiled=False)

    def extended(weight, rows_now, at):
        weight = jnp.pad(weight, ((0, rows_now - weight.shape[0]), (0, SIDE)))
        spot = (jnp.arange(rows_now) == at)[:, None] & (jnp.arange(sent_width) == width)[None, :]
        return jnp.where(spot, jnp.ones((), bf16), weight)

    lane_dim = jnp.arange(head_width, dtype=jnp.int32) % HEAD_DIM
    target = jnp.where(jnp.repeat(upper, HEAD_DIM), HEAD_DIM, 0) + lane_dim
    target = jnp.concatenate([target, target + pair])
    side_now = jnp.arange(2 * head_width, dtype=jnp.int32) // head_width
    spread = (target[None, :] == jnp.arange(2 * pair, dtype=jnp.int32)[:, None]) & (
        side_now[None, :] == (jnp.arange(2 * pair, dtype=jnp.int32) // pair)[:, None]
    )
    spread = spread.astype(bf16)

    others = c ^ jnp.array(masks(n), dtype=jnp.int32)
    firsts = deal_table[others]
    places = jnp.stack([firsts, count - 1 - firsts], axis=1).reshape(count)
    ids = jnp.arange(count, dtype=jnp.int32)
    order = jnp.sum(jnp.where(places[None, :] == ids[:, None], ids[None, :], 0), axis=1)
    position = (places[:, None] * block + jnp.arange(block, dtype=jnp.int32)[None, :]).reshape(-1)

    small_t = pad_to(small.astype(f32).T, 1, wide)
    select_own = pad_to(
        jnp.concatenate(
            [
                pad_to(small[:, :RANK], 1, 128),
                pad_to(small[:, RANK : RANK + 2 * NS], 1, 128),
            ],
            axis=1,
        ),
        0,
        wide,
    )
    step_own = pad_to(small_t[RANK + 2 * NS : 2 * RANK + 2 * NS], 0, 128).astype(bf16)
    at = 2 * RANK + 2 * NS
    decay_own = -jnp.exp(small_t[at : at + NS])
    at += NS
    vecs = jnp.concatenate([small_t[at + CONV + 1 : at + CONV + 4], small_t[at + CONV : at + CONV + 1], small_t[at : at + CONV]])

    def halves(values):
        return values[: total_rows // 2], values[total_rows // 2 :]

    upstream_all = assemble(upstream_parts)

    forward = lambda i: i
    reverse = lambda i: count - 1 - i
    mixed_in, selected_part = block_call(
        filter_forward_body(block),
        order,
        count,
        [
            (projected, rows(block, 2 * held, forward)),
            (vecs, whole(vecs.shape)),
            (select_own, whole(select_own.shape)),
        ],
        [
            (leaf((total_rows, wide), bf16), rows(block, wide, forward)),
            (leaf((total_rows, 256), bf16), rows(block, 256, forward)),
        ],
        [pltpu.VMEM((block + 8, wide), f32)],
        "filter_forward",
    )
    selected_own = scatter_ctx(*halves(selected_part), n, own_index)
    pair_weight = gather_z(after(pair_local, selected_own))
    attend_all = after(attend_all, selected_own)
    heads_in = dot(hidden, attend_all).astype(bf16)
    pair_in = dot(heads_in[:, head_width:], spread).astype(bf16)
    mixer_out_own = extended(rows_all[:, :piece_rows].reshape(held, width), wide, held)
    out_columns = rows_all[:, piece_rows:].reshape(m, -1)[:, : shard * out_piece]
    out_columns = out_columns.reshape(width, out_piece)
    out_own = lax.all_to_all(
        pad_to(out_columns, 0, n * head_width).reshape(n, head_width, out_piece), "ctx", 0, 0
    )
    out_own = jnp.moveaxis(out_own, 0, 1).reshape(head_width, width)
    out_own = extended(out_own, head_width + 128, head_width)

    query_block = min(256, total_rows)
    query_count = total_rows // query_block
    query_pos = position[:, None]
    key_pos = position[None, :]
    own_gain = lax.dynamic_slice_in_dim(
        pad_to(attend_gain, 1, n * head_width), c * head_width, head_width, axis=1
    )

    def part(index):
        return pl.BlockSpec((total_rows, head_width), lambda i, order: (0, index))

    def tall(size):
        return pl.BlockSpec((query_block, size), lambda i, order: (i, 0))

    attend_ins = [
        (heads_in, tall(head_width)),
        (pair_in, part(0)),
        (pair_in, part(1)),
        (query_pos, tall(1)),
        (key_pos, whole(key_pos.shape)),
        (own_gain, whole(own_gain.shape)),
    ]
    attended, attended_scaled = block_call(
        attention_forward_body,
        valid,
        query_count,
        attend_ins,
        [
            (leaf((total_rows, head_width), f32), tall(head_width)),
            (leaf((total_rows, head_width + 128), bf16), tall(head_width + 128)),
        ],
        [],
        "attention_forward",
    )


    def branch_out(scaled, weight):
        return scatter_ctx(*split_columns(scaled, weight, "branch_out"), n, own_index)

    attend_sum = branch_out(attended_scaled, out_own)

    start_spec = lambda pick: pl.BlockSpec((1, NS, wide), lambda i, order: (order[pick(i)], 0, 0))
    selected = assemble(swaps(after(selected_own, pair_in), n), attended)
    scanned, starts, mixer_scaled = block_call(
        scan_forward_body(block),
        order,
        count,
        [
            (selected, rows(block, 256, forward)),
            (mixed_in, rows(block, wide, forward)),
            (projected, rows(block, 2 * held, forward)),
            (step_own, whole(step_own.shape)),
            (vecs, whole(vecs.shape)),
            (decay_own, whole(decay_own.shape)),
        ],
        [
            (leaf((total_rows, wide), f32), rows(block, wide, forward)),
            (leaf((count, NS, wide), f32), start_spec(forward)),
            (leaf((total_rows, wide), bf16), rows(block, wide, forward)),
        ],
        [
            pltpu.VMEM((NS, wide), f32),
            pltpu.VMEM((block, wide), f32),
            pltpu.VMEM((block, wide), f32),
            pltpu.VMEM((block, wide), f32),
            pltpu.VMEM((block // STEP, 2 * NS, STEP), f32),
        ],
        "scan_forward",
    )
    down_own = gather_z(after(down_local, scanned))
    mixer_sum = branch_out(mixer_scaled, mixer_out_own)

    def normed_sum(total, size):
        return total[:, :width] * lax.rsqrt(total[:, width : width + 1] / size + EPS)

    mixed = inputs + 0.5 * (
        normed_sum(attend_sum, HEADS * HEAD_DIM) + normed_sum(mixer_sum, inner_all)
    )
    post_norm = inverse_rms(mixed)
    post = gather_ctx((mixed * post_norm * after_gain).astype(bf16), n)
    both = dot(post, pair_weight)
    dunit = product_rows([(upstream_all, down_own)], 0, total_rows, f32, "units_backward")

    def strip(size):
        return pl.BlockSpec((own, size), lambda i: (i, 0))

    unit, dboth = pl.pallas_call(
        unit_body,
        grid=(n,),
        in_specs=[strip(2 * hidden_held), strip(hidden_held)],
        out_specs=[strip(hidden_held), strip(2 * hidden_held)],
        out_shape=[
            leaf((total_rows, hidden_held), bf16),
            leaf((total_rows, 2 * hidden_held), bf16),
        ],
        compiler_params=pltpu.CompilerParams(vmem_limit_bytes=VMEM),
        name="hidden_units",
    )(both, dunit)

    pair_part = dot_tn(post, dboth).astype(bf16)
    dpost_parts = scatter_parts(
        *split_rows([(dboth, pair_weight)], "post_backward", [pair_part]), n, own_index
    )
    half = n // 2
    strips = [(own, width)] * (half + 5)
    strips[half + 1] = (1, width)
    strips[half + 3] = strips[half + 4] = (own, sent_width)
    payload, dmixed, post_gain_part = block_call(
        branch_grad_body(half, inner_all),
        own_index,
        1,
        [
            (value, whole(shape))
            for value, shape in zip(
                dpost_parts + [mixed, after_gain, upstream, attend_sum, mixer_sum], strips
            )
        ],
        [
            (leaf((own, sent_width), bf16), whole((own, sent_width))),
            (leaf((own, width), f32), whole((own, width))),
            (leaf((8, width), f32), whole((8, width))),
        ],
        [],
        "branch_gradient",
    )
    post_gain_part = post_gain_part[0]

    def scatter_z(values):
        return lax.psum_scatter(values, "fsdp", scatter_dimension=0, tiled=True)

    payload_parts = swaps(payload, n)
    unit = after(unit, payload)
    down_part = dot_tn(unit, upstream_all).astype(bf16)
    pair_grad = scatter_z(pair_part)
    down_grad = scatter_z(down_part)
    payload = assemble(payload_parts)
    dattend_in = product_rows(
        [(payload, out_own)],
        0,
        total_rows,
        f32,
        "attended_backward",
        [down_part],
    )
    dmixer_in = product_rows(
        [(payload, mixer_out_own)], 0, total_rows, f32, "gated_backward", [dattend_in]
    )

    dquery, dpair, normed_a, attend_gain_part = block_call(
        attention_backward_body,
        valid,
        query_count,
        attend_ins
        + [
            (attended, tall(head_width)),
            (dattend_in, tall(head_width + 128)),
            (payload, pl.BlockSpec((query_block, 128), lambda i, order: (i, width // 128))),
        ],
        [
            (leaf((total_rows, head_width), bf16), tall(head_width)),
            (leaf((total_rows, 2 * head_width), bf16), whole((total_rows, 2 * head_width))),
            (leaf((total_rows, head_width), bf16), tall(head_width)),
            (leaf((8, head_width), f32), whole((8, head_width))),
        ],
        [
            pltpu.VMEM((total_rows, head_width), f32),
            pltpu.VMEM((total_rows, head_width), f32),
        ],
        "attention_backward",
    )
    pair_grad = after(pair_grad, dpair)
    pair_parts = swaps(pair_grad, n)
    dheads = jnp.concatenate([dquery, dot_nt(dpair, spread).astype(bf16)], axis=1)

    normed_s, dgate_z, dmixed_in, dselected_part, scan_vecs, step_part, decay_part = block_call(
        scan_backward_body(block),
        order,
        count,
        [
            (selected, rows(block, 256, reverse)),
            (mixed_in, rows(block, wide, reverse)),
            (projected, rows(block, 2 * held, reverse)),
            (scanned, rows(block, wide, reverse)),
            (dmixer_in, rows(block, wide, reverse)),
            (payload, columns_at(block, 128, reverse, width // 128)),
            (starts, start_spec(reverse)),
            (step_own, whole(step_own.shape)),
            (vecs, whole(vecs.shape)),
            (decay_own, whole(decay_own.shape)),
        ],
        [
            (leaf((total_rows, held), bf16), rows(block, held, reverse)),
            (leaf((total_rows, held), bf16), rows(block, held, reverse)),
            (leaf((total_rows, wide), f32), rows(block, wide, reverse)),
            (leaf((total_rows, 256), bf16), rows(block, 256, reverse)),
            (leaf((8, wide), f32), whole((8, wide))),
            (leaf((128, wide), f32), whole((128, wide))),
            (leaf((NS, wide), f32), whole((NS, wide))),
        ],
        [
            pltpu.VMEM((block // STEP, 2 * NS, STEP), f32),
            pltpu.VMEM((block, wide), f32),
            pltpu.VMEM((NS, wide), f32),
            pltpu.VMEM((block, wide), f32),
            pltpu.VMEM((block, wide), f32),
            pltpu.VMEM((block, wide), f32),
            pltpu.VMEM((block, wide), f32),
            pltpu.VMEM((block, wide), f32),
            pltpu.VMEM((block + 1, NS, wide), f32),
            pltpu.VMEM((block, NS, wide), f32),
            pltpu.VMEM((block * NS, 128), f32),
            pltpu.VMEM((block * NS, 128), f32),
        ],
        "scan_backward",
        [dpair, pair_grad],
    )
    dselected_part = after(dselected_part, *pair_parts[1 : n // 2])
    dselected_parts = scatter_parts(*halves(dselected_part), n, own_index)
    dselected = dselected_parts[0]
    for item in dselected_parts[1:]:
        dselected = dselected + item.astype(f32)
    dselected = gather_ctx(dselected.astype(bf16), n)
    hidden = after(hidden, dselected_parts[0])
    gate_part = dot_tn(hidden, dgate_z).astype(bf16)
    gate_half = scatter_z(gate_part)
    payload = after(payload, gate_part)
    mixer_part = dot_tn(normed_s, payload).astype(bf16)
    mixer_out_grad = scatter_z(mixer_part)


    out_part = dot_tn(after(normed_a, mixer_part), payload)[:, :width].astype(bf16)
    out_part = lax.all_to_all(
        jnp.moveaxis(out_part.reshape(head_width, n, out_piece), 1, 0), "ctx", 0, 0
    )
    out_part = out_part.reshape(n * head_width, out_piece)[:width]
    attend_part = jnp.concatenate(
        [dot_tn(hidden, dheads).astype(bf16), pad_to(out_part, 1, out_wide)], axis=1
    )
    attend_grad = scatter_z(attend_part)

    dprojected, select_part, filter_vecs = block_call(
        filter_backward_body(block, count),
        order,
        count,
        [
            (projected, rows(block, 2 * held, reverse)),
            (projected, rows(block, 2 * held, lambda i: jnp.maximum(count - 2 - i, 0))),
            (dgate_z, rows(block, held, reverse)),
            (mixed_in, rows(block, wide, reverse)),
            (dmixed_in, rows(block, wide, reverse)),
            (dselected, rows(block, 256, reverse)),
            (select_own, whole(select_own.shape)),
            (vecs, whole(vecs.shape)),
        ],
        [
            (leaf((total_rows, 2 * held), bf16), rows(block, 2 * held, reverse)),
            (leaf((256, wide), f32), whole((256, wide))),
            (leaf((8, wide), f32), whole((8, wide))),
        ],
        [
            pltpu.VMEM((block + 8, wide), f32),
            pltpu.VMEM((block + 8, wide), f32),
            pltpu.VMEM((block, 2 * held), f32),
        ],
        "filter_backward",
        [attend_part, down_grad],
    )
    hidden_near, hidden_far = split_rows(
        [(dprojected, in_weight), (dheads, attend_all)], "hidden_backward"
    )
    half_rows = total_rows // 2
    first_gain_part = (
        jnp.sum(hidden_near.astype(f32) * hidden[:half_rows].astype(f32), axis=0)
        + jnp.sum(hidden_far.astype(f32) * hidden[half_rows:].astype(f32), axis=0)
    ) / first_gain[0]
    small_grad = jnp.concatenate(
        [
            select_part[:RANK],
            select_part[128 : 128 + 2 * NS],
            step_part[:RANK],
            decay_part,
            filter_vecs[4 : 4 + CONV],
            filter_vecs[3:4],
            scan_vecs[0:3],
        ]
    )[:, :held]
    attend_gain_full = lax.dynamic_update_slice_in_dim(
        jnp.zeros((1, n * head_width), f32), attend_gain_part[0:1], c * head_width, axis=1
    )[0, :width]
    gain_part = jnp.stack([first_gain_part, attend_gain_full, post_gain_part]).reshape(3, m, shard)
    gain_part = pad_to(
        jnp.moveaxis(gain_part, 1, 0).reshape(m, 3 * shard), 1, gain_rows * small_width
    )
    small_part = jnp.concatenate(
        [
            small_grad.T.reshape(m, piece_rows, small_width)[:, :piece],
            gain_part.reshape(m, gain_rows, small_width),
        ],
        axis=1,
    )
    small_count = up_to(-(-small_part.shape[1] * small_width // held), 16)
    small_part = pad_to(small_part.reshape(m, -1), 1, small_count * held)
    small_part = small_part.reshape(m, small_count, held).astype(bf16)
    inner_part = dot_tn(hidden, dprojected[:, :held]).astype(bf16)
    in_part = weave(inner_part, small_part.reshape(-1, held), m, own_index)
    in_grad = scatter_z(in_part)

    dhidden = scatter_ctx(
        after(hidden_near, in_part, gate_half), hidden_far, n, own_index
    )
    dfirst = norm_backward(inputs, first_norm, first_gain, dhidden)
    tokens_grad = (dmixed + dfirst).astype(bf16)[None]
    ffn_sums = scatter_parts(*split_columns(unit, down_own, "unit_out", [in_part]), n, own_index)
    layer_out = mixed
    for item in ffn_sums:
        layer_out = layer_out + item.astype(f32)
    layer_out = layer_out.astype(bf16)[None]

    spots = jnp.array([masks(n).index(mask) for mask in range(n)], dtype=jnp.int32)
    where = spots[c ^ jnp.arange(n, dtype=jnp.int32)]
    gate_grad, up_grad = unpack_columns(
        [pair_parts],
        where,
        [
            (k, f * shard_hidden, hidden_piece, k * hidden_held + f * hidden_rows, hidden_piece)
            for k in range(2)
            for f in range(m)
        ],
        [weight.shape[1] for weight in (gate_weight, up_weight)],
        "unpack_pair",
    )
    down_turned = unpack_rows(
        swaps(down_grad, n), where, hidden_piece, width, True, "unpack_down"
    )
    mixer_out_grad = unpack_rows(
        swaps(mixer_out_grad, n), where, piece, width, False, "unpack_mixer"
    )
    attend_grad = swaps(attend_grad, n)
    kv_wide = n * pair
    out_at = head_width + 2 * pair
    query_grad, key_parts, value_parts, out_grad = unpack_columns(
        [attend_grad],
        where,
        [
            (0, 0, head_width, 0, head_width),
            (1, 0, pair, head_width, pair),
            (2, 0, pair, head_width + pair, pair),
            (3, 0, out_piece, out_at, out_piece),
        ],
        [width, kv_wide, kv_wide, width],
        "unpack_attention",
    )

    def group_sum(parts):
        total = jnp.zeros((shard, kv_pad), f32)
        for index in range(n):
            low_at = min(index * heads // GROUP, KV_HEADS - 1) * HEAD_DIM
            item = parts[:, index * pair : (index + 1) * pair]
            total = total + jnp.pad(item, ((0, 0), (low_at, kv_pad - pair - low_at)))
        return total[:, : KV_HEADS * HEAD_DIM]

    in_grad = after(in_grad, gate_grad, down_turned, query_grad, mixer_out_grad)
    in_grad = swaps(in_grad, n)
    (mixer_in_grad,) = unpack_columns(
        [in_grad, swaps(gate_half, n)],
        where,
        [
            (0, p * inner_all + f * shard_channels, piece, p * held + f * piece_rows, piece)
            for p in range(2)
            for f in range(m)
        ],
        [2 * inner_all],
        "unpack_inner",
        shard,
    )
    small_sum = jnp.stack([item[shard:] for item in in_grad]).astype(f32)
    small_sum = small_sum.reshape(n, -1)[:, : (piece + gain_rows) * small_width]
    small_sum = small_sum[where].reshape(n, piece + gain_rows, small_width)
    channel_grad = small_sum[:, :piece].reshape(shard_channels, small_width)
    gain_grad = jnp.sum(small_sum[:, piece:], axis=0).reshape(-1)[: 3 * shard].reshape(3, shard)

    at = RANK + 2 * NS
    select_grad = channel_grad[:, :at]
    step_grad = channel_grad[:, at : at + RANK].T
    at += RANK
    decay_grad = channel_grad[:, at : at + NS]
    at += NS
    kernel_grad = channel_grad[:, at : at + CONV].T
    at += CONV
    return (
        layer_out,
        tokens_grad,
        gain_grad[0],
        query_grad,
        group_sum(key_parts),
        group_sum(value_parts),
        out_grad,
        gain_grad[1],
        mixer_in_grad,
        kernel_grad,
        channel_grad[:, at],
        select_grad,
        step_grad,
        channel_grad[:, at + 1],
        decay_grad,
        channel_grad[:, at + 2],
        channel_grad[:, at + 3],
        mixer_out_grad,
        gain_grad[2],
        gate_grad,
        up_grad,
        down_turned.T,
    )


def solution(mesh):
    rows_spec = P("fsdp", None)
    lanes_spec = P(None, "fsdp")
    flat = P("fsdp")
    activations = P("fsdp", "ctx", None)
    weight_specs = (
        flat, rows_spec, rows_spec, rows_spec, rows_spec, flat, rows_spec, lanes_spec, flat, rows_spec,
        lanes_spec, flat, rows_spec, flat, flat, rows_spec, flat, rows_spec, rows_spec, rows_spec,
    )
    return jax.shard_map(
        on_device,
        mesh=mesh,
        in_specs=(activations, activations, P()) + weight_specs,
        out_specs=(activations, activations) + weight_specs,
        check_vma=False,
    )
```

```python
import math

import jax
import jax.numpy as jnp
from jax import lax
from jax.experimental import pallas as pl
from jax.experimental.pallas import tpu as pltpu
from jax.sharding import PartitionSpec as P

HEADS = 25
KV_HEADS = 5
HEAD_DIM = 64
GROUP = HEADS // KV_HEADS
CONV = 4
RANK = 100
NS = 16
EPS = 1e-05
NEG = -1e30
SCALE = 1.0 / math.sqrt(HEAD_DIM)
STEP = 16
VMEM = 56 * 1024 * 1024
SIDE = 64
SIDE_AT = HEADS * HEAD_DIM % 128
bf16 = jnp.bfloat16
f32 = jnp.float32


def up_to(value, unit):
    return -(-value // unit) * unit


def dot(left, right, contract=((1,), (0,)), precision=None):
    return lax.dot_general(
        left, right, (contract, ((), ())), preferred_element_type=f32, precision=precision
    )


def dot_tn(left, right):
    return dot(left, right, ((0,), (0,)))


def dot_nt(left, right):
    return dot(left, right, ((1,), (1,)))


def pad_to(values, axis, size):
    widths = [(0, 0)] * values.ndim
    widths[axis] = (0, size - values.shape[axis])
    return jnp.pad(values, widths)


def masks(size):
    return list(range(0, size, 2)) + list(range(1, size, 2))


def swap(values, mask, size):
    return lax.ppermute(values, "ctx", [(i, i ^ mask) for i in range(size)])


def swaps(values, size):
    near = [values] + [swap(values, m, size) for m in range(2, size, 2)]
    return near + [swap(item, 1, size) for item in near]


def assemble(parts, *earlier):
    count = len(parts)
    step = parts[0].shape[0]
    shape = (count * step,) + parts[0].shape[1:]

    def body(*refs):
        for j in range(count):
            refs[-1][j * step : (j + 1) * step] = refs[j][...]

    spec = pl.BlockSpec(parts[0].shape, lambda: (0,) * len(shape))
    return pl.pallas_call(
        body,
        in_specs=[spec] * count + [pl.BlockSpec(memory_space=pl.ANY)] * len(earlier),
        out_specs=pl.BlockSpec(shape, lambda: (0,) * len(shape)),
        out_shape=leaf(shape, parts[0].dtype),
        compiler_params=pltpu.CompilerParams(vmem_limit_bytes=VMEM),
        name="assemble",
    )(*parts, *earlier)


def gather_ctx(values, size):
    return assemble(swaps(values, size))


def product_rows(pairs, at, rows_now, dtype, name, earlier=()):
    count = pairs[0][1].shape[0]
    step = min(256, count)

    def body(*refs):
        total = dot_nt(refs[0][...], refs[1][...])
        for k in range(2, 2 * len(pairs), 2):
            total = total + dot_nt(refs[k][...], refs[k + 1][...])
        refs[-1][...] = total.astype(dtype)

    specs, values = [], []
    for left, right in pairs:
        depth = left.shape[1]
        specs.append(pl.BlockSpec((rows_now, depth), lambda i: (at, 0)))
        specs.append(pl.BlockSpec((step, depth), lambda i: (i, 0)))
        values += [left, right]
    return pl.pallas_call(
        body,
        grid=(-(-count // step),),
        in_specs=specs + [pl.BlockSpec(memory_space=pl.ANY)] * len(earlier),
        out_specs=pl.BlockSpec((rows_now, step), lambda i: (0, i)),
        out_shape=leaf((rows_now, count), dtype),
        compiler_params=pltpu.CompilerParams(vmem_limit_bytes=VMEM),
        name=name,
    )(*values, *earlier)


def product_columns(left, right, at, rows_now, name, earlier=()):
    depth, count = right.shape
    step = min(256, count)

    def body(*refs):
        refs[-1][...] = dot(refs[0][...], refs[1][...]).astype(bf16)

    return pl.pallas_call(
        body,
        grid=(-(-count // step),),
        in_specs=[
            pl.BlockSpec((rows_now, depth), lambda i: (at, 0)),
            pl.BlockSpec((depth, step), lambda i: (0, i)),
        ]
        + [pl.BlockSpec(memory_space=pl.ANY)] * len(earlier),
        out_specs=pl.BlockSpec((rows_now, step), lambda i: (0, i)),
        out_shape=leaf((rows_now, count), bf16),
        compiler_params=pltpu.CompilerParams(vmem_limit_bytes=VMEM),
        name=name,
    )(left, right, *earlier)


def split_columns(left, right, name, earlier=()):
    half = left.shape[0] // 2
    far = product_columns(left, right, 1, half, name, earlier)
    return product_columns(left, right, 0, half, name), far


def split_rows(pairs, name, earlier=()):
    half = pairs[0][0].shape[0] // 2
    far = product_rows(pairs, 1, half, bf16, name, earlier)
    return product_rows(pairs, 0, half, bf16, name), far


def fold_body(count, step):
    def body(index, near, got, own_o, *sent_o):
        for j in range(count):
            rows_now = slice(j * step, (j + 1) * step)
            total = near[rows_now, :].astype(f32) + got[rows_now, :].astype(f32)
            if j == 0:
                own_o[...] = total
            else:
                sent_o[j - 1][...] = total.astype(bf16)

    return body


def scatter_parts(near, far, size, index):
    half = size // 2
    step, width = near.shape[0] // half, near.shape[1]
    got = swap(far, 1, size)
    total, *sent = block_call(
        fold_body(half, step),
        index,
        1,
        [(near, whole(near.shape)), (got, whole(near.shape))],
        [(leaf((step, width), f32), whole((step, width)))]
        + [(leaf((step, width), bf16), whole((step, width)))] * (half - 1),
        [],
        "fold_halves",
    )
    return [total] + [swap(sent[k - 1], 2 * k, size) for k in range(1, half)]


def scatter_ctx(near, far, size, index):
    total, *others = scatter_parts(near, far, size, index)
    for item in others:
        total = total + item.astype(f32)
    return total


def block_call(body, order, count, ins, outs, scratch, name, earlier=()):
    given = len(ins)
    ins = list(ins) + [(value, pl.BlockSpec(memory_space=pl.ANY)) for value in earlier]

    def trimmed(*refs):
        return body(*refs[: 1 + given], *refs[1 + len(ins) :])

    return pl.pallas_call(
        trimmed,
        grid_spec=pltpu.PrefetchScalarGridSpec(
            num_scalar_prefetch=1,
            grid=(count,),
            in_specs=[spec for _, spec in ins],
            out_specs=[spec for _, spec in outs],
            scratch_shapes=scratch,
        ),
        out_shape=[shape for shape, _ in outs],
        compiler_params=pltpu.CompilerParams(
            dimension_semantics=("arbitrary",), vmem_limit_bytes=VMEM
        ),
        name=name,
    )(order, *[value for value, _ in ins])


def after(values, *earlier):
    def body(*refs):
        del refs

    spec = pl.BlockSpec(memory_space=pl.ANY)
    return pl.pallas_call(
        body,
        in_specs=[spec] * (1 + len(earlier)),
        out_specs=spec,
        out_shape=leaf(values.shape, values.dtype),
        input_output_aliases={0: 0},
        name="after",
    )(values, *earlier)


def whole(shape):
    zeros = (0,) * len(shape)
    return pl.BlockSpec(shape, lambda i, order: zeros)


def rows(block, width, pick):
    return pl.BlockSpec((block, width), lambda i, order: (order[pick(i)], 0))


def columns_at(block, width, pick, index):
    return pl.BlockSpec((block, width), lambda i, order: (order[pick(i)], index))


def leaf(shape, dtype):
    return jax.ShapeDtypeStruct(shape, dtype)


def filter_taps(ext, vecs, block):
    total = vecs[3:4, :]
    for j in range(CONV):
        total = total + vecs[4 + j : 5 + j, :] * ext[5 + j : 5 + j + block, :]
    return total


def filter_forward_body(block):
    def body(order, projected, vecs, select, mixed_o, selected_o, ext):
        step = pl.program_id(0)
        held = projected.shape[1] // 2

        @pl.when(step == 0)
        def _():
            ext[...] = jnp.zeros_like(ext)

        @pl.when(step > 0)
        def _():
            ext[0:8, :] = ext[block : block + 8, :]

        ext[8 : block + 8, 0:held] = projected[:, 0:held].astype(bf16).astype(f32)
        total = filter_taps(ext, vecs, block)
        mixed = (total * jax.nn.sigmoid(total)).astype(bf16)
        mixed_o[...] = mixed
        selected_o[...] = dot(mixed, select[...]).astype(bf16)

    return body


def side_scalar(scalars, index):
    at = SIDE_AT + 2 * index
    values = scalars[...].astype(f32)
    return values[:, at : at + 1] + values[:, at + 1 : at + 2]


def turn_sides(selected, sides_s):
    turned = selected[:, 128:256].T
    for g in range(sides_s.shape[0]):
        sides_s[g] = turned[: 2 * NS, g * STEP : (g + 1) * STEP]


def rate_of(selected, step_weight, vecs):
    rank = selected[:, 0:128].astype(bf16)
    raw = dot(rank, step_weight[...]) + vecs[0:1, :]
    rate = jnp.maximum(raw, 0.0) + jnp.log1p(jnp.exp(-jnp.abs(raw)))
    return rank, raw, rate


def scan_forward_body(block):
    def body(
        order, selected, mixed, projected, step_weight, vecs, decay,
        scanned_o, starts_o, scaled_o, state_s, rate_s, drive_s, gate_s, sides_s,
    ):
        held = projected.shape[1] // 2

        @pl.when(pl.program_id(0) == 0)
        def _():
            state_s[...] = jnp.zeros_like(state_s)
            gate_s[...] = jnp.zeros_like(gate_s)

        gate_s[:, 0:held] = projected[...][:, held:]
        turn_sides(selected, sides_s)

        _, _, rate = rate_of(selected, step_weight, vecs)
        wide = mixed[...].astype(f32)
        rate_s[...] = rate
        drive_s[...] = rate * wide
        starts_o[0] = state_s[...]
        decay_mat = decay[...]

        def group(g, state):
            base = pl.multiple_of(g * STEP, STEP)
            rates = rate_s[pl.ds(base, STEP), :]
            drives = drive_s[pl.ds(base, STEP), :]
            side = sides_s[g]
            for j in range(STEP):
                state = (
                    jnp.exp(rates[j : j + 1, :] * decay_mat) * state
                    + drives[j : j + 1, :] * side[:NS, j : j + 1]
                )
                scanned_o[pl.ds(base + j, 1), :] = jnp.sum(
                    state * side[NS:, j : j + 1], axis=0, keepdims=True
                )
            return state

        state_s[...] = lax.fori_loop(0, block // STEP, group, state_s[...])
        gate = gate_s[...]
        gated = (scanned_o[...] + vecs[1:2, :] * wide) * (gate * jax.nn.sigmoid(gate))
        lane = lax.broadcasted_iota(jnp.int32, gated.shape, 1)
        squares = jnp.sum(gated * gated, axis=1, keepdims=True)
        scaled_o[...] = jnp.where(lane == held, squares, gated * vecs[2:3, :]).astype(bf16)

    return body


def scan_backward_body(block):
    def body(
        order, selected, mixed, projected, scanned, grad_in, scalars, starts, step_weight, vecs, decay,
        normed_o, dgate_o, dmixed_o, dselected_o, vec_o, step_o, decay_o,
        sides_s, gate_s, lam_s, rate_s, drive_s, dscan_s, drate_s, pull_s, hist_s, factor_s, read_s, write_s,
    ):
        width = decay.shape[1]
        held = projected.shape[1] // 2

        @pl.when(pl.program_id(0) == 0)
        def _():
            gate_s[...] = jnp.zeros_like(gate_s)
            lam_s[...] = jnp.zeros_like(lam_s)
            vec_o[...] = jnp.zeros_like(vec_o)
            step_o[...] = jnp.zeros_like(step_o)
            decay_o[...] = jnp.zeros_like(decay_o)

        rank, raw, rate = rate_of(selected, step_weight, vecs)
        wide = mixed[...].astype(f32)
        rate_s[...] = rate
        drive_s[...] = rate * wide
        turn_sides(selected, sides_s)
        gate_s[:, 0:held] = projected[...][:, held:]
        gate = gate_s[...]
        sig = jax.nn.sigmoid(gate)
        act = gate * sig
        before = scanned[...] + vecs[1:2, :] * wide
        gated = before * act
        norm = side_scalar(scalars, 2)
        centre = side_scalar(scalars, 3)
        grad = grad_in[...]
        gated_norm = gated * norm
        normed_o[...] = (gated_norm * vecs[2:3, :])[:, 0:held].astype(bf16)
        dgated = norm * (vecs[2:3, :] * grad) - gated * centre
        dscan = dgated * act
        dscan_s[...] = dscan
        dgate = dgated * before * (sig * (1.0 + gate * (1.0 - sig)))
        dgate_o[...] = dgate[:, 0:held].astype(bf16)
        vec_o[1:2, :] += jnp.sum(dscan * wide, axis=0, keepdims=True)
        vec_o[2:3, :] += jnp.sum(grad * gated_norm, axis=0, keepdims=True)
        decay_mat = decay[...]

        def forward(g, state):
            base = pl.multiple_of(g * STEP, STEP)
            rates = rate_s[pl.ds(base, STEP), :]
            drives = drive_s[pl.ds(base, STEP), :]
            side = sides_s[g]
            for j in range(STEP):
                factor = jnp.exp(rates[j : j + 1, :] * decay_mat)
                factor_s[base + j] = factor
                state = factor * state + drives[j : j + 1, :] * side[:NS, j : j + 1]
                hist_s[base + j + 1] = state
            return state

        hist_s[0] = starts[0]
        lax.fori_loop(0, block // STEP, forward, starts[0])

        def fold(values):
            total = values[:, 0:128]
            for at in range(128, width, 128):
                total = total + values[:, at : at + 128]
            return total

        def backward(i, carry):
            lam_in, decay_sum = carry
            g = block // STEP - 1 - i
            base = pl.multiple_of(g * STEP, STEP)
            rates = rate_s[pl.ds(base, STEP), :]
            drives = drive_s[pl.ds(base, STEP), :]
            dscans = dscan_s[pl.ds(base, STEP), :]
            side = sides_s[g]
            for j in range(STEP - 1, -1, -1):
                at = base + j
                row = dscans[j : j + 1, :]
                lam = lam_in + row * side[NS:, j : j + 1]
                read_s[pl.ds(at * NS, NS), :] = fold(hist_s[at + 1] * row)
                write_s[pl.ds(at * NS, NS), :] = fold(lam * drives[j : j + 1, :])
                pull = jnp.sum(lam * side[:NS, j : j + 1], axis=0, keepdims=True)
                lam_in = factor_s[at] * lam
                kept = lam_in * hist_s[at]
                decay_sum = decay_sum + rates[j : j + 1, :] * kept
                drate_s[pl.ds(at, 1), :] = jnp.sum(decay_mat * kept, axis=0, keepdims=True)
                pull_s[pl.ds(at, 1), :] = pull
            return (lam_in, decay_sum)

        lam, decay_sum = lax.fori_loop(
            0, block // STEP, backward, (lam_s[...], jnp.zeros_like(lam_s))
        )
        lam_s[...] = lam
        decay_o[...] += decay_sum * decay_mat
        pulled = pull_s[...]
        draw = (drate_s[...] + wide * pulled) * jax.nn.sigmoid(raw)
        vec_o[0:1, :] += jnp.sum(draw, axis=0, keepdims=True)
        low = draw.astype(bf16)
        dmixed_o[...] = vecs[1:2, :] * dscan + rate * pulled
        step_o[...] += dot_tn(rank, low)
        ones = jnp.ones((128, 128), f32)
        high = lax.Precision.HIGHEST
        row = lax.broadcasted_iota(jnp.int32, (block * NS, 128), 0) % NS
        lane = lax.broadcasted_iota(jnp.int32, (block * NS, 128), 1)
        summed = jnp.where(
            lane == row, dot(write_s[...], ones, precision=high), 0.0
        ) + jnp.where(lane == row + NS, dot(read_s[...], ones, precision=high), 0.0)
        token = lax.broadcasted_iota(jnp.int32, (block, block * NS), 0)
        spot = lax.broadcasted_iota(jnp.int32, (block, block * NS), 1) // NS
        collect = jnp.where(token == spot, 1.0, 0.0)
        dselected_o[:, 0:128] = dot_nt(low, step_weight[...]).astype(bf16)
        dselected_o[:, 128:256] = dot(collect, summed, precision=high).astype(bf16)

    return body


def filter_backward_body(block, count):
    def body(
        order, projected, before, dgate, mixed, dmixed, dselected, select, vecs,
        dprojected_o, select_o, vec_o, ext, ext_grad, both_s,
    ):
        step = pl.program_id(0)
        held = projected.shape[1] // 2

        @pl.when(step == 0)
        def _():
            ext[...] = jnp.zeros_like(ext)
            ext_grad[block : block + 8, :] = jnp.zeros((8, ext.shape[1]), f32)
            select_o[...] = jnp.zeros_like(select_o)
            vec_o[...] = jnp.zeros_like(vec_o)

        @pl.when(step > 0)
        def _():
            ext_grad[block : block + 8, :] = ext_grad[0:8, :]

        first = jnp.where(step == count - 1, 0.0, 1.0)
        ext[0:8, 0:held] = before[block - 8 :, 0:held].astype(bf16).astype(f32) * first
        ext[8 : block + 8, 0:held] = projected[:, 0:held].astype(bf16).astype(f32)
        total = filter_taps(ext, vecs, block)
        sig = jax.nn.sigmoid(total)
        low = dselected[...]
        dmix = dmixed[...] + dot_nt(low, select[...])
        dfilt = dmix * (sig * (1.0 + total * (1.0 - sig)))
        ext_grad[0:block, :] = dfilt
        dinner = jnp.zeros_like(dfilt)
        vec_o[3:4, :] += jnp.sum(dfilt, axis=0, keepdims=True)
        for j in range(CONV):
            at = CONV - 1 - j
            dinner = dinner + vecs[4 + j : 5 + j, :] * ext_grad[at : at + block, :]
            vec_o[4 + j : 5 + j, :] += jnp.sum(
                dfilt * ext[5 + j : 5 + j + block, :], axis=0, keepdims=True
            )
        both_s[:, 0:held] = dinner[:, 0:held]
        both_s[:, held:] = dgate[...].astype(f32)
        dprojected_o[...] = both_s[...].astype(bf16)
        select_o[...] += dot_tn(low, mixed[...])

    return body


def half_mask(half):
    lane = lax.broadcasted_iota(jnp.int32, (1, 128), 1)
    return jnp.where((lane >= 64 * half) & (lane < 64 * half + 64), 1.0, 0.0)


def softmax_rows(query, key, allowed):
    scores = jnp.where(allowed, dot_nt(query, key) * SCALE, NEG)
    weights = jnp.exp(scores - jnp.max(scores, axis=-1, keepdims=True))
    return weights * (1.0 / jnp.sum(weights, axis=-1, keepdims=True))


def attention_forward_body(valid, query, key, value, query_pos, key_pos, gain, out_o, scaled_o):
    allowed = key_pos[...] <= query_pos[...]
    squares = jnp.zeros((query.shape[0], 1), f32)
    for at in range(0, query.shape[1], 128):
        key_tile = key[:, at : at + 128]
        value_tile = value[:, at : at + 128]
        tile = jnp.zeros((query.shape[0], 128), f32)
        for half in range(2):
            mask = half_mask(half)
            part = query[:, at : at + 128] * mask.astype(bf16)
            probs = softmax_rows(part, key_tile, allowed).astype(bf16)
            live = valid[at // 64 + half].astype(f32)
            tile = tile + dot(probs, value_tile) * (mask * live)
        out_o[:, at : at + 128] = tile
        scaled_o[:, at : at + 128] = (tile * gain[:, at : at + 128]).astype(bf16)
        squares = squares + jnp.sum(tile * tile, axis=1, keepdims=True)
    at = query.shape[1]
    lane = lax.broadcasted_iota(jnp.int32, (query.shape[0], 128), 1)
    scaled_o[:, at : at + 128] = jnp.where(lane == 0, squares, 0.0).astype(bf16)


def unit_body(both, dunit, unit_o, dboth_o):
    held = dunit.shape[1]
    values = both[...]
    gate, up = values[:, :held], values[:, held:]
    grad = dunit[...]
    sig = jax.nn.sigmoid(gate)
    act = gate * sig
    unit_o[...] = (act * up).astype(bf16)
    dgate = grad * up * (sig * (1.0 + gate * (1.0 - sig)))
    dboth_o[...] = jnp.concatenate([dgate, grad * act], axis=1).astype(bf16)


def branch_grad_body(half, inner_all):
    def body(index, *refs):
        parts = refs[:half]
        mixed, gain, upstream, attend_sum, mixer_sum = refs[half : half + 5]
        payload_o, dmixed_o, gain_o = refs[half + 5 :]
        grad = parts[0][...]
        for item in parts[1:]:
            grad = grad + item[...].astype(f32)
        values = mixed[...]
        width = values.shape[1]
        norm = lax.rsqrt(jnp.mean(values * values, axis=1, keepdims=True) + EPS)
        scaled = grad * gain[...]
        centre = norm * norm * norm * jnp.mean(values * scaled, axis=1, keepdims=True)
        dmixed = upstream[...].astype(f32) + norm * scaled - values * centre
        dmixed_o[...] = dmixed
        total = jnp.sum(grad * values * norm, axis=0, keepdims=True)
        gain_o[...] = jnp.broadcast_to(total, gain_o.shape)
        low = (0.5 * dmixed).astype(bf16)
        payload_o[:, 0:width] = low
        wide_low = low.astype(f32)
        lane = lax.broadcasted_iota(jnp.int32, (values.shape[0], SIDE), 1)
        side = jnp.zeros((values.shape[0], SIDE), f32)
        at = 0
        for source, size in ((attend_sum, HEADS * HEAD_DIM), (mixer_sum, inner_all)):
            sums = source[...]
            factor = lax.rsqrt(sums[:, width : width + 1] / size + EPS)
            mean = jnp.sum(wide_low * sums[:, 0:width], axis=1, keepdims=True) / size
            for item in (factor, factor * factor * factor * mean):
                high = item.astype(bf16).astype(f32)
                side = jnp.where(lane == at, high, side)
                side = jnp.where(lane == at + 1, item - high, side)
                at += 2
        payload_o[:, width:] = side.astype(bf16)

    return body


def norm_body(index, gain, *refs):
    out = refs[-1]
    step = refs[0].shape[0]
    for j, ref in enumerate(refs[:-1]):
        values = ref[...].astype(f32)
        norm = lax.rsqrt(jnp.mean(values * values, axis=1, keepdims=True) + EPS)
        out[j * step : (j + 1) * step, :] = (values * norm * gain[...]).astype(bf16)


def attention_backward_body(
    valid, query, key, value, query_pos, key_pos, gain, out, grad_in, scalars,
    dquery_o, dpair_o, normed_o, gain_o, dkey_s, dvalue_s,
):
    @pl.when(pl.program_id(0) == 0)
    def _():
        dkey_s[...] = jnp.zeros_like(dkey_s)
        dvalue_s[...] = jnp.zeros_like(dvalue_s)
        gain_o[...] = jnp.zeros_like(gain_o)

    allowed = key_pos[...] <= query_pos[...]
    norm = side_scalar(scalars, 0)
    centre = side_scalar(scalars, 1)
    for at in range(0, query.shape[1], 128):
        lanes = slice(at, at + 128)
        key_tile = key[:, lanes]
        value_tile = value[:, lanes]
        attended = out[:, lanes]
        grad = grad_in[:, lanes]
        normed = attended * norm
        normed_o[:, lanes] = (normed * gain[:, lanes]).astype(bf16)
        gain_o[0:1, lanes] += jnp.sum(grad * normed, axis=0, keepdims=True)
        dout = (norm * (gain[:, lanes] * grad) - attended * centre).astype(bf16)
        dquery = jnp.zeros(attended.shape, f32)
        dkey = jnp.zeros((key.shape[0], 128), f32)
        dvalue = jnp.zeros((key.shape[0], 128), f32)
        for half in range(2):
            mask = half_mask(half)
            part = query[:, lanes] * mask.astype(bf16)
            dpart = dout * mask.astype(bf16)
            probs = softmax_rows(part, key_tile, allowed)
            dprobs = dot_nt(dpart, value_tile)
            mean = jnp.sum(dprobs * probs, axis=-1, keepdims=True)
            dscores = (probs * (dprobs - mean)).astype(bf16)
            dvalue = dvalue + dot_tn(probs.astype(bf16), dpart)
            dquery = dquery + dot(dscores, key_tile) * (mask * SCALE)
            dkey = dkey + dot_tn(dscores, part) * SCALE
        dquery_o[:, lanes] = dquery.astype(bf16)
        dkey_s[:, lanes] += dkey
        dvalue_s[:, lanes] += dvalue

    @pl.when(pl.program_id(0) == pl.num_programs(0) - 1)
    def _():
        held = dkey_s.shape[1]
        dpair_o[:, :held] = dkey_s[...].astype(bf16)
        dpair_o[:, held:] = dvalue_s[...].astype(bf16)


def pack_body(groups, width, piece):
    window = up_to(piece + 127, 128)

    def body(index, *refs):
        out_o, acc = refs[-2:]
        acc[...] = jnp.zeros_like(acc)
        for which, start, at in groups:
            weight = refs[which]
            source = start + index[0] * piece
            tile = jnp.minimum(source // 128, (width - window) // 128)
            base = pl.multiple_of(tile * 128, 128)
            low = at % 128
            span = up_to(low + piece, 128)
            row = lax.broadcasted_iota(jnp.int32, (window, span), 0)
            lane = lax.broadcasted_iota(jnp.int32, (window, span), 1) - low
            pick = (row - (source - base) == lane) & (lane >= 0) & (lane < piece)
            pick = jnp.where(pick, 1.0, 0.0).astype(bf16)
            acc[:, at - low : at - low + span] += dot(weight[:, pl.ds(base, window)], pick)
        out_o[...] = acc[:, : out_o.shape[1]].astype(bf16)

    return body


def row_block(count):
    return 80 if count % 80 == 0 else count


def join_body(axis):
    def body(index, *refs):
        at = 0
        for ref in refs[:-1]:
            size = ref.shape[axis]
            if axis == 0:
                refs[-1][at : at + size, :] = ref[...]
            else:
                refs[-1][:, at : at + size] = ref[...]
            at += size

    return body


def join(parts, index, axis, name, earlier):
    shape = list(parts[0].shape)
    shape[axis] = sum(part.shape[axis] for part in parts)
    return block_call(
        join_body(axis),
        index,
        1,
        [(part, whole(part.shape)) for part in parts],
        [(leaf(tuple(shape), bf16), whole(tuple(shape)))],
        [],
        name,
        earlier,
    )[0]


def pack_columns(weights, index, groups, out_wide, piece, name, earlier=()):
    count, width = weights[0].shape
    block = row_block(count)
    return block_call(
        pack_body(groups, width, piece),
        index,
        count // block,
        [(weight, pl.BlockSpec((block, width), lambda i, index: (i, 0))) for weight in weights],
        [
            (
                leaf((count, out_wide), bf16),
                pl.BlockSpec((block, out_wide), lambda i, index: (i, 0)),
            )
        ],
        [pltpu.VMEM((block, up_to(out_wide, 128)), f32)],
        name,
        earlier,
    )[0]


def unpack_columns(parts, where, moves, widths, name, count=None):
    joined = not isinstance(parts, list)
    size = len(parts)
    width = parts[0].shape[1]
    count = count or parts[0].shape[0]
    block = row_block(count)

    def body(where, *refs):
        outs = refs[1 if joined else size :][: len(widths)]
        kept = refs[0] if joined else refs[-1]
        if not joined:
            for j in range(size):
                kept[j] = refs[j][...]
        for index in range(size):
            values = kept[where[index]].astype(f32)
            for out, first, stride, at, piece in moves:
                start = first + index * stride
                piece = min(piece, widths[out] - start)
                if piece > 0:
                    outs[out][:, start : start + piece] = values[:, at : at + piece]

    if joined:
        ins = [(parts, pl.BlockSpec((size, block, width), lambda i, where: (0, i, 0)))]
    else:
        ins = [(part, pl.BlockSpec((block, width), lambda i, where: (i, 0))) for part in parts]
    return block_call(
        body,
        where,
        count // block,
        ins,
        [
            (leaf((count, wide), f32), pl.BlockSpec((block, wide), lambda i, where: (i, 0)))
            for wide in widths
        ],
        [] if joined else [pltpu.VMEM((size, block, width), bf16)],
        name,
    )


def unpack_rows(parts, where, piece, width, turned, name):
    joined = not isinstance(parts, list)
    size = len(parts)
    count = parts[0].shape[0]
    lanes = 256

    def body(where, *refs):
        out = refs[1 if joined else size]
        kept = refs[0] if joined else refs[-1]
        if not joined:
            for j in range(size):
                kept[j] = refs[j][...]
        for index in range(size):
            values = kept[where[index]].astype(f32)
            put = slice(index * piece, (index + 1) * piece)
            if turned:
                out[:, put] = values.T[:, :piece]
            else:
                out[put, :] = values[:piece]

    shape = (width, size * piece) if turned else (size * piece, width)
    out_block = (lanes, size * piece) if turned else (size * piece, lanes)
    spot = (lambda i, where: (i, 0)) if turned else (lambda i, where: (0, i))
    if joined:
        ins = [(parts, pl.BlockSpec((size, count, lanes), lambda i, where: (0, 0, i)))]
    else:
        ins = [(part, pl.BlockSpec((count, lanes), lambda i, where: (0, i))) for part in parts]
    return block_call(
        body,
        where,
        -(-width // lanes),
        ins,
        [(leaf(shape, f32), pl.BlockSpec(out_block, spot))],
        [] if joined else [pltpu.VMEM((size, count, lanes), bf16)],
        name,
    )[0]


def inverse_rms(values):
    return lax.rsqrt(jnp.mean(values * values, axis=-1, keepdims=True) + EPS)


def norm_backward(values, norm, gain, grad):
    scaled = grad * gain
    centre = norm**3 * jnp.mean(values * scaled, axis=-1, keepdims=True)
    return norm * scaled - values * centre


def split_low(values):
    high = lax.reduce_precision(values, 8, 7)
    return [high.astype(bf16), (values - high).astype(bf16)]


def on_device(
    tokens, cotangent, deal_table, norm_gain, query_weight, key_weight, value_weight, attention_out,
    attention_gain, mixer_in, filter_kernel, filter_bias, select_weight, step_weight, step_bias, decay_log,
    skip_gain, mixer_gain, mixer_out, post_gain, gate_weight, up_weight, down_weight,
):
    n = lax.axis_size("ctx")
    m = lax.axis_size("fsdp")
    c = lax.axis_index("ctx")
    z = lax.axis_index("fsdp")
    own = tokens.shape[1]
    block = own // 2
    total_rows = own * n
    count = 2 * n
    width = tokens.shape[2]
    shard = width // m
    heads = -(-HEADS // n)
    heads += heads % 2
    head_width = heads * HEAD_DIM
    shard_channels = filter_bias.shape[0]
    piece = shard_channels // n
    channels = m * piece
    inner_all = shard_channels * m
    shard_hidden = down_weight.shape[0]
    hidden_piece = shard_hidden // n
    piece_rows, hidden_rows = up_to(piece, 16), up_to(hidden_piece, 16)
    held, hidden_held = m * piece_rows, m * hidden_rows
    wide = up_to(held + 1, 128)
    sent_width = width + SIDE
    out_piece = width // n
    out_wide = up_to(out_piece, 128)

    def gather_z(values, tiled=True):
        return lax.all_gather(values, "fsdp", axis=0, tiled=tiled)

    def columns(values, start, size):
        return lax.dynamic_slice_in_dim(values, start, size, axis=1)

    in_groups = [
        (0, p * inner_all + f * shard_channels, p * held + f * piece_rows)
        for p in range(2)
        for f in range(m)
    ]
    in_local = pack_columns([mixer_in], c.reshape(1), in_groups, 2 * held, piece, "pack_mixer")
    in_weight = gather_z(in_local)
    upstream = cotangent[0]
    upstream_parts = swaps(after(upstream, in_local), n)

    def turn_z(values):
        turned = [
            lax.ppermute(values, "fsdp", [(i, (i + k) % m) for i in range(m)])
            for k in range(m - 1, 0, -1)
        ] + [values]
        return lax.dynamic_slice_in_dim(jnp.stack(turned + turned), m - 1 - z, m, axis=0)

    first_gain = turn_z(norm_gain).reshape(1, width).astype(f32)
    token_parts = swaps(after(tokens[0], upstream_parts[1], first_gain), n)
    own_index = after(c.reshape(1), upstream_parts[1])
    c = own_index[0]
    small_rows = jnp.concatenate(
        [
            select_weight,
            step_weight.T,
            decay_log,
            filter_kernel.T,
            filter_bias[:, None],
            step_bias[:, None],
            skip_gain[:, None],
            mixer_gain[:, None],
        ],
        axis=1,
    )
    small_width = small_rows.shape[1]
    small_rows = lax.dynamic_slice_in_dim(small_rows, c * piece, piece, axis=0)
    gains = jnp.stack([norm_gain, attention_gain, post_gain]).reshape(-1)
    gain_rows = -(-3 * shard // small_width)
    gains = pad_to(gains, 0, gain_rows * small_width).reshape(gain_rows, small_width)
    small_local = jnp.concatenate([small_rows, gains])
    small_all = turn_z(small_local)
    small = pad_to(small_all[:, :piece], 1, piece_rows).reshape(held, small_width)
    gains_all = small_all[:, piece:].reshape(m, gain_rows * small_width)[:, : 3 * shard]
    gains_all = jnp.moveaxis(gains_all.reshape(m, 3, shard), 0, 1).reshape(3, width).astype(f32)
    attend_gain, after_gain = gains_all[1:2], gains_all[2:3]

    def first_group(index):
        return jnp.minimum(index * heads // GROUP, KV_HEADS - 1)

    group_at = first_group(c)
    kv_pad = (KV_HEADS + 1) * HEAD_DIM
    pair = 2 * HEAD_DIM
    attend_local = join(
        [
            columns(pad_to(query_weight, 1, n * head_width), c * head_width, head_width),
            columns(pad_to(key_weight, 1, kv_pad), group_at * HEAD_DIM, pair),
            columns(pad_to(value_weight, 1, kv_pad), group_at * HEAD_DIM, pair),
        ],
        own_index,
        1,
        "pack_attention",
        [in_local],
    )
    head_ids = c * heads + jnp.arange(heads, dtype=jnp.int32)
    valid = (head_ids < HEADS).astype(jnp.int32)
    upper = jnp.minimum(head_ids // GROUP, KV_HEADS - 1) > group_at

    def row_slice(weight, size):
        cut = lax.dynamic_slice_in_dim(weight, c * size, size, axis=0)
        return pad_to(cut, 0, up_to(size, 16))

    out_cut = columns(attention_out, c * out_piece, out_piece).reshape(-1)
    out_rows = up_to(-(-out_cut.shape[0] // width), 16)
    rows_local = join(
        [
            row_slice(mixer_out, piece),
            pad_to(out_cut, 0, out_rows * width).reshape(out_rows, width),
        ],
        own_index,
        0,
        "pack_rows",
        [in_local],
    )
    pair_groups = [
        (k, f * shard_hidden, k * hidden_held + f * hidden_rows) for k in range(2) for f in range(m)
    ]
    pair_local = pack_columns(
        [gate_weight, up_weight],
        own_index,
        pair_groups,
        2 * hidden_held,
        hidden_piece,
        "pack_pair",
        [in_local, token_parts[1]],
    )

    down_local = row_slice(down_weight, hidden_piece)
    rows_all = gather_z(rows_local, tiled=False)

    inputs = tokens[0].astype(f32)
    first_norm = inverse_rms(inputs)
    hidden = block_call(
        norm_body,
        own_index,
        1,
        [(first_gain, whole(first_gain.shape))]
        + [(item, whole(item.shape)) for item in token_parts],
        [(leaf((total_rows, width), bf16), whole((total_rows, width)))],
        [],
        "norm_tokens",
        [attend_local, rows_local, pair_local, upstream_parts[-1]],
    )[0]

    projected = dot(hidden, in_weight)
    attend_all = gather_z(after(attend_local, projected))

    def extended(weight, rows_now, at):
        weight = jnp.pad(weight, ((0, rows_now - weight.shape[0]), (0, SIDE)))
        spot = (jnp.arange(rows_now) == at)[:, None] & (jnp.arange(sent_width) == width)[None, :]
        return jnp.where(spot, jnp.ones((), bf16), weight)

    lane_dim = jnp.arange(head_width, dtype=jnp.int32) % HEAD_DIM
    target = jnp.where(jnp.repeat(upper, HEAD_DIM), HEAD_DIM, 0) + lane_dim
    target = jnp.concatenate([target, target + pair])
    side_now = jnp.arange(2 * head_width, dtype=jnp.int32) // head_width
    spread = (target[None, :] == jnp.arange(2 * pair, dtype=jnp.int32)[:, None]) & (
        side_now[None, :] == (jnp.arange(2 * pair, dtype=jnp.int32) // pair)[:, None]
    )
    spread = spread.astype(bf16)

    others = c ^ jnp.array(masks(n), dtype=jnp.int32)
    firsts = deal_table[others]
    places = jnp.stack([firsts, count - 1 - firsts], axis=1).reshape(count)
    ids = jnp.arange(count, dtype=jnp.int32)
    order = jnp.sum(jnp.where(places[None, :] == ids[:, None], ids[None, :], 0), axis=1)
    position = (places[:, None] * block + jnp.arange(block, dtype=jnp.int32)[None, :]).reshape(-1)

    small_t = pad_to(small.astype(f32).T, 1, wide)
    select_own = pad_to(
        jnp.concatenate(
            [
                pad_to(small[:, :RANK], 1, 128),
                pad_to(small[:, RANK : RANK + 2 * NS], 1, 128),
            ],
            axis=1,
        ),
        0,
        wide,
    )
    step_own = pad_to(small_t[RANK + 2 * NS : 2 * RANK + 2 * NS], 0, 128).astype(bf16)
    at = 2 * RANK + 2 * NS
    decay_own = -jnp.exp(small_t[at : at + NS])
    at += NS
    vecs = jnp.concatenate([small_t[at + CONV + 1 : at + CONV + 4], small_t[at + CONV : at + CONV + 1], small_t[at : at + CONV]])

    def halves(values):
        return values[: total_rows // 2], values[total_rows // 2 :]

    upstream_all = assemble(upstream_parts)

    forward = lambda i: i
    reverse = lambda i: count - 1 - i
    start_spec = lambda pick: pl.BlockSpec((1, NS, wide), lambda i, order: (order[pick(i)], 0, 0))
    mixed_in, selected_part = block_call(
        filter_forward_body(block),
        order,
        count,
        [
            (projected, rows(block, 2 * held, forward)),
            (vecs, whole(vecs.shape)),
            (select_own, whole(select_own.shape)),
        ],
        [
            (leaf((total_rows, wide), bf16), rows(block, wide, forward)),
            (leaf((total_rows, 256), bf16), rows(block, 256, forward)),
        ],
        [pltpu.VMEM((block + 8, wide), f32)],
        "filter_forward",
    )
    selected_own = scatter_ctx(*halves(selected_part), n, own_index)
    selected = gather_ctx(selected_own, n)
    scanned, starts, mixer_scaled = block_call(
        scan_forward_body(block),
        order,
        count,
        [
            (selected, rows(block, 256, forward)),
            (mixed_in, rows(block, wide, forward)),
            (projected, rows(block, 2 * held, forward)),
            (step_own, whole(step_own.shape)),
            (vecs, whole(vecs.shape)),
            (decay_own, whole(decay_own.shape)),
        ],
        [
            (leaf((total_rows, wide), f32), rows(block, wide, forward)),
            (leaf((count, NS, wide), f32), start_spec(forward)),
            (leaf((total_rows, wide), bf16), rows(block, wide, forward)),
        ],
        [
            pltpu.VMEM((NS, wide), f32),
            pltpu.VMEM((block, wide), f32),
            pltpu.VMEM((block, wide), f32),
            pltpu.VMEM((block, wide), f32),
            pltpu.VMEM((block // STEP, 2 * NS, STEP), f32),
        ],
        "scan_forward",
    )
    pair_weight = gather_z(after(pair_local, scanned))
    attend_all = after(attend_all, scanned)
    heads_in = dot(hidden, attend_all).astype(bf16)
    pair_in = dot(heads_in[:, head_width:], spread).astype(bf16)
    mixer_out_own = extended(rows_all[:, :piece_rows].reshape(held, width), wide, held)
    down_own = gather_z(after(down_local, selected_own))
    out_columns = rows_all[:, piece_rows : piece_rows + out_rows].reshape(m, -1)
    out_columns = out_columns[:, : shard * out_piece]
    out_columns = out_columns.reshape(width, out_piece)
    out_own = lax.all_to_all(
        pad_to(out_columns, 0, n * head_width).reshape(n, head_width, out_piece), "ctx", 0, 0
    )
    out_own = jnp.moveaxis(out_own, 0, 1).reshape(head_width, width)
    out_own = extended(out_own, head_width + 128, head_width)

    query_block = min(256, total_rows)
    query_count = total_rows // query_block
    query_pos = position[:, None]
    key_pos = position[None, :]
    own_gain = lax.dynamic_slice_in_dim(
        pad_to(attend_gain, 1, n * head_width), c * head_width, head_width, axis=1
    )

    def part(index):
        return pl.BlockSpec((total_rows, head_width), lambda i, order: (0, index))

    def tall(size):
        return pl.BlockSpec((query_block, size), lambda i, order: (i, 0))

    attend_ins = [
        (heads_in, tall(head_width)),
        (pair_in, part(0)),
        (pair_in, part(1)),
        (query_pos, tall(1)),
        (key_pos, whole(key_pos.shape)),
        (own_gain, whole(own_gain.shape)),
    ]
    attended, attended_scaled = block_call(
        attention_forward_body,
        valid,
        query_count,
        attend_ins,
        [
            (leaf((total_rows, head_width), f32), tall(head_width)),
            (leaf((total_rows, head_width + 128), bf16), tall(head_width + 128)),
        ],
        [],
        "attention_forward",
    )


    def branch_out(scaled, weight):
        far = dot(scaled[total_rows // 2 :], weight).astype(bf16)
        near = dot(scaled[: total_rows // 2], weight).astype(bf16)
        return scatter_ctx(near, far, n, own_index)

    attend_sum = branch_out(attended_scaled, out_own)

    mixer_sum = branch_out(mixer_scaled, mixer_out_own)

    def normed_sum(total, size):
        return total[:, :width] * lax.rsqrt(total[:, width : width + 1] / size + EPS)

    mixed = inputs + 0.5 * (
        normed_sum(attend_sum, HEADS * HEAD_DIM) + normed_sum(mixer_sum, inner_all)
    )
    post_norm = inverse_rms(mixed)
    dunit = product_rows([(upstream_all, down_own)], 0, total_rows, f32, "units_backward")
    post = assemble(swaps((mixed * post_norm * after_gain).astype(bf16), n), dunit)
    both = dot(post, pair_weight)

    def strip(size):
        return pl.BlockSpec((own, size), lambda i: (i, 0))

    unit, dboth = pl.pallas_call(
        unit_body,
        grid=(n,),
        in_specs=[strip(2 * hidden_held), strip(hidden_held)],
        out_specs=[strip(hidden_held), strip(2 * hidden_held)],
        out_shape=[
            leaf((total_rows, hidden_held), bf16),
            leaf((total_rows, 2 * hidden_held), bf16),
        ],
        compiler_params=pltpu.CompilerParams(vmem_limit_bytes=VMEM),
        name="hidden_units",
    )(both, dunit)

    pair_part = dot_tn(post, dboth).astype(bf16)
    dpost_parts = scatter_parts(
        *split_rows([(dboth, pair_weight)], "post_backward", [pair_part]), n, own_index
    )
    half = n // 2
    strips = [(own, width)] * (half + 5)
    strips[half + 1] = (1, width)
    strips[half + 3] = strips[half + 4] = (own, sent_width)
    payload, dmixed, post_gain_part = block_call(
        branch_grad_body(half, inner_all),
        own_index,
        1,
        [
            (value, whole(shape))
            for value, shape in zip(
                dpost_parts + [mixed, after_gain, upstream, attend_sum, mixer_sum], strips
            )
        ],
        [
            (leaf((own, sent_width), bf16), whole((own, sent_width))),
            (leaf((own, width), f32), whole((own, width))),
            (leaf((8, width), f32), whole((8, width))),
        ],
        [],
        "branch_gradient",
    )
    post_gain_part = post_gain_part[0]

    def scatter_z(values):
        return lax.psum_scatter(values, "fsdp", scatter_dimension=0, tiled=True)

    payload_parts = swaps(payload, n)
    unit = after(unit, payload)
    down_part = dot_tn(unit, upstream_all).astype(bf16)
    pair_grad = scatter_z(pair_part)
    down_grad = scatter_z(down_part)
    payload = assemble(payload_parts)
    ffn_sums = scatter_parts(*split_columns(unit, down_own, "unit_out", [payload]), n, own_index)
    dattend_in = product_rows(
        [(payload, out_own)],
        0,
        total_rows,
        f32,
        "attended_backward",
        [down_part],
    )
    dmixer_in = product_rows(
        [(payload, mixer_out_own)], 0, total_rows, f32, "gated_backward", [dattend_in]
    )

    dquery, dpair, normed_a, attend_gain_part = block_call(
        attention_backward_body,
        valid,
        query_count,
        attend_ins
        + [
            (attended, tall(head_width)),
            (dattend_in, tall(head_width + 128)),
            (payload, pl.BlockSpec((query_block, 128), lambda i, order: (i, width // 128))),
        ],
        [
            (leaf((total_rows, head_width), bf16), tall(head_width)),
            (leaf((total_rows, 2 * head_width), bf16), whole((total_rows, 2 * head_width))),
            (leaf((total_rows, head_width), bf16), tall(head_width)),
            (leaf((8, head_width), f32), whole((8, head_width))),
        ],
        [
            pltpu.VMEM((total_rows, head_width), f32),
            pltpu.VMEM((total_rows, head_width), f32),
        ],
        "attention_backward",
    )
    pair_grad = after(pair_grad, dpair)

    def gather_rows(values):
        return lax.all_gather(values, "ctx", axis=0, tiled=False)

    pair_all = gather_rows(pair_grad)
    down_all = gather_rows(after(down_grad, dpair))
    dheads = jnp.concatenate([dquery, dot_nt(dpair, spread).astype(bf16)], axis=1)

    normed_s, dgate_z, dmixed_in, dselected_part, scan_vecs, step_part, decay_part = block_call(
        scan_backward_body(block),
        order,
        count,
        [
            (selected, rows(block, 256, reverse)),
            (mixed_in, rows(block, wide, reverse)),
            (projected, rows(block, 2 * held, reverse)),
            (scanned, rows(block, wide, reverse)),
            (dmixer_in, rows(block, wide, reverse)),
            (payload, columns_at(block, 128, reverse, width // 128)),
            (starts, start_spec(reverse)),
            (step_own, whole(step_own.shape)),
            (vecs, whole(vecs.shape)),
            (decay_own, whole(decay_own.shape)),
        ],
        [
            (leaf((total_rows, held), bf16), rows(block, held, reverse)),
            (leaf((total_rows, held), bf16), rows(block, held, reverse)),
            (leaf((total_rows, wide), f32), rows(block, wide, reverse)),
            (leaf((total_rows, 256), bf16), rows(block, 256, reverse)),
            (leaf((8, wide), f32), whole((8, wide))),
            (leaf((128, wide), f32), whole((128, wide))),
            (leaf((NS, wide), f32), whole((NS, wide))),
        ],
        [
            pltpu.VMEM((block // STEP, 2 * NS, STEP), f32),
            pltpu.VMEM((block, wide), f32),
            pltpu.VMEM((NS, wide), f32),
            pltpu.VMEM((block, wide), f32),
            pltpu.VMEM((block, wide), f32),
            pltpu.VMEM((block, wide), f32),
            pltpu.VMEM((block, wide), f32),
            pltpu.VMEM((block, wide), f32),
            pltpu.VMEM((block + 1, NS, wide), f32),
            pltpu.VMEM((block, NS, wide), f32),
            pltpu.VMEM((block * NS, 128), f32),
            pltpu.VMEM((block * NS, 128), f32),
        ],
        "scan_backward",
        [dpair, pair_grad],
    )
    dselected_part = after(dselected_part, pair_all)
    dselected_parts = scatter_parts(*halves(dselected_part), n, own_index)
    dselected = dselected_parts[0]
    for item in dselected_parts[1:]:
        dselected = dselected + item.astype(f32)
    dselected = gather_ctx(dselected.astype(bf16), n)
    hidden = after(hidden, dselected_parts[0])
    payload = after(payload, dselected_parts[0], down_all)
    mixer_part = dot_tn(normed_s, payload).astype(bf16)
    mixer_out_grad = scatter_z(mixer_part)


    out_part = dot_tn(after(normed_a, mixer_part), payload)[:, :width].astype(bf16)
    out_part = lax.all_to_all(
        jnp.moveaxis(out_part.reshape(head_width, n, out_piece), 1, 0), "ctx", 0, 0
    )
    out_part = out_part.reshape(n * head_width, out_piece)[:width]
    attend_part = jnp.concatenate(
        [dot_tn(hidden, dheads).astype(bf16), pad_to(out_part, 1, out_wide)], axis=1
    )
    attend_grad = scatter_z(attend_part)

    dprojected, select_part, filter_vecs = block_call(
        filter_backward_body(block, count),
        order,
        count,
        [
            (projected, rows(block, 2 * held, reverse)),
            (projected, rows(block, 2 * held, lambda i: jnp.maximum(count - 2 - i, 0))),
            (dgate_z, rows(block, held, reverse)),
            (mixed_in, rows(block, wide, reverse)),
            (dmixed_in, rows(block, wide, reverse)),
            (dselected, rows(block, 256, reverse)),
            (select_own, whole(select_own.shape)),
            (vecs, whole(vecs.shape)),
        ],
        [
            (leaf((total_rows, 2 * held), bf16), rows(block, 2 * held, reverse)),
            (leaf((256, wide), f32), whole((256, wide))),
            (leaf((8, wide), f32), whole((8, wide))),
        ],
        [
            pltpu.VMEM((block + 8, wide), f32),
            pltpu.VMEM((block + 8, wide), f32),
            pltpu.VMEM((block, 2 * held), f32),
        ],
        "filter_backward",
        [attend_part, ffn_sums[0]],
    )
    in_part = dot_tn(hidden, dprojected).astype(bf16)
    in_grad = scatter_z(in_part)
    hidden_near, hidden_far = split_rows(
        [(dprojected, in_weight), (dheads, attend_all)], "hidden_backward", [in_part]
    )
    half_rows = total_rows // 2
    first_gain_part = (
        jnp.sum(hidden_near.astype(f32) * hidden[:half_rows].astype(f32), axis=0)
        + jnp.sum(hidden_far.astype(f32) * hidden[half_rows:].astype(f32), axis=0)
    ) / first_gain[0]
    small_grad = jnp.concatenate(
        [
            select_part[:RANK],
            select_part[128 : 128 + 2 * NS],
            step_part[:RANK],
            decay_part,
            filter_vecs[4 : 4 + CONV],
            filter_vecs[3:4],
            scan_vecs[0:3],
        ]
    )[:, :held]
    attend_gain_full = lax.dynamic_update_slice_in_dim(
        jnp.zeros((1, n * head_width), f32), attend_gain_part[0:1], c * head_width, axis=1
    )[0, :width]
    gain_part = jnp.stack([first_gain_part, attend_gain_full, post_gain_part]).reshape(3, m, shard)
    gain_part = pad_to(
        jnp.moveaxis(gain_part, 1, 0).reshape(m, 3 * shard), 1, gain_rows * small_width
    )
    small_part = jnp.concatenate(
        [
            small_grad.T.reshape(m, piece_rows, small_width)[:, :piece],
            gain_part.reshape(m, gain_rows, small_width),
        ],
        axis=1,
    )
    small_grads = scatter_z(small_part.reshape(-1, small_width))
    dhidden = scatter_ctx(
        after(hidden_near, small_part), hidden_far, n, own_index
    )
    dfirst = norm_backward(inputs, first_norm, first_gain, dhidden)
    tokens_grad = (dmixed + dfirst).astype(bf16)[None]
    layer_out = mixed
    for item in ffn_sums:
        layer_out = layer_out + item.astype(f32)
    layer_out = layer_out.astype(bf16)[None]

    spots = jnp.array([masks(n).index(mask) for mask in range(n)], dtype=jnp.int32)
    plain = jnp.arange(n, dtype=jnp.int32)
    where = spots[c ^ plain]
    gate_grad, up_grad = unpack_columns(
        pair_all,
        plain,
        [
            (k, f * shard_hidden, hidden_piece, k * hidden_held + f * hidden_rows, hidden_piece)
            for k in range(2)
            for f in range(m)
        ],
        [weight.shape[1] for weight in (gate_weight, up_weight)],
        "unpack_pair",
    )
    down_turned = unpack_rows(
        down_all, plain, hidden_piece, width, True, "unpack_down"
    )
    mixer_out_grad = unpack_rows(
        swaps(mixer_out_grad, n), where, piece, width, False, "unpack_mixer"
    )
    attend_grad = swaps(attend_grad, n)
    kv_wide = n * pair
    out_at = head_width + 2 * pair
    query_grad, key_parts, value_parts, out_grad = unpack_columns(
        attend_grad,
        where,
        [
            (0, 0, head_width, 0, head_width),
            (1, 0, pair, head_width, pair),
            (2, 0, pair, head_width + pair, pair),
            (3, 0, out_piece, out_at, out_piece),
        ],
        [width, kv_wide, kv_wide, width],
        "unpack_attention",
    )

    def group_sum(parts):
        total = jnp.zeros((shard, kv_pad), f32)
        for index in range(n):
            low_at = min(index * heads // GROUP, KV_HEADS - 1) * HEAD_DIM
            item = parts[:, index * pair : (index + 1) * pair]
            total = total + jnp.pad(item, ((0, 0), (low_at, kv_pad - pair - low_at)))
        return total[:, : KV_HEADS * HEAD_DIM]

    in_grad = after(in_grad, gate_grad, down_turned)
    small_grads = jnp.stack(swaps(small_grads, n))[where]
    in_grad = swaps(in_grad, n)
    (mixer_in_grad,) = unpack_columns(
        in_grad,
        where,
        [
            (0, p * inner_all + f * shard_channels, piece, p * held + f * piece_rows, piece)
            for p in range(2)
            for f in range(m)
        ],
        [2 * inner_all],
        "unpack_inner",
    )
    small_sum = small_grads.reshape(n, piece + gain_rows, small_width)
    channel_grad = small_sum[:, :piece].reshape(shard_channels, small_width)
    gain_grad = jnp.sum(small_sum[:, piece:], axis=0).reshape(-1)[: 3 * shard].reshape(3, shard)

    at = RANK + 2 * NS
    select_grad = channel_grad[:, :at]
    step_grad = channel_grad[:, at : at + RANK].T
    at += RANK
    decay_grad = channel_grad[:, at : at + NS]
    at += NS
    kernel_grad = channel_grad[:, at : at + CONV].T
    at += CONV
    return (
        layer_out,
        tokens_grad,
        gain_grad[0],
        query_grad,
        group_sum(key_parts),
        group_sum(value_parts),
        out_grad,
        gain_grad[1],
        mixer_in_grad,
        kernel_grad,
        channel_grad[:, at],
        select_grad,
        step_grad,
        channel_grad[:, at + 1],
        decay_grad,
        channel_grad[:, at + 2],
        channel_grad[:, at + 3],
        mixer_out_grad,
        gain_grad[2],
        gate_grad,
        up_grad,
        down_turned.T,
    )


def solution(mesh):
    rows_spec = P("fsdp", None)
    lanes_spec = P(None, "fsdp")
    flat = P("fsdp")
    activations = P("fsdp", "ctx", None)
    weight_specs = (
        flat, rows_spec, rows_spec, rows_spec, rows_spec, flat, rows_spec, lanes_spec, flat, rows_spec,
        lanes_spec, flat, rows_spec, flat, flat, rows_spec, flat, rows_spec, rows_spec, rows_spec,
    )
    return jax.shard_map(
        on_device,
        mesh=mesh,
        in_specs=(activations, activations, P()) + weight_specs,
        out_specs=(activations, activations) + weight_specs,
        check_vma=False,
    )
```

```python
import math

import jax
import jax.numpy as jnp
from jax import lax
from jax.experimental import pallas as pl
from jax.experimental.pallas import tpu as pltpu
from jax.sharding import PartitionSpec as P

HEADS = 25
KV_HEADS = 5
HEAD_DIM = 64
GROUP = HEADS // KV_HEADS
CONV = 4
RANK = 100
NS = 16
EPS = 1e-05
NEG = -1e30
SCALE = 1.0 / math.sqrt(HEAD_DIM)
STEP = 16
VMEM = 56 * 1024 * 1024
SIDE = 64
SIDE_AT = HEADS * HEAD_DIM % 128
bf16 = jnp.bfloat16
f32 = jnp.float32


def up_to(value, unit):
    return -(-value // unit) * unit


def dot(left, right, contract=((1,), (0,)), precision=None):
    return lax.dot_general(
        left, right, (contract, ((), ())), preferred_element_type=f32, precision=precision
    )


def dot_tn(left, right):
    return dot(left, right, ((0,), (0,)))


def dot_nt(left, right):
    return dot(left, right, ((1,), (1,)))


def pad_to(values, axis, size):
    widths = [(0, 0)] * values.ndim
    widths[axis] = (0, size - values.shape[axis])
    return jnp.pad(values, widths)


def masks(size):
    return list(range(0, size, 2)) + list(range(1, size, 2))


def swap(values, mask, size):
    return lax.ppermute(values, "ctx", [(i, i ^ mask) for i in range(size)])


def swaps(values, size):
    near = [values] + [swap(values, m, size) for m in range(2, size, 2)]
    return near + [swap(item, 1, size) for item in near]


def assemble(parts, *earlier):
    count = len(parts)
    step = parts[0].shape[0]
    shape = (count * step,) + parts[0].shape[1:]

    def body(*refs):
        for j in range(count):
            refs[-1][j * step : (j + 1) * step] = refs[j][...]

    spec = pl.BlockSpec(parts[0].shape, lambda: (0,) * len(shape))
    return pl.pallas_call(
        body,
        in_specs=[spec] * count + [pl.BlockSpec(memory_space=pl.ANY)] * len(earlier),
        out_specs=pl.BlockSpec(shape, lambda: (0,) * len(shape)),
        out_shape=leaf(shape, parts[0].dtype),
        compiler_params=pltpu.CompilerParams(vmem_limit_bytes=VMEM),
        name="assemble",
    )(*parts, *earlier)


def gather_ctx(values, size):
    return assemble(swaps(values, size))


def product_rows(pairs, at, rows_now, dtype, name, earlier=()):
    count = pairs[0][1].shape[0]
    step = min(256, count)

    def body(*refs):
        total = dot_nt(refs[0][...], refs[1][...])
        for k in range(2, 2 * len(pairs), 2):
            total = total + dot_nt(refs[k][...], refs[k + 1][...])
        refs[-1][...] = total.astype(dtype)

    specs, values = [], []
    for left, right in pairs:
        depth = left.shape[1]
        specs.append(pl.BlockSpec((rows_now, depth), lambda i: (at, 0)))
        specs.append(pl.BlockSpec((step, depth), lambda i: (i, 0)))
        values += [left, right]
    return pl.pallas_call(
        body,
        grid=(-(-count // step),),
        in_specs=specs + [pl.BlockSpec(memory_space=pl.ANY)] * len(earlier),
        out_specs=pl.BlockSpec((rows_now, step), lambda i: (0, i)),
        out_shape=leaf((rows_now, count), dtype),
        compiler_params=pltpu.CompilerParams(vmem_limit_bytes=VMEM),
        name=name,
    )(*values, *earlier)


def product_columns(left, right, at, rows_now, name, earlier=()):
    depth, count = right.shape
    step = min(256, count)

    def body(*refs):
        refs[-1][...] = dot(refs[0][...], refs[1][...]).astype(bf16)

    return pl.pallas_call(
        body,
        grid=(-(-count // step),),
        in_specs=[
            pl.BlockSpec((rows_now, depth), lambda i: (at, 0)),
            pl.BlockSpec((depth, step), lambda i: (0, i)),
        ]
        + [pl.BlockSpec(memory_space=pl.ANY)] * len(earlier),
        out_specs=pl.BlockSpec((rows_now, step), lambda i: (0, i)),
        out_shape=leaf((rows_now, count), bf16),
        compiler_params=pltpu.CompilerParams(vmem_limit_bytes=VMEM),
        name=name,
    )(left, right, *earlier)


def split_columns(left, right, name, earlier=()):
    half = left.shape[0] // 2
    far = product_columns(left, right, 1, half, name, earlier)
    return product_columns(left, right, 0, half, name), far


def split_rows(pairs, name, earlier=()):
    half = pairs[0][0].shape[0] // 2
    far = product_rows(pairs, 1, half, bf16, name, earlier)
    return product_rows(pairs, 0, half, bf16, name), far


def fold_body(count, step):
    def body(index, near, got, own_o, *sent_o):
        for j in range(count):
            rows_now = slice(j * step, (j + 1) * step)
            total = near[rows_now, :].astype(f32) + got[rows_now, :].astype(f32)
            if j == 0:
                own_o[...] = total
            else:
                sent_o[j - 1][...] = total.astype(bf16)

    return body


def scatter_parts(near, far, size, index):
    half = size // 2
    step, width = near.shape[0] // half, near.shape[1]
    got = swap(far, 1, size)
    total, *sent = block_call(
        fold_body(half, step),
        index,
        1,
        [(near, whole(near.shape)), (got, whole(near.shape))],
        [(leaf((step, width), f32), whole((step, width)))]
        + [(leaf((step, width), bf16), whole((step, width)))] * (half - 1),
        [],
        "fold_halves",
    )
    return [total] + [swap(sent[k - 1], 2 * k, size) for k in range(1, half)]


def scatter_ctx(near, far, size, index):
    total, *others = scatter_parts(near, far, size, index)
    for item in others:
        total = total + item.astype(f32)
    return total


def block_call(body, order, count, ins, outs, scratch, name, earlier=()):
    given = len(ins)
    ins = list(ins) + [(value, pl.BlockSpec(memory_space=pl.ANY)) for value in earlier]

    def trimmed(*refs):
        return body(*refs[: 1 + given], *refs[1 + len(ins) :])

    return pl.pallas_call(
        trimmed,
        grid_spec=pltpu.PrefetchScalarGridSpec(
            num_scalar_prefetch=1,
            grid=(count,),
            in_specs=[spec for _, spec in ins],
            out_specs=[spec for _, spec in outs],
            scratch_shapes=scratch,
        ),
        out_shape=[shape for shape, _ in outs],
        compiler_params=pltpu.CompilerParams(
            dimension_semantics=("arbitrary",), vmem_limit_bytes=VMEM
        ),
        name=name,
    )(order, *[value for value, _ in ins])


def after(values, *earlier):
    def body(*refs):
        del refs

    spec = pl.BlockSpec(memory_space=pl.ANY)
    return pl.pallas_call(
        body,
        in_specs=[spec] * (1 + len(earlier)),
        out_specs=spec,
        out_shape=leaf(values.shape, values.dtype),
        input_output_aliases={0: 0},
        name="after",
    )(values, *earlier)


def whole(shape):
    zeros = (0,) * len(shape)
    return pl.BlockSpec(shape, lambda i, order: zeros)


def rows(block, width, pick):
    return pl.BlockSpec((block, width), lambda i, order: (order[pick(i)], 0))


def columns_at(block, width, pick, index):
    return pl.BlockSpec((block, width), lambda i, order: (order[pick(i)], index))


def leaf(shape, dtype):
    return jax.ShapeDtypeStruct(shape, dtype)


def filter_taps(ext, vecs, block):
    total = vecs[3:4, :]
    for j in range(CONV):
        total = total + vecs[4 + j : 5 + j, :] * ext[5 + j : 5 + j + block, :]
    return total


def place(order, index, block):
    return pl.ds(pl.multiple_of(order[index] * block, block), block)


def filter_forward_body(block, count):
    def body(order, projected, vecs, select, mixed_o, selected_o, ext):
        held = projected.shape[1] // 2
        ext[...] = jnp.zeros_like(ext)

        def step(index, carry):
            rows_now = place(order, index, block)
            ext[0:8, :] = ext[block : block + 8, :]
            ext[8 : block + 8, 0:held] = projected[rows_now, 0:held].astype(bf16).astype(f32)
            total = filter_taps(ext, vecs, block)
            mixed_o[rows_now, :] = (total * jax.nn.sigmoid(total)).astype(bf16)
            return carry

        lax.fori_loop(0, count, step, 0)
        selected_o[...] = dot(mixed_o[...], select[...]).astype(bf16)

    return body


def side_scalar(scalars, index):
    at = SIDE_AT + 2 * index
    values = scalars[...].astype(f32)
    return values[:, at : at + 1] + values[:, at + 1 : at + 2]


def turn_sides(selected, sides_s):
    turned = selected[:, 128:256].T
    for g in range(sides_s.shape[0]):
        sides_s[g] = turned[: 2 * NS, g * STEP : (g + 1) * STEP]


def rate_of(selected, step_weight, vecs):
    rank = selected[:, 0:128].astype(bf16)
    raw = dot(rank, step_weight[...]) + vecs[0:1, :]
    rate = jnp.maximum(raw, 0.0) + jnp.log1p(jnp.exp(-jnp.abs(raw)))
    return rank, raw, rate


def scan_forward_body(block):
    def body(
        order, selected, mixed, projected, step_weight, vecs, decay,
        scanned_o, starts_o, scaled_o, state_s, rate_s, drive_s, gate_s, sides_s,
    ):
        held = projected.shape[1] // 2

        @pl.when(pl.program_id(0) == 0)
        def _():
            state_s[...] = jnp.zeros_like(state_s)
            gate_s[...] = jnp.zeros_like(gate_s)

        gate_s[:, 0:held] = projected[...][:, held:]
        turn_sides(selected, sides_s)

        _, _, rate = rate_of(selected, step_weight, vecs)
        wide = mixed[...].astype(f32)
        rate_s[...] = rate
        drive_s[...] = rate * wide
        starts_o[0] = state_s[...]
        decay_mat = decay[...]

        def group(g, state):
            base = pl.multiple_of(g * STEP, STEP)
            rates = rate_s[pl.ds(base, STEP), :]
            drives = drive_s[pl.ds(base, STEP), :]
            side = sides_s[g]
            for j in range(STEP):
                state = (
                    jnp.exp(rates[j : j + 1, :] * decay_mat) * state
                    + drives[j : j + 1, :] * side[:NS, j : j + 1]
                )
                scanned_o[pl.ds(base + j, 1), :] = jnp.sum(
                    state * side[NS:, j : j + 1], axis=0, keepdims=True
                )
            return state

        state_s[...] = lax.fori_loop(0, block // STEP, group, state_s[...])
        gate = gate_s[...]
        gated = (scanned_o[...] + vecs[1:2, :] * wide) * (gate * jax.nn.sigmoid(gate))
        lane = lax.broadcasted_iota(jnp.int32, gated.shape, 1)
        squares = jnp.sum(gated * gated, axis=1, keepdims=True)
        scaled_o[...] = jnp.where(lane == held, squares, gated * vecs[2:3, :]).astype(bf16)

    return body


def collector(block, size):
    token = lax.broadcasted_iota(jnp.int32, (block, block * size), 0)
    spot = lax.broadcasted_iota(jnp.int32, (block, block * size), 1) // size
    return jnp.where(token == spot, 1.0, 0.0).astype(bf16)


def scan_backward_body(block):
    def body(
        order, selected, mixed, projected, scanned, grad_in, scalars, starts, step_weight, vecs, decay,
        normed_o, dgate_o, dmixed_o, dselected_o, vec_o, step_o, decay_o,
        sides_s, gate_s, lam_s, rate_s, drive_s, dscan_s, hist_s, factor_s, read_s, write_s, drate_s, pull_s,
    ):
        width = decay.shape[1]
        held = projected.shape[1] // 2

        @pl.when(pl.program_id(0) == 0)
        def _():
            gate_s[...] = jnp.zeros_like(gate_s)
            lam_s[...] = jnp.zeros_like(lam_s)
            vec_o[...] = jnp.zeros_like(vec_o)
            step_o[...] = jnp.zeros_like(step_o)
            decay_o[...] = jnp.zeros_like(decay_o)

        rank, raw, rate = rate_of(selected, step_weight, vecs)
        wide = mixed[...].astype(f32)
        rate_s[...] = rate
        drive_s[...] = rate * wide
        turn_sides(selected, sides_s)
        gate_s[:, 0:held] = projected[...][:, held:]
        gate = gate_s[...]
        sig = jax.nn.sigmoid(gate)
        act = gate * sig
        before = scanned[...] + vecs[1:2, :] * wide
        gated = before * act
        norm = side_scalar(scalars, 2)
        centre = side_scalar(scalars, 3)
        grad = grad_in[...]
        gated_norm = gated * norm
        normed_o[...] = (gated_norm * vecs[2:3, :])[:, 0:held].astype(bf16)
        dgated = norm * (vecs[2:3, :] * grad) - gated * centre
        dscan = dgated * act
        dscan_s[...] = dscan
        dgate = dgated * before * (sig * (1.0 + gate * (1.0 - sig)))
        dgate_o[...] = dgate[:, 0:held].astype(bf16)
        vec_o[1:2, :] += jnp.sum(dscan * wide, axis=0, keepdims=True)
        vec_o[2:3, :] += jnp.sum(grad * gated_norm, axis=0, keepdims=True)
        decay_mat = decay[...]

        def forward(g, state):
            base = pl.multiple_of(g * STEP, STEP)
            rates = rate_s[pl.ds(base, STEP), :]
            drives = drive_s[pl.ds(base, STEP), :]
            side = sides_s[g]
            for j in range(STEP):
                factor = jnp.exp(rates[j : j + 1, :] * decay_mat)
                factor_s[base + j] = factor
                state = factor * state + drives[j : j + 1, :] * side[:NS, j : j + 1]
                hist_s[base + j + 1] = state
            return state

        hist_s[0] = starts[0]
        lax.fori_loop(0, block // STEP, forward, starts[0])

        def fold(values):
            total = values[:, 0:128]
            for at in range(128, width, 128):
                total = total + values[:, at : at + 128]
            return total

        def backward(i, carry):
            lam_in, decay_sum = carry
            g = block // STEP - 1 - i
            base = pl.multiple_of(g * STEP, STEP)
            rates = rate_s[pl.ds(base, STEP), :]
            drives = drive_s[pl.ds(base, STEP), :]
            dscans = dscan_s[pl.ds(base, STEP), :]
            side = sides_s[g]
            later = None
            for j in range(STEP - 1, -1, -1):
                at = base + j
                row = dscans[j : j + 1, :]
                lam = lam_in + row * side[NS:, j : j + 1]
                put = pl.ds(pl.multiple_of(at * NS, NS), NS)
                read_s[put, :] = fold(hist_s[at + 1] * row).astype(bf16)
                write_s[put, :] = fold(lam * drives[j : j + 1, :]).astype(bf16)
                pull = lam * side[:NS, j : j + 1]
                lam_in = factor_s[at] * lam
                kept = lam_in * hist_s[at]
                decay_sum = decay_sum + rates[j : j + 1, :] * kept
                drate = decay_mat * kept
                sums = (pull[:8] + pull[8:], drate[:8] + drate[8:])
                if j % 2 == 1:
                    later = sums
                else:
                    put = pl.ds(pl.multiple_of(at * 8, 16), 16)
                    pull_s[put, :] = jnp.concatenate([sums[0], later[0]]).astype(bf16)
                    drate_s[put, :] = jnp.concatenate([sums[1], later[1]]).astype(bf16)
            return (lam_in, decay_sum)

        lam, decay_sum = lax.fori_loop(
            0, block // STEP, backward, (lam_s[...], jnp.zeros_like(lam_s))
        )
        lam_s[...] = lam
        decay_o[...] += decay_sum * decay_mat
        by_token = collector(block, 8)
        pulled = dot(by_token, pull_s[...])
        draw = (dot(by_token, drate_s[...]) + wide * pulled) * jax.nn.sigmoid(raw)
        vec_o[0:1, :] += jnp.sum(draw, axis=0, keepdims=True)
        low = draw.astype(bf16)
        dmixed_o[...] = vecs[1:2, :] * dscan + rate * pulled
        step_o[...] += dot_tn(rank, low)
        ones = jnp.ones((128, 128), bf16)
        row = lax.broadcasted_iota(jnp.int32, (block * NS, 128), 0) % NS
        lane = lax.broadcasted_iota(jnp.int32, (block * NS, 128), 1)
        summed = jnp.where(lane == row, dot(write_s[...], ones), 0.0)
        summed = summed + jnp.where(lane == row + NS, dot(read_s[...], ones), 0.0)
        dselected_o[:, 0:128] = dot_nt(low, step_weight[...]).astype(bf16)
        dselected_o[:, 128:256] = dot(collector(block, NS), summed.astype(bf16)).astype(
            bf16
        )

    return body


def filter_backward_body(block, count):
    def body(
        order, projected, dgate, mixed, dmixed, dselected, select, vecs,
        dprojected_o, select_o, vec_o, ext, ext_grad, both_s, added_s,
    ):
        held = projected.shape[1] // 2
        ext[...] = jnp.zeros_like(ext)
        ext_grad[block : block + 8, :] = jnp.zeros((8, ext.shape[1]), f32)
        vec_o[...] = jnp.zeros_like(vec_o)
        low = dselected[...]
        added_s[...] = dot_nt(low, select[...])
        select_o[...] = dot_tn(low, mixed[...])

        def step(i, carry):
            index = count - 1 - i
            rows_now = place(order, index, block)
            past = order[jnp.maximum(index - 1, 0)] * block + block - 16
            past = projected[pl.ds(pl.multiple_of(past, 16), 16), 0:held][8:16]
            first = jnp.where(index == 0, 0.0, 1.0)

            @pl.when(i > 0)
            def _():
                ext_grad[block : block + 8, :] = ext_grad[0:8, :]

            ext[0:8, 0:held] = past.astype(bf16).astype(f32) * first
            ext[8 : block + 8, 0:held] = projected[rows_now, 0:held].astype(bf16).astype(f32)
            total = filter_taps(ext, vecs, block)
            sig = jax.nn.sigmoid(total)
            dmix = dmixed[rows_now, :] + added_s[rows_now, :]
            dfilt = dmix * (sig * (1.0 + total * (1.0 - sig)))
            ext_grad[0:block, :] = dfilt
            dinner = jnp.zeros_like(dfilt)
            vec_o[3:4, :] += jnp.sum(dfilt, axis=0, keepdims=True)
            for j in range(CONV):
                at = CONV - 1 - j
                dinner = dinner + vecs[4 + j : 5 + j, :] * ext_grad[at : at + block, :]
                vec_o[4 + j : 5 + j, :] += jnp.sum(
                    dfilt * ext[5 + j : 5 + j + block, :], axis=0, keepdims=True
                )
            both_s[:, 0:held] = dinner[:, 0:held]
            both_s[:, held:] = dgate[rows_now, :].astype(f32)
            dprojected_o[rows_now, :] = both_s[...].astype(bf16)
            return carry

        lax.fori_loop(0, count, step, 0)

    return body


def half_mask(half):
    lane = lax.broadcasted_iota(jnp.int32, (1, 128), 1)
    return jnp.where((lane >= 64 * half) & (lane < 64 * half + 64), 1.0, 0.0)


def softmax_rows(query, key, allowed):
    scores = jnp.where(allowed, dot_nt(query, key), NEG)
    weights = jnp.exp(scores - jnp.max(scores, axis=-1, keepdims=True))
    return weights, 1.0 / jnp.sum(weights, axis=-1, keepdims=True)


def natural(order, source, target, block):
    for index in range(target.shape[0] // block):
        target[index * block : (index + 1) * block, :] = source[place(order, index, block), :]


def causal(rows_now, start, stop):
    return lax.broadcasted_iota(jnp.int32, (rows_now, stop), 1) <= (
        lax.broadcasted_iota(jnp.int32, (rows_now, stop), 0) + start
    )


def attention_forward_body(block, count):
    def body(marks, query, key, value, gain, out_o, scaled_o, query_s, key_s, value_s, out_s, scaled_s):
        total, width = key.shape
        step = min(256, total)
        natural(marks, query, query_s, block)
        natural(marks, key, key_s, block)
        natural(marks, value, value_s, block)
        for start in range(0, total, step):
            stop = start + step
            allowed = causal(step, start, stop)
            squares = jnp.zeros((step, 1), f32)
            for at in range(0, width, 128):
                lanes = slice(at, at + 128)
                tile = jnp.zeros((step, 128), f32)
                for half in range(2):
                    mask = half_mask(half)
                    part = query_s[start:stop, lanes] * (mask * SCALE).astype(bf16)
                    weights, inverse = softmax_rows(part, key_s[0:stop, lanes], allowed)
                    live = marks[count + at // 64 + half].astype(f32)
                    tile = tile + dot(weights.astype(bf16), value_s[0:stop, lanes]) * (
                        inverse * (mask * live)
                    )
                out_s[start:stop, lanes] = tile
                scaled_s[start:stop, lanes] = (tile * gain[:, lanes]).astype(bf16)
                squares = squares + jnp.sum(tile * tile, axis=1, keepdims=True)
            lane = lax.broadcasted_iota(jnp.int32, (step, 128), 1)
            scaled_s[start:stop, width:] = jnp.where(lane == 0, squares, 0.0).astype(bf16)
        for index in range(count):
            rows_now = slice(index * block, (index + 1) * block)
            out_o[place(marks, index, block), :] = out_s[rows_now, :]
            scaled_o[place(marks, index, block), :] = scaled_s[rows_now, :]

    return body


def unit_body(both, dunit, unit_o, dboth_o):
    held = dunit.shape[1]
    values = both[...]
    gate, up = values[:, :held], values[:, held:]
    grad = dunit[...]
    sig = jax.nn.sigmoid(gate)
    act = gate * sig
    unit_o[...] = (act * up).astype(bf16)
    dgate = grad * up * (sig * (1.0 + gate * (1.0 - sig)))
    dboth_o[...] = jnp.concatenate([dgate, grad * act], axis=1).astype(bf16)


def branch_grad_body(half, inner_all):
    def body(index, *refs):
        parts = refs[:half]
        mixed, gain, upstream, attend_sum, mixer_sum = refs[half : half + 5]
        payload_o, dmixed_o, gain_o = refs[half + 5 :]
        grad = parts[0][...]
        for item in parts[1:]:
            grad = grad + item[...].astype(f32)
        values = mixed[...]
        width = values.shape[1]
        norm = lax.rsqrt(jnp.mean(values * values, axis=1, keepdims=True) + EPS)
        scaled = grad * gain[...]
        centre = norm * norm * norm * jnp.mean(values * scaled, axis=1, keepdims=True)
        dmixed = upstream[...].astype(f32) + norm * scaled - values * centre
        dmixed_o[...] = dmixed
        total = jnp.sum(grad * values * norm, axis=0, keepdims=True)
        gain_o[...] = jnp.broadcast_to(total, gain_o.shape)
        low = (0.5 * dmixed).astype(bf16)
        payload_o[:, 0:width] = low
        wide_low = low.astype(f32)
        lane = lax.broadcasted_iota(jnp.int32, (values.shape[0], SIDE), 1)
        side = jnp.zeros((values.shape[0], SIDE), f32)
        at = 0
        for source, size in ((attend_sum, HEADS * HEAD_DIM), (mixer_sum, inner_all)):
            sums = source[...]
            factor = lax.rsqrt(sums[:, width : width + 1] / size + EPS)
            mean = jnp.sum(wide_low * sums[:, 0:width], axis=1, keepdims=True) / size
            for item in (factor, factor * factor * factor * mean):
                high = item.astype(bf16).astype(f32)
                side = jnp.where(lane == at, high, side)
                side = jnp.where(lane == at + 1, item - high, side)
                at += 2
        payload_o[:, width:] = side.astype(bf16)

    return body


def norm_body(index, gain, *refs):
    out = refs[-1]
    step = refs[0].shape[0]
    for j, ref in enumerate(refs[:-1]):
        values = ref[...].astype(f32)
        norm = lax.rsqrt(jnp.mean(values * values, axis=1, keepdims=True) + EPS)
        out[j * step : (j + 1) * step, :] = (values * norm * gain[...]).astype(bf16)


def attention_backward_body(block, count):
    def body(
        marks, query, key, value, gain, out, grad_in, scalars,
        dquery_o, dpair_o, normed_o, gain_o,
        query_s, key_s, value_s, dout_s, dout_n, dquery_s, dkey_s, dvalue_s,
    ):
        total, width = key.shape
        step = min(256, total)
        natural(marks, query, query_s, block)
        natural(marks, key, key_s, block)
        natural(marks, value, value_s, block)
        norm = side_scalar(scalars, 0)
        centre = side_scalar(scalars, 1)
        attended = out[...]
        grad = grad_in[:, 0:width]
        normed = attended * norm
        normed_o[...] = (normed * gain[...]).astype(bf16)
        gain_sum = jnp.sum(grad * normed, axis=0, keepdims=True)
        gain_o[...] = jnp.broadcast_to(gain_sum, gain_o.shape)
        dout_s[...] = (norm * (gain[...] * grad) - attended * centre).astype(bf16)
        natural(marks, dout_s, dout_n, block)
        dkey_s[...] = jnp.zeros_like(dkey_s)
        dvalue_s[...] = jnp.zeros_like(dvalue_s)
        for start in range(0, total, step):
            stop = start + step
            allowed = causal(step, start, stop)
            for at in range(0, width, 128):
                lanes = slice(at, at + 128)
                key_tile = key_s[0:stop, lanes]
                dquery = jnp.zeros((step, 128), f32)
                dkey = jnp.zeros((stop, 128), f32)
                dvalue = jnp.zeros((stop, 128), f32)
                for half in range(2):
                    mask = half_mask(half)
                    part = query_s[start:stop, lanes] * (mask * SCALE).astype(bf16)
                    dpart = dout_n[start:stop, lanes] * mask.astype(bf16)
                    weights, inverse = softmax_rows(part, key_tile, allowed)
                    probs = weights * inverse
                    dprobs = dot_nt(dpart, value_s[0:stop, lanes])
                    mean = jnp.sum(dprobs * probs, axis=-1, keepdims=True)
                    dscores = (probs * (dprobs - mean)).astype(bf16)
                    dvalue = dvalue + dot_tn(probs.astype(bf16), dpart)
                    dquery = dquery + dot(dscores, key_tile) * (mask * SCALE)
                    dkey = dkey + dot_tn(dscores, part)
                dquery_s[start:stop, lanes] = dquery.astype(bf16)
                dkey_s[0:stop, lanes] += dkey
                dvalue_s[0:stop, lanes] += dvalue
        for index in range(count):
            rows_now = slice(index * block, (index + 1) * block)
            spot = place(marks, index, block)
            dquery_o[spot, :] = dquery_s[rows_now, :]
            dpair_o[spot, 0:width] = dkey_s[rows_now, :].astype(bf16)
            dpair_o[spot, width:] = dvalue_s[rows_now, :].astype(bf16)

    return body


def pack_body(groups, width, piece):
    window = up_to(piece + 127, 128)

    def body(index, *refs):
        out_o, acc = refs[-2:]
        acc[...] = jnp.zeros_like(acc)
        for which, start, at in groups:
            weight = refs[which]
            source = start + index[0] * piece
            tile = jnp.minimum(source // 128, (width - window) // 128)
            base = pl.multiple_of(tile * 128, 128)
            low = at % 128
            span = up_to(low + piece, 128)
            row = lax.broadcasted_iota(jnp.int32, (window, span), 0)
            lane = lax.broadcasted_iota(jnp.int32, (window, span), 1) - low
            pick = (row - (source - base) == lane) & (lane >= 0) & (lane < piece)
            pick = jnp.where(pick, 1.0, 0.0).astype(bf16)
            acc[:, at - low : at - low + span] += dot(weight[:, pl.ds(base, window)], pick)
        out_o[...] = acc[:, : out_o.shape[1]].astype(bf16)

    return body


def row_block(count):
    return 80 if count % 80 == 0 else count


def join_body(axis):
    def body(index, *refs):
        at = 0
        for ref in refs[:-1]:
            size = ref.shape[axis]
            if axis == 0:
                refs[-1][at : at + size, :] = ref[...]
            else:
                refs[-1][:, at : at + size] = ref[...]
            at += size

    return body


def join(parts, index, axis, name, earlier):
    shape = list(parts[0].shape)
    shape[axis] = sum(part.shape[axis] for part in parts)
    return block_call(
        join_body(axis),
        index,
        1,
        [(part, whole(part.shape)) for part in parts],
        [(leaf(tuple(shape), bf16), whole(tuple(shape)))],
        [],
        name,
        earlier,
    )[0]


def pack_columns(weights, index, groups, out_wide, piece, name, earlier=()):
    count, width = weights[0].shape
    block = row_block(count)
    return block_call(
        pack_body(groups, width, piece),
        index,
        count // block,
        [(weight, pl.BlockSpec((block, width), lambda i, index: (i, 0))) for weight in weights],
        [
            (
                leaf((count, out_wide), bf16),
                pl.BlockSpec((block, out_wide), lambda i, index: (i, 0)),
            )
        ],
        [pltpu.VMEM((block, up_to(out_wide, 128)), f32)],
        name,
        earlier,
    )[0]


def unpack_columns(parts, where, moves, widths, name, count=None):
    joined = not isinstance(parts, list)
    size = len(parts)
    width = parts[0].shape[1]
    count = count or parts[0].shape[0]
    block = row_block(count)

    def body(where, *refs):
        outs = refs[1 if joined else size :][: len(widths)]
        kept = refs[0] if joined else refs[-1]
        if not joined:
            for j in range(size):
                kept[j] = refs[j][...]
        for index in range(size):
            values = kept[where[index]].astype(f32)
            for out, first, stride, at, piece in moves:
                start = first + index * stride
                piece = min(piece, widths[out] - start)
                if piece > 0:
                    outs[out][:, start : start + piece] = values[:, at : at + piece]

    if joined:
        ins = [(parts, pl.BlockSpec((size, block, width), lambda i, where: (0, i, 0)))]
    else:
        ins = [(part, pl.BlockSpec((block, width), lambda i, where: (i, 0))) for part in parts]
    return block_call(
        body,
        where,
        count // block,
        ins,
        [
            (leaf((count, wide), f32), pl.BlockSpec((block, wide), lambda i, where: (i, 0)))
            for wide in widths
        ],
        [] if joined else [pltpu.VMEM((size, block, width), bf16)],
        name,
    )


def unpack_rows(parts, where, piece, width, turned, name):
    joined = not isinstance(parts, list)
    size = len(parts)
    count = parts[0].shape[0]
    lanes = 256

    def body(where, *refs):
        out = refs[1 if joined else size]
        kept = refs[0] if joined else refs[-1]
        if not joined:
            for j in range(size):
                kept[j] = refs[j][...]
        for index in range(size):
            values = kept[where[index]].astype(f32)
            put = slice(index * piece, (index + 1) * piece)
            if turned:
                out[:, put] = values.T[:, :piece]
            else:
                out[put, :] = values[:piece]

    shape = (width, size * piece) if turned else (size * piece, width)
    out_block = (lanes, size * piece) if turned else (size * piece, lanes)
    spot = (lambda i, where: (i, 0)) if turned else (lambda i, where: (0, i))
    if joined:
        ins = [(parts, pl.BlockSpec((size, count, lanes), lambda i, where: (0, 0, i)))]
    else:
        ins = [(part, pl.BlockSpec((count, lanes), lambda i, where: (0, i))) for part in parts]
    return block_call(
        body,
        where,
        -(-width // lanes),
        ins,
        [(leaf(shape, f32), pl.BlockSpec(out_block, spot))],
        [] if joined else [pltpu.VMEM((size, count, lanes), bf16)],
        name,
    )[0]


def inverse_rms(values):
    return lax.rsqrt(jnp.mean(values * values, axis=-1, keepdims=True) + EPS)


def norm_backward(values, norm, gain, grad):
    scaled = grad * gain
    centre = norm**3 * jnp.mean(values * scaled, axis=-1, keepdims=True)
    return norm * scaled - values * centre


def split_low(values):
    high = lax.reduce_precision(values, 8, 7)
    return [high.astype(bf16), (values - high).astype(bf16)]


def on_device(
    tokens, cotangent, deal_table, norm_gain, query_weight, key_weight, value_weight, attention_out,
    attention_gain, mixer_in, filter_kernel, filter_bias, select_weight, step_weight, step_bias, decay_log,
    skip_gain, mixer_gain, mixer_out, post_gain, gate_weight, up_weight, down_weight,
):
    n = lax.axis_size("ctx")
    m = lax.axis_size("fsdp")
    c = lax.axis_index("ctx")
    z = lax.axis_index("fsdp")
    own = tokens.shape[1]
    block = own // 2
    total_rows = own * n
    count = 2 * n
    width = tokens.shape[2]
    shard = width // m
    heads = -(-HEADS // n)
    heads += heads % 2
    head_width = heads * HEAD_DIM
    shard_channels = filter_bias.shape[0]
    piece = shard_channels // n
    channels = m * piece
    inner_all = shard_channels * m
    shard_hidden = down_weight.shape[0]
    hidden_piece = shard_hidden // n
    piece_rows, hidden_rows = up_to(piece, 16), up_to(hidden_piece, 16)
    held, hidden_held = m * piece_rows, m * hidden_rows
    wide = up_to(held + 1, 128)
    sent_width = width + SIDE
    out_piece = width // n
    out_wide = up_to(out_piece, 128)

    def gather_z(values, tiled=True):
        return lax.all_gather(values, "fsdp", axis=0, tiled=tiled)

    def columns(values, start, size):
        return lax.dynamic_slice_in_dim(values, start, size, axis=1)

    in_groups = [
        (0, p * inner_all + f * shard_channels, p * held + f * piece_rows)
        for p in range(2)
        for f in range(m)
    ]
    in_local = pack_columns([mixer_in], c.reshape(1), in_groups, 2 * held, piece, "pack_mixer")
    in_weight = gather_z(in_local)
    upstream = cotangent[0]
    upstream_parts = swaps(after(upstream, in_local), n)

    def turn_z(values):
        turned = [
            lax.ppermute(values, "fsdp", [(i, (i + k) % m) for i in range(m)])
            for k in range(m - 1, 0, -1)
        ] + [values]
        return lax.dynamic_slice_in_dim(jnp.stack(turned + turned), m - 1 - z, m, axis=0)

    first_gain = turn_z(norm_gain).reshape(1, width).astype(f32)
    token_parts = swaps(after(tokens[0], upstream_parts[1], first_gain), n)
    own_index = after(c.reshape(1), upstream_parts[1])
    c = own_index[0]
    small_rows = jnp.concatenate(
        [
            select_weight,
            step_weight.T,
            decay_log,
            filter_kernel.T,
            filter_bias[:, None],
            step_bias[:, None],
            skip_gain[:, None],
            mixer_gain[:, None],
        ],
        axis=1,
    )
    small_width = small_rows.shape[1]
    small_rows = lax.dynamic_slice_in_dim(small_rows, c * piece, piece, axis=0)
    gains = jnp.stack([norm_gain, attention_gain, post_gain]).reshape(-1)
    gain_rows = -(-3 * shard // small_width)
    gains = pad_to(gains, 0, gain_rows * small_width).reshape(gain_rows, small_width)
    small_local = jnp.concatenate([small_rows, gains])
    small_all = turn_z(small_local)
    small = pad_to(small_all[:, :piece], 1, piece_rows).reshape(held, small_width)
    gains_all = small_all[:, piece:].reshape(m, gain_rows * small_width)[:, : 3 * shard]
    gains_all = jnp.moveaxis(gains_all.reshape(m, 3, shard), 0, 1).reshape(3, width).astype(f32)
    attend_gain, after_gain = gains_all[1:2], gains_all[2:3]

    def first_group(index):
        return jnp.minimum(index * heads // GROUP, KV_HEADS - 1)

    group_at = first_group(c)
    kv_pad = (KV_HEADS + 1) * HEAD_DIM
    pair = 2 * HEAD_DIM
    attend_local = join(
        [
            columns(pad_to(query_weight, 1, n * head_width), c * head_width, head_width),
            columns(pad_to(key_weight, 1, kv_pad), group_at * HEAD_DIM, pair),
            columns(pad_to(value_weight, 1, kv_pad), group_at * HEAD_DIM, pair),
        ],
        own_index,
        1,
        "pack_attention",
        [in_local],
    )
    head_ids = c * heads + jnp.arange(heads, dtype=jnp.int32)
    valid = (head_ids < HEADS).astype(jnp.int32)
    upper = jnp.minimum(head_ids // GROUP, KV_HEADS - 1) > group_at

    def row_slice(weight, size):
        cut = lax.dynamic_slice_in_dim(weight, c * size, size, axis=0)
        return pad_to(cut, 0, up_to(size, 16))

    out_cut = columns(attention_out, c * out_piece, out_piece).reshape(-1)
    out_rows = up_to(-(-out_cut.shape[0] // width), 16)
    rows_local = join(
        [
            row_slice(mixer_out, piece),
            pad_to(out_cut, 0, out_rows * width).reshape(out_rows, width),
        ],
        own_index,
        0,
        "pack_rows",
        [in_local],
    )
    pair_groups = [
        (k, f * shard_hidden, k * hidden_held + f * hidden_rows) for k in range(2) for f in range(m)
    ]
    pair_local = pack_columns(
        [gate_weight, up_weight],
        own_index,
        pair_groups,
        2 * hidden_held,
        hidden_piece,
        "pack_pair",
        [in_local, token_parts[1]],
    )

    down_local = row_slice(down_weight, hidden_piece)
    rows_all = gather_z(rows_local, tiled=False)

    inputs = tokens[0].astype(f32)
    first_norm = inverse_rms(inputs)
    hidden = block_call(
        norm_body,
        own_index,
        1,
        [(first_gain, whole(first_gain.shape))]
        + [(item, whole(item.shape)) for item in token_parts],
        [(leaf((total_rows, width), bf16), whole((total_rows, width)))],
        [],
        "norm_tokens",
        [attend_local, rows_local, upstream_parts[-1]],
    )[0]

    projected = dot(hidden, in_weight)
    attend_all = gather_z(after(attend_local, projected))

    def extended(weight, rows_now, at):
        weight = jnp.pad(weight, ((0, rows_now - weight.shape[0]), (0, SIDE)))
        spot = (jnp.arange(rows_now) == at)[:, None] & (jnp.arange(sent_width) == width)[None, :]
        return jnp.where(spot, jnp.ones((), bf16), weight)

    lane_dim = jnp.arange(head_width, dtype=jnp.int32) % HEAD_DIM
    target = jnp.where(jnp.repeat(upper, HEAD_DIM), HEAD_DIM, 0) + lane_dim
    target = jnp.concatenate([target, target + pair])
    side_now = jnp.arange(2 * head_width, dtype=jnp.int32) // head_width
    spread = (target[None, :] == jnp.arange(2 * pair, dtype=jnp.int32)[:, None]) & (
        side_now[None, :] == (jnp.arange(2 * pair, dtype=jnp.int32) // pair)[:, None]
    )
    spread = spread.astype(bf16)

    others = c ^ jnp.array(masks(n), dtype=jnp.int32)
    firsts = deal_table[others]
    places = jnp.stack([firsts, count - 1 - firsts], axis=1).reshape(count)
    ids = jnp.arange(count, dtype=jnp.int32)
    order = jnp.sum(jnp.where(places[None, :] == ids[:, None], ids[None, :], 0), axis=1)

    small_t = pad_to(small.astype(f32).T, 1, wide)
    select_own = pad_to(
        jnp.concatenate(
            [
                pad_to(small[:, :RANK], 1, 128),
                pad_to(small[:, RANK : RANK + 2 * NS], 1, 128),
            ],
            axis=1,
        ),
        0,
        wide,
    )
    step_own = pad_to(small_t[RANK + 2 * NS : 2 * RANK + 2 * NS], 0, 128).astype(bf16)
    at = 2 * RANK + 2 * NS
    decay_own = -jnp.exp(small_t[at : at + NS])
    at += NS
    vecs = jnp.concatenate([small_t[at + CONV + 1 : at + CONV + 4], small_t[at + CONV : at + CONV + 1], small_t[at : at + CONV]])

    def halves(values):
        return values[: total_rows // 2], values[total_rows // 2 :]

    upstream_all = assemble(upstream_parts)

    forward = lambda i: i
    reverse = lambda i: count - 1 - i
    start_spec = lambda pick: pl.BlockSpec((1, NS, wide), lambda i, order: (order[pick(i)], 0, 0))
    mixed_in, selected_part = block_call(
        filter_forward_body(block, count),
        order,
        1,
        [
            (projected, whole(projected.shape)),
            (vecs, whole(vecs.shape)),
            (select_own, whole(select_own.shape)),
        ],
        [
            (leaf((total_rows, wide), bf16), whole((total_rows, wide))),
            (leaf((total_rows, 256), bf16), whole((total_rows, 256))),
        ],
        [pltpu.VMEM((block + 8, wide), f32)],
        "filter_forward",
    )
    selected_own = scatter_ctx(*halves(selected_part), n, own_index)
    selected = gather_ctx(selected_own, n)
    scanned, starts, mixer_scaled = block_call(
        scan_forward_body(block),
        order,
        count,
        [
            (selected, rows(block, 256, forward)),
            (mixed_in, rows(block, wide, forward)),
            (projected, rows(block, 2 * held, forward)),
            (step_own, whole(step_own.shape)),
            (vecs, whole(vecs.shape)),
            (decay_own, whole(decay_own.shape)),
        ],
        [
            (leaf((total_rows, wide), f32), rows(block, wide, forward)),
            (leaf((count, NS, wide), f32), start_spec(forward)),
            (leaf((total_rows, wide), bf16), rows(block, wide, forward)),
        ],
        [
            pltpu.VMEM((NS, wide), f32),
            pltpu.VMEM((block, wide), f32),
            pltpu.VMEM((block, wide), f32),
            pltpu.VMEM((block, wide), f32),
            pltpu.VMEM((block // STEP, 2 * NS, STEP), f32),
        ],
        "scan_forward",
        [pair_local],
    )
    pair_weight = gather_z(after(pair_local, scanned))
    attend_all = after(attend_all, scanned)
    heads_in = dot(hidden, attend_all).astype(bf16)
    pair_in = dot(heads_in[:, head_width:], spread).astype(bf16)
    mixer_out_own = extended(rows_all[:, :piece_rows].reshape(held, width), wide, held)
    down_own = gather_z(after(down_local, selected_own))
    out_columns = rows_all[:, piece_rows : piece_rows + out_rows].reshape(m, -1)
    out_columns = out_columns[:, : shard * out_piece]
    out_columns = out_columns.reshape(width, out_piece)
    out_own = lax.all_to_all(
        pad_to(out_columns, 0, n * head_width).reshape(n, head_width, out_piece), "ctx", 0, 0
    )
    out_own = jnp.moveaxis(out_own, 0, 1).reshape(head_width, width)
    out_own = extended(out_own, head_width + 128, head_width)

    own_gain = lax.dynamic_slice_in_dim(
        pad_to(attend_gain, 1, n * head_width), c * head_width, head_width, axis=1
    )

    def full(size, index=0):
        return pl.BlockSpec((total_rows, size), lambda i, order: (0, index))

    marks = jnp.concatenate([order, valid])
    attend_ins = [
        (heads_in, full(head_width)),
        (pair_in, full(head_width, 0)),
        (pair_in, full(head_width, 1)),
        (own_gain, whole(own_gain.shape)),
    ]
    low_rows = pltpu.VMEM((total_rows, head_width), bf16)
    wide_rows = pltpu.VMEM((total_rows, head_width), f32)
    attended, attended_scaled = block_call(
        attention_forward_body(block, count),
        marks,
        1,
        attend_ins,
        [
            (leaf((total_rows, head_width), f32), full(head_width)),
            (leaf((total_rows, head_width + 128), bf16), full(head_width + 128)),
        ],
        [low_rows] * 3 + [wide_rows, pltpu.VMEM((total_rows, head_width + 128), bf16)],
        "attention_forward",
    )

    def branch_out(scaled, weight):
        far = dot(scaled[total_rows // 2 :], weight).astype(bf16)
        near = dot(scaled[: total_rows // 2], weight).astype(bf16)
        return scatter_ctx(near, far, n, own_index)

    attend_sum = branch_out(attended_scaled, out_own)

    mixer_sum = branch_out(mixer_scaled, mixer_out_own)

    def normed_sum(total, size):
        return total[:, :width] * lax.rsqrt(total[:, width : width + 1] / size + EPS)

    mixed = inputs + 0.5 * (
        normed_sum(attend_sum, HEADS * HEAD_DIM) + normed_sum(mixer_sum, inner_all)
    )
    post_norm = inverse_rms(mixed)
    dunit = product_rows([(upstream_all, down_own)], 0, total_rows, f32, "units_backward")
    post = assemble(swaps((mixed * post_norm * after_gain).astype(bf16), n), dunit)
    both = dot(post, pair_weight)

    def strip(size):
        return pl.BlockSpec((own, size), lambda i: (i, 0))

    unit, dboth = pl.pallas_call(
        unit_body,
        grid=(n,),
        in_specs=[strip(2 * hidden_held), strip(hidden_held)],
        out_specs=[strip(hidden_held), strip(2 * hidden_held)],
        out_shape=[
            leaf((total_rows, hidden_held), bf16),
            leaf((total_rows, 2 * hidden_held), bf16),
        ],
        compiler_params=pltpu.CompilerParams(vmem_limit_bytes=VMEM),
        name="hidden_units",
    )(both, dunit)

    pair_part = dot_tn(post, dboth).astype(bf16)
    dpost_parts = scatter_parts(
        *split_rows([(dboth, pair_weight)], "post_backward", [pair_part]), n, own_index
    )
    half = n // 2
    strips = [(own, width)] * (half + 5)
    strips[half + 1] = (1, width)
    strips[half + 3] = strips[half + 4] = (own, sent_width)
    payload, dmixed, post_gain_part = block_call(
        branch_grad_body(half, inner_all),
        own_index,
        1,
        [
            (value, whole(shape))
            for value, shape in zip(
                dpost_parts + [mixed, after_gain, upstream, attend_sum, mixer_sum], strips
            )
        ],
        [
            (leaf((own, sent_width), bf16), whole((own, sent_width))),
            (leaf((own, width), f32), whole((own, width))),
            (leaf((8, width), f32), whole((8, width))),
        ],
        [],
        "branch_gradient",
    )
    post_gain_part = post_gain_part[0]

    def scatter_z(values):
        return lax.psum_scatter(values, "fsdp", scatter_dimension=0, tiled=True)

    payload_parts = swaps(payload, n)
    unit = after(unit, payload)
    down_part = dot_tn(unit, upstream_all).astype(bf16)
    pair_grad = scatter_z(pair_part)
    down_grad = scatter_z(down_part)
    payload = assemble(payload_parts)
    ffn_sums = scatter_parts(*split_columns(unit, down_own, "unit_out", [payload]), n, own_index)
    dattend_in = product_rows(
        [(payload, out_own)],
        0,
        total_rows,
        f32,
        "attended_backward",
        [down_part],
    )
    dmixer_in = product_rows(
        [(payload, mixer_out_own)], 0, total_rows, f32, "gated_backward", [dattend_in]
    )

    dquery, dpair, normed_a, attend_gain_part = block_call(
        attention_backward_body(block, count),
        marks,
        1,
        attend_ins
        + [
            (attended, full(head_width)),
            (dattend_in, full(head_width + 128)),
            (payload, full(128, width // 128)),
        ],
        [
            (leaf((total_rows, head_width), bf16), full(head_width)),
            (leaf((total_rows, 2 * head_width), bf16), full(2 * head_width)),
            (leaf((total_rows, head_width), bf16), full(head_width)),
            (leaf((8, head_width), f32), whole((8, head_width))),
        ],
        [low_rows] * 6 + [wide_rows] * 2,
        "attention_backward",
    )
    pair_grad = after(pair_grad, dpair)

    def gather_rows(values):
        return lax.all_gather(values, "ctx", axis=0, tiled=False)

    pair_all = gather_rows(pair_grad)
    down_all = gather_rows(after(down_grad, dpair))
    dheads = jnp.concatenate([dquery, dot_nt(dpair, spread).astype(bf16)], axis=1)

    normed_s, dgate_z, dmixed_in, dselected_part, scan_vecs, step_part, decay_part = block_call(
        scan_backward_body(block),
        order,
        count,
        [
            (selected, rows(block, 256, reverse)),
            (mixed_in, rows(block, wide, reverse)),
            (projected, rows(block, 2 * held, reverse)),
            (scanned, rows(block, wide, reverse)),
            (dmixer_in, rows(block, wide, reverse)),
            (payload, columns_at(block, 128, reverse, width // 128)),
            (starts, start_spec(reverse)),
            (step_own, whole(step_own.shape)),
            (vecs, whole(vecs.shape)),
            (decay_own, whole(decay_own.shape)),
        ],
        [
            (leaf((total_rows, held), bf16), rows(block, held, reverse)),
            (leaf((total_rows, held), bf16), rows(block, held, reverse)),
            (leaf((total_rows, wide), f32), rows(block, wide, reverse)),
            (leaf((total_rows, 256), bf16), rows(block, 256, reverse)),
            (leaf((8, wide), f32), whole((8, wide))),
            (leaf((128, wide), f32), whole((128, wide))),
            (leaf((NS, wide), f32), whole((NS, wide))),
        ],
        [
            pltpu.VMEM((block // STEP, 2 * NS, STEP), f32),
            pltpu.VMEM((block, wide), f32),
            pltpu.VMEM((NS, wide), f32),
            pltpu.VMEM((block, wide), f32),
            pltpu.VMEM((block, wide), f32),
            pltpu.VMEM((block, wide), f32),
            pltpu.VMEM((block + 1, NS, wide), f32),
            pltpu.VMEM((block, NS, wide), f32),
            pltpu.VMEM((block * NS, 128), bf16),
            pltpu.VMEM((block * NS, 128), bf16),
            pltpu.VMEM((block * 8, wide), bf16),
            pltpu.VMEM((block * 8, wide), bf16),
        ],
        "scan_backward",
        [dpair, pair_grad],
    )
    dselected_part = after(dselected_part, pair_all)
    dselected_parts = scatter_parts(*halves(dselected_part), n, own_index)
    dselected = dselected_parts[0]
    for item in dselected_parts[1:]:
        dselected = dselected + item.astype(f32)
    dselected = gather_ctx(dselected.astype(bf16), n)
    hidden = after(hidden, dselected_parts[0])
    payload = after(payload, dselected_parts[0], down_all)
    mixer_part = dot_tn(normed_s, payload).astype(bf16)
    mixer_out_grad = scatter_z(mixer_part)


    out_part = dot_tn(after(normed_a, mixer_part), payload)[:, :width].astype(bf16)
    out_part = lax.all_to_all(
        jnp.moveaxis(out_part.reshape(head_width, n, out_piece), 1, 0), "ctx", 0, 0
    )
    out_part = out_part.reshape(n * head_width, out_piece)[:width]
    attend_part = jnp.concatenate(
        [dot_tn(hidden, dheads).astype(bf16), pad_to(out_part, 1, out_wide)], axis=1
    )
    attend_grad = scatter_z(attend_part)

    dprojected, select_part, filter_vecs = block_call(
        filter_backward_body(block, count),
        order,
        1,
        [
            (value, whole(value.shape))
            for value in (projected, dgate_z, mixed_in, dmixed_in, dselected, select_own, vecs)
        ],
        [
            (leaf((total_rows, 2 * held), bf16), whole((total_rows, 2 * held))),
            (leaf((256, wide), f32), whole((256, wide))),
            (leaf((8, wide), f32), whole((8, wide))),
        ],
        [
            pltpu.VMEM((block + 8, wide), f32),
            pltpu.VMEM((block + 8, wide), f32),
            pltpu.VMEM((block, 2 * held), f32),
            pltpu.VMEM((total_rows, wide), f32),
        ],
        "filter_backward",
        [attend_part, ffn_sums[0]],
    )
    in_part = dot_tn(hidden, dprojected).astype(bf16)
    in_grad = scatter_z(in_part)
    hidden_near, hidden_far = split_rows(
        [(dprojected, in_weight), (dheads, attend_all)], "hidden_backward", [in_part]
    )
    half_rows = total_rows // 2
    first_gain_part = (
        jnp.sum(hidden_near.astype(f32) * hidden[:half_rows].astype(f32), axis=0)
        + jnp.sum(hidden_far.astype(f32) * hidden[half_rows:].astype(f32), axis=0)
    ) / first_gain[0]
    small_grad = jnp.concatenate(
        [
            select_part[:RANK],
            select_part[128 : 128 + 2 * NS],
            step_part[:RANK],
            decay_part,
            filter_vecs[4 : 4 + CONV],
            filter_vecs[3:4],
            scan_vecs[0:3],
        ]
    )[:, :held]
    attend_gain_full = lax.dynamic_update_slice_in_dim(
        jnp.zeros((1, n * head_width), f32), attend_gain_part[0:1], c * head_width, axis=1
    )[0, :width]
    gain_part = jnp.stack([first_gain_part, attend_gain_full, post_gain_part]).reshape(3, m, shard)
    gain_part = pad_to(
        jnp.moveaxis(gain_part, 1, 0).reshape(m, 3 * shard), 1, gain_rows * small_width
    )
    small_part = jnp.concatenate(
        [
            small_grad.T.reshape(m, piece_rows, small_width)[:, :piece],
            gain_part.reshape(m, gain_rows, small_width),
        ],
        axis=1,
    )
    small_grads = jnp.sum(lax.all_to_all(small_part, "fsdp", 0, 0), axis=0)
    dhidden = scatter_ctx(
        after(hidden_near, small_part), hidden_far, n, own_index
    )
    dfirst = norm_backward(inputs, first_norm, first_gain, dhidden)
    tokens_grad = (dmixed + dfirst).astype(bf16)[None]
    layer_out = mixed
    for item in ffn_sums:
        layer_out = layer_out + item.astype(f32)
    layer_out = layer_out.astype(bf16)[None]

    spots = jnp.array([masks(n).index(mask) for mask in range(n)], dtype=jnp.int32)
    plain = jnp.arange(n, dtype=jnp.int32)
    where = spots[c ^ plain]
    gate_grad, up_grad = unpack_columns(
        pair_all,
        plain,
        [
            (k, f * shard_hidden, hidden_piece, k * hidden_held + f * hidden_rows, hidden_piece)
            for k in range(2)
            for f in range(m)
        ],
        [weight.shape[1] for weight in (gate_weight, up_weight)],
        "unpack_pair",
    )
    down_turned = unpack_rows(
        down_all, plain, hidden_piece, width, True, "unpack_down"
    )
    mixer_out_grad = unpack_rows(
        swaps(mixer_out_grad, n), where, piece, width, False, "unpack_mixer"
    )
    attend_grad = swaps(attend_grad, n)
    kv_wide = n * pair
    out_at = head_width + 2 * pair
    query_grad, key_parts, value_parts, out_grad = unpack_columns(
        attend_grad,
        where,
        [
            (0, 0, head_width, 0, head_width),
            (1, 0, pair, head_width, pair),
            (2, 0, pair, head_width + pair, pair),
            (3, 0, out_piece, out_at, out_piece),
        ],
        [width, kv_wide, kv_wide, width],
        "unpack_attention",
    )

    def group_sum(parts):
        total = jnp.zeros((shard, kv_pad), f32)
        for index in range(n):
            low_at = min(index * heads // GROUP, KV_HEADS - 1) * HEAD_DIM
            item = parts[:, index * pair : (index + 1) * pair]
            total = total + jnp.pad(item, ((0, 0), (low_at, kv_pad - pair - low_at)))
        return total[:, : KV_HEADS * HEAD_DIM]

    in_grad = after(in_grad, gate_grad, down_turned)
    small_grads = jnp.stack(swaps(small_grads, n))[where]
    in_grad = swaps(in_grad, n)
    (mixer_in_grad,) = unpack_columns(
        in_grad,
        where,
        [
            (0, p * inner_all + f * shard_channels, piece, p * held + f * piece_rows, piece)
            for p in range(2)
            for f in range(m)
        ],
        [2 * inner_all],
        "unpack_inner",
    )
    small_sum = small_grads.reshape(n, piece + gain_rows, small_width)
    channel_grad = small_sum[:, :piece].reshape(shard_channels, small_width)
    gain_grad = jnp.sum(small_sum[:, piece:], axis=0).reshape(-1)[: 3 * shard].reshape(3, shard)

    at = RANK + 2 * NS
    select_grad = channel_grad[:, :at]
    step_grad = channel_grad[:, at : at + RANK].T
    at += RANK
    decay_grad = channel_grad[:, at : at + NS]
    at += NS
    kernel_grad = channel_grad[:, at : at + CONV].T
    at += CONV
    return (
        layer_out,
        tokens_grad,
        gain_grad[0],
        query_grad,
        group_sum(key_parts),
        group_sum(value_parts),
        out_grad,
        gain_grad[1],
        mixer_in_grad,
        kernel_grad,
        channel_grad[:, at],
        select_grad,
        step_grad,
        channel_grad[:, at + 1],
        decay_grad,
        channel_grad[:, at + 2],
        channel_grad[:, at + 3],
        mixer_out_grad,
        gain_grad[2],
        gate_grad,
        up_grad,
        down_turned.T,
    )


def solution(mesh):
    rows_spec = P("fsdp", None)
    lanes_spec = P(None, "fsdp")
    flat = P("fsdp")
    activations = P("fsdp", "ctx", None)
    weight_specs = (
        flat, rows_spec, rows_spec, rows_spec, rows_spec, flat, rows_spec, lanes_spec, flat, rows_spec,
        lanes_spec, flat, rows_spec, flat, flat, rows_spec, flat, rows_spec, rows_spec, rows_spec,
    )
    return jax.shard_map(
        on_device,
        mesh=mesh,
        in_specs=(activations, activations, P()) + weight_specs,
        out_specs=(activations, activations) + weight_specs,
        check_vma=False,
    )
```

```python
import math

import jax
import jax.numpy as jnp
from jax import lax
from jax.experimental import pallas as pl
from jax.experimental.pallas import tpu as pltpu
from jax.sharding import PartitionSpec as P

HEADS = 25
KV_HEADS = 5
HEAD_DIM = 64
GROUP = HEADS // KV_HEADS
CONV = 4
RANK = 100
NS = 16
EPS = 1e-05
NEG = -1e30
SCALE = 1.0 / math.sqrt(HEAD_DIM)
STEP = 16
VMEM = 56 * 1024 * 1024
SIDE = 64
SIDE_AT = HEADS * HEAD_DIM % 128
bf16 = jnp.bfloat16
f32 = jnp.float32


def up_to(value, unit):
    return -(-value // unit) * unit


def dot(left, right, contract=((1,), (0,)), precision=None):
    return lax.dot_general(
        left, right, (contract, ((), ())), preferred_element_type=f32, precision=precision
    )


def dot_tn(left, right):
    return dot(left, right, ((0,), (0,)))


def dot_nt(left, right):
    return dot(left, right, ((1,), (1,)))


def pad_to(values, axis, size):
    widths = [(0, 0)] * values.ndim
    widths[axis] = (0, size - values.shape[axis])
    return jnp.pad(values, widths)


def masks(size):
    return list(range(0, size, 2)) + list(range(1, size, 2))


def swap(values, mask, size):
    return lax.ppermute(values, "ctx", [(i, i ^ mask) for i in range(size)])


def swaps(values, size):
    near = [values] + [swap(values, m, size) for m in range(2, size, 2)]
    return near + [swap(item, 1, size) for item in near]


def assemble(parts, *earlier):
    count = len(parts)
    step = parts[0].shape[0]
    shape = (count * step,) + parts[0].shape[1:]

    def body(*refs):
        for j in range(count):
            refs[-1][j * step : (j + 1) * step] = refs[j][...]

    spec = pl.BlockSpec(parts[0].shape, lambda: (0,) * len(shape))
    return pl.pallas_call(
        body,
        in_specs=[spec] * count + [pl.BlockSpec(memory_space=pl.ANY)] * len(earlier),
        out_specs=pl.BlockSpec(shape, lambda: (0,) * len(shape)),
        out_shape=leaf(shape, parts[0].dtype),
        compiler_params=pltpu.CompilerParams(vmem_limit_bytes=VMEM),
        name="assemble",
    )(*parts, *earlier)


def gather_ctx(values, size):
    return assemble(swaps(values, size))


def product_rows(pairs, at, rows_now, dtype, name, earlier=()):
    count = pairs[0][1].shape[0]
    step = min(256, count)

    def body(*refs):
        total = dot_nt(refs[0][...], refs[1][...])
        for k in range(2, 2 * len(pairs), 2):
            total = total + dot_nt(refs[k][...], refs[k + 1][...])
        refs[-1][...] = total.astype(dtype)

    specs, values = [], []
    for left, right in pairs:
        depth = left.shape[1]
        specs.append(pl.BlockSpec((rows_now, depth), lambda i: (at, 0)))
        specs.append(pl.BlockSpec((step, depth), lambda i: (i, 0)))
        values += [left, right]
    return pl.pallas_call(
        body,
        grid=(-(-count // step),),
        in_specs=specs + [pl.BlockSpec(memory_space=pl.ANY)] * len(earlier),
        out_specs=pl.BlockSpec((rows_now, step), lambda i: (0, i)),
        out_shape=leaf((rows_now, count), dtype),
        compiler_params=pltpu.CompilerParams(vmem_limit_bytes=VMEM),
        name=name,
    )(*values, *earlier)


def product_columns(left, right, at, rows_now, name, earlier=()):
    depth, count = right.shape
    step = min(256, count)

    def body(*refs):
        refs[-1][...] = dot(refs[0][...], refs[1][...]).astype(bf16)

    return pl.pallas_call(
        body,
        grid=(-(-count // step),),
        in_specs=[
            pl.BlockSpec((rows_now, depth), lambda i: (at, 0)),
            pl.BlockSpec((depth, step), lambda i: (0, i)),
        ]
        + [pl.BlockSpec(memory_space=pl.ANY)] * len(earlier),
        out_specs=pl.BlockSpec((rows_now, step), lambda i: (0, i)),
        out_shape=leaf((rows_now, count), bf16),
        compiler_params=pltpu.CompilerParams(vmem_limit_bytes=VMEM),
        name=name,
    )(left, right, *earlier)


def split_columns(left, right, name, earlier=()):
    half = left.shape[0] // 2
    far = product_columns(left, right, 1, half, name, earlier)
    return product_columns(left, right, 0, half, name), far


def split_rows(pairs, name, earlier=()):
    half = pairs[0][0].shape[0] // 2
    far = product_rows(pairs, 1, half, bf16, name, earlier)
    return product_rows(pairs, 0, half, bf16, name), far


def fold_body(count, step):
    def body(index, near, got, own_o, *sent_o):
        for j in range(count):
            rows_now = slice(j * step, (j + 1) * step)
            total = near[rows_now, :].astype(f32) + got[rows_now, :].astype(f32)
            if j == 0:
                own_o[...] = total
            else:
                sent_o[j - 1][...] = total.astype(bf16)

    return body


def scatter_parts(near, far, size, index):
    half = size // 2
    step, width = near.shape[0] // half, near.shape[1]
    got = swap(far, 1, size)
    total, *sent = block_call(
        fold_body(half, step),
        index,
        1,
        [(near, whole(near.shape)), (got, whole(near.shape))],
        [(leaf((step, width), f32), whole((step, width)))]
        + [(leaf((step, width), bf16), whole((step, width)))] * (half - 1),
        [],
        "fold_halves",
    )
    return [total] + [swap(sent[k - 1], 2 * k, size) for k in range(1, half)]


def scatter_ctx(near, far, size, index):
    total, *others = scatter_parts(near, far, size, index)
    for item in others:
        total = total + item.astype(f32)
    return total


def block_call(body, order, count, ins, outs, scratch, name, earlier=()):
    given = len(ins)
    ins = list(ins) + [(value, pl.BlockSpec(memory_space=pl.ANY)) for value in earlier]

    def trimmed(*refs):
        return body(*refs[: 1 + given], *refs[1 + len(ins) :])

    return pl.pallas_call(
        trimmed,
        grid_spec=pltpu.PrefetchScalarGridSpec(
            num_scalar_prefetch=1,
            grid=(count,),
            in_specs=[spec for _, spec in ins],
            out_specs=[spec for _, spec in outs],
            scratch_shapes=scratch,
        ),
        out_shape=[shape for shape, _ in outs],
        compiler_params=pltpu.CompilerParams(
            dimension_semantics=("arbitrary",), vmem_limit_bytes=VMEM
        ),
        name=name,
    )(order, *[value for value, _ in ins])


def after(values, *earlier):
    def body(*refs):
        del refs

    spec = pl.BlockSpec(memory_space=pl.ANY)
    return pl.pallas_call(
        body,
        in_specs=[spec] * (1 + len(earlier)),
        out_specs=spec,
        out_shape=leaf(values.shape, values.dtype),
        input_output_aliases={0: 0},
        name="after",
    )(values, *earlier)


def whole(shape):
    zeros = (0,) * len(shape)
    return pl.BlockSpec(shape, lambda i, order: zeros)


def rows(block, width, pick):
    return pl.BlockSpec((block, width), lambda i, order: (order[pick(i)], 0))


def columns_at(block, width, pick, index):
    return pl.BlockSpec((block, width), lambda i, order: (order[pick(i)], index))


def leaf(shape, dtype):
    return jax.ShapeDtypeStruct(shape, dtype)


def filter_taps(ext, vecs, block):
    total = vecs[3:4, :]
    for j in range(CONV):
        total = total + vecs[4 + j : 5 + j, :] * ext[5 + j : 5 + j + block, :]
    return total


def place(order, index, block):
    return pl.ds(pl.multiple_of(order[index] * block, block), block)


def filter_forward_body(block, count):
    def body(order, projected, vecs, select, mixed_o, selected_o, ext):
        held = projected.shape[1] // 2
        ext[...] = jnp.zeros_like(ext)

        def step(index, carry):
            rows_now = place(order, index, block)
            ext[0:8, :] = ext[block : block + 8, :]
            ext[8 : block + 8, 0:held] = projected[rows_now, 0:held].astype(bf16).astype(f32)
            total = filter_taps(ext, vecs, block)
            mixed_o[rows_now, :] = (total * jax.nn.sigmoid(total)).astype(bf16)
            return carry

        lax.fori_loop(0, count, step, 0)
        selected_o[...] = dot(mixed_o[...], select[...]).astype(bf16)

    return body


def side_scalar(scalars, index):
    at = SIDE_AT + 2 * index
    values = scalars[...].astype(f32)
    return values[:, at : at + 1] + values[:, at + 1 : at + 2]


def turn_sides(selected, sides_s):
    turned = selected[:, 128:256].T
    for g in range(sides_s.shape[0]):
        sides_s[g] = turned[: 2 * NS, g * STEP : (g + 1) * STEP]


def rate_of(selected, step_weight, vecs):
    rank = selected[:, 0:128].astype(bf16)
    raw = dot(rank, step_weight[...]) + vecs[0:1, :]
    rate = jnp.maximum(raw, 0.0) + jnp.log1p(jnp.exp(-jnp.abs(raw)))
    return rank, raw, rate


def scan_forward_body(block):
    def body(
        order, selected, mixed, projected, step_weight, vecs, decay,
        scanned_o, starts_o, scaled_o, state_s, rate_s, drive_s, gate_s, sides_s,
    ):
        held = projected.shape[1] // 2

        @pl.when(pl.program_id(0) == 0)
        def _():
            state_s[...] = jnp.zeros_like(state_s)
            gate_s[...] = jnp.zeros_like(gate_s)

        gate_s[:, 0:held] = projected[...][:, held:]
        turn_sides(selected, sides_s)

        _, _, rate = rate_of(selected, step_weight, vecs)
        wide = mixed[...].astype(f32)
        rate_s[...] = rate
        drive_s[...] = rate * wide
        starts_o[0] = state_s[...]
        decay_mat = decay[...]

        def group(g, state):
            base = pl.multiple_of(g * STEP, STEP)
            rates = rate_s[pl.ds(base, STEP), :]
            drives = drive_s[pl.ds(base, STEP), :]
            side = sides_s[g]
            for j in range(STEP):
                state = (
                    jnp.exp(rates[j : j + 1, :] * decay_mat) * state
                    + drives[j : j + 1, :] * side[:NS, j : j + 1]
                )
                scanned_o[pl.ds(base + j, 1), :] = jnp.sum(
                    state * side[NS:, j : j + 1], axis=0, keepdims=True
                )
            return state

        state_s[...] = lax.fori_loop(0, block // STEP, group, state_s[...])
        gate = gate_s[...]
        gated = (scanned_o[...] + vecs[1:2, :] * wide) * (gate * jax.nn.sigmoid(gate))
        lane = lax.broadcasted_iota(jnp.int32, gated.shape, 1)
        squares = jnp.sum(gated * gated, axis=1, keepdims=True)
        scaled_o[...] = jnp.where(lane == held, squares, gated * vecs[2:3, :]).astype(bf16)

    return body


def collector(block, size):
    token = lax.broadcasted_iota(jnp.int32, (block, block * size), 0)
    spot = lax.broadcasted_iota(jnp.int32, (block, block * size), 1) // size
    return jnp.where(token == spot, 1.0, 0.0).astype(bf16)


def scan_backward_body(block):
    def body(
        order, selected, mixed, projected, scanned, grad_in, scalars, starts, step_weight, vecs, decay,
        normed_o, dgate_o, dmixed_o, dselected_o, vec_o, step_o, decay_o,
        sides_s, gate_s, lam_s, rate_s, drive_s, dscan_s, hist_s, factor_s, read_s, write_s, drate_s, pull_s,
    ):
        width = decay.shape[1]
        held = projected.shape[1] // 2

        @pl.when(pl.program_id(0) == 0)
        def _():
            gate_s[...] = jnp.zeros_like(gate_s)
            lam_s[...] = jnp.zeros_like(lam_s)
            vec_o[...] = jnp.zeros_like(vec_o)
            step_o[...] = jnp.zeros_like(step_o)
            decay_o[...] = jnp.zeros_like(decay_o)

        rank, raw, rate = rate_of(selected, step_weight, vecs)
        wide = mixed[...].astype(f32)
        rate_s[...] = rate
        drive_s[...] = rate * wide
        turn_sides(selected, sides_s)
        gate_s[:, 0:held] = projected[...][:, held:]
        gate = gate_s[...]
        sig = jax.nn.sigmoid(gate)
        act = gate * sig
        before = scanned[...] + vecs[1:2, :] * wide
        gated = before * act
        norm = side_scalar(scalars, 2)
        centre = side_scalar(scalars, 3)
        grad = grad_in[...]
        gated_norm = gated * norm
        normed_o[...] = (gated_norm * vecs[2:3, :])[:, 0:held].astype(bf16)
        dgated = norm * (vecs[2:3, :] * grad) - gated * centre
        dscan = dgated * act
        dscan_s[...] = dscan
        dgate = dgated * before * (sig * (1.0 + gate * (1.0 - sig)))
        dgate_o[...] = dgate[:, 0:held].astype(bf16)
        vec_o[1:2, :] += jnp.sum(dscan * wide, axis=0, keepdims=True)
        vec_o[2:3, :] += jnp.sum(grad * gated_norm, axis=0, keepdims=True)
        decay_mat = decay[...]

        def forward(g, state):
            base = pl.multiple_of(g * STEP, STEP)
            rates = rate_s[pl.ds(base, STEP), :]
            drives = drive_s[pl.ds(base, STEP), :]
            side = sides_s[g]
            for j in range(STEP):
                factor = jnp.exp(rates[j : j + 1, :] * decay_mat)
                factor_s[base + j] = factor
                state = factor * state + drives[j : j + 1, :] * side[:NS, j : j + 1]
                hist_s[base + j + 1] = state
            return state

        hist_s[0] = starts[0]
        lax.fori_loop(0, block // STEP, forward, starts[0])

        def fold(values):
            total = values[:, 0:128]
            for at in range(128, width, 128):
                total = total + values[:, at : at + 128]
            return total

        def backward(i, carry):
            lam_in, decay_sum = carry
            g = block // STEP - 1 - i
            base = pl.multiple_of(g * STEP, STEP)
            rates = rate_s[pl.ds(base, STEP), :]
            drives = drive_s[pl.ds(base, STEP), :]
            dscans = dscan_s[pl.ds(base, STEP), :]
            side = sides_s[g]
            later = None
            for j in range(STEP - 1, -1, -1):
                at = base + j
                row = dscans[j : j + 1, :]
                lam = lam_in + row * side[NS:, j : j + 1]
                put = pl.ds(pl.multiple_of(at * NS, NS), NS)
                read_s[put, :] = fold(hist_s[at + 1] * row).astype(bf16)
                write_s[put, :] = fold(lam * drives[j : j + 1, :]).astype(bf16)
                pull = lam * side[:NS, j : j + 1]
                lam_in = factor_s[at] * lam
                kept = lam_in * hist_s[at]
                decay_sum = decay_sum + rates[j : j + 1, :] * kept
                drate = decay_mat * kept
                sums = (pull[:8] + pull[8:], drate[:8] + drate[8:])
                if j % 2 == 1:
                    later = sums
                else:
                    put = pl.ds(pl.multiple_of(at * 8, 16), 16)
                    pull_s[put, :] = jnp.concatenate([sums[0], later[0]]).astype(bf16)
                    drate_s[put, :] = jnp.concatenate([sums[1], later[1]]).astype(bf16)
            return (lam_in, decay_sum)

        lam, decay_sum = lax.fori_loop(
            0, block // STEP, backward, (lam_s[...], jnp.zeros_like(lam_s))
        )
        lam_s[...] = lam
        decay_o[...] += decay_sum * decay_mat
        by_token = collector(block, 8)
        pulled = dot(by_token, pull_s[...])
        draw = (dot(by_token, drate_s[...]) + wide * pulled) * jax.nn.sigmoid(raw)
        vec_o[0:1, :] += jnp.sum(draw, axis=0, keepdims=True)
        low = draw.astype(bf16)
        dmixed_o[...] = vecs[1:2, :] * dscan + rate * pulled
        step_o[...] += dot_tn(rank, low)
        ones = jnp.ones((128, 128), bf16)
        row = lax.broadcasted_iota(jnp.int32, (block * NS, 128), 0) % NS
        lane = lax.broadcasted_iota(jnp.int32, (block * NS, 128), 1)
        summed = jnp.where(lane == row, dot(write_s[...], ones), 0.0)
        summed = summed + jnp.where(lane == row + NS, dot(read_s[...], ones), 0.0)
        dselected_o[:, 0:128] = dot_nt(low, step_weight[...]).astype(bf16)
        dselected_o[:, 128:256] = dot(collector(block, NS), summed.astype(bf16)).astype(
            bf16
        )

    return body


def filter_backward_body(block, count):
    def body(
        order, projected, dgate, mixed, dmixed, dselected, select, vecs,
        dprojected_o, select_o, vec_o, ext, ext_grad, both_s, added_s,
    ):
        held = projected.shape[1] // 2
        ext[...] = jnp.zeros_like(ext)
        ext_grad[block : block + 8, :] = jnp.zeros((8, ext.shape[1]), f32)
        vec_o[...] = jnp.zeros_like(vec_o)
        low = dselected[...]
        added_s[...] = dot_nt(low, select[...])
        select_o[...] = dot_tn(low, mixed[...])

        def step(i, carry):
            index = count - 1 - i
            rows_now = place(order, index, block)
            past = order[jnp.maximum(index - 1, 0)] * block + block - 16
            past = projected[pl.ds(pl.multiple_of(past, 16), 16), 0:held][8:16]
            first = jnp.where(index == 0, 0.0, 1.0)

            @pl.when(i > 0)
            def _():
                ext_grad[block : block + 8, :] = ext_grad[0:8, :]

            ext[0:8, 0:held] = past.astype(bf16).astype(f32) * first
            ext[8 : block + 8, 0:held] = projected[rows_now, 0:held].astype(bf16).astype(f32)
            total = filter_taps(ext, vecs, block)
            sig = jax.nn.sigmoid(total)
            dmix = dmixed[rows_now, :] + added_s[rows_now, :]
            dfilt = dmix * (sig * (1.0 + total * (1.0 - sig)))
            ext_grad[0:block, :] = dfilt
            dinner = jnp.zeros_like(dfilt)
            vec_o[3:4, :] += jnp.sum(dfilt, axis=0, keepdims=True)
            for j in range(CONV):
                at = CONV - 1 - j
                dinner = dinner + vecs[4 + j : 5 + j, :] * ext_grad[at : at + block, :]
                vec_o[4 + j : 5 + j, :] += jnp.sum(
                    dfilt * ext[5 + j : 5 + j + block, :], axis=0, keepdims=True
                )
            both_s[:, 0:held] = dinner[:, 0:held]
            both_s[:, held:] = dgate[rows_now, :].astype(f32)
            dprojected_o[rows_now, :] = both_s[...].astype(bf16)
            return carry

        lax.fori_loop(0, count, step, 0)

    return body


def half_mask(half):
    lane = lax.broadcasted_iota(jnp.int32, (1, 128), 1)
    return jnp.where((lane >= 64 * half) & (lane < 64 * half + 64), 1.0, 0.0)


def softmax_rows(query, key, allowed):
    scores = jnp.where(allowed, dot_nt(query, key), NEG)
    weights = jnp.exp(scores - jnp.max(scores, axis=-1, keepdims=True))
    return weights, 1.0 / jnp.sum(weights, axis=-1, keepdims=True)


def natural(order, source, target, block):
    for index in range(target.shape[0] // block):
        target[index * block : (index + 1) * block, :] = source[place(order, index, block), :]


def causal(rows_now, start, stop):
    return lax.broadcasted_iota(jnp.int32, (rows_now, stop), 1) <= (
        lax.broadcasted_iota(jnp.int32, (rows_now, stop), 0) + start
    )


def attention_forward_body(block, count):
    def body(marks, query, key, value, gain, out_o, scaled_o, query_s, key_s, value_s, out_s, scaled_s):
        total, width = key.shape
        step = min(256, total)
        natural(marks, query, query_s, block)
        natural(marks, key, key_s, block)
        natural(marks, value, value_s, block)
        for start in range(0, total, step):
            stop = start + step
            allowed = causal(step, start, stop)
            squares = jnp.zeros((step, 1), f32)
            for at in range(0, width, 128):
                lanes = slice(at, at + 128)
                tile = jnp.zeros((step, 128), f32)
                for half in range(2):
                    mask = half_mask(half)
                    part = query_s[start:stop, lanes] * (mask * SCALE).astype(bf16)
                    weights, inverse = softmax_rows(part, key_s[0:stop, lanes], allowed)
                    live = marks[count + at // 64 + half].astype(f32)
                    tile = tile + dot(weights.astype(bf16), value_s[0:stop, lanes]) * (
                        inverse * (mask * live)
                    )
                out_s[start:stop, lanes] = tile
                scaled_s[start:stop, lanes] = (tile * gain[:, lanes]).astype(bf16)
                squares = squares + jnp.sum(tile * tile, axis=1, keepdims=True)
            lane = lax.broadcasted_iota(jnp.int32, (step, 128), 1)
            scaled_s[start:stop, width:] = jnp.where(lane == 0, squares, 0.0).astype(bf16)
        for index in range(count):
            rows_now = slice(index * block, (index + 1) * block)
            out_o[place(marks, index, block), :] = out_s[rows_now, :]
            scaled_o[place(marks, index, block), :] = scaled_s[rows_now, :]

    return body


def unit_body(both, dunit, unit_o, dboth_o):
    held = dunit.shape[1]
    values = both[...]
    gate, up = values[:, :held], values[:, held:]
    grad = dunit[...]
    sig = jax.nn.sigmoid(gate)
    act = gate * sig
    unit_o[...] = (act * up).astype(bf16)
    dgate = grad * up * (sig * (1.0 + gate * (1.0 - sig)))
    dboth_o[...] = jnp.concatenate([dgate, grad * act], axis=1).astype(bf16)


def branch_grad_body(half, inner_all):
    def body(index, *refs):
        parts = refs[:half]
        mixed, gain, upstream, attend_sum, mixer_sum = refs[half : half + 5]
        payload_o, dmixed_o, gain_o = refs[half + 5 :]
        grad = parts[0][...]
        for item in parts[1:]:
            grad = grad + item[...].astype(f32)
        values = mixed[...]
        width = values.shape[1]
        norm = lax.rsqrt(jnp.mean(values * values, axis=1, keepdims=True) + EPS)
        scaled = grad * gain[...]
        centre = norm * norm * norm * jnp.mean(values * scaled, axis=1, keepdims=True)
        dmixed = upstream[...].astype(f32) + norm * scaled - values * centre
        dmixed_o[...] = dmixed
        total = jnp.sum(grad * values * norm, axis=0, keepdims=True)
        gain_o[...] = jnp.broadcast_to(total, gain_o.shape)
        low = (0.5 * dmixed).astype(bf16)
        payload_o[:, 0:width] = low
        wide_low = low.astype(f32)
        lane = lax.broadcasted_iota(jnp.int32, (values.shape[0], SIDE), 1)
        side = jnp.zeros((values.shape[0], SIDE), f32)
        at = 0
        for source, size in ((attend_sum, HEADS * HEAD_DIM), (mixer_sum, inner_all)):
            sums = source[...]
            factor = lax.rsqrt(sums[:, width : width + 1] / size + EPS)
            mean = jnp.sum(wide_low * sums[:, 0:width], axis=1, keepdims=True) / size
            for item in (factor, factor * factor * factor * mean):
                high = item.astype(bf16).astype(f32)
                side = jnp.where(lane == at, high, side)
                side = jnp.where(lane == at + 1, item - high, side)
                at += 2
        payload_o[:, width:] = side.astype(bf16)

    return body


def norm_body(index, gain, *refs):
    out = refs[-1]
    step = refs[0].shape[0]
    for j, ref in enumerate(refs[:-1]):
        values = ref[...].astype(f32)
        norm = lax.rsqrt(jnp.mean(values * values, axis=1, keepdims=True) + EPS)
        out[j * step : (j + 1) * step, :] = (values * norm * gain[...]).astype(bf16)


def attention_backward_body(block, count):
    def body(
        marks, query, key, value, gain, out, grad_in, scalars,
        dquery_o, dpair_o, normed_o, gain_o,
        query_s, key_s, value_s, dout_s, dout_n, dquery_s, dkey_s, dvalue_s,
    ):
        total, width = key.shape
        step = min(256, total)
        natural(marks, query, query_s, block)
        natural(marks, key, key_s, block)
        natural(marks, value, value_s, block)
        norm = side_scalar(scalars, 0)
        centre = side_scalar(scalars, 1)
        attended = out[...]
        grad = grad_in[:, 0:width]
        normed = attended * norm
        normed_o[...] = (normed * gain[...]).astype(bf16)
        gain_sum = jnp.sum(grad * normed, axis=0, keepdims=True)
        gain_o[...] = jnp.broadcast_to(gain_sum, gain_o.shape)
        dout_s[...] = (norm * (gain[...] * grad) - attended * centre).astype(bf16)
        natural(marks, dout_s, dout_n, block)
        dkey_s[...] = jnp.zeros_like(dkey_s)
        dvalue_s[...] = jnp.zeros_like(dvalue_s)
        for start in range(0, total, step):
            stop = start + step
            allowed = causal(step, start, stop)
            for at in range(0, width, 128):
                lanes = slice(at, at + 128)
                key_tile = key_s[0:stop, lanes]
                dquery = jnp.zeros((step, 128), f32)
                dkey = jnp.zeros((stop, 128), f32)
                dvalue = jnp.zeros((stop, 128), f32)
                for half in range(2):
                    mask = half_mask(half)
                    part = query_s[start:stop, lanes] * (mask * SCALE).astype(bf16)
                    dpart = dout_n[start:stop, lanes] * mask.astype(bf16)
                    weights, inverse = softmax_rows(part, key_tile, allowed)
                    probs = weights * inverse
                    dprobs = dot_nt(dpart, value_s[0:stop, lanes])
                    mean = jnp.sum(dprobs * probs, axis=-1, keepdims=True)
                    dscores = (probs * (dprobs - mean)).astype(bf16)
                    dvalue = dvalue + dot_tn(probs.astype(bf16), dpart)
                    dquery = dquery + dot(dscores, key_tile) * (mask * SCALE)
                    dkey = dkey + dot_tn(dscores, part)
                dquery_s[start:stop, lanes] = dquery.astype(bf16)
                dkey_s[0:stop, lanes] += dkey
                dvalue_s[0:stop, lanes] += dvalue
        for index in range(count):
            rows_now = slice(index * block, (index + 1) * block)
            spot = place(marks, index, block)
            dquery_o[spot, :] = dquery_s[rows_now, :]
            dpair_o[spot, 0:width] = dkey_s[rows_now, :].astype(bf16)
            dpair_o[spot, width:] = dvalue_s[rows_now, :].astype(bf16)

    return body


def pack_body(groups, width, piece):
    window = up_to(piece + 127, 128)

    def body(index, *refs):
        out_o, acc = refs[-2:]
        acc[...] = jnp.zeros_like(acc)
        for which, start, at in groups:
            weight = refs[which]
            source = start + index[0] * piece
            tile = jnp.minimum(source // 128, (width - window) // 128)
            base = pl.multiple_of(tile * 128, 128)
            low = at % 128
            span = up_to(low + piece, 128)
            row = lax.broadcasted_iota(jnp.int32, (window, span), 0)
            lane = lax.broadcasted_iota(jnp.int32, (window, span), 1) - low
            pick = (row - (source - base) == lane) & (lane >= 0) & (lane < piece)
            pick = jnp.where(pick, 1.0, 0.0).astype(bf16)
            acc[:, at - low : at - low + span] += dot(weight[:, pl.ds(base, window)], pick)
        out_o[...] = acc[:, : out_o.shape[1]].astype(bf16)

    return body


def row_block(count):
    return 80 if count % 80 == 0 else count


def join_body(axis):
    def body(index, *refs):
        at = 0
        for ref in refs[:-1]:
            size = ref.shape[axis]
            if axis == 0:
                refs[-1][at : at + size, :] = ref[...]
            else:
                refs[-1][:, at : at + size] = ref[...]
            at += size

    return body


def join(parts, index, axis, name, earlier):
    shape = list(parts[0].shape)
    shape[axis] = sum(part.shape[axis] for part in parts)
    return block_call(
        join_body(axis),
        index,
        1,
        [(part, whole(part.shape)) for part in parts],
        [(leaf(tuple(shape), bf16), whole(tuple(shape)))],
        [],
        name,
        earlier,
    )[0]


def pack_columns(weights, index, groups, out_wide, piece, name, earlier=()):
    count, width = weights[0].shape
    block = row_block(count)
    return block_call(
        pack_body(groups, width, piece),
        index,
        count // block,
        [(weight, pl.BlockSpec((block, width), lambda i, index: (i, 0))) for weight in weights],
        [
            (
                leaf((count, out_wide), bf16),
                pl.BlockSpec((block, out_wide), lambda i, index: (i, 0)),
            )
        ],
        [pltpu.VMEM((block, up_to(out_wide, 128)), f32)],
        name,
        earlier,
    )[0]


def unpack_columns(parts, where, moves, widths, name, count=None):
    joined = not isinstance(parts, list)
    size = len(parts)
    width = parts[0].shape[1]
    count = count or parts[0].shape[0]
    block = row_block(count)

    def body(where, *refs):
        outs = refs[1 if joined else size :][: len(widths)]
        kept = refs[0] if joined else refs[-1]
        if not joined:
            for j in range(size):
                kept[j] = refs[j][...]
        for index in range(size):
            values = kept[where[index]].astype(f32)
            for out, first, stride, at, piece in moves:
                start = first + index * stride
                piece = min(piece, widths[out] - start)
                if piece > 0:
                    outs[out][:, start : start + piece] = values[:, at : at + piece]

    if joined:
        ins = [(parts, pl.BlockSpec((size, block, width), lambda i, where: (0, i, 0)))]
    else:
        ins = [(part, pl.BlockSpec((block, width), lambda i, where: (i, 0))) for part in parts]
    return block_call(
        body,
        where,
        count // block,
        ins,
        [
            (leaf((count, wide), f32), pl.BlockSpec((block, wide), lambda i, where: (i, 0)))
            for wide in widths
        ],
        [] if joined else [pltpu.VMEM((size, block, width), bf16)],
        name,
    )


def unpack_rows(parts, where, piece, width, turned, name):
    joined = not isinstance(parts, list)
    size = len(parts)
    count = parts[0].shape[0]
    lanes = 256

    def body(where, *refs):
        out = refs[1 if joined else size]
        kept = refs[0] if joined else refs[-1]
        if not joined:
            for j in range(size):
                kept[j] = refs[j][...]
        for index in range(size):
            values = kept[where[index]].astype(f32)
            put = slice(index * piece, (index + 1) * piece)
            if turned:
                out[:, put] = values.T[:, :piece]
            else:
                out[put, :] = values[:piece]

    shape = (width, size * piece) if turned else (size * piece, width)
    out_block = (lanes, size * piece) if turned else (size * piece, lanes)
    spot = (lambda i, where: (i, 0)) if turned else (lambda i, where: (0, i))
    if joined:
        ins = [(parts, pl.BlockSpec((size, count, lanes), lambda i, where: (0, 0, i)))]
    else:
        ins = [(part, pl.BlockSpec((count, lanes), lambda i, where: (0, i))) for part in parts]
    return block_call(
        body,
        where,
        -(-width // lanes),
        ins,
        [(leaf(shape, f32), pl.BlockSpec(out_block, spot))],
        [] if joined else [pltpu.VMEM((size, count, lanes), bf16)],
        name,
    )[0]


def inverse_rms(values):
    return lax.rsqrt(jnp.mean(values * values, axis=-1, keepdims=True) + EPS)


def norm_backward(values, norm, gain, grad):
    scaled = grad * gain
    centre = norm**3 * jnp.mean(values * scaled, axis=-1, keepdims=True)
    return norm * scaled - values * centre


def split_low(values):
    high = lax.reduce_precision(values, 8, 7)
    return [high.astype(bf16), (values - high).astype(bf16)]


def on_device(
    tokens, cotangent, deal_table, norm_gain, query_weight, key_weight, value_weight, attention_out,
    attention_gain, mixer_in, filter_kernel, filter_bias, select_weight, step_weight, step_bias, decay_log,
    skip_gain, mixer_gain, mixer_out, post_gain, gate_weight, up_weight, down_weight,
):
    n = lax.axis_size("ctx")
    m = lax.axis_size("fsdp")
    c = lax.axis_index("ctx")
    z = lax.axis_index("fsdp")
    own = tokens.shape[1]
    block = own // 2
    total_rows = own * n
    count = 2 * n
    width = tokens.shape[2]
    shard = width // m
    heads = -(-HEADS // n)
    heads += heads % 2
    head_width = heads * HEAD_DIM
    shard_channels = filter_bias.shape[0]
    piece = shard_channels // n
    channels = m * piece
    inner_all = shard_channels * m
    shard_hidden = down_weight.shape[0]
    hidden_piece = shard_hidden // n
    piece_rows, hidden_rows = up_to(piece, 16), up_to(hidden_piece, 16)
    held, hidden_held = m * piece_rows, m * hidden_rows
    wide = up_to(held + 1, 128)
    sent_width = width + SIDE
    out_piece = width // n
    out_wide = up_to(out_piece, 128)

    def gather_z(values, tiled=True):
        return lax.all_gather(values, "fsdp", axis=0, tiled=tiled)

    def columns(values, start, size):
        return lax.dynamic_slice_in_dim(values, start, size, axis=1)

    in_groups = [
        (0, p * inner_all + f * shard_channels, p * held + f * piece_rows)
        for p in range(2)
        for f in range(m)
    ]
    in_local = pack_columns([mixer_in], c.reshape(1), in_groups, 2 * held, piece, "pack_mixer")
    in_weight = gather_z(in_local)
    upstream = cotangent[0]
    upstream_parts = swaps(after(upstream, in_local), n)

    def turn_z(values):
        turned = [
            lax.ppermute(values, "fsdp", [(i, (i + k) % m) for i in range(m)])
            for k in range(m - 1, 0, -1)
        ] + [values]
        return lax.dynamic_slice_in_dim(jnp.stack(turned + turned), m - 1 - z, m, axis=0)

    first_gain = turn_z(norm_gain).reshape(1, width).astype(f32)
    token_parts = swaps(after(tokens[0], upstream_parts[1], first_gain), n)
    own_index = after(c.reshape(1), upstream_parts[1])
    c = own_index[0]
    small_rows = jnp.concatenate(
        [
            select_weight,
            step_weight.T,
            decay_log,
            filter_kernel.T,
            filter_bias[:, None],
            step_bias[:, None],
            skip_gain[:, None],
            mixer_gain[:, None],
        ],
        axis=1,
    )
    small_width = small_rows.shape[1]
    small_rows = lax.dynamic_slice_in_dim(small_rows, c * piece, piece, axis=0)
    gains = jnp.stack([norm_gain, attention_gain, post_gain]).reshape(-1)
    gain_rows = -(-3 * shard // small_width)
    gains = pad_to(gains, 0, gain_rows * small_width).reshape(gain_rows, small_width)
    small_local = jnp.concatenate([small_rows, gains])
    small_all = turn_z(small_local)
    small = pad_to(small_all[:, :piece], 1, piece_rows).reshape(held, small_width)
    gains_all = small_all[:, piece:].reshape(m, gain_rows * small_width)[:, : 3 * shard]
    gains_all = jnp.moveaxis(gains_all.reshape(m, 3, shard), 0, 1).reshape(3, width).astype(f32)
    attend_gain, after_gain = gains_all[1:2], gains_all[2:3]

    def first_group(index):
        return jnp.minimum(index * heads // GROUP, KV_HEADS - 1)

    group_at = first_group(c)
    kv_pad = (KV_HEADS + 1) * HEAD_DIM
    pair = 2 * HEAD_DIM
    attend_local = join(
        [
            columns(pad_to(query_weight, 1, n * head_width), c * head_width, head_width),
            columns(pad_to(key_weight, 1, kv_pad), group_at * HEAD_DIM, pair),
            columns(pad_to(value_weight, 1, kv_pad), group_at * HEAD_DIM, pair),
        ],
        own_index,
        1,
        "pack_attention",
        [in_local],
    )
    head_ids = c * heads + jnp.arange(heads, dtype=jnp.int32)
    valid = (head_ids < HEADS).astype(jnp.int32)
    upper = jnp.minimum(head_ids // GROUP, KV_HEADS - 1) > group_at

    def row_slice(weight, size):
        cut = lax.dynamic_slice_in_dim(weight, c * size, size, axis=0)
        return pad_to(cut, 0, up_to(size, 16))

    out_cut = columns(attention_out, c * out_piece, out_piece).reshape(-1)
    out_rows = up_to(-(-out_cut.shape[0] // width), 16)
    rows_local = join(
        [
            row_slice(mixer_out, piece),
            pad_to(out_cut, 0, out_rows * width).reshape(out_rows, width),
        ],
        own_index,
        0,
        "pack_rows",
        [in_local],
    )
    pair_groups = [
        (k, f * shard_hidden, k * hidden_held + f * hidden_rows) for k in range(2) for f in range(m)
    ]
    pair_local = pack_columns(
        [gate_weight, up_weight],
        own_index,
        pair_groups,
        2 * hidden_held,
        hidden_piece,
        "pack_pair",
        [in_local, token_parts[1]],
    )

    down_local = row_slice(down_weight, hidden_piece)
    rows_all = gather_z(rows_local, tiled=False)

    inputs = tokens[0].astype(f32)
    first_norm = inverse_rms(inputs)
    hidden = block_call(
        norm_body,
        own_index,
        1,
        [(first_gain, whole(first_gain.shape))]
        + [(item, whole(item.shape)) for item in token_parts],
        [(leaf((total_rows, width), bf16), whole((total_rows, width)))],
        [],
        "norm_tokens",
        [attend_local, rows_local, upstream_parts[-1]],
    )[0]

    projected = dot(hidden, in_weight)
    attend_all = gather_z(after(attend_local, projected))

    def extended(weight, rows_now, at):
        weight = jnp.pad(weight, ((0, rows_now - weight.shape[0]), (0, SIDE)))
        spot = (jnp.arange(rows_now) == at)[:, None] & (jnp.arange(sent_width) == width)[None, :]
        return jnp.where(spot, jnp.ones((), bf16), weight)

    lane_dim = jnp.arange(head_width, dtype=jnp.int32) % HEAD_DIM
    target = jnp.where(jnp.repeat(upper, HEAD_DIM), HEAD_DIM, 0) + lane_dim
    target = jnp.concatenate([target, target + pair])
    side_now = jnp.arange(2 * head_width, dtype=jnp.int32) // head_width
    spread = (target[None, :] == jnp.arange(2 * pair, dtype=jnp.int32)[:, None]) & (
        side_now[None, :] == (jnp.arange(2 * pair, dtype=jnp.int32) // pair)[:, None]
    )
    spread = spread.astype(bf16)

    others = c ^ jnp.array(masks(n), dtype=jnp.int32)
    firsts = deal_table[others]
    places = jnp.stack([firsts, count - 1 - firsts], axis=1).reshape(count)
    ids = jnp.arange(count, dtype=jnp.int32)
    order = jnp.sum(jnp.where(places[None, :] == ids[:, None], ids[None, :], 0), axis=1)

    small_t = pad_to(small.astype(f32).T, 1, wide)
    select_own = pad_to(
        jnp.concatenate(
            [
                pad_to(small[:, :RANK], 1, 128),
                pad_to(small[:, RANK : RANK + 2 * NS], 1, 128),
            ],
            axis=1,
        ),
        0,
        wide,
    )
    step_own = pad_to(small_t[RANK + 2 * NS : 2 * RANK + 2 * NS], 0, 128).astype(bf16)
    at = 2 * RANK + 2 * NS
    decay_own = -jnp.exp(small_t[at : at + NS])
    at += NS
    vecs = jnp.concatenate([small_t[at + CONV + 1 : at + CONV + 4], small_t[at + CONV : at + CONV + 1], small_t[at : at + CONV]])

    def halves(values):
        return values[: total_rows // 2], values[total_rows // 2 :]

    upstream_all = assemble(upstream_parts)

    forward = lambda i: i
    reverse = lambda i: count - 1 - i
    start_spec = lambda pick: pl.BlockSpec((1, NS, wide), lambda i, order: (order[pick(i)], 0, 0))
    mixed_in, selected_part = block_call(
        filter_forward_body(block, count),
        order,
        1,
        [
            (projected, whole(projected.shape)),
            (vecs, whole(vecs.shape)),
            (select_own, whole(select_own.shape)),
        ],
        [
            (leaf((total_rows, wide), bf16), whole((total_rows, wide))),
            (leaf((total_rows, 256), bf16), whole((total_rows, 256))),
        ],
        [pltpu.VMEM((block + 8, wide), f32)],
        "filter_forward",
    )
    selected_own = scatter_ctx(*halves(selected_part), n, own_index)
    selected = gather_ctx(selected_own, n)
    scanned, starts, mixer_scaled = block_call(
        scan_forward_body(block),
        order,
        count,
        [
            (selected, rows(block, 256, forward)),
            (mixed_in, rows(block, wide, forward)),
            (projected, rows(block, 2 * held, forward)),
            (step_own, whole(step_own.shape)),
            (vecs, whole(vecs.shape)),
            (decay_own, whole(decay_own.shape)),
        ],
        [
            (leaf((total_rows, wide), f32), rows(block, wide, forward)),
            (leaf((count, NS, wide), f32), start_spec(forward)),
            (leaf((total_rows, wide), bf16), rows(block, wide, forward)),
        ],
        [
            pltpu.VMEM((NS, wide), f32),
            pltpu.VMEM((block, wide), f32),
            pltpu.VMEM((block, wide), f32),
            pltpu.VMEM((block, wide), f32),
            pltpu.VMEM((block // STEP, 2 * NS, STEP), f32),
        ],
        "scan_forward",
        [pair_local],
    )
    pair_weight = gather_z(after(pair_local, scanned))
    attend_all = after(attend_all, scanned)
    heads_in = dot(hidden, attend_all).astype(bf16)
    pair_in = dot(heads_in[:, head_width:], spread).astype(bf16)
    mixer_out_own = extended(rows_all[:, :piece_rows].reshape(held, width), wide, held)
    down_own = gather_z(after(down_local, selected_own))
    out_columns = rows_all[:, piece_rows : piece_rows + out_rows].reshape(m, -1)
    out_columns = out_columns[:, : shard * out_piece]
    out_columns = out_columns.reshape(width, out_piece)
    out_own = lax.all_to_all(
        pad_to(out_columns, 0, n * head_width).reshape(n, head_width, out_piece), "ctx", 0, 0
    )
    out_own = jnp.moveaxis(out_own, 0, 1).reshape(head_width, width)
    out_own = extended(out_own, head_width + 128, head_width)

    own_gain = lax.dynamic_slice_in_dim(
        pad_to(attend_gain, 1, n * head_width), c * head_width, head_width, axis=1
    )

    def full(size, index=0):
        return pl.BlockSpec((total_rows, size), lambda i, order: (0, index))

    marks = jnp.concatenate([order, valid])
    attend_ins = [
        (heads_in, full(head_width)),
        (pair_in, full(head_width, 0)),
        (pair_in, full(head_width, 1)),
        (own_gain, whole(own_gain.shape)),
    ]
    low_rows = pltpu.VMEM((total_rows, head_width), bf16)
    wide_rows = pltpu.VMEM((total_rows, head_width), f32)
    attended, attended_scaled = block_call(
        attention_forward_body(block, count),
        marks,
        1,
        attend_ins,
        [
            (leaf((total_rows, head_width), f32), full(head_width)),
            (leaf((total_rows, head_width + 128), bf16), full(head_width + 128)),
        ],
        [low_rows] * 3 + [wide_rows, pltpu.VMEM((total_rows, head_width + 128), bf16)],
        "attention_forward",
    )

    def branch_out(scaled, weight):
        far = dot(scaled[total_rows // 2 :], weight).astype(bf16)
        near = dot(scaled[: total_rows // 2], weight).astype(bf16)
        return scatter_ctx(near, far, n, own_index)

    attend_sum = branch_out(attended_scaled, out_own)

    mixer_sum = branch_out(mixer_scaled, mixer_out_own)

    def normed_sum(total, size):
        return total[:, :width] * lax.rsqrt(total[:, width : width + 1] / size + EPS)

    mixed = inputs + 0.5 * (
        normed_sum(attend_sum, HEADS * HEAD_DIM) + normed_sum(mixer_sum, inner_all)
    )
    post_norm = inverse_rms(mixed)
    dunit = product_rows([(upstream_all, down_own)], 0, total_rows, f32, "units_backward")
    post = assemble(swaps((mixed * post_norm * after_gain).astype(bf16), n), dunit)
    both = dot(post, pair_weight)

    def strip(size):
        return pl.BlockSpec((own, size), lambda i: (i, 0))

    unit, dboth = pl.pallas_call(
        unit_body,
        grid=(n,),
        in_specs=[strip(2 * hidden_held), strip(hidden_held)],
        out_specs=[strip(hidden_held), strip(2 * hidden_held)],
        out_shape=[
            leaf((total_rows, hidden_held), bf16),
            leaf((total_rows, 2 * hidden_held), bf16),
        ],
        compiler_params=pltpu.CompilerParams(vmem_limit_bytes=VMEM),
        name="hidden_units",
    )(both, dunit)

    pair_part = dot_tn(post, dboth).astype(bf16)
    dpost_parts = scatter_parts(
        *split_rows([(dboth, pair_weight)], "post_backward", [pair_part]), n, own_index
    )
    half = n // 2
    strips = [(own, width)] * (half + 5)
    strips[half + 1] = (1, width)
    strips[half + 3] = strips[half + 4] = (own, sent_width)
    payload, dmixed, post_gain_part = block_call(
        branch_grad_body(half, inner_all),
        own_index,
        1,
        [
            (value, whole(shape))
            for value, shape in zip(
                dpost_parts + [mixed, after_gain, upstream, attend_sum, mixer_sum], strips
            )
        ],
        [
            (leaf((own, sent_width), bf16), whole((own, sent_width))),
            (leaf((own, width), f32), whole((own, width))),
            (leaf((8, width), f32), whole((8, width))),
        ],
        [],
        "branch_gradient",
    )
    post_gain_part = post_gain_part[0]

    def scatter_z(values):
        return lax.psum_scatter(values, "fsdp", scatter_dimension=0, tiled=True)

    payload_parts = swaps(payload, n)
    unit = after(unit, payload)
    down_part = dot_tn(unit, upstream_all).astype(bf16)
    pair_grad = scatter_z(pair_part)

    def gather_rows(values):
        return lax.all_gather(values, "ctx", axis=0, tiled=False)

    payload = assemble(payload_parts)
    ffn_sums = scatter_parts(*split_columns(unit, down_own, "unit_out", [payload]), n, own_index)
    pair_all = gather_rows(after(pair_grad, payload))
    dattend_in = product_rows(
        [(payload, out_own)],
        0,
        total_rows,
        f32,
        "attended_backward",
        [down_part],
    )
    down_grad = scatter_z(after(down_part, dattend_in))
    dmixer_in = product_rows(
        [(payload, mixer_out_own)], 0, total_rows, f32, "gated_backward", [dattend_in]
    )

    dquery, dpair, normed_a, attend_gain_part = block_call(
        attention_backward_body(block, count),
        marks,
        1,
        attend_ins
        + [
            (attended, full(head_width)),
            (dattend_in, full(head_width + 128)),
            (payload, full(128, width // 128)),
        ],
        [
            (leaf((total_rows, head_width), bf16), full(head_width)),
            (leaf((total_rows, 2 * head_width), bf16), full(2 * head_width)),
            (leaf((total_rows, head_width), bf16), full(head_width)),
            (leaf((8, head_width), f32), whole((8, head_width))),
        ],
        [low_rows] * 6 + [wide_rows] * 2,
        "attention_backward",
    )
    dheads = jnp.concatenate([dquery, dot_nt(dpair, spread).astype(bf16)], axis=1)

    normed_s, dgate_z, dmixed_in, dselected_part, scan_vecs, step_part, decay_part = block_call(
        scan_backward_body(block),
        order,
        count,
        [
            (selected, rows(block, 256, reverse)),
            (mixed_in, rows(block, wide, reverse)),
            (projected, rows(block, 2 * held, reverse)),
            (scanned, rows(block, wide, reverse)),
            (dmixer_in, rows(block, wide, reverse)),
            (payload, columns_at(block, 128, reverse, width // 128)),
            (starts, start_spec(reverse)),
            (step_own, whole(step_own.shape)),
            (vecs, whole(vecs.shape)),
            (decay_own, whole(decay_own.shape)),
        ],
        [
            (leaf((total_rows, held), bf16), rows(block, held, reverse)),
            (leaf((total_rows, held), bf16), rows(block, held, reverse)),
            (leaf((total_rows, wide), f32), rows(block, wide, reverse)),
            (leaf((total_rows, 256), bf16), rows(block, 256, reverse)),
            (leaf((8, wide), f32), whole((8, wide))),
            (leaf((128, wide), f32), whole((128, wide))),
            (leaf((NS, wide), f32), whole((NS, wide))),
        ],
        [
            pltpu.VMEM((block // STEP, 2 * NS, STEP), f32),
            pltpu.VMEM((block, wide), f32),
            pltpu.VMEM((NS, wide), f32),
            pltpu.VMEM((block, wide), f32),
            pltpu.VMEM((block, wide), f32),
            pltpu.VMEM((block, wide), f32),
            pltpu.VMEM((block + 1, NS, wide), f32),
            pltpu.VMEM((block, NS, wide), f32),
            pltpu.VMEM((block * NS, 128), bf16),
            pltpu.VMEM((block * NS, 128), bf16),
            pltpu.VMEM((block * 8, wide), bf16),
            pltpu.VMEM((block * 8, wide), bf16),
        ],
        "scan_backward",
        [dpair],
    )
    dselected_part = after(dselected_part, pair_all)
    dselected_parts = scatter_parts(*halves(dselected_part), n, own_index)
    dselected = dselected_parts[0]
    for item in dselected_parts[1:]:
        dselected = dselected + item.astype(f32)
    dselected = gather_ctx(dselected.astype(bf16), n)
    hidden = after(hidden, dselected_parts[0])
    payload = after(payload, dselected_parts[0])
    mixer_part = dot_tn(normed_s, payload).astype(bf16)
    mixer_out_grad = scatter_z(mixer_part)


    out_part = dot_tn(after(normed_a, mixer_part), payload)[:, :width].astype(bf16)
    out_part = lax.all_to_all(
        jnp.moveaxis(out_part.reshape(head_width, n, out_piece), 1, 0), "ctx", 0, 0
    )
    out_part = out_part.reshape(n * head_width, out_piece)[:width]
    attend_part = jnp.concatenate(
        [dot_tn(hidden, dheads).astype(bf16), pad_to(out_part, 1, out_wide)], axis=1
    )
    attend_grad = scatter_z(attend_part)

    dprojected, select_part, filter_vecs = block_call(
        filter_backward_body(block, count),
        order,
        1,
        [
            (value, whole(value.shape))
            for value in (projected, dgate_z, mixed_in, dmixed_in, dselected, select_own, vecs)
        ],
        [
            (leaf((total_rows, 2 * held), bf16), whole((total_rows, 2 * held))),
            (leaf((256, wide), f32), whole((256, wide))),
            (leaf((8, wide), f32), whole((8, wide))),
        ],
        [
            pltpu.VMEM((block + 8, wide), f32),
            pltpu.VMEM((block + 8, wide), f32),
            pltpu.VMEM((block, 2 * held), f32),
            pltpu.VMEM((total_rows, wide), f32),
        ],
        "filter_backward",
        [attend_part, ffn_sums[0]],
    )
    in_part = dot_tn(hidden, dprojected).astype(bf16)
    in_grad = scatter_z(in_part)
    down_all = gather_rows(after(down_grad, in_part))
    hidden_near, hidden_far = split_rows(
        [(dprojected, in_weight), (dheads, attend_all)], "hidden_backward", [in_part]
    )
    half_rows = total_rows // 2
    first_gain_part = (
        jnp.sum(hidden_near.astype(f32) * hidden[:half_rows].astype(f32), axis=0)
        + jnp.sum(hidden_far.astype(f32) * hidden[half_rows:].astype(f32), axis=0)
    ) / first_gain[0]
    small_grad = jnp.concatenate(
        [
            select_part[:RANK],
            select_part[128 : 128 + 2 * NS],
            step_part[:RANK],
            decay_part,
            filter_vecs[4 : 4 + CONV],
            filter_vecs[3:4],
            scan_vecs[0:3],
        ]
    )[:, :held]
    attend_gain_full = lax.dynamic_update_slice_in_dim(
        jnp.zeros((1, n * head_width), f32), attend_gain_part[0:1], c * head_width, axis=1
    )[0, :width]
    gain_part = jnp.stack([first_gain_part, attend_gain_full, post_gain_part]).reshape(3, m, shard)
    gain_part = pad_to(
        jnp.moveaxis(gain_part, 1, 0).reshape(m, 3 * shard), 1, gain_rows * small_width
    )
    small_part = jnp.concatenate(
        [
            small_grad.T.reshape(m, piece_rows, small_width)[:, :piece],
            gain_part.reshape(m, gain_rows, small_width),
        ],
        axis=1,
    )
    small_grads = jnp.sum(lax.all_to_all(small_part, "fsdp", 0, 0), axis=0)
    dhidden = scatter_ctx(
        after(hidden_near, small_part), hidden_far, n, own_index
    )
    dfirst = norm_backward(inputs, first_norm, first_gain, dhidden)
    tokens_grad = (dmixed + dfirst).astype(bf16)[None]
    layer_out = mixed
    for item in ffn_sums:
        layer_out = layer_out + item.astype(f32)
    layer_out = layer_out.astype(bf16)[None]

    spots = jnp.array([masks(n).index(mask) for mask in range(n)], dtype=jnp.int32)
    plain = jnp.arange(n, dtype=jnp.int32)
    where = spots[c ^ plain]
    gate_grad, up_grad = unpack_columns(
        pair_all,
        plain,
        [
            (k, f * shard_hidden, hidden_piece, k * hidden_held + f * hidden_rows, hidden_piece)
            for k in range(2)
            for f in range(m)
        ],
        [weight.shape[1] for weight in (gate_weight, up_weight)],
        "unpack_pair",
    )
    down_turned = unpack_rows(
        down_all, plain, hidden_piece, width, True, "unpack_down"
    )
    mixer_out_grad = unpack_rows(
        swaps(mixer_out_grad, n), where, piece, width, False, "unpack_mixer"
    )
    attend_grad = swaps(attend_grad, n)
    kv_wide = n * pair
    out_at = head_width + 2 * pair
    query_grad, key_parts, value_parts, out_grad = unpack_columns(
        attend_grad,
        where,
        [
            (0, 0, head_width, 0, head_width),
            (1, 0, pair, head_width, pair),
            (2, 0, pair, head_width + pair, pair),
            (3, 0, out_piece, out_at, out_piece),
        ],
        [width, kv_wide, kv_wide, width],
        "unpack_attention",
    )

    def group_sum(parts):
        total = jnp.zeros((shard, kv_pad), f32)
        for index in range(n):
            low_at = min(index * heads // GROUP, KV_HEADS - 1) * HEAD_DIM
            item = parts[:, index * pair : (index + 1) * pair]
            total = total + jnp.pad(item, ((0, 0), (low_at, kv_pad - pair - low_at)))
        return total[:, : KV_HEADS * HEAD_DIM]

    in_grad = after(in_grad, query_grad)
    small_grads = jnp.stack(swaps(small_grads, n))[where]
    in_grad = swaps(in_grad, n)
    (mixer_in_grad,) = unpack_columns(
        in_grad,
        where,
        [
            (0, p * inner_all + f * shard_channels, piece, p * held + f * piece_rows, piece)
            for p in range(2)
            for f in range(m)
        ],
        [2 * inner_all],
        "unpack_inner",
    )
    small_sum = small_grads.reshape(n, piece + gain_rows, small_width)
    channel_grad = small_sum[:, :piece].reshape(shard_channels, small_width)
    gain_grad = jnp.sum(small_sum[:, piece:], axis=0).reshape(-1)[: 3 * shard].reshape(3, shard)

    at = RANK + 2 * NS
    select_grad = channel_grad[:, :at]
    step_grad = channel_grad[:, at : at + RANK].T
    at += RANK
    decay_grad = channel_grad[:, at : at + NS]
    at += NS
    kernel_grad = channel_grad[:, at : at + CONV].T
    at += CONV
    return (
        layer_out,
        tokens_grad,
        gain_grad[0],
        query_grad,
        group_sum(key_parts),
        group_sum(value_parts),
        out_grad,
        gain_grad[1],
        mixer_in_grad,
        kernel_grad,
        channel_grad[:, at],
        select_grad,
        step_grad,
        channel_grad[:, at + 1],
        decay_grad,
        channel_grad[:, at + 2],
        channel_grad[:, at + 3],
        mixer_out_grad,
        gain_grad[2],
        gate_grad,
        up_grad,
        down_turned.T,
    )


def solution(mesh):
    rows_spec = P("fsdp", None)
    lanes_spec = P(None, "fsdp")
    flat = P("fsdp")
    activations = P("fsdp", "ctx", None)
    weight_specs = (
        flat, rows_spec, rows_spec, rows_spec, rows_spec, flat, rows_spec, lanes_spec, flat, rows_spec,
        lanes_spec, flat, rows_spec, flat, flat, rows_spec, flat, rows_spec, rows_spec, rows_spec,
    )
    return jax.shard_map(
        on_device,
        mesh=mesh,
        in_specs=(activations, activations, P()) + weight_specs,
        out_specs=(activations, activations) + weight_specs,
        check_vma=False,
    )
```
